32 devices in a mesh: rows: 8 (over y, x, core), cols: 4 (over z).
Axes of the slice: x: 2, y: 2, z: 4, core: 2. Of those that a mesh axis runs over, the one named last changes fastest.
Arguments:
- inputs: bfloat16 [8, 64, 512, 77], P(None, 'rows', 'cols'), may hold values from -6 to 6
- targets: bfloat16 [8, 64, 512, 77], P(None, 'rows', 'cols'), may hold values from -6 to 6
- land_mask: int32 [64, 512], P('rows', 'cols'), may hold values 0 or 1
- volume: float32 [64, 512], P('rows', 'cols'), as said below
- date_index: int32 [2], replicated, may hold values from 0 to 7
- perm_narrow: int32 [800], replicated, may hold values from 0 to 799, each once
- perm_wide: int32 [3200], replicated, may hold values from 0 to 3199, each once
- w_in: bfloat16 [693, 200], replicated, may hold values from -0.21875 to 0.21875
- w_down: bfloat16 [800, 800], replicated, may hold values from -0.21875 to 0.21875
- w_dw: bfloat16 [49, 800], replicated, may hold values from -0.875 to 0.875
- w_hidden: bfloat16 [800, 3200], replicated, may hold values from -0.21875 to 0.21875
- w_out: bfloat16 [3200, 800], replicated, may hold values from -0.15625 to 0.15625
- w_up: bfloat16 [800, 800], replicated, may hold values from -0.21875 to 0.21875
- w_head: bfloat16 [200, 77], replicated, may hold values from -0.4375 to 0.4375
- biases_gains: float32 [7677], replicated
- moment_first: float32 [6602752], P(('rows', 'cols')), may hold values from -0.00061035156 to 0.00061035156
- moment_second: float32 [6602752], P(('rows', 'cols')), may hold values from 1.5300997e-09 to 6.120399e-09
Outputs:
- new_w_in: float32 [693, 200], replicated
- new_w_down: float32 [800, 800], replicated
- new_w_dw: float32 [49, 800], replicated
- new_w_hidden: float32 [800, 3200], replicated
- new_w_out: float32 [3200, 800], replicated
- new_w_up: float32 [800, 800], replicated
- new_w_head: float32 [200, 77], replicated
- new_biases_gains: float32 [7677], replicated
- first_moment: float32 [6602752], P(('rows', 'cols'))
- second_moment: float32 [6602752], P(('rows', 'cols'))
- loss_sum: float32 [], replicated
- loss_weight: float32 [], replicated
- grad_norm: float32 [], replicated
The draws below stay inside these ranges and needn't reach their ends.
Inputs may be any that keep to these rules, and one draw needn't show every extreme that they name: `perm_narrow`: each value once. `perm_wide`: each value once. `volume`: positive.
All inputs are finite; a program needn't handle non-finite values. No bound on the sum of `land_mask` on one device may be relied on, other than what follows from the above.
Results may differ from the reference program's by a relative error of at most 0.0017.
Values may be sent and summed in bfloat16 or wider, within the bound.
A program may use at most 256 MiB of HBM per device.

```python
import math
import jax
import jax.numpy as jnp
from jax import lax

CI = 77
C0 = 200
C1 = 800
CH = 3200
MB = 2
DATES = 8
STEP = 5
H = 64
W = 512
VEC = 7677
PARAMS = 6600877
PADP = 6602752


def draw_volume(key, part):
    key = jax.random.fold_in(key, 3)
    rows = jnp.arange(H, dtype=jnp.float32)[:, None] / H
    cols = jnp.arange(W, dtype=jnp.float32)[None, :] / W
    ramp = 1.0 + rows + cols
    rough = jnp.exp(jax.random.uniform(key, (H, W), jnp.float32, -0.7, 0.7))
    return ramp * rough


def draw_biases_gains(key, part):
    key = jax.random.fold_in(key, 5)
    noise = 0.3 * jax.random.normal(key, (VEC,), jnp.float32)
    place = jnp.arange(VEC)
    start = 2 * C0 + 2 * C1
    inside = (place >= start) & (place < start + C1)
    return jnp.where(inside, 1.0 + noise / 3.0, noise)


def with_ends(entries, rng, smallest, largest):
    shape = entries.shape
    index_at = [jax.random.randint(jax.random.fold_in(rng, axis), (), 0, shape[axis]) for axis in range(len(shape))]
    entries = entries.at[tuple(index_at)].set(smallest)
    longest = shape.index(max(shape))
    index_at[longest] = (index_at[longest] + 1) % shape[longest]
    return entries.at[tuple(index_at)].set(largest)


def level_of(key, extent, cuts, least, top_value):
    loudness, own = 1.0, jax.random.fold_in(key, 6)
    for dim, parts in cuts:
        heights = jnp.exp(jax.random.uniform(jax.random.fold_in(own, dim), (parts,), jnp.float32, least / len(cuts), top_value / len(cuts)))
        loudness = loudness * jnp.repeat(heights, extent[dim] // parts).reshape([-1 if axis == dim else 1 for axis in range(len(extent))])
    return loudness


def gaussian(rng, dims, scale, limit, cuts=(), kind=jnp.bfloat16):
    array = scale * jax.random.normal(rng, dims, jnp.float32)
    if cuts:
        array = array * level_of(rng, dims, cuts, -0.22, 0.18)
    return jnp.clip(array, -limit, limit).astype(kind)


def setup_inputs(seed: int = 0) -> dict:
    seeds = jax.random.split(jax.random.key(seed), 18)
    return {
        "inputs": gaussian(seeds[0], (DATES, H, W, CI), 1.0, 6.0, ((1, 8), (2, 4))),
        "targets": gaussian(seeds[1], (DATES, H, W, CI), 1.0, 6.0, ((1, 8), (2, 4))),
        "land_mask": with_ends((jax.random.randint(seeds[2], (H, W), 0, 10) < 7).astype(jnp.int32), jax.random.fold_in(seeds[2], 1), 0, 1),
        "volume": draw_volume(jax.random.fold_in(seeds[17], 71), 0),
        "date_index": jax.random.randint(seeds[4], (MB,), 0, DATES).astype(jnp.int32),
        "perm_narrow": jax.random.permutation(seeds[5], C1).astype(jnp.int32),
        "perm_wide": jax.random.permutation(seeds[6], CH).astype(jnp.int32),
        "w_in": gaussian(seeds[7], (9 * CI, C0), (9 * CI) ** -0.5, 0.21875),
        "w_down": gaussian(seeds[8], (4 * C0, C1), (4 * C0) ** -0.5, 0.21875),
        "w_dw": gaussian(seeds[9], (49, C1), 49 ** -0.5, 0.875),
        "w_hidden": gaussian(seeds[10], (C1, CH), C1 ** -0.5, 0.21875),
        "w_out": gaussian(seeds[11], (CH, C1), (CH // 2) ** -0.5, 0.15625),
        "w_up": gaussian(seeds[12], (C1, 4 * C0), C1 ** -0.5, 0.21875),
        "w_head": gaussian(seeds[13], (C0, CI), C0 ** -0.5, 0.4375),
        "biases_gains": draw_biases_gains(jax.random.fold_in(seeds[17], 71), 0),
        "moment_first": gaussian(seeds[15], (PADP,), (0.111 / PARAMS ** 0.5), 0.00061035156, ((0, 32),), jnp.float32),
        "moment_second": jnp.clip(jnp.exp(math.log(6.120398854392306e-09) - 1.3862944 * jax.random.uniform(seeds[16], (PADP,), jnp.float32) ** level_of(seeds[16], (PADP,), ((0, 32),), -0.2, 0.2)), 1.5300997135980765e-09, 6.120398854392306e-09),
    }


@jax.custom_vjp
def low(v):
    return lax.optimization_barrier(v.astype(jnp.bfloat16)).astype(jnp.float32)

@jax.custom_vjp
def low_back(v):
    return v

def low_keep(v):
    return (low(v), None)

def low_pass(kept, grad):
    return (grad,)

def back_keep(v):
    return (v, None)

def back_low(kept, grad):
    return (low(grad),)
low.defvjp(low_keep, low_pass)
low_back.defvjp(back_keep, back_low)
decay_first = 0.9
decay_second = 0.99
epsilon = 1e-08
learn_rate = 0.02
weight_decay = 0.1
clip_limit = 1.0

def matmul(left, right):
    return jnp.einsum('...i,ij->...j', left, right, precision=lax.Precision.HIGHEST)

def split_vector(vector):
    lengths = [C0, C1, C1, C1, C1, CH, C1, C0, CI]
    pieces = []
    start = 0
    for length in lengths:
        pieces.append(vector[start:start + length])
        start = start + length
    return pieces

def padded_map(field, width):
    field = jnp.pad(field, ((width, width), (0, 0), (0, 0)))
    return jnp.concatenate([field[:, -width:], field, field[:, :width]], axis=1)

def input_conv(field, w_in):
    height, breadth = (field.shape[0], field.shape[1])
    padded = padded_map(field, 1)
    total = jnp.zeros((height, breadth, C0), jnp.float32)
    for shift_y in range(3):
        for shift_x in range(3):
            tap = shift_y * 3 + shift_x
            total = total + matmul(padded[shift_y:shift_y + height, shift_x:shift_x + breadth], w_in[tap * CI:(tap + 1) * CI])
    return total

def depthwise(field, w_dw):
    height, breadth = (field.shape[0], field.shape[1])
    padded = padded_map(field, 3)
    total = jnp.zeros(field.shape, jnp.float32)
    for shift_y in range(7):
        for shift_x in range(7):
            total = total + padded[shift_y:shift_y + height, shift_x:shift_x + breadth] * w_dw[shift_y * 7 + shift_x]
    return total

def forward(params, state, target, weight):
    w_in, w_down, w_dw, w_hidden, w_out, w_up, w_head, vector = params
    b_in, b_down, b_dw, gain, shift, b_hidden, b_out, b_up, b_head = split_vector(vector)
    height, breadth = (state.shape[0], state.shape[1])
    half_h, half_w = (height // 2, breadth // 2)
    a_zero = low_back(input_conv(state, w_in) + b_in)
    h_zero = jax.nn.gelu(a_zero)
    h_low = low(h_zero)
    patches = h_low.reshape(half_h, 2, half_w, 2, C0).transpose(0, 2, 1, 3, 4).reshape(half_h, half_w, 4 * C0)
    coarse = low_back(matmul(patches, w_down) + b_down)
    coarse_low = low(coarse)
    conv_out = low_back(depthwise(coarse_low, w_dw) + b_dw)
    mean = lax.optimization_barrier(jnp.mean(conv_out, -1, keepdims=True))
    centered = conv_out - mean
    var = lax.optimization_barrier(jnp.mean(centered * centered, -1, keepdims=True))
    normed = low(centered * lax.rsqrt(var + 1e-06) * gain + shift)

    def pointwise(row):
        pre = low_back(matmul(row, w_hidden) + b_hidden)
        act = low(jax.nn.gelu(pre))
        return low_back(matmul(act, w_out) + b_out)
    branch = lax.map(jax.checkpoint(pointwise), normed)
    mixed = low(coarse + branch)
    upper = low_back(matmul(mixed, w_up) + jnp.tile(b_up, 4))
    upper = upper.reshape(half_h, half_w, 2, 2, C0).transpose(0, 2, 1, 3, 4).reshape(height, breadth, C0)
    summed = low(upper + h_zero)
    output = low_back(matmul(summed, w_head) + b_head)
    error = output - target
    return jnp.sum(weight[:, :, None] * error * error)

def reference(inputs, targets, land_mask, volume, date_index, perm_narrow, perm_wide, w_in, w_down, w_dw, w_hidden, w_out, w_up, w_head, biases_gains, moment_first, moment_second):
    matrices = tuple((m.astype(jnp.float32) for m in (w_in, w_down, w_dw, w_hidden, w_out, w_up, w_head)))
    params = matrices + (biases_gains,)
    weight = land_mask.astype(jnp.float32) * volume

    def total_loss(params):

        def one_batch(carry, date):
            state = lax.dynamic_index_in_dim(inputs, date, 0, keepdims=False).astype(jnp.float32)
            target = lax.dynamic_index_in_dim(targets, date, 0, keepdims=False).astype(jnp.float32)
            return (carry + jax.checkpoint(forward)(params, state, target, weight), None)
        loss, unused = lax.scan(one_batch, jnp.zeros((), jnp.float32), date_index)
        return loss
    loss_sum, pull = jax.vjp(total_loss, params)
    grads = pull(jnp.ones((), jnp.float32))[0]
    rotated = list(grads)
    rotated[3] = grads[3][perm_narrow][:, perm_wide]
    rotated[4] = grads[4][perm_wide][:, perm_narrow]
    flat = jnp.concatenate([g.reshape(-1) for g in rotated])
    lead = moment_first.shape[0] - flat.shape[0]
    flat = jnp.pad(flat, (lead, 0))
    grad_norm = jnp.sqrt(jnp.sum(flat * flat))
    clipped = flat * jnp.minimum(1.0, clip_limit / grad_norm)
    first = decay_first * moment_first + (1.0 - decay_first) * clipped
    second = decay_second * moment_second + (1.0 - decay_second) * clipped * clipped
    direction = first / (1.0 - decay_first ** STEP) / (jnp.sqrt(second / (1.0 - decay_second ** STEP)) + epsilon)
    news = []
    start = lead
    back_narrow = jnp.argsort(perm_narrow)
    back_wide = jnp.argsort(perm_wide)
    for index, old in enumerate(params):
        count = old.size
        piece = direction[start:start + count].reshape(old.shape)
        start = start + count
        if index == 3:
            piece = piece[back_narrow][:, back_wide]
        if index == 4:
            piece = piece[back_wide][:, back_narrow]
        if index < 7:
            news.append(old * (1.0 - learn_rate * weight_decay) - learn_rate * piece)
        else:
            news.append(old - learn_rate * piece)
    loss_weight = MB * CI * jnp.sum(weight)
    return (news[0], news[1], news[2], news[3], news[4], news[5], news[6], news[7], first, second, loss_sum, loss_weight, grad_norm)
```

```python
import functools

import jax
import jax.numpy as jnp
from jax import lax
from jax.experimental import pallas as pl
from jax.experimental.pallas import tpu as pltpu
from jax.sharding import PartitionSpec as P

CI = 77
C0 = 200
C1 = 800
CH = 3200
MB = 2
STEP = 5
LANES = 128
MESH = pl.DeviceIdType.MESH
ROUNDER = 12582912.0

decay_first = 0.9
decay_second = 0.99
epsilon = 1e-08
learn_rate = 0.02
weight_decay = 0.1
clip_limit = 1.0

VEC = 4 * C1 + CH + C1 + 2 * C0 + CI
SIZES = (9 * CI * C0, 4 * C0 * C1, 49 * C1, C1 * CH, CH * C1, C1 * 4 * C0, C0 * CI, VEC)
PADDED = 6602752
FLAT_AT = []
ROW_AT = []
for size in SIZES:
    flat_here = FLAT_AT[-1] + SIZES[len(FLAT_AT) - 1] if FLAT_AT else PADDED - sum(SIZES)
    row_here = ROW_AT[-1] + -(-SIZES[len(ROW_AT) - 1] // 1024) * 8 if ROW_AT else 0
    row_here = max(row_here, -(-flat_here // 1024) * 8)
    FLAT_AT.append(flat_here)
    ROW_AT.append(row_here)
SHIFTS = []
for flat_here, row_here, size in zip(FLAT_AT, ROW_AT, SIZES):
    moved = divmod(row_here * LANES - flat_here, LANES)
    if SHIFTS and SHIFTS[-1][:2] == moved:
        SHIFTS[-1] = moved + (SHIFTS[-1][2], flat_here + size)
    else:
        SHIFTS.append(moved + (flat_here, flat_here + size))
MAX_SHIFT = max(s[0] for s in SHIFTS) + 1


def bit_masks(bits):
    masks = [()]
    for bit in bits:
        masks = masks + [m + (bit,) for m in masks]
    return sorted(masks, key=lambda m: -len(m))


class Plan:
    def __init__(self, rows, cols, total):
        self.rows, self.cols, self.count = rows, cols, rows * cols
        self.share = total // LANES // self.count
        self.bits = rows.bit_length() - 1
        need = 7 + self.share + MAX_SHIFT + 1
        self.block = 64 if need > 1024 else 32
        self.window = -(-need // (2 * self.block)) * 2 * self.block
        self.part = self.window // 2
        self.blocks = self.part // self.block
        self.scales = self.blocks
        upper = list(range(1, self.bits))
        self.orders = [upper, upper[1:] + upper[:1]]
        self.stages = len(upper)
        self.space = (self.share * (self.count - 1)) // 8 * 8 + self.window
        self.padded = -(-self.share // 16) * 16
        cut = -(-self.padded // 32) * 16
        self.cuts = [(0, cut), (cut, self.padded - cut)]
        self.local = self.count // 2


def exchange_kernel(
    plan, grad, m_first, m_second, extra, full, first, second, totals,
    acc, near, q_send, q_recv, s_send, s_recv, z_send, z_recv, zs_send, zs_recv,
    rolled, step, low, stats,
    sem_load, sem_near_s, sem_near_r, sem_qs, sem_qr, sem_ss, sem_sr,
    sem_zs, sem_zr, sem_zss, sem_zsr, sem_ts, sem_tr, sem_own,
    sem_gs, sem_gr, sem_hs, sem_hr, sem_cs, sem_cr,
):
    nr, nc, n = plan.rows, plan.cols, plan.count
    r = lax.axis_index("rows")
    c = lax.axis_index("cols")
    me = r * nc + c
    part, window, share = plan.part, plan.window, plan.share

    def flipped(mask):
        out = r
        for bit in mask:
            here = (r // (1 << bit)) % 2
            out = out + (1 - 2 * here) * (1 << bit)
        return out

    def remote(src, dst, send, recv, row, col):
        return pltpu.make_async_remote_copy(
            src_ref=src, dst_ref=dst, send_sem=send, recv_sem=recv,
            device_id=(row, col), device_id_type=MESH,
        )

    barrier = pltpu.get_barrier_semaphore()

    def greet(d, carry):
        k = lax.rem(me + d, n)
        pl.semaphore_signal(barrier, inc=1, device_id=(k // nc, k % nc), device_id_type=MESH)
        return carry

    lax.fori_loop(1, n, greet, 0)
    pl.semaphore_wait(barrier, n - 1)

    upper = list(range(1, plan.bits))
    masks = bit_masks(upper)

    def local_index(mask, col):
        return (flipped(mask) // 2) * nc + col

    def window_start(row, col):
        return pl.multiple_of((share * (row * nc + col)) // 8 * 8, 8)

    def near_copy(mask, col):
        row = flipped(mask + (0,))
        return remote(
            grad.at[pl.ds(window_start(row, col), window)],
            near.at[local_index(mask, col)],
            sem_near_s.at[local_index(mask, col)], sem_near_r.at[local_index(mask, col)],
            flipped((0,)), c,
        )

    def load_copy(mask, col):
        index = local_index(mask, col)
        return pltpu.make_async_copy(
            grad.at[pl.ds(window_start(flipped(mask), col), window)], acc.at[index], sem_load.at[index]
        )

    for mask in masks:
        def begin(col, carry, mask=mask):
            near_copy(mask, col).start()
            load_copy(mask, col).start()
            return carry

        lax.fori_loop(0, nc, begin, 0)

    def encode(index, p, q_ref, s_ref):
        def body(b, carry):
            at = pl.ds(pl.multiple_of(b * plan.block, plan.block), plan.block)
            rows_at = pl.ds(pl.multiple_of(p * part + b * plan.block, 8), plan.block)
            values = acc[index, rows_at, :]
            top = jnp.maximum(jnp.max(jnp.abs(values), axis=0, keepdims=True), 1e-30)
            scaled = values * (32766.0 / top)
            scaled = (scaled + ROUNDER) - ROUNDER
            q_ref[at, :] = scaled.astype(jnp.int32).astype(jnp.int16)
            s_ref[pl.ds(b, 1), :] = top * (1.0 / 32766.0)
            return carry

        lax.fori_loop(0, plan.blocks, body, 0)

    def decode(index, p, q_ref, s_ref):
        def body(b, carry):
            at = pl.ds(pl.multiple_of(b * plan.block, plan.block), plan.block)
            rows_at = pl.ds(pl.multiple_of(p * part + b * plan.block, 8), plan.block)
            acc[index, rows_at, :] += q_ref[at, :].astype(jnp.float32) * s_ref[pl.ds(b, 1), :]
            return carry

        lax.fori_loop(0, plan.blocks, body, 0)

    def stage_base(stage):
        return sum((1 << (plan.stages - 1 - s)) for s in range(stage)) * nc

    def hop(p, stage, slot):
        row = flipped((plan.orders[p][stage],))
        at = stage_base(stage) + slot
        return (
            remote(q_send.at[p, at], q_recv.at[p, at], sem_qs.at[p, at], sem_qr.at[p, at], row, c),
            remote(s_send.at[p, at], s_recv.at[p, at], sem_ss.at[p, at], sem_sr.at[p, at], row, c),
        )

    def send_stage(p, stage, number, mask, col):
        bit = plan.orders[p][stage]
        index = local_index(mask + (bit,), col)
        slot = number * nc + col
        at = stage_base(stage) + slot
        encode(index, p, q_send.at[p, at], s_send.at[p, at])
        for copy in hop(p, stage, slot):
            copy.start()

    def take_stage(p, stage, number, mask, col):
        slot = number * nc + col
        for copy in hop(p, stage, slot):
            copy.wait_recv()
        at = stage_base(stage) + slot
        decode(local_index(mask, col), p, q_recv.at[p, at], s_recv.at[p, at])

    def free_masks(p, stage):
        rest = plan.orders[p][stage + 1 :]
        found = bit_masks(rest)
        if rest:
            found = [m for m in found if rest[0] in m] + [m for m in found if rest[0] not in m]
        return found

    for mask in masks:
        def join(col, carry, mask=mask):
            index = local_index(mask, col)
            near_copy(mask, col).wait_recv()
            load_copy(mask, col).wait()

            def body(b, inner):
                at = pl.ds(pl.multiple_of(b * plan.block, plan.block), plan.block)
                acc[index, at, :] += near[index, at, :]
                return inner

            lax.fori_loop(0, 2 * plan.blocks, body, 0)
            for p in range(2):
                bit = plan.orders[p][0]
                if bit in mask:
                    rest = tuple(b for b in mask if b != bit)
                    options = free_masks(p, 0)
                    number = [sorted(o) for o in options].index(sorted(rest))
                    send_stage(p, 0, number, rest, col)
            return carry

        lax.fori_loop(0, nc, join, 0)

    def far_copy(p, d):
        col = lax.rem(c + d, nc)
        return (
            remote(z_send.at[p, d - 1], z_recv.at[p, d - 1], sem_zs.at[p, d - 1], sem_zr.at[p, d - 1], r, col),
            remote(zs_send.at[p, d - 1], zs_recv.at[p, d - 1], sem_zss.at[p, d - 1], sem_zsr.at[p, d - 1], r, col),
        )

    for stage in range(plan.stages):
        for number in range(1 << (plan.stages - 1 - stage)):
            def take(d, carry, stage=stage, number=number):
                col = lax.rem(c + d, nc)
                for p in range(2):
                    mask = free_masks(p, stage)[number]
                    take_stage(p, stage, number, mask, col)
                    if stage + 1 < plan.stages:
                        bit = plan.orders[p][stage + 1]
                        if bit in mask:
                            rest = tuple(b for b in mask if b != bit)
                            options = free_masks(p, stage + 1)
                            following = [sorted(o) for o in options].index(sorted(rest))
                            send_stage(p, stage + 1, following, rest, col)
                return carry

            if stage + 1 < plan.stages:
                lax.fori_loop(1, nc + 1, take, 0)
            else:
                def take_last(d, carry, take=take):
                    take(d, 0)
                    col = lax.rem(c + d, nc)
                    for p in range(2):
                        encode(local_index((), col), p, z_send.at[p, d - 1], zs_send.at[p, d - 1])
                        for copy in far_copy(p, d):
                            copy.start()
                    return carry

                lax.fori_loop(1, nc, take_last, 0)
                take(nc, 0)

    mine = local_index((), c)

    def gather_far(d, carry):
        for p in range(2):
            for copy in far_copy(p, d):
                copy.wait_recv()
            decode(mine, p, z_recv.at[p, d - 1], zs_recv.at[p, d - 1])
        return carry

    lax.fori_loop(1, nc, gather_far, 0)

    offset = lax.rem(share * me, 8)
    for number, (shift_rows, shift_lanes, begin, end) in enumerate(SHIFTS):
        def turn(b, carry, number=number, shift_lanes=shift_lanes):
            at = pl.ds(pl.multiple_of(b * plan.block, plan.block), plan.block)
            rolled[number, at, :] = pltpu.roll(acc[mine, at, :], LANES - shift_lanes, 1)
            return carry

        lax.fori_loop(0, 2 * plan.blocks, turn, 0)

    def share_rows(start, length):
        lane = lax.broadcasted_iota(jnp.int32, (length, LANES), 1)
        line = lax.broadcasted_iota(jnp.int32, (length, LANES), 0)
        flat = (share * me + start + line) * LANES + lane
        out = jnp.zeros((length, LANES), jnp.float32)
        for number, (shift_rows, shift_lanes, begin, end) in enumerate(SHIFTS):
            here = rolled[number, pl.ds(offset + start + shift_rows, length), :]
            after = rolled[number, pl.ds(offset + start + shift_rows + 1, length), :]
            value = jnp.where(lane < LANES - shift_lanes, here, after)
            out = jnp.where((flat >= begin) & (flat < end), value, out)
        return out

    chunk = 32
    whole, tail = share // chunk, share % chunk

    def square(b, total):
        start = pl.multiple_of(b * chunk, chunk)
        value = share_rows(start, chunk)
        step[pl.ds(start, chunk), :] = value
        return total + jnp.sum((value * value).reshape(chunk // 8, 8, LANES), axis=0)

    total = lax.fori_loop(0, whole, square, jnp.zeros((8, LANES), jnp.float32))
    stats[me, 8:16, :] = extra[...]
    stats[me, 0:8, :] = total
    if tail:
        value = share_rows(whole * chunk, tail)
        step[whole * chunk : share, :] = value
        stats[me, 0:1, :] += jnp.sum(value * value, axis=0, keepdims=True)

    def stat_copy(target, source):
        return remote(
            stats.at[me], stats.at[me], sem_ts.at[target], sem_tr.at[me], target // nc, target % nc
        )

    def stat_wait(source):
        return remote(
            stats.at[source], stats.at[source], sem_ts.at[source], sem_tr.at[source],
            source // nc, source % nc,
        )

    def send_stat(d, carry):
        stat_copy(lax.rem(me + d, n), me).start()
        return carry

    lax.fori_loop(1, n, send_stat, 0)

    def wait_stat(d, carry):
        stat_wait(lax.rem(me + d, n)).wait_recv()
        return carry

    lax.fori_loop(1, n, wait_stat, 0)

    def add_stat(k, total):
        return total + stats[k]

    sums = lax.fori_loop(0, n, add_stat, jnp.zeros((16, LANES), jnp.float32))
    norm = jnp.sqrt(jnp.sum(sums[0:8], keepdims=True))
    totals[0:8, :] = sums[8:16]
    totals[8:16, :] = jnp.broadcast_to(norm, (8, LANES))
    clip = jnp.minimum(1.0, clip_limit / norm)

    def update(start, length):
        clipped = step[pl.ds(start, length), :] * clip
        one = decay_first * m_first[pl.ds(start, length), :] + (1.0 - decay_first) * clipped
        two = decay_second * m_second[pl.ds(start, length), :] + (1.0 - decay_second) * clipped * clipped
        first[pl.ds(start, length), :] = one
        second[pl.ds(start, length), :] = two
        step[pl.ds(start, length), :] = (
            one / (1.0 - decay_first**STEP) / (jnp.sqrt(two / (1.0 - decay_second**STEP)) + epsilon)
        )

    def update_chunk(b, carry):
        update(pl.multiple_of(b * chunk, chunk), chunk)
        return carry

    lax.fori_loop(0, whole, update_chunk, 0)
    if tail:
        update(whole * chunk, tail)
    if plan.padded > share:
        step[share : plan.padded, :] = jnp.zeros((plan.padded - share, LANES), jnp.float32)

    def narrow(b, carry):
        at = pl.ds(pl.multiple_of(b * 16, 16), 16)
        low[at, :] = step[at, :].astype(jnp.bfloat16)
        return carry

    lax.fori_loop(0, plan.padded // 16, narrow, 0)

    own = pltpu.make_async_copy(low, full.at[me], sem_own)
    own.start()
    own.wait()

    back = [list(reversed(order)) for order in plan.orders]

    def piece(mask, col, p):
        begin, length = plan.cuts[p]
        return full.at[flipped(mask) * nc + col, pl.ds(begin, length)]

    def along(direction, col, p, receive):
        step_col = 1 if direction == 0 else -1
        target = c - step_col if receive else c + step_col
        ref = piece((), col, p)
        return remote(ref, ref, sem_gs.at[direction, col, p], sem_gr.at[direction, col, p], r, target)

    def gather_masks(p, stage):
        return bit_masks(back[p][:stage])

    def gather_base(stage):
        return sum(1 << s for s in range(stage)) * nc

    def across(p, stage, number, mask, col):
        at = gather_base(stage) + number * nc + col
        ref = piece(mask, col, p)
        return remote(ref, ref, sem_hs.at[p, at], sem_hr.at[p, at], flipped((back[p][stage],)), c)

    def across_recv(p, stage, number, mask, col):
        at = gather_base(stage) + number * nc + col
        ref = piece(mask + (back[p][stage],), col, p)
        return remote(ref, ref, sem_hs.at[p, at], sem_hr.at[p, at], flipped((back[p][stage],)), c)

    def inward(p, mask, col):
        number = masks.index(tuple(sorted(mask)))
        at = number * nc + col
        ref = piece(mask, col, p)
        return remote(ref, ref, sem_cs.at[p, at], sem_cr.at[p, at], flipped((0,)), c)

    def inward_recv(p, mask, col):
        number = masks.index(tuple(sorted(mask)))
        at = number * nc + col
        ref = piece(mask + (0,), col, p)
        return remote(ref, ref, sem_cs.at[p, at], sem_cr.at[p, at], flipped((0,)), c)

    def spread(p, mask, col, stage):
        for later in range(stage, plan.stages):
            options = [sorted(o) for o in gather_masks(p, later)]
            if sorted(mask) in options:
                across(p, later, options.index(sorted(mask)), mask, col).start()
        inward(p, mask, col).start()

    def near_cols(t):
        if t == 0:
            return [(0, c)]
        return [(0, c - t), (1, c + t)]

    def inside(col):
        return (col >= 0) & (col < nc)

    for time in range(nc + plan.stages):
        for stage in range(plan.stages + 1):
            t = time - stage
            if not 0 <= t < nc:
                continue
            if stage == 0:
                if t == 0:
                    for p in range(2):
                        @pl.when(c < nc - 1)
                        def _(p=p):
                            along(0, c, p, False).start()

                        @pl.when(c > 0)
                        def _(p=p):
                            along(1, c, p, False).start()

                        spread(p, (), c, 0)
                else:
                    for direction, col in near_cols(t):
                        @pl.when(inside(col))
                        def _(direction=direction, col=col):
                            for p in range(2):
                                along(direction, col, p, True).wait_recv()
                                if direction == 0:
                                    @pl.when(c < nc - 1)
                                    def _():
                                        along(0, col, p, False).start()
                                else:
                                    @pl.when(c > 0)
                                    def _():
                                        along(1, col, p, False).start()
                                spread(p, (), col, 0)
            else:
                for direction, col in near_cols(t):
                    @pl.when(inside(col))
                    def _(col=col, stage=stage):
                        for number in range(1 << (stage - 1)):
                            for p in range(2):
                                mask = gather_masks(p, stage - 1)[number]
                                across_recv(p, stage - 1, number, mask, col).wait_recv()
                                spread(p, mask + (back[p][stage - 1],), col, stage)

    for mask in masks:
        def finish(col, carry, mask=mask):
            for p in range(2):
                inward_recv(p, mask, col).wait_recv()
                inward(p, mask, col).wait_send()
            near_copy(mask, col).wait_send()
            return carry

        lax.fori_loop(0, nc, finish, 0)
    for p in range(2):
        for stage in range(plan.stages):
            for number, mask in enumerate(gather_masks(p, stage)):
                def sent(col, carry, p=p, stage=stage, number=number, mask=mask):
                    across(p, stage, number, mask, col).wait_send()
                    return carry

                lax.fori_loop(0, nc, sent, 0)
            for number in range(1 << (plan.stages - 1 - stage)):
                def left(col, carry, p=p, stage=stage, number=number):
                    for copy in hop(p, stage, number * nc + col):
                        copy.wait_send()
                    return carry

                lax.fori_loop(0, nc, left, 0)

        def gone(col, carry, p=p):
            @pl.when((col <= c) & (c < nc - 1))
            def _():
                along(0, col, p, False).wait_send()

            @pl.when((col >= c) & (c > 0))
            def _():
                along(1, col, p, False).wait_send()

            return carry

        lax.fori_loop(0, nc, gone, 0)

        def far_gone(d, carry, p=p):
            for copy in far_copy(p, d):
                copy.wait_send()
            return carry

        lax.fori_loop(1, nc, far_gone, 0)

    def stat_gone(d, carry):
        stat_copy(lax.rem(me + d, n), me).wait_send()
        return carry

    lax.fori_loop(1, n, stat_gone, 0)


def exchange(rows, cols, grad, m_first, m_second, extra):
    plan = Plan(rows, cols, m_first.size * rows * cols)
    n, nc, share = plan.count, plan.cols, plan.share
    hops = sum(1 << s for s in range(plan.stages)) * nc
    dma = pltpu.SemaphoreType.DMA
    far = max(nc - 1, 1)
    vmem = pl.BlockSpec(memory_space=pltpu.VMEM)
    hbm = pl.BlockSpec(memory_space=pl.ANY)
    return plan, pl.pallas_call(
        functools.partial(exchange_kernel, plan),
        out_shape=(
            jax.ShapeDtypeStruct((n, plan.padded, LANES), jnp.bfloat16),
            jax.ShapeDtypeStruct((share, LANES), jnp.float32),
            jax.ShapeDtypeStruct((share, LANES), jnp.float32),
            jax.ShapeDtypeStruct((16, LANES), jnp.float32),
        ),
        in_specs=[hbm, vmem, vmem, vmem],
        out_specs=(hbm, vmem, vmem, vmem),
        scratch_shapes=[
            pltpu.VMEM((plan.local, plan.window, LANES), jnp.float32),
            pltpu.VMEM((plan.local, plan.window, LANES), jnp.float32),
            pltpu.VMEM((2, hops, plan.part, LANES), jnp.int16),
            pltpu.VMEM((2, hops, plan.part, LANES), jnp.int16),
            pltpu.VMEM((2, hops, plan.scales, LANES), jnp.float32),
            pltpu.VMEM((2, hops, plan.scales, LANES), jnp.float32),
            pltpu.VMEM((2, far, plan.part, LANES), jnp.int16),
            pltpu.VMEM((2, far, plan.part, LANES), jnp.int16),
            pltpu.VMEM((2, far, plan.scales, LANES), jnp.float32),
            pltpu.VMEM((2, far, plan.scales, LANES), jnp.float32),
            pltpu.VMEM((len(SHIFTS), plan.window, LANES), jnp.float32),
            pltpu.VMEM((plan.padded, LANES), jnp.float32),
            pltpu.VMEM((plan.padded, LANES), jnp.bfloat16),
            pltpu.VMEM((n, 16, LANES), jnp.float32),
            dma((plan.local,)), dma((plan.local,)), dma((plan.local,)),
            dma((2, hops)), dma((2, hops)), dma((2, hops)), dma((2, hops)),
            dma((2, far)), dma((2, far)), dma((2, far)), dma((2, far)),
            dma((n,)), dma((n,)), dma,
            dma((2, nc, 2)), dma((2, nc, 2)),
            dma((2, hops)), dma((2, hops)),
            dma((2, plan.local)), dma((2, plan.local)),
        ],
        compiler_params=pltpu.CompilerParams(
            collective_id=0, has_side_effects=True, vmem_limit_bytes=56 << 20
        ),
    )(grad, m_first.reshape(share, LANES), m_second.reshape(share, LANES), extra)


def padded_2(cells, sides, width):
    for axis, dim in sides:
        count = lax.axis_size(axis)
        head = lax.slice_in_dim(cells, 0, width, axis=dim)
        tail = lax.slice_in_dim(cells, cells.shape[dim] - width, cells.shape[dim], axis=dim)
        cells = jnp.concatenate(
            [
                lax.ppermute(tail, axis, [(i, (i + 1) % count) for i in range(count)]),
                cells,
                lax.ppermute(head, axis, [((i + 1) % count, i) for i in range(count)]),
            ],
            axis=dim,
        )
    return cells


def split_vector(vector):
    lengths = [C0, C1, C1, C1, C1, CH, C1, C0, CI]
    pieces = []
    start = 0
    for length in lengths:
        pieces.append(vector[start : start + length])
        start = start + length
    return pieces


def product(left, right):
    return jnp.dot(left, right, preferred_element_type=jnp.float32)


def inner_rows(left, right):
    return jnp.einsum("nk,nd->kd", left, right, preferred_element_type=jnp.float32)


def outer_cols(left, right):
    return jnp.einsum("nd,kd->nk", left, right, preferred_element_type=jnp.float32)


def column_sum(values):
    return jnp.sum(values, axis=0, dtype=jnp.float32)


def clear_edges(padded, width):
    place = lax.axis_index("rows")
    count = lax.axis_size("rows")
    line = jnp.arange(padded.shape[1])[None, :, None, None]
    top = (place == 0) & (line < width)
    bottom = (place == count - 1) & (line >= padded.shape[1] - width)
    return jnp.where(top | bottom, jnp.zeros((), padded.dtype), padded)


def to_coarse(field, height, breadth):
    chans = field.shape[-1]
    return (
        field.reshape(MB, height // 2, 2, breadth // 2, 2, chans)
        .transpose(0, 1, 3, 2, 4, 5)
        .reshape(-1, 4 * chans)
    )


def to_fine(field, height, breadth):
    chans = field.shape[-1] // 4
    return (
        field.reshape(MB, height // 2, breadth // 2, 2, 2, chans)
        .transpose(0, 1, 3, 2, 4, 5)
        .reshape(-1, chans)
    )


def layer_norm(values, gain, shift):
    mean = jnp.mean(values, -1, keepdims=True)
    centered = values - mean
    var = jnp.mean(centered * centered, -1, keepdims=True)
    return centered * lax.rsqrt(var + 1e-06) * gain + shift


def depthwise(padded, w_dw, height, breadth, back):
    total = jnp.zeros((MB, height, breadth, padded.shape[-1]), jnp.float32)
    for y in range(7):
        for x in range(7):
            at_y, at_x = (6 - y, 6 - x) if back else (y, x)
            window = padded[:, at_y : at_y + height, at_x : at_x + breadth].astype(jnp.float32)
            total = total + window * w_dw[y * 7 + x].astype(jnp.float32)
    return total


def depthwise_kernel_grad(padded, grad_map, height, breadth):
    rows_out = []
    grad_float = grad_map.astype(jnp.float32)
    for y in range(7):
        for x in range(7):
            window = padded[:, y : y + height, x : x + breadth].astype(jnp.float32)
            rows_out.append(jnp.sum(window * grad_float, axis=(0, 1, 2)))
    return jnp.stack(rows_out)


def as_rows(piece, rows):
    flat = piece.reshape(-1)
    return jnp.pad(flat, (0, rows * LANES - flat.shape[0])).reshape(rows, LANES)


def on_device(
    inputs,
    targets,
    land_mask,
    volume,
    date_index,
    perm_narrow,
    perm_wide,
    w_in,
    w_down,
    w_dw,
    w_hidden,
    w_out,
    w_up,
    w_head,
    biases_gains,
    moment_first,
    moment_second,
):
    b_in, b_down, b_dw, gain, shift, b_hidden, b_out, b_up, b_head = split_vector(biases_gains)
    weight = land_mask.astype(jnp.float32) * volume
    height, breadth = weight.shape
    half_h, half_w = (height // 2, breadth // 2)
    weight_col = jnp.tile(weight.reshape(-1, 1), (MB, 1))
    matrices = (w_in, w_down, w_dw, w_hidden, w_out, w_up, w_head)
    sides = (("rows", 1), ("cols", 2))

    def dates(field):
        return jnp.concatenate(
            [lax.dynamic_slice_in_dim(field, date_index[m], 1, 0) for m in range(MB)]
        )

    narrow_turn = (jnp.arange(C1)[:, None] == perm_narrow[None, :]).astype(jnp.bfloat16)
    wide_turn = (jnp.arange(CH)[:, None] == perm_wide[None, :]).astype(jnp.bfloat16)

    def turned(values, turn):
        return product(values, turn).astype(jnp.bfloat16)

    state, target = dates(inputs), dates(targets)
    state_pad = clear_edges(padded_2(state, sides, 1), 1)
    taps = jnp.concatenate(
        [state_pad[:, y : y + height, x : x + breadth] for y in range(3) for x in range(3)], -1
    ).reshape(-1, 9 * CI)
    a_zero = product(taps, w_in) + b_in
    h_zero, gelu_zero = jax.vjp(jax.nn.gelu, a_zero)
    h_low = h_zero.astype(jnp.bfloat16)
    patches = to_coarse(h_low.reshape(MB, height, breadth, C0), height, breadth)
    coarse = product(patches, w_down) + b_down
    coarse_low = coarse.astype(jnp.bfloat16).reshape(MB, half_h, half_w, C1)
    coarse_pad = clear_edges(padded_2(coarse_low, sides, 3), 3)
    conv_out = depthwise(coarse_pad, w_dw, half_h, half_w, False).reshape(-1, C1) + b_dw
    normed, norm_pull = jax.vjp(layer_norm, conv_out, gain, shift)
    normed_low = normed.astype(jnp.bfloat16)
    pre = product(normed_low, w_hidden) + b_hidden
    act, act_pull = jax.vjp(jax.nn.gelu, pre)
    act_low = act.astype(jnp.bfloat16)
    branch = product(act_low, w_out) + b_out
    mixed_low = (coarse + branch).astype(jnp.bfloat16)
    upper = product(mixed_low, w_up) + jnp.tile(b_up, 4)
    summed_low = (to_fine(upper, height, breadth) + h_zero).astype(jnp.bfloat16)
    output = product(summed_low, w_head) + b_head
    error = output - target.reshape(-1, CI).astype(jnp.float32)
    loss_local = jnp.sum(weight_col * error * error)
    grad_out = (2.0 * weight_col * error).astype(jnp.bfloat16)
    d_head = inner_rows(summed_low, grad_out)
    grad_summed = outer_cols(grad_out, w_head)
    grad_upper = to_coarse(
        grad_summed.astype(jnp.bfloat16).reshape(MB, height, breadth, C0), height, breadth
    )
    d_up = inner_rows(mixed_low, grad_upper)
    grad_mixed = outer_cols(grad_upper, w_up)
    grad_branch = grad_mixed.astype(jnp.bfloat16)
    d_out = inner_rows(turned(act_low, wide_turn), turned(grad_branch, narrow_turn))
    grad_act = outer_cols(grad_branch, w_out)
    grad_pre = act_pull(grad_act)[0].astype(jnp.bfloat16)
    d_hidden = inner_rows(turned(normed_low, narrow_turn), turned(grad_pre, wide_turn))
    grad_normed = outer_cols(grad_pre, w_hidden)
    grad_conv, d_gain, d_shift = norm_pull(grad_normed)
    grad_conv = grad_conv.astype(jnp.bfloat16)
    grad_map = grad_conv.reshape(MB, half_h, half_w, C1)
    d_dw = depthwise_kernel_grad(coarse_pad, grad_map, half_h, half_w)
    grad_pad = clear_edges(padded_2(grad_map, sides, 3), 3)
    grad_coarse_low = depthwise(grad_pad, w_dw, half_h, half_w, True).reshape(-1, C1)
    grad_coarse = (grad_coarse_low + grad_mixed).astype(jnp.bfloat16)
    d_down = inner_rows(patches, grad_coarse)
    grad_h = to_fine(outer_cols(grad_coarse, w_down), height, breadth) + grad_summed
    grad_a = gelu_zero(grad_h)[0].astype(jnp.bfloat16)
    d_in = inner_rows(taps, grad_a)
    d_vector = jnp.concatenate(
        [
            column_sum(grad_a),
            column_sum(grad_coarse),
            column_sum(grad_conv),
            d_gain,
            d_shift,
            column_sum(grad_pre),
            column_sum(grad_branch),
            jnp.sum(column_sum(grad_upper).reshape(4, C0), 0),
            column_sum(grad_out),
        ]
    )
    terms = (d_in, d_down, d_dw, d_hidden, d_out, d_up, d_head, d_vector)
    rows, cols = lax.axis_size("rows"), lax.axis_size("cols")
    space = Plan(rows, cols, PADDED).space
    ends = ROW_AT[1:] + [space]
    blocks = [jnp.zeros((ROW_AT[0], LANES), jnp.float32)]
    for term, begin, end in zip(terms, ROW_AT, ends):
        blocks.append(as_rows(term, end - begin))
    grad = jnp.concatenate(blocks)
    line = jnp.arange(8)[:, None]
    extra = jnp.where(line == 0, loss_local, jnp.where(line == 1, jnp.sum(weight), 0.0))
    extra = jnp.where(jnp.arange(LANES)[None, :] == 0, extra, 0.0)
    plan, (gathered, first, second, totals) = exchange(
        rows, cols, grad, moment_first, moment_second, extra
    )
    full = gathered[:, : plan.share, :].astype(jnp.float32).reshape(-1)
    back_narrow = jnp.zeros((C1,), jnp.int32).at[perm_narrow].set(jnp.arange(C1, dtype=jnp.int32))
    back_wide = jnp.zeros((CH,), jnp.int32).at[perm_wide].set(jnp.arange(CH, dtype=jnp.int32))
    olds = matrices + (biases_gains,)
    news = []
    for index, old in enumerate(olds):
        start = FLAT_AT[index]
        piece = full[start : start + old.size].reshape(old.shape)
        if index == 3:
            piece = piece[back_narrow][:, back_wide]
        if index == 4:
            piece = piece[back_wide][:, back_narrow]
        if index < 7:
            news.append(
                old.astype(jnp.float32) * (1.0 - learn_rate * weight_decay) - learn_rate * piece
            )
        else:
            news.append(old - learn_rate * piece)
    return tuple(news) + (
        first.reshape(-1),
        second.reshape(-1),
        totals[0, 0],
        MB * CI * totals[1, 0],
        totals[8, 0],
    )


def solution(mesh):
    return jax.shard_map(
        on_device,
        mesh=mesh,
        in_specs=(
            P(None, "rows", "cols", None),
            P(None, "rows", "cols", None),
            P("rows", "cols"),
            P("rows", "cols"),
            P(),
            P(),
            P(),
            P(),
            P(),
            P(),
            P(),
            P(),
            P(),
            P(),
            P(),
            P(("rows", "cols")),
            P(("rows", "cols")),
        ),
        out_specs=(
            P(),
            P(),
            P(),
            P(),
            P(),
            P(),
            P(),
            P(),
            P(("rows", "cols")),
            P(("rows", "cols")),
            P(),
            P(),
            P(),
        ),
        check_vma=False,
    )
```

```python
import functools

import jax
import jax.numpy as jnp
from jax import lax
from jax.experimental import pallas as pl
from jax.experimental.pallas import tpu as pltpu
from jax.sharding import PartitionSpec as P

CI = 77
C0 = 200
C1 = 800
CH = 3200
MB = 2
STEP = 5
LANES = 128
MESH = pl.DeviceIdType.MESH
ROUNDER = 12582912.0

decay_first = 0.9
decay_second = 0.99
epsilon = 1e-08
learn_rate = 0.02
weight_decay = 0.1
clip_limit = 1.0

VEC = 4 * C1 + CH + C1 + 2 * C0 + CI
SIZES = (9 * CI * C0, 4 * C0 * C1, 49 * C1, C1 * CH, CH * C1, C1 * 4 * C0, C0 * CI, VEC)
PADDED = 6602752
FLAT_AT = []
ROW_AT = []
for size in SIZES:
    flat_here = FLAT_AT[-1] + SIZES[len(FLAT_AT) - 1] if FLAT_AT else PADDED - sum(SIZES)
    row_here = ROW_AT[-1] + -(-SIZES[len(ROW_AT) - 1] // 1024) * 8 if ROW_AT else 0
    row_here = max(row_here, -(-flat_here // 1024) * 8)
    FLAT_AT.append(flat_here)
    ROW_AT.append(row_here)
SHIFTS = []
for flat_here, row_here, size in zip(FLAT_AT, ROW_AT, SIZES):
    moved = divmod(row_here * LANES - flat_here, LANES)
    if SHIFTS and SHIFTS[-1][:2] == moved:
        SHIFTS[-1] = moved + (SHIFTS[-1][2], flat_here + size)
    else:
        SHIFTS.append(moved + (flat_here, flat_here + size))
MAX_SHIFT = max(s[0] for s in SHIFTS) + 1


def bit_masks(bits):
    masks = [()]
    for bit in bits:
        masks = masks + [m + (bit,) for m in masks]
    return sorted(masks, key=lambda m: -len(m))


class Plan:
    def __init__(self, rows, cols, total):
        self.rows, self.cols, self.count = rows, cols, rows * cols
        self.share = total // LANES // self.count
        self.bits = rows.bit_length() - 1
        need = 7 + self.share + MAX_SHIFT + 1
        self.block = 64 if need > 1024 else 32
        self.window = -(-need // (2 * self.block)) * 2 * self.block
        self.part = self.window // 2
        self.blocks = self.part // self.block
        self.scales = self.blocks
        upper = list(range(1, self.bits))
        self.orders = [upper, upper[1:] + upper[:1]]
        self.stages = len(upper)
        self.space = (self.share * (self.count - 1)) // 8 * 8 + self.window
        self.padded = -(-self.share // 16) * 16
        cut = -(-self.padded // 32) * 16
        self.cuts = [(0, cut), (cut, self.padded - cut)]
        self.local = self.count // 2


def exchange_kernel(
    plan, grad, m_first, m_second, extra, full, first, second, totals,
    acc, near, q_send, q_recv, s_send, s_recv, z_send, z_recv, zs_send, zs_recv,
    rolled, step, low, stats,
    sem_load, sem_near_s, sem_near_r, sem_qs, sem_qr, sem_ss, sem_sr,
    sem_zs, sem_zr, sem_zss, sem_zsr, sem_ts, sem_tr, sem_own,
    sem_gs, sem_gr, sem_hs, sem_hr, sem_cs, sem_cr,
):
    nr, nc, n = plan.rows, plan.cols, plan.count
    r = lax.axis_index("rows")
    c = lax.axis_index("cols")
    me = r * nc + c
    part, window, share = plan.part, plan.window, plan.share

    def flipped(mask):
        out = r
        for bit in mask:
            here = (r // (1 << bit)) % 2
            out = out + (1 - 2 * here) * (1 << bit)
        return out

    def remote(src, dst, send, recv, row, col):
        return pltpu.make_async_remote_copy(
            src_ref=src, dst_ref=dst, send_sem=send, recv_sem=recv,
            device_id=(row, col), device_id_type=MESH,
        )

    barrier = pltpu.get_barrier_semaphore()

    def greet(d, carry):
        k = lax.rem(me + d, n)
        pl.semaphore_signal(barrier, inc=1, device_id=(k // nc, k % nc), device_id_type=MESH)
        return carry

    lax.fori_loop(1, n, greet, 0)
    pl.semaphore_wait(barrier, n - 1)

    upper = list(range(1, plan.bits))
    masks = bit_masks(upper)

    def local_index(mask, col):
        return (flipped(mask) // 2) * nc + col

    def window_start(row, col):
        return pl.multiple_of((share * (row * nc + col)) // 8 * 8, 8)

    def near_copy(mask, col):
        row = flipped(mask + (0,))
        return remote(
            grad.at[pl.ds(window_start(row, col), window)],
            near.at[local_index(mask, col)],
            sem_near_s.at[local_index(mask, col)], sem_near_r.at[local_index(mask, col)],
            flipped((0,)), c,
        )

    def load_copy(mask, col):
        index = local_index(mask, col)
        return pltpu.make_async_copy(
            grad.at[pl.ds(window_start(flipped(mask), col), window)], acc.at[index], sem_load.at[index]
        )

    for mask in masks:
        def begin(col, carry, mask=mask):
            near_copy(mask, col).start()
            load_copy(mask, col).start()
            return carry

        lax.fori_loop(0, nc, begin, 0)

    def encode(index, p, q_ref, s_ref):
        def body(b, carry):
            at = pl.ds(pl.multiple_of(b * plan.block, plan.block), plan.block)
            rows_at = pl.ds(pl.multiple_of(p * part + b * plan.block, 8), plan.block)
            values = acc[index, rows_at, :]
            top = jnp.maximum(jnp.max(jnp.abs(values), axis=0, keepdims=True), 1e-30)
            scaled = values * (32766.0 / top)
            scaled = (scaled + ROUNDER) - ROUNDER
            q_ref[at, :] = scaled.astype(jnp.int32).astype(jnp.int16)
            s_ref[pl.ds(b, 1), :] = top * (1.0 / 32766.0)
            return carry

        lax.fori_loop(0, plan.blocks, body, 0)

    def decode(index, p, q_ref, s_ref):
        def body(b, carry):
            at = pl.ds(pl.multiple_of(b * plan.block, plan.block), plan.block)
            rows_at = pl.ds(pl.multiple_of(p * part + b * plan.block, 8), plan.block)
            acc[index, rows_at, :] += q_ref[at, :].astype(jnp.float32) * s_ref[pl.ds(b, 1), :]
            return carry

        lax.fori_loop(0, plan.blocks, body, 0)

    def stage_base(stage):
        return sum((1 << (plan.stages - 1 - s)) for s in range(stage)) * nc

    def hop(p, stage, slot):
        row = flipped((plan.orders[p][stage],))
        at = stage_base(stage) + slot
        return (
            remote(q_send.at[p, at], q_recv.at[p, at], sem_qs.at[p, at], sem_qr.at[p, at], row, c),
            remote(s_send.at[p, at], s_recv.at[p, at], sem_ss.at[p, at], sem_sr.at[p, at], row, c),
        )

    def send_stage(p, stage, number, mask, col):
        bit = plan.orders[p][stage]
        index = local_index(mask + (bit,), col)
        slot = number * nc + col
        at = stage_base(stage) + slot
        encode(index, p, q_send.at[p, at], s_send.at[p, at])
        for copy in hop(p, stage, slot):
            copy.start()

    def take_stage(p, stage, number, mask, col):
        slot = number * nc + col
        for copy in hop(p, stage, slot):
            copy.wait_recv()
        at = stage_base(stage) + slot
        decode(local_index(mask, col), p, q_recv.at[p, at], s_recv.at[p, at])

    def free_masks(p, stage):
        rest = plan.orders[p][stage + 1 :]
        found = bit_masks(rest)
        if rest:
            found = [m for m in found if rest[0] in m] + [m for m in found if rest[0] not in m]
        return found

    for mask in masks:
        def join(col, carry, mask=mask):
            index = local_index(mask, col)
            near_copy(mask, col).wait_recv()
            load_copy(mask, col).wait()

            def body(b, inner):
                at = pl.ds(pl.multiple_of(b * plan.block, plan.block), plan.block)
                acc[index, at, :] += near[index, at, :]
                return inner

            lax.fori_loop(0, 2 * plan.blocks, body, 0)
            for p in range(2):
                bit = plan.orders[p][0]
                if bit in mask:
                    rest = tuple(b for b in mask if b != bit)
                    options = free_masks(p, 0)
                    number = [sorted(o) for o in options].index(sorted(rest))
                    send_stage(p, 0, number, rest, col)
            return carry

        lax.fori_loop(0, nc, join, 0)

    def far_copy(p, d):
        col = lax.rem(c + d, nc)
        return (
            remote(z_send.at[p, d - 1], z_recv.at[p, d - 1], sem_zs.at[p, d - 1], sem_zr.at[p, d - 1], r, col),
            remote(zs_send.at[p, d - 1], zs_recv.at[p, d - 1], sem_zss.at[p, d - 1], sem_zsr.at[p, d - 1], r, col),
        )

    for stage in range(plan.stages):
        for number in range(1 << (plan.stages - 1 - stage)):
            def take(d, carry, stage=stage, number=number):
                col = lax.rem(c + d, nc)
                for p in range(2):
                    mask = free_masks(p, stage)[number]
                    take_stage(p, stage, number, mask, col)
                    if stage + 1 < plan.stages:
                        bit = plan.orders[p][stage + 1]
                        if bit in mask:
                            rest = tuple(b for b in mask if b != bit)
                            options = free_masks(p, stage + 1)
                            following = [sorted(o) for o in options].index(sorted(rest))
                            send_stage(p, stage + 1, following, rest, col)
                return carry

            if stage + 1 < plan.stages:
                lax.fori_loop(1, nc + 1, take, 0)
            else:
                def take_last(d, carry, take=take):
                    take(d, 0)
                    col = lax.rem(c + d, nc)
                    for p in range(2):
                        encode(local_index((), col), p, z_send.at[p, d - 1], zs_send.at[p, d - 1])
                        for copy in far_copy(p, d):
                            copy.start()
                    return carry

                lax.fori_loop(1, nc, take_last, 0)
                take(nc, 0)

    mine = local_index((), c)

    def gather_far(d, carry):
        for p in range(2):
            for copy in far_copy(p, d):
                copy.wait_recv()
            decode(mine, p, z_recv.at[p, d - 1], zs_recv.at[p, d - 1])
        return carry

    lax.fori_loop(1, nc, gather_far, 0)

    offset = lax.rem(share * me, 8)
    for number, (shift_rows, shift_lanes, begin, end) in enumerate(SHIFTS):
        def turn(b, carry, number=number, shift_lanes=shift_lanes):
            at = pl.ds(pl.multiple_of(b * plan.block, plan.block), plan.block)
            rolled[number, at, :] = pltpu.roll(acc[mine, at, :], LANES - shift_lanes, 1)
            return carry

        lax.fori_loop(0, 2 * plan.blocks, turn, 0)

    def share_rows(start, length):
        lane = lax.broadcasted_iota(jnp.int32, (length, LANES), 1)
        line = lax.broadcasted_iota(jnp.int32, (length, LANES), 0)
        flat = (share * me + start + line) * LANES + lane
        out = jnp.zeros((length, LANES), jnp.float32)
        for number, (shift_rows, shift_lanes, begin, end) in enumerate(SHIFTS):
            here = rolled[number, pl.ds(offset + start + shift_rows, length), :]
            after = rolled[number, pl.ds(offset + start + shift_rows + 1, length), :]
            value = jnp.where(lane < LANES - shift_lanes, here, after)
            out = jnp.where((flat >= begin) & (flat < end), value, out)
        return out

    chunk = 32
    whole, tail = share // chunk, share % chunk

    def square(b, total):
        start = pl.multiple_of(b * chunk, chunk)
        value = share_rows(start, chunk)
        step[pl.ds(start, chunk), :] = value
        return total + jnp.sum((value * value).reshape(chunk // 8, 8, LANES), axis=0)

    total = lax.fori_loop(0, whole, square, jnp.zeros((8, LANES), jnp.float32))
    stats[me, 8:16, :] = extra[...]
    stats[me, 0:8, :] = total
    if tail:
        value = share_rows(whole * chunk, tail)
        step[whole * chunk : share, :] = value
        stats[me, 0:1, :] += jnp.sum(value * value, axis=0, keepdims=True)

    def stat_copy(target, source):
        return remote(
            stats.at[me], stats.at[me], sem_ts.at[target], sem_tr.at[me], target // nc, target % nc
        )

    def stat_wait(source):
        return remote(
            stats.at[source], stats.at[source], sem_ts.at[source], sem_tr.at[source],
            source // nc, source % nc,
        )

    def send_stat(d, carry):
        stat_copy(lax.rem(me + d, n), me).start()
        return carry

    lax.fori_loop(1, n, send_stat, 0)

    def wait_stat(d, carry):
        stat_wait(lax.rem(me + d, n)).wait_recv()
        return carry

    lax.fori_loop(1, n, wait_stat, 0)

    def add_stat(k, total):
        return total + stats[k]

    sums = lax.fori_loop(0, n, add_stat, jnp.zeros((16, LANES), jnp.float32))
    norm = jnp.sqrt(jnp.sum(sums[0:8], keepdims=True))
    totals[0:8, :] = sums[8:16]
    totals[8:16, :] = jnp.broadcast_to(norm, (8, LANES))
    clip = jnp.minimum(1.0, clip_limit / norm)

    def update(start, length):
        clipped = step[pl.ds(start, length), :] * clip
        one = decay_first * m_first[pl.ds(start, length), :] + (1.0 - decay_first) * clipped
        two = decay_second * m_second[pl.ds(start, length), :] + (1.0 - decay_second) * clipped * clipped
        first[pl.ds(start, length), :] = one
        second[pl.ds(start, length), :] = two
        step[pl.ds(start, length), :] = (
            one / (1.0 - decay_first**STEP) / (jnp.sqrt(two / (1.0 - decay_second**STEP)) + epsilon)
        )

    def update_chunk(b, carry):
        update(pl.multiple_of(b * chunk, chunk), chunk)
        return carry

    lax.fori_loop(0, whole, update_chunk, 0)
    if tail:
        update(whole * chunk, tail)
    if plan.padded > share:
        step[share : plan.padded, :] = jnp.zeros((plan.padded - share, LANES), jnp.float32)

    def narrow(b, carry):
        at = pl.ds(pl.multiple_of(b * 16, 16), 16)
        low[at, :] = step[at, :].astype(jnp.bfloat16)
        return carry

    lax.fori_loop(0, plan.padded // 16, narrow, 0)

    own = pltpu.make_async_copy(low, full.at[me], sem_own)
    own.start()
    own.wait()

    back = [list(reversed(order)) for order in plan.orders]

    def piece(mask, col, p):
        begin, length = plan.cuts[p]
        return full.at[flipped(mask) * nc + col, pl.ds(begin, length)]

    def along(direction, col, p, receive):
        step_col = 1 if direction == 0 else -1
        target = c - step_col if receive else c + step_col
        ref = piece((), col, p)
        return remote(ref, ref, sem_gs.at[direction, col, p], sem_gr.at[direction, col, p], r, target)

    def gather_masks(p, stage):
        return bit_masks(back[p][:stage])

    def gather_base(stage):
        return sum(1 << s for s in range(stage)) * nc

    def across(p, stage, number, mask, col):
        at = gather_base(stage) + number * nc + col
        ref = piece(mask, col, p)
        return remote(ref, ref, sem_hs.at[p, at], sem_hr.at[p, at], flipped((back[p][stage],)), c)

    def across_recv(p, stage, number, mask, col):
        at = gather_base(stage) + number * nc + col
        ref = piece(mask + (back[p][stage],), col, p)
        return remote(ref, ref, sem_hs.at[p, at], sem_hr.at[p, at], flipped((back[p][stage],)), c)

    def inward(p, mask, col):
        number = masks.index(tuple(sorted(mask)))
        at = number * nc + col
        ref = piece(mask, col, p)
        return remote(ref, ref, sem_cs.at[p, at], sem_cr.at[p, at], flipped((0,)), c)

    def inward_recv(p, mask, col):
        number = masks.index(tuple(sorted(mask)))
        at = number * nc + col
        ref = piece(mask + (0,), col, p)
        return remote(ref, ref, sem_cs.at[p, at], sem_cr.at[p, at], flipped((0,)), c)

    def spread(p, mask, col, stage):
        for later in range(stage, plan.stages):
            options = [sorted(o) for o in gather_masks(p, later)]
            if sorted(mask) in options:
                across(p, later, options.index(sorted(mask)), mask, col).start()
        inward(p, mask, col).start()

    def near_cols(t):
        if t == 0:
            return [(0, c)]
        return [(0, c - t), (1, c + t)]

    def inside(col):
        return (col >= 0) & (col < nc)

    for time in range(nc + plan.stages):
        for stage in range(plan.stages + 1):
            t = time - stage
            if not 0 <= t < nc:
                continue
            if stage == 0:
                if t == 0:
                    for p in range(2):
                        @pl.when(c < nc - 1)
                        def _(p=p):
                            along(0, c, p, False).start()

                        @pl.when(c > 0)
                        def _(p=p):
                            along(1, c, p, False).start()

                        spread(p, (), c, 0)
                else:
                    for direction, col in near_cols(t):
                        @pl.when(inside(col))
                        def _(direction=direction, col=col):
                            for p in range(2):
                                along(direction, col, p, True).wait_recv()
                                if direction == 0:
                                    @pl.when(c < nc - 1)
                                    def _():
                                        along(0, col, p, False).start()
                                else:
                                    @pl.when(c > 0)
                                    def _():
                                        along(1, col, p, False).start()
                                spread(p, (), col, 0)
            else:
                for direction, col in near_cols(t):
                    @pl.when(inside(col))
                    def _(col=col, stage=stage):
                        for number in range(1 << (stage - 1)):
                            for p in range(2):
                                mask = gather_masks(p, stage - 1)[number]
                                across_recv(p, stage - 1, number, mask, col).wait_recv()
                                spread(p, mask + (back[p][stage - 1],), col, stage)

    for mask in masks:
        def finish(col, carry, mask=mask):
            for p in range(2):
                inward_recv(p, mask, col).wait_recv()
                inward(p, mask, col).wait_send()
            near_copy(mask, col).wait_send()
            return carry

        lax.fori_loop(0, nc, finish, 0)
    for p in range(2):
        for stage in range(plan.stages):
            for number, mask in enumerate(gather_masks(p, stage)):
                def sent(col, carry, p=p, stage=stage, number=number, mask=mask):
                    across(p, stage, number, mask, col).wait_send()
                    return carry

                lax.fori_loop(0, nc, sent, 0)
            for number in range(1 << (plan.stages - 1 - stage)):
                def left(col, carry, p=p, stage=stage, number=number):
                    for copy in hop(p, stage, number * nc + col):
                        copy.wait_send()
                    return carry

                lax.fori_loop(0, nc, left, 0)

        def gone(col, carry, p=p):
            @pl.when((col <= c) & (c < nc - 1))
            def _():
                along(0, col, p, False).wait_send()

            @pl.when((col >= c) & (c > 0))
            def _():
                along(1, col, p, False).wait_send()

            return carry

        lax.fori_loop(0, nc, gone, 0)

        def far_gone(d, carry, p=p):
            for copy in far_copy(p, d):
                copy.wait_send()
            return carry

        lax.fori_loop(1, nc, far_gone, 0)

    def stat_gone(d, carry):
        stat_copy(lax.rem(me + d, n), me).wait_send()
        return carry

    lax.fori_loop(1, n, stat_gone, 0)


def exchange(rows, cols, grad, m_first, m_second, extra):
    plan = Plan(rows, cols, m_first.size * rows * cols)
    n, nc, share = plan.count, plan.cols, plan.share
    hops = sum(1 << s for s in range(plan.stages)) * nc
    dma = pltpu.SemaphoreType.DMA
    far = max(nc - 1, 1)
    vmem = pl.BlockSpec(memory_space=pltpu.VMEM)
    hbm = pl.BlockSpec(memory_space=pl.ANY)
    return plan, pl.pallas_call(
        functools.partial(exchange_kernel, plan),
        out_shape=(
            jax.ShapeDtypeStruct((n, plan.padded, LANES), jnp.bfloat16),
            jax.ShapeDtypeStruct((share, LANES), jnp.float32),
            jax.ShapeDtypeStruct((share, LANES), jnp.float32),
            jax.ShapeDtypeStruct((16, LANES), jnp.float32),
        ),
        in_specs=[hbm, vmem, vmem, vmem],
        out_specs=(hbm, vmem, vmem, vmem),
        scratch_shapes=[
            pltpu.VMEM((plan.local, plan.window, LANES), jnp.float32),
            pltpu.VMEM((plan.local, plan.window, LANES), jnp.float32),
            pltpu.VMEM((2, hops, plan.part, LANES), jnp.int16),
            pltpu.VMEM((2, hops, plan.part, LANES), jnp.int16),
            pltpu.VMEM((2, hops, plan.scales, LANES), jnp.float32),
            pltpu.VMEM((2, hops, plan.scales, LANES), jnp.float32),
            pltpu.VMEM((2, far, plan.part, LANES), jnp.int16),
            pltpu.VMEM((2, far, plan.part, LANES), jnp.int16),
            pltpu.VMEM((2, far, plan.scales, LANES), jnp.float32),
            pltpu.VMEM((2, far, plan.scales, LANES), jnp.float32),
            pltpu.VMEM((len(SHIFTS), plan.window, LANES), jnp.float32),
            pltpu.VMEM((plan.padded, LANES), jnp.float32),
            pltpu.VMEM((plan.padded, LANES), jnp.bfloat16),
            pltpu.VMEM((n, 16, LANES), jnp.float32),
            dma((plan.local,)), dma((plan.local,)), dma((plan.local,)),
            dma((2, hops)), dma((2, hops)), dma((2, hops)), dma((2, hops)),
            dma((2, far)), dma((2, far)), dma((2, far)), dma((2, far)),
            dma((n,)), dma((n,)), dma,
            dma((2, nc, 2)), dma((2, nc, 2)),
            dma((2, hops)), dma((2, hops)),
            dma((2, plan.local)), dma((2, plan.local)),
        ],
        compiler_params=pltpu.CompilerParams(
            collective_id=0, has_side_effects=True, vmem_limit_bytes=56 << 20
        ),
    )(grad, m_first.reshape(share, LANES), m_second.reshape(share, LANES), extra)


WIDE = CH + LANES
KEPT = ((8, 1104), (6096, 6408), (51400, 51584))
PLACES = tuple(divmod(FLAT_AT[i], LANES) for i in (3, 4, 5, 1))

def unpack_kernel(plan, gathered, old_up, old_down, hidden, out, up, down, small_a, small_b, small_c, held, flat, woven, sems):
    n, share = plan.count, plan.share
    step = CH // LANES

    def fetch(k, slot):
        return pltpu.make_async_copy(gathered.at[k], held.at[slot], sems.at[slot])

    fetch(0, 0).start()

    def widen(k, carry):
        slot = lax.rem(k, 2)

        @pl.when(k + 1 < n)
        def _():
            fetch(k + 1, 1 - slot).start()

        fetch(k, slot).wait()

        def body(b, inner):
            at = pl.ds(pl.multiple_of(b * 16, 16), 16)
            flat[pl.ds(share * k + b * 16, 16), :] = held[slot, at, :].astype(jnp.float32)
            return inner

        lax.fori_loop(0, plan.padded // 16, body, 0, unroll=4)
        return carry

    lax.fori_loop(0, n, widen, 0)

    for ref, (row, lane) in zip((hidden, out), PLACES):
        def column(t, carry, ref=ref, row=row):
            for begin in range(0, C1, 160):
                values = flat[pl.ds(row + begin * step + t, 160, stride=step), :]
                ref[begin : begin + 160, pl.ds(pl.multiple_of(t * LANES, LANES), LANES)] = values.astype(
                    jnp.bfloat16
                )
            return carry

        lax.fori_loop(0, WIDE // LANES, column, 0)

    quarter = C1 // 4
    for ref, old, (row, lane) in zip((up, down), (old_up, old_down), PLACES[2:]):
        for u in range(-(-C1 // LANES)):
            width = min(LANES, C1 - u * LANES)
            place = lax.broadcasted_iota(jnp.int32, (quarter, LANES), 1)
            for b in range(4):
                first, rest = divmod(C1 * b + lane, LANES)
                here = flat[pl.ds(row + first + u, quarter, stride=step), :]
                after = flat[pl.ds(row + first + u + 1, quarter, stride=step), :]
                value = pltpu.roll(jnp.where(place >= rest, here, after), LANES - rest, 1)
                woven[pl.ds(b, quarter, stride=4), :] = value
            at = slice(u * LANES, u * LANES + width)
            ref[:, at] = moved(old[:, at], woven[:, :width])
    for ref, (begin, end) in zip((small_a, small_b, small_c), KEPT):
        ref[...] = flat[begin:end, :]


def unpack(plan, gathered, old_up, old_down):
    lines = PADDED // LANES
    vmem = pl.BlockSpec(memory_space=pltpu.VMEM)
    return pl.pallas_call(
        functools.partial(unpack_kernel, plan),
        out_shape=tuple(jax.ShapeDtypeStruct((C1, WIDE), jnp.bfloat16) for _ in range(2))
        + tuple(jax.ShapeDtypeStruct((C1, C1), jnp.float32) for _ in range(2))
        + tuple(jax.ShapeDtypeStruct((end - begin, LANES), jnp.float32) for begin, end in KEPT),
        in_specs=[pl.BlockSpec(memory_space=pl.ANY), vmem, vmem],
        out_specs=tuple([vmem] * 7),
        scratch_shapes=[
            pltpu.VMEM((2, plan.padded, LANES), jnp.bfloat16),
            pltpu.VMEM((-(-lines // 8) * 8 + 16, LANES), jnp.float32),
            pltpu.VMEM((C1, LANES), jnp.float32),
            pltpu.SemaphoreType.DMA((2,)),
        ],
        compiler_params=pltpu.CompilerParams(vmem_limit_bytes=54 << 20),
    )(gathered, old_up, old_down)


def moved(old, direction):
    return old.astype(jnp.float32) * (1.0 - learn_rate * weight_decay) - learn_rate * direction


def one_hot(condition):
    return jnp.where(condition, 1.0, 0.0).astype(jnp.bfloat16)


def product(left, right):
    return jnp.dot(left, right, preferred_element_type=jnp.float32)


def product_t(left, right):
    return lax.dot_general(left, right, (((1,), (1,)), ((), ())), preferred_element_type=jnp.float32)


TILE = 640


def turn_kernel(prepare, packed, narrow, wide, old, new, lines, hot):
    depth = lines.shape[1]

    @pl.when(pl.program_id(0) == 0)
    def _():
        prepare(packed, narrow, lines)

    base = pl.program_id(0) * TILE

    def build(b, carry):
        at = pl.ds(pl.multiple_of(b * LANES, LANES), LANES)
        column = lax.broadcasted_iota(jnp.int32, (LANES, TILE), 1) + base
        hot[at, :] = one_hot(column == wide[at, 0:1])
        return carry

    lax.fori_loop(0, depth // LANES, build, 0)
    new[...] = moved(old[...], product(lines[...], hot[...]))


def prepare_hidden(packed, narrow, lines):
    turn = one_hot(lax.broadcasted_iota(jnp.int32, (C1, C1), 0) == narrow[...])
    for begin in range(0, WIDE, 832):
        lines[:, begin : begin + 832] = product(turn, packed[:, begin : begin + 832]).astype(jnp.bfloat16)


def quarter_spans(lane):
    spans = []
    for b in range(4):
        begin = (C1 * b + lane) // LANES * LANES
        end = -(-(C1 * b + lane + C1) // LANES) * LANES
        spans.append((begin, end))
    return spans


def prepare_out(packed, narrow, lines):
    for b, (begin, end) in enumerate(quarter_spans(PLACES[1][1])):
        turn = one_hot(
            lax.broadcasted_iota(jnp.int32, (C1, end - begin), 0) == narrow[b : b + 1, begin:end]
        )
        lines[:, b * C1 : (b + 1) * C1] = product_t(turn, packed[:, begin:end]).astype(jnp.bfloat16)


def turn_back(prepare, packed, narrow, wide, old):
    depth = wide.shape[0]
    return pl.pallas_call(
        functools.partial(turn_kernel, prepare),
        out_shape=jax.ShapeDtypeStruct((C1, CH), jnp.float32),
        grid=(CH // TILE,),
        in_specs=[
            pl.BlockSpec((C1, WIDE), lambda i: (0, 0)),
            pl.BlockSpec(narrow.shape, lambda i: (0, 0)),
            pl.BlockSpec((depth, LANES), lambda i: (0, 0)),
            pl.BlockSpec((C1, TILE), lambda i: (0, i)),
        ],
        out_specs=pl.BlockSpec((C1, TILE), lambda i: (0, i)),
        scratch_shapes=[pltpu.VMEM((C1, depth), jnp.bfloat16), pltpu.VMEM((depth, TILE), jnp.bfloat16)],
        compiler_params=pltpu.CompilerParams(vmem_limit_bytes=48 << 20),
    )(packed, narrow, jnp.broadcast_to(wide[:, None], (depth, LANES)), old)


def rebuild_hidden(packed, narrow, wide, old):
    lane = PLACES[0][1]
    shifted = jnp.full((WIDE,), -1, jnp.int32).at[lane : lane + CH].set(wide)
    return turn_back(prepare_hidden, packed, narrow[None, :], shifted, old)


def rebuild_out(packed, narrow, wide, old):
    lane = PLACES[1][1]
    place = jnp.arange(WIDE)
    lanes = jnp.full((WIDE,), -1, jnp.int32).at[lane : lane + CH].set(jnp.tile(narrow, 4))
    table = jnp.stack(
        [
            jnp.where((place >= C1 * b + lane) & (place < C1 * (b + 1) + lane), lanes, -1)
            for b in range(4)
        ]
    )
    order = wide.reshape(C1, 4).T.reshape(-1)
    return turn_back(prepare_out, packed, table, order, old.T).T


def weave(source, rows, put):
    for t in range(CH // LANES):
        b, begin = divmod(t * LANES, C1)
        u, rest = divmod(begin, LANES)
        place = lax.broadcasted_iota(jnp.int32, (rows, LANES), 1)
        value = source[u, pl.ds(b, rows, stride=4), :]
        if rest:
            if begin + LANES - rest < C1:
                after = source[u + 1, pl.ds(b, rows, stride=4), :]
                value = jnp.where(place >= rest, value, after)
            value = pltpu.roll(value, LANES - rest, 1)
        left = C1 - begin
        if left < LANES:
            following = source[0, pl.ds(b + 1, rows, stride=4), :]
            value = jnp.where(place < left, value, pltpu.roll(following, left, 1))
        put(t, value)


def place_kernel(
    norm_t, branch, pre, act, wide, up, down, piece_in, piece_dw, piece_head, piece_vec,
    grad, hot, hidden, out, loose, up_rows, down_rows, sem_out, sems,
):
    step = pl.program_id(0)
    steps = pl.num_programs(0)
    ratio = CH // LANES
    lines = TILE // 4
    tiles = TILE // LANES

    def out_copy(n):
        rows = lines * ratio
        return pltpu.make_async_copy(
            out.at[pl.ds(pl.multiple_of(n * rows, 8), rows)],
            grad.at[pl.ds(pl.multiple_of(ROW_AT[4] + n * rows, 8), rows)],
            sem_out.at[n],
        )

    copies = [
        pltpu.make_async_copy(ref, grad.at[pl.ds(row, ref.shape[0])], sems.at[i])
        for i, (ref, row) in enumerate(
            (
                (piece_in, 0), (piece_dw, ROW_AT[2]), (piece_head, ROW_AT[6]), (piece_vec, ROW_AT[7]),
                (up_rows, ROW_AT[5]), (down_rows, ROW_AT[1]), (hidden, ROW_AT[3]),
            )
        )
    ]

    @pl.when(step == 0)
    def _():
        for copy in copies[:4]:
            copy.start()

    for number, (source, target) in enumerate(((up, up_rows), (down, down_rows))):
        @pl.when(step == number)
        def _(number=number, source=source, target=target):
            for u in range(-(-C1 // LANES)):
                width = min(LANES, C1 - u * LANES)
                loose[u, :, 0:width] = source[:, u * LANES : u * LANES + width]

            def put(t, value):
                target[pl.ds(t, C1 // 4, stride=ratio), :] = value

            weave(loose, C1 // 4, put)
            copies[4 + number].start()

    def build(b, carry):
        at = pl.ds(pl.multiple_of(b * LANES, LANES), LANES)
        line = lax.broadcasted_iota(jnp.int32, (LANES, TILE), 0) + b * LANES
        hot[at, :] = one_hot(line == wide[...])
        return carry

    lax.fori_loop(0, CH // LANES, build, 0)
    turned_pre = product(pre[...], hot[...]).astype(jnp.bfloat16)
    part = product(norm_t[...], turned_pre)
    for t in range(tiles):
        hidden[pl.ds(step * tiles + t, C1, stride=ratio), :] = part[:, t * LANES : (t + 1) * LANES]
    turned_act = product(act[...], hot[...]).astype(jnp.bfloat16)
    part = lax.dot_general(
        turned_act, branch[...], (((0,), (0,)), ((), ())), preferred_element_type=jnp.float32
    )
    for u in range(-(-C1 // LANES)):
        loose[u, 0:TILE, :] = part[:, u * LANES : (u + 1) * LANES]

    def put_out(t, value):
        out[pl.ds(step * (lines * ratio) + t, lines, stride=ratio), :] = value

    weave(loose, lines, put_out)
    out_copy(step).start()

    @pl.when(step == steps - 1)
    def _():
        copies[6].start()

        def finish(n, carry):
            out_copy(n).wait()
            return carry

        lax.fori_loop(0, steps, finish, 0)
        for copy in copies:
            copy.wait()


def place_gradients(space, norm_t, branch, pre, act, wide, up, down, pieces):
    whole = lambda *shape: pl.BlockSpec(shape, lambda i: (0,) * len(shape))
    hbm = pl.BlockSpec(memory_space=pl.ANY)
    rows = pre.shape[0]
    padded = -(-C1 // LANES) * LANES
    return pl.pallas_call(
        place_kernel,
        out_shape=jax.ShapeDtypeStruct((space, LANES), jnp.float32),
        grid=(CH // TILE,),
        in_specs=[
            whole(C1, rows), whole(rows, padded), whole(rows, CH), whole(rows, CH),
            pl.BlockSpec((1, TILE), lambda i: (0, i)),
            whole(C1, C1), whole(C1, C1), hbm, hbm, hbm, hbm,
        ],
        out_specs=hbm,
        scratch_shapes=[
            pltpu.VMEM((CH, TILE), jnp.bfloat16),
            pltpu.VMEM((C1 * CH // LANES, LANES), jnp.float32),
            pltpu.VMEM((C1 * CH // LANES, LANES), jnp.float32),
            pltpu.VMEM((padded // LANES, C1, LANES), jnp.float32),
            pltpu.VMEM((C1 * C1 // LANES, LANES), jnp.float32),
            pltpu.VMEM((C1 * C1 // LANES, LANES), jnp.float32),
            pltpu.SemaphoreType.DMA((CH // TILE,)),
            pltpu.SemaphoreType.DMA((7,)),
        ],
        compiler_params=pltpu.CompilerParams(vmem_limit_bytes=58 << 20),
    )(norm_t, branch, pre, act, wide[None, :], up, down, *pieces)


C0P = 256
C1P = 896
CIP = 128
EDGE = 16
CURVE = 0.7978845608028654
CUBE = 0.044715


def inner_rows(left, right):
    return lax.dot_general(left, right, (((0,), (0,)), ((), ())), preferred_element_type=jnp.float32)


def column_sum(values):
    return jnp.sum(values.astype(jnp.float32), axis=0, keepdims=True)


def gelu(t):
    return 0.5 * t * (1.0 + jnp.tanh(CURVE * (t + CUBE * (t * t * t))))


def gelu_slope(t):
    bend = jnp.tanh(CURVE * (t + CUBE * (t * t * t)))
    return 0.5 * (1.0 + bend) + 0.5 * t * (1.0 - bend * bend) * (CURVE * (1.0 + 3.0 * CUBE * (t * t)))


def halo_kernel(nr, nc, width, cells, out, sem_s, sem_r):
    r = lax.axis_index("rows")
    c = lax.axis_index("cols")
    height, breadth = cells.shape[1], cells.shape[2]
    ways = [(dr, dc) for dr in (-1, 0, 1) for dc in (-1, 0, 1) if (dr, dc) != (0, 0)]

    def there(dr):
        return (r + dr >= 0) & (r + dr < nr)

    barrier = pltpu.get_barrier_semaphore()
    for dr, dc in ways:
        @pl.when(there(dr))
        def _(dr=dr, dc=dc):
            pl.semaphore_signal(
                barrier, inc=1, device_id=(r + dr, lax.rem(c + dc + nc, nc)), device_id_type=MESH
            )

    edge = (r == 0) | (r == nr - 1)

    @pl.when(edge)
    def _():
        pl.semaphore_wait(barrier, 5)

    @pl.when(jnp.logical_not(edge))
    def _():
        pl.semaphore_wait(barrier, 8)

    def copy(i, receive):
        dr, dc = ways[i]
        rows_from = {-1: (0, width), 0: (0, height), 1: (height - width, width)}[dr]
        rows_to = {-1: height + width, 0: width, 1: 0}[dr]
        cols_from = {-1: (0, EDGE), 0: (0, breadth), 1: (breadth - EDGE, EDGE)}[dc]
        cols_to = {-1: EDGE + breadth, 0: EDGE, 1: 0}[dc]
        sign = -1 if receive else 1
        return pltpu.make_async_remote_copy(
            src_ref=cells.at[:, pl.ds(*rows_from), pl.ds(*cols_from)],
            dst_ref=out.at[:, pl.ds(rows_to, rows_from[1]), pl.ds(cols_to, cols_from[1])],
            send_sem=sem_s.at[i],
            recv_sem=sem_r.at[i],
            device_id=(r + sign * dr, lax.rem(c + sign * dc + nc, nc)),
            device_id_type=MESH,
        )

    order = sorted(range(8), key=lambda i: (ways[i][1] != 0, ways[i][0] == 0))
    for i in order:
        @pl.when(there(ways[i][0]))
        def _(i=i):
            copy(i, False).start()

    for m in range(cells.shape[0]):
        for row in range(height):
            out[m, width + row, EDGE : EDGE + breadth, :] = cells[m, row]

    @pl.when(r == 0)
    def _():
        out[:, 0:width] = jnp.zeros((out.shape[0], width) + out.shape[2:], out.dtype)

    @pl.when(r == nr - 1)
    def _():
        out[:, height + width :] = jnp.zeros((out.shape[0], width) + out.shape[2:], out.dtype)

    for i in order:
        @pl.when(there(-ways[i][0]))
        def _(i=i):
            copy(i, True).wait_recv()

        @pl.when(there(ways[i][0]))
        def _(i=i):
            copy(i, False).wait_send()


def halo(nr, nc, width, cells, identity):
    batch, height, breadth, chans = cells.shape
    vmem = pl.BlockSpec(memory_space=pltpu.VMEM)
    return pl.pallas_call(
        functools.partial(halo_kernel, nr, nc, width),
        out_shape=jax.ShapeDtypeStruct(
            (batch, height + 2 * width, breadth + 2 * EDGE, chans), cells.dtype
        ),
        in_specs=[vmem],
        out_specs=vmem,
        scratch_shapes=[pltpu.SemaphoreType.DMA((8,)), pltpu.SemaphoreType.DMA((8,))],
        compiler_params=pltpu.CompilerParams(
            collective_id=identity, has_side_effects=True, vmem_limit_bytes=24 << 20
        ),
    )(cells)


def input_kernel(state, w_in, b_in, w_down, b_down, taps, a_zero, h_zero, coarse, coarse_low, wide):
    batch, rows, breadth, _ = state.shape
    half_h, half_w = (rows - 2) // 2, (breadth - 2 * EDGE) // 2
    for m in range(batch):
        for y in range(rows):
            wide[m, y] = state[m, y].astype(jnp.float32)
    for m in range(batch):
        for y in range(rows):
            for f in range(4):
                line = wide[m, y, pl.ds(EDGE - 1 + f, half_w, stride=2), :].astype(jnp.bfloat16)
                for dy in range(3):
                    i, sy = divmod(y - dy, 2)
                    if not 0 <= i < half_h:
                        continue
                    for dx in range(3):
                        if 0 <= f - dx < 2:
                            begin = (m * half_h + i) * half_w
                            tap = (dy * 3 + dx) * CIP
                            taps[sy * 2 + f - dx, begin : begin + half_w, tap : tap + CIP] = line
    coarse[...] = jnp.broadcast_to(b_down[...], coarse.shape)
    for s in range(4):
        value = product(taps[s], w_in[...]) + b_in[...]
        a_zero[s] = value
        value = gelu(value)
        h_zero[s] = value
        coarse[...] += product(value.astype(jnp.bfloat16), w_down[s])
    coarse_low[...] = coarse[...].astype(jnp.bfloat16).reshape(coarse_low.shape)


def input_part(state, w_in, b_in, w_down, b_down):
    batch, rows, breadth, _ = state.shape
    half_h, half_w = (rows - 2) // 2, (breadth - 2 * EDGE) // 2
    cells = batch * half_h * half_w
    vmem = pl.BlockSpec(memory_space=pltpu.VMEM)
    return pl.pallas_call(
        input_kernel,
        out_shape=(
            jax.ShapeDtypeStruct((4, cells, 9 * CIP), jnp.bfloat16),
            jax.ShapeDtypeStruct((4, cells, C0P), jnp.float32),
            jax.ShapeDtypeStruct((4, cells, C0P), jnp.float32),
            jax.ShapeDtypeStruct((cells, C1P), jnp.float32),
            jax.ShapeDtypeStruct((batch, half_h, half_w, C1P), jnp.bfloat16),
        ),
        in_specs=[vmem] * 5,
        out_specs=tuple([vmem] * 5),
        scratch_shapes=[pltpu.VMEM(state.shape, jnp.float32)],
        compiler_params=pltpu.CompilerParams(vmem_limit_bytes=40 << 20),
    )(state, w_in, b_in, w_down, b_down)


def spread_lanes(padded, held):
    for m in range(padded.shape[0]):
        def body(y, carry, m=m):
            for u in range(C1P // LANES):
                held[u, m, y] = padded[m, y, :, u * LANES : (u + 1) * LANES].astype(jnp.float32)
            return carry

        lax.fori_loop(0, padded.shape[1], body, 0)


def convolve(held, w_dw, put, back):
    tiles, batch, rows, breadth = held.shape[:4]
    height, half_w = rows - 6, breadth - 2 * EDGE

    def body(number, carry):
        u, m = number // batch, number % batch
        sums = [jnp.zeros((half_w, LANES), jnp.float32) for _ in range(height)]
        for x in range(7):
            for y in range(rows):
                window = held[u, m, y, pl.ds(EDGE - 3 + x, half_w), :]
                for i in range(height):
                    if 0 <= y - i < 7:
                        tap = (6 - (y - i)) * 7 + 6 - x if back else (y - i) * 7 + x
                        sums[i] = sums[i] + window * w_dw[u, pl.ds(tap, 1), :]
        for i in range(height):
            put(u, m, i, sums[i])
        return carry

    lax.fori_loop(0, tiles * batch, body, 0)


def rows_at(m, i, height, half_w):
    return pl.ds(pl.multiple_of((m * height + i) * half_w, half_w), half_w)


def lanes_at(u):
    return pl.ds(pl.multiple_of(u * LANES, LANES), LANES)


PART = 640


def middle_kernel(
    padded, coarse, h_zero, target, weight, w_dw, w_hidden, w_out_t, w_up, w_head,
    b_dw, gain, shift, b_hidden, b_out, b_up, b_head,
    normed, act, grad_pre, grad_mixed, grad_branch, grad_summed, grad_conv, d_up, d_head, sums,
    conv, total,
):
    cells = coarse.shape[0]
    batch, rows, breadth, _ = padded.shape
    height, half_w = rows - 6, breadth - 2 * EDGE

    def depthwise(held):
        spread_lanes(padded, held)

        def put(u, m, i, value):
            conv[rows_at(m, i, height, half_w), lanes_at(u)] = value

        convolve(held, w_dw, put, False)

    pl.run_scoped(depthwise, pltpu.VMEM((C1P // LANES, batch, rows, breadth, LANES), jnp.float32))
    pl.run_scoped(
        functools.partial(
            pointwise_kernel, coarse, h_zero, target, weight, w_hidden, w_out_t, w_up, w_head,
            b_dw, gain, shift, b_hidden, b_out, b_up, b_head,
            normed, act, grad_pre, grad_mixed, grad_branch, grad_summed, grad_conv, d_up, d_head, sums,
            conv, total,
        ),
        pltpu.VMEM((cells, CH), jnp.float32),
    )


def pointwise_kernel(
    coarse, h_zero, target, weight, w_hidden, w_out_t, w_up, w_head,
    b_dw, gain, shift, b_hidden, b_out, b_up, b_head,
    normed, act, grad_pre, grad_mixed, grad_branch, grad_summed, grad_conv, d_up, d_head, sums,
    conv, total, pre,
):
    inside = lax.broadcasted_iota(jnp.int32, (1, C1P), 1) < C1
    values = conv[...] + b_dw[...]
    mean = jnp.sum(values, axis=1, keepdims=True) * (1.0 / C1)
    centered = jnp.where(inside, values - mean, 0.0)
    scale = lax.rsqrt(jnp.sum(centered * centered, axis=1, keepdims=True) * (1.0 / C1) + 1e-06)
    conv[...] = centered * scale
    normed[...] = (conv[...] * gain[...] + shift[...]).astype(jnp.bfloat16)

    total[...] = coarse[...]
    for begin in range(0, CH, PART):
        span = slice(begin, begin + PART)
        value = product(normed[:, :C1], w_hidden[:, span]) + b_hidden[:, span]
        pre[:, span] = value
        act[:, span] = gelu(value).astype(jnp.bfloat16)
        total[:, :C1] += product_t(act[:, span], w_out_t[:, span])
    mixed = (total[...] + b_out[...]).astype(jnp.bfloat16)

    grad_mixed[...] = jnp.zeros_like(grad_mixed)
    loss = jnp.zeros((1, CIP), jnp.float32)
    head_sum = jnp.zeros((1, CIP), jnp.float32)
    up_sum = jnp.zeros((1, C0P), jnp.float32)
    for s in range(4):
        upper = product(mixed[:, :C1], w_up[s]) + b_up[...]
        summed = (upper + h_zero[s]).astype(jnp.bfloat16)
        error = product(summed, w_head[...]) + b_head[...] - target[s].astype(jnp.float32)
        weighted = weight[s] * error
        loss = loss + column_sum(weighted * error)
        grad_out = (2.0 * weighted).astype(jnp.bfloat16)
        head_sum = head_sum + column_sum(grad_out)
        if s == 0:
            d_head[...] = inner_rows(summed, grad_out)
        else:
            d_head[...] += inner_rows(summed, grad_out)
        spread = product_t(grad_out, w_head[...])
        grad_summed[s] = spread
        grad_upper = spread.astype(jnp.bfloat16)
        up_sum = up_sum + column_sum(grad_upper)
        d_up[s] = inner_rows(mixed, grad_upper)
        grad_mixed[:, :C1] += product_t(grad_upper, w_up[s])
    grad_branch[...] = grad_mixed[...].astype(jnp.bfloat16)
    sums[...] = jnp.zeros_like(sums)
    sums[0:1, 0:CIP] = loss
    sums[1:2, 0:CIP] = head_sum
    sums[2:3, 0:C0P] = up_sum
    sums[3:4, 0:C1P] = column_sum(grad_branch[...])

    total[...] = jnp.zeros_like(total)
    for begin in range(0, CH, PART):
        span = slice(begin, begin + PART)
        value = product(grad_branch[:, :C1], w_out_t[:, span]) * gelu_slope(pre[:, span])
        low = value.astype(jnp.bfloat16)
        grad_pre[:, span] = low
        sums[4:5, span] = column_sum(low)
        total[:, :C1] += product_t(low, w_hidden[:, span])

    grad_normed = total[...]
    sums[5:6, 0:C1P] = column_sum(grad_normed * conv[...])
    sums[6:7, 0:C1P] = column_sum(grad_normed)
    inward = grad_normed * gain[...]
    first = jnp.sum(inward, axis=1, keepdims=True) * (1.0 / C1)
    second = jnp.sum(inward * conv[...], axis=1, keepdims=True) * (1.0 / C1)
    value = scale * jnp.where(inside, inward - first - conv[...] * second, 0.0)
    low = value.astype(jnp.bfloat16)
    sums[7:8, 0:C1P] = column_sum(low)
    grad_conv[...] = low.reshape(grad_conv.shape)


def middle_part(padded, coarse, h_zero, target, weight, *rest):
    cells = coarse.shape[0]
    batch, rows, breadth, _ = padded.shape
    half_h, half_w = rows - 6, breadth - 2 * EDGE
    vmem = pl.BlockSpec(memory_space=pltpu.VMEM)
    f32, low = jnp.float32, jnp.bfloat16
    return pl.pallas_call(
        middle_kernel,
        out_shape=(
            jax.ShapeDtypeStruct((cells, C1P), low),
            jax.ShapeDtypeStruct((cells, CH), low),
            jax.ShapeDtypeStruct((cells, CH), low),
            jax.ShapeDtypeStruct((cells, C1P), f32),
            jax.ShapeDtypeStruct((cells, C1P), low),
            jax.ShapeDtypeStruct((4, cells, C0P), f32),
            jax.ShapeDtypeStruct((batch, half_h, half_w, C1P), low),
            jax.ShapeDtypeStruct((4, C1P, C0P), f32),
            jax.ShapeDtypeStruct((C0P, CIP), f32),
            jax.ShapeDtypeStruct((8, CH), f32),
        ),
        in_specs=[vmem] * 17,
        out_specs=tuple([vmem] * 10),
        scratch_shapes=[
            pltpu.VMEM((cells, C1P), f32),
            pltpu.VMEM((cells, C1P), f32),
        ],
        compiler_params=pltpu.CompilerParams(vmem_limit_bytes=62 << 20),
    )(padded, coarse, h_zero, target, weight, *rest)


def outer_kernel(
    padded, grad_padded, grad_conv, grad_mixed, grad_summed, a_zero, h_zero, taps, w_dw, w_down,
    d_dw, d_down, d_in, sums, held, conv,
):
    batch, height, half_w, _ = grad_conv.shape
    spread_lanes(padded, held)
    tiles = C1P // LANES
    d_dw[...] = jnp.zeros_like(d_dw)

    def taps_of(number, carry):
        u, m = number // batch, number % batch
        grads = [grad_conv[m, i, :, lanes_at(u)].astype(jnp.float32) for i in range(height)]
        for x in range(7):
            found = [jnp.zeros((8, LANES), jnp.float32) for _ in range(7)]
            for y in range(height + 6):
                window = held[u, m, y, pl.ds(EDGE - 3 + x, half_w), :]
                for i in range(height):
                    if 0 <= y - i < 7:
                        term = (window * grads[i]).reshape(half_w // 8, 8, LANES)
                        found[y - i] = found[y - i] + jnp.sum(term, axis=0)
            for dy in range(7):
                d_dw[u, pl.ds(dy * 7 + x, 1), :] += jnp.sum(found[dy], axis=0, keepdims=True)
        return carry

    lax.fori_loop(0, tiles * batch, taps_of, 0)
    spread_lanes(grad_padded, held)

    def put(u, m, i, value):
        conv[rows_at(m, i, height, half_w), lanes_at(u)] = value

    convolve(held, w_dw, put, True)
    grad_coarse = (conv[...] + grad_mixed[...]).astype(jnp.bfloat16)
    sums[...] = jnp.zeros_like(sums)
    sums[0:1, 0:C1P] = column_sum(grad_coarse)
    in_sum = jnp.zeros((1, C0P), jnp.float32)
    for s in range(4):
        d_down[s] = inner_rows(h_zero[s].astype(jnp.bfloat16), grad_coarse)
        grad_h = product_t(grad_coarse, w_down[s]) + grad_summed[s]
        grad_a = (gelu_slope(a_zero[s]) * grad_h).astype(jnp.bfloat16)
        in_sum = in_sum + column_sum(grad_a)
        if s == 0:
            d_in[...] = inner_rows(taps[s], grad_a)
        else:
            d_in[...] += inner_rows(taps[s], grad_a)
    sums[1:2, 0:C0P] = in_sum


def outer_part(padded, grad_padded, grad_conv, grad_mixed, grad_summed, a_zero, h_zero, taps, w_dw, w_down):
    cells = grad_mixed.shape[0]
    batch, rows, breadth, _ = padded.shape
    vmem = pl.BlockSpec(memory_space=pltpu.VMEM)
    f32 = jnp.float32
    return pl.pallas_call(
        outer_kernel,
        out_shape=(
            jax.ShapeDtypeStruct((C1P // LANES, 56, LANES), f32),
            jax.ShapeDtypeStruct((4, C0P, C1P), f32),
            jax.ShapeDtypeStruct((9 * CIP, C0P), f32),
            jax.ShapeDtypeStruct((8, C1P), f32),
        ),
        in_specs=[vmem] * 10,
        out_specs=tuple([vmem] * 4),
        scratch_shapes=[
            pltpu.VMEM((C1P // LANES, batch, rows, breadth, LANES), f32),
            pltpu.VMEM((cells, C1P), f32),
        ],
        compiler_params=pltpu.CompilerParams(vmem_limit_bytes=62 << 20),
    )(padded, grad_padded, grad_conv, grad_mixed, grad_summed, a_zero, h_zero, taps, w_dw, w_down)


def split_vector(vector):
    lengths = [C0, C1, C1, C1, C1, CH, C1, C0, CI]
    pieces = []
    start = 0
    for length in lengths:
        pieces.append(vector[start : start + length])
        start = start + length
    return pieces


def as_rows(piece, rows):
    flat = piece.reshape(-1)
    return jnp.pad(flat, (0, rows * LANES - flat.shape[0])).reshape(rows, LANES)


def widened(array, *shape):
    return jnp.pad(array, [(0, full - now) for full, now in zip(shape, array.shape)])


def on_device(
    inputs,
    targets,
    land_mask,
    volume,
    date_index,
    perm_narrow,
    perm_wide,
    w_in,
    w_down,
    w_dw,
    w_hidden,
    w_out,
    w_up,
    w_head,
    biases_gains,
    moment_first,
    moment_second,
):
    rows, cols = lax.axis_size("rows"), lax.axis_size("cols")
    b_in, b_down, b_dw, gain, shift, b_hidden, b_out, b_up, b_head = split_vector(biases_gains)
    weight = land_mask.astype(jnp.float32) * volume
    height, breadth = weight.shape
    half_h, half_w = (height // 2, breadth // 2)
    cells = MB * half_h * half_w
    matrices = (w_in, w_down, w_dw, w_hidden, w_out, w_up, w_head)

    def dates(field):
        picked = jnp.concatenate(
            [lax.dynamic_slice_in_dim(field, date_index[m], 1, 0) for m in range(MB)]
        )
        return widened(picked, MB, height, breadth, CIP)

    def by_subcell(field):
        chans = field.shape[-1]
        return (
            field.reshape(MB, half_h, 2, half_w, 2, chans)
            .transpose(2, 4, 0, 1, 3, 5)
            .reshape(4, cells, chans)
        )

    def line(vector, size):
        return widened(vector[None, :], 1, size)

    narrow_turn = (jnp.arange(C1)[:, None] == perm_narrow[None, :]).astype(jnp.bfloat16)
    w_in_p = widened(w_in.reshape(9, CI, C0), 9, CIP, C0P).reshape(9 * CIP, C0P)
    w_down_p = widened(w_down.reshape(4, C0, C1), 4, C0P, C1P)
    w_up_p = widened(w_up.reshape(C1, 4, C0).transpose(1, 0, 2), 4, C1, C0P)
    w_dw_p = widened(w_dw.astype(jnp.float32), 56, C1P).reshape(56, C1P // LANES, LANES).transpose(1, 0, 2)
    target = by_subcell(dates(targets))
    weight_col = jnp.broadcast_to(weight[None, :, :, None], (MB, height, breadth, 1))
    weight_col = jnp.broadcast_to(by_subcell(weight_col), (4, cells, CIP))

    state = halo(rows, cols, 1, dates(inputs), 1)
    taps, a_zero, h_zero, coarse, coarse_low = input_part(
        state, w_in_p, line(b_in, C0P), w_down_p, line(b_down, C1P)
    )
    padded = halo(rows, cols, 3, coarse_low, 2)
    (
        normed, act, grad_pre, grad_mixed, grad_branch, grad_summed, grad_conv, d_up, d_head, sums
    ) = middle_part(
        padded, coarse, h_zero, target, weight_col, w_dw_p, w_hidden, w_out.T, w_up_p,
        widened(w_head, C0P, CIP), line(b_dw, C1P), line(gain, C1P), line(shift, C1P),
        line(b_hidden, CH), line(b_out, C1P), line(b_up, C0P), line(b_head, CIP),
    )
    grad_padded = halo(rows, cols, 3, grad_conv, 3)
    d_dw, d_down, d_in, sums_out = outer_part(
        padded, grad_padded, grad_conv, grad_mixed, grad_summed, a_zero, h_zero, taps, w_dw_p, w_down_p
    )
    d_up = d_up[:, :C1, :C0].transpose(1, 0, 2).reshape(C1, 4 * C0)
    d_down = d_down[:, :C0, :C1].reshape(4 * C0, C1)
    d_in = d_in.reshape(9, CIP, C0P)[:, :CI, :C0].reshape(9 * CI, C0)
    d_dw = d_dw[:, :49].transpose(1, 0, 2).reshape(49, C1P)[:, :C1]
    d_vector = jnp.concatenate(
        [
            sums_out[1, :C0], sums_out[0, :C1], sums[7, :C1], sums[5, :C1], sums[6, :C1],
            sums[4], sums[3, :C1], sums[2, :C0], sums[1, :CI],
        ]
    )
    loss_local = jnp.sum(sums[0, :CIP])
    space = Plan(rows, cols, PADDED).space
    norm_t = jnp.einsum(
        "nk,kj->jn", normed[:, :C1], narrow_turn, preferred_element_type=jnp.float32
    ).astype(jnp.bfloat16)
    branch_r = product(grad_branch[:, :C1], widened(narrow_turn, C1, C1P)).astype(jnp.bfloat16)
    pieces = (
        jnp.pad(as_rows(d_in, ROW_AT[1] - ROW_AT[0]), ((ROW_AT[0], 0), (0, 0))),
        as_rows(d_dw, ROW_AT[3] - ROW_AT[2]),
        as_rows(d_head[:C0, :CI], ROW_AT[7] - ROW_AT[6]),
        as_rows(d_vector, space - ROW_AT[7]),
    )
    grad = place_gradients(space, norm_t, branch_r, grad_pre, act, perm_wide, d_up, d_down, pieces)
    lead = jnp.arange(8)[:, None]
    extra = jnp.where(lead == 0, loss_local, jnp.where(lead == 1, jnp.sum(weight), 0.0))
    extra = jnp.where(jnp.arange(LANES)[None, :] == 0, extra, 0.0)
    plan, (gathered, first, second, totals) = exchange(
        rows, cols, grad, moment_first, moment_second, extra
    )
    hidden_p, out_p, new_up, new_down, small_a, small_b, small_c = unpack(plan, gathered, w_up, w_down)
    small = {0: (small_a, 0), 2: (small_b, 1), 6: (small_c, 2), 7: (small_c, 2)}
    whole = {
        1: new_down,
        3: rebuild_hidden(hidden_p, perm_narrow, perm_wide, w_hidden),
        4: rebuild_out(out_p, perm_narrow, perm_wide, w_out),
        5: new_up,
    }
    olds = matrices + (biases_gains,)
    news = []
    for index, old in enumerate(olds):
        if index in whole:
            news.append(whole[index])
        else:
            source, which = small[index]
            start = FLAT_AT[index] - KEPT[which][0] * LANES
            piece = source.reshape(-1)[start : start + old.size].reshape(old.shape)
            news.append(moved(old, piece) if index < 7 else old - learn_rate * piece)
    return tuple(news) + (
        first.reshape(-1),
        second.reshape(-1),
        totals[0, 0],
        MB * CI * totals[1, 0],
        totals[8, 0],
    )


def solution(mesh):
    return jax.shard_map(
        on_device,
        mesh=mesh,
        in_specs=(
            P(None, "rows", "cols", None),
            P(None, "rows", "cols", None),
            P("rows", "cols"),
            P("rows", "cols"),
            P(),
            P(),
            P(),
            P(),
            P(),
            P(),
            P(),
            P(),
            P(),
            P(),
            P(),
            P(("rows", "cols")),
            P(("rows", "cols")),
        ),
        out_specs=(
            P(),
            P(),
            P(),
            P(),
            P(),
            P(),
            P(),
            P(),
            P(("rows", "cols")),
            P(("rows", "cols")),
            P(),
            P(),
            P(),
        ),
        check_vma=False,
    )
```

```python
import functools

import jax
import jax.numpy as jnp
from jax import lax
from jax.experimental import pallas as pl
from jax.experimental.pallas import tpu as pltpu
from jax.sharding import PartitionSpec as P

CI = 77
C0 = 200
C1 = 800
CH = 3200
MB = 2
STEP = 5
LANES = 128
MESH = pl.DeviceIdType.MESH
ROUNDER = 12582912.0

decay_first = 0.9
decay_second = 0.99
epsilon = 1e-08
learn_rate = 0.02
weight_decay = 0.1
clip_limit = 1.0

VEC = 4 * C1 + CH + C1 + 2 * C0 + CI
SIZES = (9 * CI * C0, 4 * C0 * C1, 49 * C1, C1 * CH, CH * C1, C1 * 4 * C0, C0 * CI, VEC)
PADDED = 6602752
FLAT_AT = []
ROW_AT = []
for size in SIZES:
    flat_here = FLAT_AT[-1] + SIZES[len(FLAT_AT) - 1] if FLAT_AT else PADDED - sum(SIZES)
    row_here = ROW_AT[-1] + -(-SIZES[len(ROW_AT) - 1] // 1024) * 8 if ROW_AT else 0
    row_here = max(row_here, -(-flat_here // 1024) * 8)
    FLAT_AT.append(flat_here)
    ROW_AT.append(row_here)
SHIFTS = []
for flat_here, row_here, size in zip(FLAT_AT, ROW_AT, SIZES):
    moved = divmod(row_here * LANES - flat_here, LANES)
    if SHIFTS and SHIFTS[-1][:2] == moved:
        SHIFTS[-1] = moved + (SHIFTS[-1][2], flat_here + size)
    else:
        SHIFTS.append(moved + (flat_here, flat_here + size))
MAX_SHIFT = max(s[0] for s in SHIFTS) + 1


def bit_masks(bits):
    masks = [()]
    for bit in bits:
        masks = masks + [m + (bit,) for m in masks]
    return sorted(masks, key=lambda m: -len(m))


class Plan:
    def __init__(self, rows, cols, total):
        self.rows, self.cols, self.count = rows, cols, rows * cols
        self.share = total // LANES // self.count
        self.bits = rows.bit_length() - 1
        need = 7 + self.share + MAX_SHIFT + 1
        self.block = 64 if need > 1024 else 32
        self.window = -(-need // (2 * self.block)) * 2 * self.block
        self.part = self.window // 2
        self.blocks = self.part // self.block
        self.scales = self.blocks
        upper = list(range(1, self.bits))
        self.orders = [upper, upper[1:] + upper[:1]]
        self.stages = len(upper)
        self.space = (self.share * (self.count - 1)) // 8 * 8 + self.window
        self.padded = -(-self.share // 16) * 16
        cut = -(-self.padded // 32) * 16
        self.cuts = [(0, cut), (cut, self.padded - cut)]
        self.local = self.count // 2


def exchange_kernel(
    plan, grad, m_first, m_second, extra, full, first, second, totals,
    acc, near, q_send, q_recv, s_send, s_recv, z_send, z_recv, zs_send, zs_recv,
    rolled, step, low, stats,
    sem_load, sem_near_s, sem_near_r, sem_qs, sem_qr, sem_ss, sem_sr,
    sem_zs, sem_zr, sem_zss, sem_zsr, sem_ts, sem_tr, sem_own,
    sem_gs, sem_gr, sem_hs, sem_hr, sem_cs, sem_cr,
):
    nr, nc, n = plan.rows, plan.cols, plan.count
    r = lax.axis_index("rows")
    c = lax.axis_index("cols")
    me = r * nc + c
    part, window, share = plan.part, plan.window, plan.share

    def flipped(mask):
        out = r
        for bit in mask:
            here = (r // (1 << bit)) % 2
            out = out + (1 - 2 * here) * (1 << bit)
        return out

    def remote(src, dst, send, recv, row, col):
        return pltpu.make_async_remote_copy(
            src_ref=src, dst_ref=dst, send_sem=send, recv_sem=recv,
            device_id=(row, col), device_id_type=MESH,
        )

    barrier = pltpu.get_barrier_semaphore()

    def greet(d, carry):
        k = lax.rem(me + d, n)
        pl.semaphore_signal(barrier, inc=1, device_id=(k // nc, k % nc), device_id_type=MESH)
        return carry

    lax.fori_loop(1, n, greet, 0)
    pl.semaphore_wait(barrier, n - 1)

    upper = list(range(1, plan.bits))
    masks = bit_masks(upper)

    def local_index(mask, col):
        return (flipped(mask) // 2) * nc + col

    def window_start(row, col):
        return pl.multiple_of((share * (row * nc + col)) // 8 * 8, 8)

    def near_copy(mask, col):
        row = flipped(mask + (0,))
        return remote(
            grad.at[pl.ds(window_start(row, col), window)],
            near.at[local_index(mask, col)],
            sem_near_s.at[local_index(mask, col)], sem_near_r.at[local_index(mask, col)],
            flipped((0,)), c,
        )

    def load_copy(mask, col):
        index = local_index(mask, col)
        return pltpu.make_async_copy(
            grad.at[pl.ds(window_start(flipped(mask), col), window)], acc.at[index], sem_load.at[index]
        )

    def begin(d, carry):
        for mask in masks:
            near_copy(mask, lax.rem(c + d, nc)).start()
            load_copy(mask, lax.rem(c + d, nc)).start()
        return carry

    lax.fori_loop(1, nc + 1, begin, 0)

    def encode(index, p, q_ref, s_ref):
        def body(b, carry):
            at = pl.ds(pl.multiple_of(b * plan.block, plan.block), plan.block)
            rows_at = pl.ds(pl.multiple_of(p * part + b * plan.block, 8), plan.block)
            values = acc[index, rows_at, :]
            top = jnp.maximum(jnp.max(jnp.abs(values), axis=0, keepdims=True), 1e-30)
            scaled = values * (32766.0 / top)
            scaled = (scaled + ROUNDER) - ROUNDER
            q_ref[at, :] = scaled.astype(jnp.int32).astype(jnp.int16)
            s_ref[pl.ds(b, 1), :] = top * (1.0 / 32766.0)
            return carry

        lax.fori_loop(0, plan.blocks, body, 0)

    def decode(index, p, q_ref, s_ref):
        def body(b, carry):
            at = pl.ds(pl.multiple_of(b * plan.block, plan.block), plan.block)
            rows_at = pl.ds(pl.multiple_of(p * part + b * plan.block, 8), plan.block)
            acc[index, rows_at, :] += q_ref[at, :].astype(jnp.float32) * s_ref[pl.ds(b, 1), :]
            return carry

        lax.fori_loop(0, plan.blocks, body, 0)

    def stage_base(stage):
        return sum((1 << (plan.stages - 1 - s)) for s in range(stage)) * nc

    def hop(p, stage, slot):
        row = flipped((plan.orders[p][stage],))
        at = stage_base(stage) + slot
        return (
            remote(q_send.at[p, at], q_recv.at[p, at], sem_qs.at[p, at], sem_qr.at[p, at], row, c),
            remote(s_send.at[p, at], s_recv.at[p, at], sem_ss.at[p, at], sem_sr.at[p, at], row, c),
        )

    def send_stage(p, stage, number, mask, col):
        bit = plan.orders[p][stage]
        index = local_index(mask + (bit,), col)
        slot = number * nc + col
        at = stage_base(stage) + slot
        encode(index, p, q_send.at[p, at], s_send.at[p, at])
        for copy in hop(p, stage, slot):
            copy.start()

    def take_stage(p, stage, number, mask, col):
        slot = number * nc + col
        for copy in hop(p, stage, slot):
            copy.wait_recv()
        at = stage_base(stage) + slot
        decode(local_index(mask, col), p, q_recv.at[p, at], s_recv.at[p, at])

    def free_masks(p, stage):
        rest = plan.orders[p][stage + 1 :]
        found = bit_masks(rest)
        if rest:
            found = [m for m in found if rest[0] in m] + [m for m in found if rest[0] not in m]
        return found

    def far_copy(p, d):
        col = lax.rem(c + d, nc)
        return (
            remote(z_send.at[p, d - 1], z_recv.at[p, d - 1], sem_zs.at[p, d - 1], sem_zr.at[p, d - 1], r, col),
            remote(zs_send.at[p, d - 1], zs_recv.at[p, d - 1], sem_zss.at[p, d - 1], sem_zsr.at[p, d - 1], r, col),
        )

    def join(d):
        col = lax.rem(c + d, nc)
        for mask in masks:
            index = local_index(mask, col)
            near_copy(mask, col).wait_recv()
            load_copy(mask, col).wait()

            def body(b, inner, index=index):
                at = pl.ds(pl.multiple_of(b * plan.block, plan.block), plan.block)
                acc[index, at, :] += near[index, at, :]
                return inner

            lax.fori_loop(0, 2 * plan.blocks, body, 0)
            for p in range(2):
                bit = plan.orders[p][0]
                if bit in mask:
                    rest = tuple(b for b in mask if b != bit)
                    options = free_masks(p, 0)
                    number = [sorted(o) for o in options].index(sorted(rest))
                    send_stage(p, 0, number, rest, col)

    def take(stage, d):
        col = lax.rem(c + d, nc)
        for number in range(1 << (plan.stages - 1 - stage)):
            for p in range(2):
                mask = free_masks(p, stage)[number]
                take_stage(p, stage, number, mask, col)
                if stage + 1 < plan.stages:
                    bit = plan.orders[p][stage + 1]
                    if bit in mask:
                        rest = tuple(b for b in mask if b != bit)
                        options = free_masks(p, stage + 1)
                        following = [sorted(o) for o in options].index(sorted(rest))
                        send_stage(p, stage + 1, following, rest, col)
                else:
                    @pl.when(d < nc)
                    def _(p=p):
                        encode(local_index((), col), p, z_send.at[p, d - 1], zs_send.at[p, d - 1])
                        for copy in far_copy(p, d):
                            copy.start()

    def turn_of(t, carry):
        @pl.when(t <= nc)
        def _():
            join(t)

        for stage in range(plan.stages):
            d = t - 1 - stage

            @pl.when((d >= 1) & (d <= nc))
            def _(stage=stage, d=d):
                take(stage, d)

        return carry

    lax.fori_loop(1, nc + plan.stages + 1, turn_of, 0)

    mine = local_index((), c)

    def gather_far(d, carry):
        for p in range(2):
            for copy in far_copy(p, d):
                copy.wait_recv()
            decode(mine, p, z_recv.at[p, d - 1], zs_recv.at[p, d - 1])
        return carry

    lax.fori_loop(1, nc, gather_far, 0)

    offset = lax.rem(share * me, 8)
    for number, (shift_rows, shift_lanes, begin, end) in enumerate(SHIFTS):
        def turn(b, carry, number=number, shift_lanes=shift_lanes):
            at = pl.ds(pl.multiple_of(b * plan.block, plan.block), plan.block)
            rolled[number, at, :] = pltpu.roll(acc[mine, at, :], LANES - shift_lanes, 1)
            return carry

        lax.fori_loop(0, 2 * plan.blocks, turn, 0)

    def share_rows(start, length):
        lane = lax.broadcasted_iota(jnp.int32, (length, LANES), 1)
        line = lax.broadcasted_iota(jnp.int32, (length, LANES), 0)
        flat = (share * me + start + line) * LANES + lane
        out = jnp.zeros((length, LANES), jnp.float32)
        for number, (shift_rows, shift_lanes, begin, end) in enumerate(SHIFTS):
            here = rolled[number, pl.ds(offset + start + shift_rows, length), :]
            after = rolled[number, pl.ds(offset + start + shift_rows + 1, length), :]
            value = jnp.where(lane < LANES - shift_lanes, here, after)
            out = jnp.where((flat >= begin) & (flat < end), value, out)
        return out

    chunk = 32
    whole, tail = share // chunk, share % chunk

    def square(b, total):
        start = pl.multiple_of(b * chunk, chunk)
        value = share_rows(start, chunk)
        step[pl.ds(start, chunk), :] = value
        return total + jnp.sum((value * value).reshape(chunk // 8, 8, LANES), axis=0)

    total = lax.fori_loop(0, whole, square, jnp.zeros((8, LANES), jnp.float32))
    stats[me, 8:16, :] = extra[...]
    stats[me, 0:8, :] = total
    if tail:
        value = share_rows(whole * chunk, tail)
        step[whole * chunk : share, :] = value
        stats[me, 0:1, :] += jnp.sum(value * value, axis=0, keepdims=True)

    def stat_copy(target, source):
        return remote(
            stats.at[me], stats.at[me], sem_ts.at[target], sem_tr.at[me], target // nc, target % nc
        )

    def stat_wait(source):
        return remote(
            stats.at[source], stats.at[source], sem_ts.at[source], sem_tr.at[source],
            source // nc, source % nc,
        )

    def send_stat(d, carry):
        stat_copy(lax.rem(me + d, n), me).start()
        return carry

    lax.fori_loop(1, n, send_stat, 0)

    def wait_stat(d, carry):
        stat_wait(lax.rem(me + d, n)).wait_recv()
        return carry

    lax.fori_loop(1, n, wait_stat, 0)

    def add_stat(k, total):
        return total + stats[k]

    sums = lax.fori_loop(0, n, add_stat, jnp.zeros((16, LANES), jnp.float32))
    norm = jnp.sqrt(jnp.sum(sums[0:8], keepdims=True))
    totals[0:8, :] = sums[8:16]
    totals[8:16, :] = jnp.broadcast_to(norm, (8, LANES))
    clip = jnp.minimum(1.0, clip_limit / norm)

    def update(start, length):
        clipped = step[pl.ds(start, length), :] * clip
        one = decay_first * m_first[pl.ds(start, length), :] + (1.0 - decay_first) * clipped
        two = decay_second * m_second[pl.ds(start, length), :] + (1.0 - decay_second) * clipped * clipped
        first[pl.ds(start, length), :] = one
        second[pl.ds(start, length), :] = two
        step[pl.ds(start, length), :] = (
            one / (1.0 - decay_first**STEP) / (jnp.sqrt(two / (1.0 - decay_second**STEP)) + epsilon)
        )

    def update_chunk(b, carry):
        update(pl.multiple_of(b * chunk, chunk), chunk)
        return carry

    lax.fori_loop(0, whole, update_chunk, 0)
    if tail:
        update(whole * chunk, tail)
    if plan.padded > share:
        step[share : plan.padded, :] = jnp.zeros((plan.padded - share, LANES), jnp.float32)

    def narrow(b, carry):
        at = pl.ds(pl.multiple_of(b * 16, 16), 16)
        low[at, :] = step[at, :].astype(jnp.bfloat16)
        return carry

    lax.fori_loop(0, plan.padded // 16, narrow, 0)

    own = pltpu.make_async_copy(low, full.at[me], sem_own)
    own.start()
    own.wait()

    back = [list(reversed(order)) for order in plan.orders]

    def piece(mask, col, p):
        begin, length = plan.cuts[p]
        return full.at[flipped(mask) * nc + col, pl.ds(begin, length)]

    def along(direction, col, p, receive):
        step_col = 1 if direction == 0 else -1
        target = c - step_col if receive else c + step_col
        ref = piece((), col, p)
        return remote(ref, ref, sem_gs.at[direction, col, p], sem_gr.at[direction, col, p], r, target)

    def gather_masks(p, stage):
        return bit_masks(back[p][:stage])

    def gather_base(stage):
        return sum(1 << s for s in range(stage)) * nc

    def across(p, stage, number, mask, col):
        at = gather_base(stage) + number * nc + col
        ref = piece(mask, col, p)
        return remote(ref, ref, sem_hs.at[p, at], sem_hr.at[p, at], flipped((back[p][stage],)), c)

    def across_recv(p, stage, number, mask, col):
        at = gather_base(stage) + number * nc + col
        ref = piece(mask + (back[p][stage],), col, p)
        return remote(ref, ref, sem_hs.at[p, at], sem_hr.at[p, at], flipped((back[p][stage],)), c)

    def inward(p, mask, col):
        number = masks.index(tuple(sorted(mask)))
        at = number * nc + col
        ref = piece(mask, col, p)
        return remote(ref, ref, sem_cs.at[p, at], sem_cr.at[p, at], flipped((0,)), c)

    def inward_recv(p, mask, col):
        number = masks.index(tuple(sorted(mask)))
        at = number * nc + col
        ref = piece(mask + (0,), col, p)
        return remote(ref, ref, sem_cs.at[p, at], sem_cr.at[p, at], flipped((0,)), c)

    def spread(p, mask, col, stage):
        for later in range(stage, plan.stages):
            options = [sorted(o) for o in gather_masks(p, later)]
            if sorted(mask) in options:
                across(p, later, options.index(sorted(mask)), mask, col).start()
        inward(p, mask, col).start()

    def near_cols(t):
        if t == 0:
            return [(0, c)]
        return [(0, c - t), (1, c + t)]

    def inside(col):
        return (col >= 0) & (col < nc)

    for time in range(nc + plan.stages):
        for stage in range(plan.stages + 1):
            t = time - stage
            if not 0 <= t < nc:
                continue
            if stage == 0:
                if t == 0:
                    for p in range(2):
                        @pl.when(c < nc - 1)
                        def _(p=p):
                            along(0, c, p, False).start()

                        @pl.when(c > 0)
                        def _(p=p):
                            along(1, c, p, False).start()

                        spread(p, (), c, 0)
                else:
                    for direction, col in near_cols(t):
                        @pl.when(inside(col))
                        def _(direction=direction, col=col):
                            for p in range(2):
                                along(direction, col, p, True).wait_recv()
                                if direction == 0:
                                    @pl.when(c < nc - 1)
                                    def _():
                                        along(0, col, p, False).start()
                                else:
                                    @pl.when(c > 0)
                                    def _():
                                        along(1, col, p, False).start()
                                spread(p, (), col, 0)
            else:
                for direction, col in near_cols(t):
                    @pl.when(inside(col))
                    def _(col=col, stage=stage):
                        for number in range(1 << (stage - 1)):
                            for p in range(2):
                                mask = gather_masks(p, stage - 1)[number]
                                across_recv(p, stage - 1, number, mask, col).wait_recv()
                                spread(p, mask + (back[p][stage - 1],), col, stage)

    for mask in masks:
        def finish(col, carry, mask=mask):
            for p in range(2):
                inward_recv(p, mask, col).wait_recv()
                inward(p, mask, col).wait_send()
            near_copy(mask, col).wait_send()
            return carry

        lax.fori_loop(0, nc, finish, 0)
    for p in range(2):
        for stage in range(plan.stages):
            for number, mask in enumerate(gather_masks(p, stage)):
                def sent(col, carry, p=p, stage=stage, number=number, mask=mask):
                    across(p, stage, number, mask, col).wait_send()
                    return carry

                lax.fori_loop(0, nc, sent, 0)
            for number in range(1 << (plan.stages - 1 - stage)):
                def left(col, carry, p=p, stage=stage, number=number):
                    for copy in hop(p, stage, number * nc + col):
                        copy.wait_send()
                    return carry

                lax.fori_loop(0, nc, left, 0)

        def gone(col, carry, p=p):
            @pl.when((col <= c) & (c < nc - 1))
            def _():
                along(0, col, p, False).wait_send()

            @pl.when((col >= c) & (c > 0))
            def _():
                along(1, col, p, False).wait_send()

            return carry

        lax.fori_loop(0, nc, gone, 0)

        def far_gone(d, carry, p=p):
            for copy in far_copy(p, d):
                copy.wait_send()
            return carry

        lax.fori_loop(1, nc, far_gone, 0)

    def stat_gone(d, carry):
        stat_copy(lax.rem(me + d, n), me).wait_send()
        return carry

    lax.fori_loop(1, n, stat_gone, 0)


def exchange(rows, cols, grad, m_first, m_second, extra):
    plan = Plan(rows, cols, m_first.size * rows * cols)
    n, nc, share = plan.count, plan.cols, plan.share
    hops = sum(1 << s for s in range(plan.stages)) * nc
    dma = pltpu.SemaphoreType.DMA
    far = max(nc - 1, 1)
    vmem = pl.BlockSpec(memory_space=pltpu.VMEM)
    hbm = pl.BlockSpec(memory_space=pl.ANY)
    return plan, pl.pallas_call(
        functools.partial(exchange_kernel, plan),
        out_shape=(
            jax.ShapeDtypeStruct((n, plan.padded, LANES), jnp.bfloat16),
            jax.ShapeDtypeStruct((share, LANES), jnp.float32),
            jax.ShapeDtypeStruct((share, LANES), jnp.float32),
            jax.ShapeDtypeStruct((16, LANES), jnp.float32),
        ),
        in_specs=[hbm, vmem, vmem, vmem],
        out_specs=(hbm, vmem, vmem, vmem),
        scratch_shapes=[
            pltpu.VMEM((plan.local, plan.window, LANES), jnp.float32),
            pltpu.VMEM((plan.local, plan.window, LANES), jnp.float32),
            pltpu.VMEM((2, hops, plan.part, LANES), jnp.int16),
            pltpu.VMEM((2, hops, plan.part, LANES), jnp.int16),
            pltpu.VMEM((2, hops, plan.scales, LANES), jnp.float32),
            pltpu.VMEM((2, hops, plan.scales, LANES), jnp.float32),
            pltpu.VMEM((2, far, plan.part, LANES), jnp.int16),
            pltpu.VMEM((2, far, plan.part, LANES), jnp.int16),
            pltpu.VMEM((2, far, plan.scales, LANES), jnp.float32),
            pltpu.VMEM((2, far, plan.scales, LANES), jnp.float32),
            pltpu.VMEM((len(SHIFTS), plan.window, LANES), jnp.float32),
            pltpu.VMEM((plan.padded, LANES), jnp.float32),
            pltpu.VMEM((plan.padded, LANES), jnp.bfloat16),
            pltpu.VMEM((n, 16, LANES), jnp.float32),
            dma((plan.local,)), dma((plan.local,)), dma((plan.local,)),
            dma((2, hops)), dma((2, hops)), dma((2, hops)), dma((2, hops)),
            dma((2, far)), dma((2, far)), dma((2, far)), dma((2, far)),
            dma((n,)), dma((n,)), dma,
            dma((2, nc, 2)), dma((2, nc, 2)),
            dma((2, hops)), dma((2, hops)),
            dma((2, plan.local)), dma((2, plan.local)),
        ],
        compiler_params=pltpu.CompilerParams(
            collective_id=0, has_side_effects=True, vmem_limit_bytes=56 << 20
        ),
    )(grad, m_first.reshape(share, LANES), m_second.reshape(share, LANES), extra)


WIDE = CH + LANES
KEPT = ((8, 1104), (6096, 6408), (51400, 51584))
PLACES = tuple(divmod(FLAT_AT[i], LANES) for i in (3, 4, 5, 1))

def unpack_kernel(plan, gathered, old_up, old_down, hidden, out, up, down, small_a, small_b, small_c, held, flat, woven, sems):
    n, share = plan.count, plan.share
    step = CH // LANES

    def fetch(k, slot):
        return pltpu.make_async_copy(gathered.at[k], held.at[slot], sems.at[slot])

    fetch(0, 0).start()

    def widen(k, carry):
        slot = lax.rem(k, 2)

        @pl.when(k + 1 < n)
        def _():
            fetch(k + 1, 1 - slot).start()

        fetch(k, slot).wait()

        def body(b, inner):
            at = pl.ds(pl.multiple_of(b * 16, 16), 16)
            flat[pl.ds(share * k + b * 16, 16), :] = held[slot, at, :].astype(jnp.float32)
            return inner

        lax.fori_loop(0, plan.padded // 16, body, 0, unroll=4)
        return carry

    lax.fori_loop(0, n, widen, 0)

    for ref, (row, lane) in zip((hidden, out), PLACES):
        def column(t, carry, ref=ref, row=row):
            for begin in range(0, C1, 160):
                values = flat[pl.ds(row + begin * step + t, 160, stride=step), :]
                ref[begin : begin + 160, pl.ds(pl.multiple_of(t * LANES, LANES), LANES)] = values.astype(
                    jnp.bfloat16
                )
            return carry

        lax.fori_loop(0, WIDE // LANES, column, 0)

    quarter = C1 // 4
    for ref, old, (row, lane) in zip((up, down), (old_up, old_down), PLACES[2:]):
        for u in range(-(-C1 // LANES)):
            width = min(LANES, C1 - u * LANES)
            place = lax.broadcasted_iota(jnp.int32, (quarter, LANES), 1)
            for b in range(4):
                first, rest = divmod(C1 * b + lane, LANES)
                here = flat[pl.ds(row + first + u, quarter, stride=step), :]
                after = flat[pl.ds(row + first + u + 1, quarter, stride=step), :]
                value = pltpu.roll(jnp.where(place >= rest, here, after), LANES - rest, 1)
                woven[pl.ds(b, quarter, stride=4), :] = value
            at = slice(u * LANES, u * LANES + width)
            ref[:, at] = moved(old[:, at], woven[:, :width])
    for ref, (begin, end) in zip((small_a, small_b, small_c), KEPT):
        ref[...] = flat[begin:end, :]


def unpack(plan, gathered, old_up, old_down):
    lines = PADDED // LANES
    vmem = pl.BlockSpec(memory_space=pltpu.VMEM)
    return pl.pallas_call(
        functools.partial(unpack_kernel, plan),
        out_shape=tuple(jax.ShapeDtypeStruct((C1, WIDE), jnp.bfloat16) for _ in range(2))
        + tuple(jax.ShapeDtypeStruct((C1, C1), jnp.float32) for _ in range(2))
        + tuple(jax.ShapeDtypeStruct((end - begin, LANES), jnp.float32) for begin, end in KEPT),
        in_specs=[pl.BlockSpec(memory_space=pl.ANY), vmem, vmem],
        out_specs=tuple([vmem] * 7),
        scratch_shapes=[
            pltpu.VMEM((2, plan.padded, LANES), jnp.bfloat16),
            pltpu.VMEM((-(-lines // 8) * 8 + 16, LANES), jnp.float32),
            pltpu.VMEM((C1, LANES), jnp.float32),
            pltpu.SemaphoreType.DMA((2,)),
        ],
        compiler_params=pltpu.CompilerParams(vmem_limit_bytes=54 << 20),
    )(gathered, old_up, old_down)


def moved(old, direction):
    return old.astype(jnp.float32) * (1.0 - learn_rate * weight_decay) - learn_rate * direction


def one_hot(condition):
    return jnp.where(condition, 1.0, 0.0).astype(jnp.bfloat16)


def product(left, right):
    return jnp.dot(left, right, preferred_element_type=jnp.float32)


def product_t(left, right):
    return lax.dot_general(left, right, (((1,), (1,)), ((), ())), preferred_element_type=jnp.float32)


TILE = 640


DEEP = 256


def turn_kernel(prepare, packed, narrow, wide, old, new, lines):
    depth = lines.shape[1]

    @pl.when(pl.program_id(0) == 0)
    def _():
        prepare(packed, narrow, lines)

    base = pl.program_id(0) * TILE
    direction = None
    for begin in range(0, depth, DEEP):
        end = min(begin + DEEP, depth)
        place = wide[begin:end, :] - base
        lane = lax.broadcasted_iota(jnp.int32, (end - begin, LANES), 1)
        hot = jnp.concatenate([one_hot(lane + u == place) for u in range(0, TILE, LANES)], axis=1)
        term = product(lines[:, begin:end], hot)
        direction = term if direction is None else direction + term
    new[...] = moved(old[...], direction)


def prepare_hidden(packed, narrow, lines):
    turn = one_hot(lax.broadcasted_iota(jnp.int32, (C1, C1), 0) == narrow[...])
    for begin in range(0, WIDE, 832):
        lines[:, begin : begin + 832] = product(turn, packed[:, begin : begin + 832]).astype(jnp.bfloat16)


def quarter_spans(lane):
    spans = []
    for b in range(4):
        begin = (C1 * b + lane) // LANES * LANES
        end = -(-(C1 * b + lane + C1) // LANES) * LANES
        spans.append((begin, end))
    return spans


def prepare_out(packed, narrow, lines):
    for b, (begin, end) in enumerate(quarter_spans(PLACES[1][1])):
        turn = one_hot(
            lax.broadcasted_iota(jnp.int32, (C1, end - begin), 0) == narrow[b : b + 1, begin:end]
        )
        lines[:, b * C1 : (b + 1) * C1] = product_t(turn, packed[:, begin:end]).astype(jnp.bfloat16)


def turn_back(prepare, packed, narrow, wide, old):
    depth = wide.shape[0]
    return pl.pallas_call(
        functools.partial(turn_kernel, prepare),
        out_shape=jax.ShapeDtypeStruct((C1, CH), jnp.float32),
        grid=(CH // TILE,),
        in_specs=[
            pl.BlockSpec((C1, WIDE), lambda i: (0, 0)),
            pl.BlockSpec(narrow.shape, lambda i: (0, 0)),
            pl.BlockSpec((depth, LANES), lambda i: (0, 0)),
            pl.BlockSpec((C1, TILE), lambda i: (0, i)),
        ],
        out_specs=pl.BlockSpec((C1, TILE), lambda i: (0, i)),
        scratch_shapes=[pltpu.VMEM((C1, depth), jnp.bfloat16)],
        compiler_params=pltpu.CompilerParams(vmem_limit_bytes=48 << 20),
    )(packed, narrow, jnp.broadcast_to(wide[:, None], (depth, LANES)), old)


def rebuild_hidden(packed, narrow, wide, old):
    lane = PLACES[0][1]
    shifted = jnp.full((WIDE,), -1, jnp.int32).at[lane : lane + CH].set(wide)
    return turn_back(prepare_hidden, packed, narrow[None, :], shifted, old)


def rebuild_out(packed, narrow, wide, old):
    lane = PLACES[1][1]
    place = jnp.arange(WIDE)
    lanes = jnp.full((WIDE,), -1, jnp.int32).at[lane : lane + CH].set(jnp.tile(narrow, 4))
    table = jnp.stack(
        [
            jnp.where((place >= C1 * b + lane) & (place < C1 * (b + 1) + lane), lanes, -1)
            for b in range(4)
        ]
    )
    order = wide.reshape(C1, 4).T.reshape(-1)
    return turn_back(prepare_out, packed, table, order, old.T).T


def weave(source, rows, put):
    for t in range(CH // LANES):
        b, begin = divmod(t * LANES, C1)
        u, rest = divmod(begin, LANES)
        place = lax.broadcasted_iota(jnp.int32, (rows, LANES), 1)
        value = source[u, pl.ds(b, rows, stride=4), :]
        if rest:
            if begin + LANES - rest < C1:
                after = source[u + 1, pl.ds(b, rows, stride=4), :]
                value = jnp.where(place >= rest, value, after)
            value = pltpu.roll(value, LANES - rest, 1)
        left = C1 - begin
        if left < LANES:
            following = source[0, pl.ds(b + 1, rows, stride=4), :]
            value = jnp.where(place < left, value, pltpu.roll(following, left, 1))
        put(t, value)


def place_kernel(
    nr, nc, normed, branch, pre, act, narrow_row, narrow_col, wide, up, cells,
    grad, padded, hidden, out, loose, up_rows, norm_t, branch_r, halo_cells,
    sem_out, sems, sem_halo_s, sem_halo_r,
):
    step = pl.program_id(0)
    steps = pl.num_programs(0)
    ratio = CH // LANES
    lines = TILE // 4
    tiles = TILE // LANES

    def out_copy(n):
        rows = lines * ratio
        return pltpu.make_async_copy(
            out.at[pl.ds(pl.multiple_of(n * rows, 8), rows)],
            grad.at[pl.ds(pl.multiple_of(ROW_AT[4] + n * rows, 8), rows)],
            sem_out.at[n],
        )

    copies = [
        pltpu.make_async_copy(ref, grad.at[pl.ds(row, ref.shape[0])], sems.at[i])
        for i, (ref, row) in enumerate(((up_rows, ROW_AT[5]), (hidden, ROW_AT[3])))
    ] + [pltpu.make_async_copy(halo_cells, padded, sems.at[2])]

    @pl.when(step == 0)
    def _():
        halo_start(nr, nc, 3, cells, halo_cells, sem_halo_s, sem_halo_r)
        line = lax.broadcasted_iota(jnp.int32, (C1, C1), 1)
        norm_t[...] = product_t(one_hot(line == narrow_col[:, 0:1]), normed[:, :C1]).astype(jnp.bfloat16)
        line = lax.broadcasted_iota(jnp.int32, (C1, C1P), 0)
        branch_r[...] = product(branch[:, :C1], one_hot(line == narrow_row[...])).astype(jnp.bfloat16)
        for u in range(-(-C1 // LANES)):
            width = min(LANES, C1 - u * LANES)
            loose[u, :, 0:width] = up[0:C1, u * LANES : u * LANES + width]

        def put(t, value):
            up_rows[pl.ds(t, C1 // 4, stride=ratio), :] = value

        weave(loose, C1 // 4, put)
        copies[0].start()

    turned_pre = turned_act = None
    for begin in range(0, CH, DEEP):
        end = min(begin + DEEP, CH)
        line = lax.broadcasted_iota(jnp.int32, (end - begin, TILE), 0) + begin
        hot = one_hot(line == wide[...])
        one = product(pre[:, begin:end], hot)
        two = product(act[:, begin:end], hot)
        turned_pre = one if turned_pre is None else turned_pre + one
        turned_act = two if turned_act is None else turned_act + two
    part = product(norm_t[...], turned_pre.astype(jnp.bfloat16))
    for t in range(tiles):
        hidden[pl.ds(step * tiles + t, C1, stride=ratio), :] = part[:, t * LANES : (t + 1) * LANES]
    part = inner_rows(turned_act.astype(jnp.bfloat16), branch_r[...])
    for u in range(-(-C1 // LANES)):
        loose[u, 0:TILE, :] = part[:, u * LANES : (u + 1) * LANES]

    def put_out(t, value):
        out[pl.ds(step * (lines * ratio) + t, lines, stride=ratio), :] = value

    weave(loose, lines, put_out)
    out_copy(step).start()

    @pl.when(step == steps - 1)
    def _():
        copies[1].start()
        halo_finish(nr, nc, 3, cells, halo_cells, sem_halo_s, sem_halo_r)
        copies[2].start()

        def finish(n, carry):
            out_copy(n).wait()
            return carry

        lax.fori_loop(0, steps, finish, 0)
        for copy in copies:
            copy.wait()


def place_gradients(nr, nc, space, normed, branch, pre, act, narrow, wide, up, cells):
    def whole(array):
        return pl.BlockSpec(
            array.shape, lambda i: (0,) * len(array.shape), pipeline_mode=pl.Buffered(1)
        )

    hbm = pl.BlockSpec(memory_space=pl.ANY)
    rows = pre.shape[0]
    batch, height, breadth, chans = cells.shape
    narrow_row = jnp.pad(narrow, (0, C1P - C1), constant_values=-1)[None, :]
    narrow_col = jnp.broadcast_to(narrow[:, None], (C1, LANES))
    framed = jax.ShapeDtypeStruct((batch, height + 6, breadth + 2 * EDGE, chans), cells.dtype)
    dma = pltpu.SemaphoreType.DMA
    return pl.pallas_call(
        functools.partial(place_kernel, nr, nc),
        out_shape=(jax.ShapeDtypeStruct((space, LANES), jnp.float32), framed),
        grid=(CH // TILE,),
        in_specs=[
            whole(normed), whole(branch), whole(pre), whole(act), whole(narrow_row), whole(narrow_col),
            pl.BlockSpec((1, TILE), lambda i: (0, i)),
            whole(up), whole(cells),
        ],
        out_specs=(hbm, hbm),
        scratch_shapes=[
            pltpu.VMEM((C1 * CH // LANES, LANES), jnp.float32),
            pltpu.VMEM((C1 * CH // LANES, LANES), jnp.float32),
            pltpu.VMEM((C1P // LANES, C1, LANES), jnp.float32),
            pltpu.VMEM((C1 * C1 // LANES, LANES), jnp.float32),
            pltpu.VMEM((C1, rows), jnp.bfloat16),
            pltpu.VMEM((rows, C1P), jnp.bfloat16),
            pltpu.VMEM(framed.shape, framed.dtype),
            dma((CH // TILE,)), dma((3,)), dma((8,)), dma((8,)),
        ],
        compiler_params=pltpu.CompilerParams(
            collective_id=3, has_side_effects=True, vmem_limit_bytes=60 << 20
        ),
    )(normed, branch, pre, act, narrow_row, narrow_col, wide[None, :], up, cells)


def complete_kernel(before, down, piece_in, piece_dw, piece_head, piece_vec, grad, loose, down_rows, sems):
    copies = [
        pltpu.make_async_copy(ref, grad.at[pl.ds(row, ref.shape[0])], sems.at[i])
        for i, (ref, row) in enumerate(
            (
                (piece_in, 0), (piece_dw, ROW_AT[2]), (piece_head, ROW_AT[6]), (piece_vec, ROW_AT[7]),
                (down_rows, ROW_AT[1]),
            )
        )
    ]
    for copy in copies[:4]:
        copy.start()
    for u in range(C1P // LANES):
        loose[u] = down[:, u * LANES : (u + 1) * LANES]

    def put(t, value):
        down_rows[pl.ds(t, C1 // 4, stride=CH // LANES), :] = value

    weave(loose, C1 // 4, put)
    copies[4].start()
    for copy in copies:
        copy.wait()


def complete_gradients(grad, down, pieces):
    vmem = pl.BlockSpec(memory_space=pltpu.VMEM)
    hbm = pl.BlockSpec(memory_space=pl.ANY)
    return pl.pallas_call(
        complete_kernel,
        out_shape=jax.ShapeDtypeStruct(grad.shape, grad.dtype),
        in_specs=[hbm, vmem, vmem, vmem, vmem, vmem],
        out_specs=hbm,
        input_output_aliases={0: 0},
        scratch_shapes=[
            pltpu.VMEM((C1P // LANES, C1, LANES), jnp.float32),
            pltpu.VMEM((C1 * C1 // LANES, LANES), jnp.float32),
            pltpu.SemaphoreType.DMA((5,)),
        ],
        compiler_params=pltpu.CompilerParams(vmem_limit_bytes=60 << 20),
    )(grad, down, *pieces)


C0P = 256
C1P = 896
CIP = 128
EDGE = 16
CURVE = 0.7978845608028654
CUBE = 0.044715


def inner_rows(left, right):
    return lax.dot_general(left, right, (((0,), (0,)), ((), ())), preferred_element_type=jnp.float32)


def column_sum(values):
    return jnp.sum(values.astype(jnp.float32), axis=0, keepdims=True)


def gelu(t):
    return 0.5 * t * (1.0 + jnp.tanh(CURVE * (t + CUBE * (t * t * t))))


def gelu_slope(t):
    bend = jnp.tanh(CURVE * (t + CUBE * (t * t * t)))
    return 0.5 * (1.0 + bend) + 0.5 * t * (1.0 - bend * bend) * (CURVE * (1.0 + 3.0 * CUBE * (t * t)))


WAYS = [(dr, dc) for dr in (-1, 0, 1) for dc in (-1, 0, 1) if (dr, dc) != (0, 0)]
ORDER = sorted(range(8), key=lambda i: (WAYS[i][1] != 0, WAYS[i][0] == 0))


def halo_place(nr, nc):
    r = lax.axis_index("rows")
    return r, lax.axis_index("cols"), lambda dr: (r + dr >= 0) & (r + dr < nr)


def halo_copy(nr, nc, width, cells, out, sem_s, sem_r, i, receive):
    r, c, there = halo_place(nr, nc)
    height, breadth = cells.shape[1], cells.shape[2]
    dr, dc = WAYS[i]
    rows_from = {-1: (0, width), 0: (0, height), 1: (height - width, width)}[dr]
    rows_to = {-1: height + width, 0: width, 1: 0}[dr]
    cols_from = {-1: (0, EDGE), 0: (0, breadth), 1: (breadth - EDGE, EDGE)}[dc]
    cols_to = {-1: EDGE + breadth, 0: EDGE, 1: 0}[dc]
    sign = -1 if receive else 1
    return pltpu.make_async_remote_copy(
        src_ref=cells.at[:, pl.ds(*rows_from), pl.ds(*cols_from)],
        dst_ref=out.at[:, pl.ds(rows_to, rows_from[1]), pl.ds(cols_to, cols_from[1])],
        send_sem=sem_s.at[i],
        recv_sem=sem_r.at[i],
        device_id=(r + sign * dr, lax.rem(c + sign * dc + nc, nc)),
        device_id_type=MESH,
    )


def halo_start(nr, nc, width, cells, out, sem_s, sem_r):
    r, c, there = halo_place(nr, nc)
    height, breadth = cells.shape[1], cells.shape[2]
    barrier = pltpu.get_barrier_semaphore()
    for dr, dc in WAYS:
        @pl.when(there(dr))
        def _(dr=dr, dc=dc):
            pl.semaphore_signal(
                barrier, inc=1, device_id=(r + dr, lax.rem(c + dc + nc, nc)), device_id_type=MESH
            )

    edge = (r == 0) | (r == nr - 1)

    @pl.when(edge)
    def _():
        pl.semaphore_wait(barrier, 5)

    @pl.when(jnp.logical_not(edge))
    def _():
        pl.semaphore_wait(barrier, 8)

    for i in ORDER:
        @pl.when(there(WAYS[i][0]))
        def _(i=i):
            halo_copy(nr, nc, width, cells, out, sem_s, sem_r, i, False).start()

    for m in range(cells.shape[0]):
        for row in range(height):
            out[m, width + row, EDGE : EDGE + breadth, :] = cells[m, row]

    @pl.when(r == 0)
    def _():
        out[:, 0:width] = jnp.zeros((out.shape[0], width) + out.shape[2:], out.dtype)

    @pl.when(r == nr - 1)
    def _():
        out[:, height + width :] = jnp.zeros((out.shape[0], width) + out.shape[2:], out.dtype)


def halo_finish(nr, nc, width, cells, out, sem_s, sem_r):
    r, c, there = halo_place(nr, nc)
    for i in ORDER:
        @pl.when(there(-WAYS[i][0]))
        def _(i=i):
            halo_copy(nr, nc, width, cells, out, sem_s, sem_r, i, True).wait_recv()

        @pl.when(there(WAYS[i][0]))
        def _(i=i):
            halo_copy(nr, nc, width, cells, out, sem_s, sem_r, i, False).wait_send()


def halo_kernel(nr, nc, width, cells, out, sem_s, sem_r):
    halo_start(nr, nc, width, cells, out, sem_s, sem_r)
    halo_finish(nr, nc, width, cells, out, sem_s, sem_r)


def halo(nr, nc, width, cells, identity):
    batch, height, breadth, chans = cells.shape
    vmem = pl.BlockSpec(memory_space=pltpu.VMEM)
    return pl.pallas_call(
        functools.partial(halo_kernel, nr, nc, width),
        out_shape=jax.ShapeDtypeStruct(
            (batch, height + 2 * width, breadth + 2 * EDGE, chans), cells.dtype
        ),
        in_specs=[vmem],
        out_specs=vmem,
        scratch_shapes=[pltpu.SemaphoreType.DMA((8,)), pltpu.SemaphoreType.DMA((8,))],
        compiler_params=pltpu.CompilerParams(
            collective_id=identity, has_side_effects=True, vmem_limit_bytes=24 << 20
        ),
    )(cells)


def input_kernel(state, w_in, b_in, w_down, b_down, taps, a_zero, h_zero, coarse, coarse_low, wide):
    batch, rows, breadth, _ = state.shape
    half_h, half_w = (rows - 2) // 2, (breadth - 2 * EDGE) // 2
    for m in range(batch):
        for y in range(rows):
            wide[m, y] = state[m, y].astype(jnp.float32)
    for m in range(batch):
        for y in range(rows):
            for f in range(4):
                line = wide[m, y, pl.ds(EDGE - 1 + f, half_w, stride=2), :].astype(jnp.bfloat16)
                for dy in range(3):
                    i, sy = divmod(y - dy, 2)
                    if not 0 <= i < half_h:
                        continue
                    for dx in range(3):
                        if 0 <= f - dx < 2:
                            begin = (m * half_h + i) * half_w
                            tap = (dy * 3 + dx) * CIP
                            taps[sy * 2 + f - dx, begin : begin + half_w, tap : tap + CIP] = line
    coarse[...] = jnp.broadcast_to(b_down[...], coarse.shape)
    for s in range(4):
        value = product(taps[s], w_in[...]) + b_in[...]
        a_zero[s] = value
        value = gelu(value)
        h_zero[s] = value
        coarse[...] += product(value.astype(jnp.bfloat16), w_down[s])
    coarse_low[...] = coarse[...].astype(jnp.bfloat16).reshape(coarse_low.shape)


def input_part(state, w_in, b_in, w_down, b_down):
    batch, rows, breadth, _ = state.shape
    half_h, half_w = (rows - 2) // 2, (breadth - 2 * EDGE) // 2
    cells = batch * half_h * half_w
    vmem = pl.BlockSpec(memory_space=pltpu.VMEM)
    return pl.pallas_call(
        input_kernel,
        out_shape=(
            jax.ShapeDtypeStruct((4, cells, 9 * CIP), jnp.bfloat16),
            jax.ShapeDtypeStruct((4, cells, C0P), jnp.float32),
            jax.ShapeDtypeStruct((4, cells, C0P), jnp.float32),
            jax.ShapeDtypeStruct((cells, C1P), jnp.float32),
            jax.ShapeDtypeStruct((batch, half_h, half_w, C1P), jnp.bfloat16),
        ),
        in_specs=[vmem] * 5,
        out_specs=tuple([vmem] * 5),
        scratch_shapes=[pltpu.VMEM(state.shape, jnp.float32)],
        compiler_params=pltpu.CompilerParams(vmem_limit_bytes=40 << 20),
    )(state, w_in, b_in, w_down, b_down)


def spread_lanes(padded, held):
    for m in range(padded.shape[0]):
        def body(y, carry, m=m):
            for u in range(C1P // LANES):
                held[u, m, y] = padded[m, y, :, u * LANES : (u + 1) * LANES].astype(jnp.float32)
            return carry

        lax.fori_loop(0, padded.shape[1], body, 0)


def convolve(held, w_dw, put, back):
    tiles, batch, rows, breadth = held.shape[:4]
    height, half_w = rows - 6, breadth - 2 * EDGE

    def body(number, carry):
        u, m = number // batch, number % batch
        sums = [jnp.zeros((half_w, LANES), jnp.float32) for _ in range(height)]
        for x in range(7):
            for y in range(rows):
                window = held[u, m, y, pl.ds(EDGE - 3 + x, half_w), :]
                for i in range(height):
                    if 0 <= y - i < 7:
                        tap = (6 - (y - i)) * 7 + 6 - x if back else (y - i) * 7 + x
                        sums[i] = sums[i] + window * w_dw[u, pl.ds(tap, 1), :]
        for i in range(height):
            put(u, m, i, sums[i])
        return carry

    lax.fori_loop(0, tiles * batch, body, 0)


def rows_at(m, i, height, half_w):
    return pl.ds(pl.multiple_of((m * height + i) * half_w, half_w), half_w)


def lanes_at(u):
    return pl.ds(pl.multiple_of(u * LANES, LANES), LANES)


PART = 640


def middle_kernel(
    padded, coarse, h_zero, target, weight, w_dw, w_hidden, w_out_t, w_up, w_head,
    b_dw, gain, shift, b_hidden, b_out, b_up, b_head,
    normed, act, grad_pre, grad_mixed, grad_branch, grad_summed, grad_conv, d_up, d_head, sums,
    conv, total,
):
    cells = coarse.shape[0]
    batch, rows, breadth, _ = padded.shape
    height, half_w = rows - 6, breadth - 2 * EDGE

    def depthwise(held):
        spread_lanes(padded, held)

        def put(u, m, i, value):
            conv[rows_at(m, i, height, half_w), lanes_at(u)] = value

        convolve(held, w_dw, put, False)

    pl.run_scoped(depthwise, pltpu.VMEM((C1P // LANES, batch, rows, breadth, LANES), jnp.float32))
    pl.run_scoped(
        functools.partial(
            pointwise_kernel, coarse, h_zero, target, weight, w_hidden, w_out_t, w_up, w_head,
            b_dw, gain, shift, b_hidden, b_out, b_up, b_head,
            normed, act, grad_pre, grad_mixed, grad_branch, grad_summed, grad_conv, d_up, d_head, sums,
            conv, total,
        ),
        pltpu.VMEM((cells, CH), jnp.float32),
        pltpu.VMEM((cells, C1), jnp.bfloat16),
    )


def pointwise_kernel(
    coarse, h_zero, target, weight, w_hidden, w_out_t, w_up, w_head,
    b_dw, gain, shift, b_hidden, b_out, b_up, b_head,
    normed, act, grad_pre, grad_mixed, grad_branch, grad_summed, grad_conv, d_up, d_head, sums,
    conv, total, pre, spread_all,
):
    inside = lax.broadcasted_iota(jnp.int32, (1, C1P), 1) < C1
    values = conv[...] + b_dw[...]
    mean = jnp.sum(values, axis=1, keepdims=True) * (1.0 / C1)
    centered = jnp.where(inside, values - mean, 0.0)
    scale = lax.rsqrt(jnp.sum(centered * centered, axis=1, keepdims=True) * (1.0 / C1) + 1e-06)
    conv[...] = centered * scale
    normed[...] = (conv[...] * gain[...] + shift[...]).astype(jnp.bfloat16)

    total[...] = coarse[...]
    for begin in range(0, CH, PART):
        span = slice(begin, begin + PART)
        value = product(normed[:, :C1], w_hidden[:, span]) + b_hidden[:, span]
        pre[:, span] = value
        act[:, span] = gelu(value).astype(jnp.bfloat16)
        total[:, :C1] += product_t(act[:, span], w_out_t[:, span])
    mixed = (total[...] + b_out[...]).astype(jnp.bfloat16)

    grad_mixed[...] = jnp.zeros_like(grad_mixed)
    loss = jnp.zeros((1, CIP), jnp.float32)
    head_sum = jnp.zeros((1, CIP), jnp.float32)
    up_sum = jnp.zeros((1, C0P), jnp.float32)
    for s in range(4):
        upper = product(mixed[:, :C1], w_up[s]) + b_up[...]
        summed = (upper + h_zero[s]).astype(jnp.bfloat16)
        error = product(summed, w_head[...]) + b_head[...] - target[s].astype(jnp.float32)
        weighted = weight[s] * error
        loss = loss + column_sum(weighted * error)
        grad_out = (2.0 * weighted).astype(jnp.bfloat16)
        head_sum = head_sum + column_sum(grad_out)
        if s == 0:
            d_head[...] = inner_rows(summed, grad_out)
        else:
            d_head[...] += inner_rows(summed, grad_out)
        spread = product_t(grad_out, w_head[...])
        grad_summed[s] = spread
        grad_upper = spread.astype(jnp.bfloat16)
        up_sum = up_sum + column_sum(grad_upper)
        spread_all[:, s * C0 : (s + 1) * C0] = grad_upper[:, :C0]
        grad_mixed[:, :C1] += product_t(grad_upper, w_up[s])
    d_up[...] = inner_rows(mixed, spread_all[...])
    grad_branch[...] = grad_mixed[...].astype(jnp.bfloat16)
    sums[...] = jnp.zeros_like(sums)
    sums[0:1, 0:CIP] = loss
    sums[1:2, 0:CIP] = head_sum
    sums[2:3, 0:C0P] = up_sum
    sums[3:4, 0:C1P] = column_sum(grad_branch[...])

    total[...] = jnp.zeros_like(total)
    for begin in range(0, CH, PART):
        span = slice(begin, begin + PART)
        value = product(grad_branch[:, :C1], w_out_t[:, span]) * gelu_slope(pre[:, span])
        low = value.astype(jnp.bfloat16)
        grad_pre[:, span] = low
        sums[4:5, span] = column_sum(low)
        total[:, :C1] += product_t(low, w_hidden[:, span])

    grad_normed = total[...]
    sums[5:6, 0:C1P] = column_sum(grad_normed * conv[...])
    sums[6:7, 0:C1P] = column_sum(grad_normed)
    inward = grad_normed * gain[...]
    first = jnp.sum(inward, axis=1, keepdims=True) * (1.0 / C1)
    second = jnp.sum(inward * conv[...], axis=1, keepdims=True) * (1.0 / C1)
    value = scale * jnp.where(inside, inward - first - conv[...] * second, 0.0)
    low = value.astype(jnp.bfloat16)
    sums[7:8, 0:C1P] = column_sum(low)
    grad_conv[...] = low.reshape(grad_conv.shape)


def middle_part(padded, coarse, h_zero, target, weight, *rest):
    cells = coarse.shape[0]
    batch, rows, breadth, _ = padded.shape
    half_h, half_w = rows - 6, breadth - 2 * EDGE
    vmem = pl.BlockSpec(memory_space=pltpu.VMEM)
    f32, low = jnp.float32, jnp.bfloat16
    return pl.pallas_call(
        middle_kernel,
        out_shape=(
            jax.ShapeDtypeStruct((cells, C1P), low),
            jax.ShapeDtypeStruct((cells, CH), low),
            jax.ShapeDtypeStruct((cells, CH), low),
            jax.ShapeDtypeStruct((cells, C1P), f32),
            jax.ShapeDtypeStruct((cells, C1P), low),
            jax.ShapeDtypeStruct((4, cells, C0P), f32),
            jax.ShapeDtypeStruct((batch, half_h, half_w, C1P), low),
            jax.ShapeDtypeStruct((C1P, C1), f32),
            jax.ShapeDtypeStruct((C0P, CIP), f32),
            jax.ShapeDtypeStruct((8, CH), f32),
        ),
        in_specs=[vmem] * 17,
        out_specs=tuple([vmem] * 10),
        scratch_shapes=[
            pltpu.VMEM((cells, C1P), f32),
            pltpu.VMEM((cells, C1P), f32),
        ],
        compiler_params=pltpu.CompilerParams(vmem_limit_bytes=62 << 20),
    )(padded, coarse, h_zero, target, weight, *rest)


def outer_kernel(
    padded, grad_padded, grad_conv, grad_mixed, grad_summed, a_zero, h_zero, taps, w_dw, w_down,
    d_dw, d_down, d_in, sums, held, conv,
):
    batch, height, half_w, _ = grad_conv.shape
    spread_lanes(padded, held)
    tiles = C1P // LANES
    d_dw[...] = jnp.zeros_like(d_dw)

    def taps_of(number, carry):
        u, m = number // batch, number % batch
        grads = [grad_conv[m, i, :, lanes_at(u)].astype(jnp.float32) for i in range(height)]
        for x in range(7):
            found = [jnp.zeros((8, LANES), jnp.float32) for _ in range(7)]
            for y in range(height + 6):
                window = held[u, m, y, pl.ds(EDGE - 3 + x, half_w), :]
                for i in range(height):
                    if 0 <= y - i < 7:
                        term = (window * grads[i]).reshape(half_w // 8, 8, LANES)
                        found[y - i] = found[y - i] + jnp.sum(term, axis=0)
            for dy in range(7):
                d_dw[u, pl.ds(dy * 7 + x, 1), :] += jnp.sum(found[dy], axis=0, keepdims=True)
        return carry

    lax.fori_loop(0, tiles * batch, taps_of, 0)
    spread_lanes(grad_padded, held)

    def put(u, m, i, value):
        conv[rows_at(m, i, height, half_w), lanes_at(u)] = value

    convolve(held, w_dw, put, True)
    grad_coarse = (conv[...] + grad_mixed[...]).astype(jnp.bfloat16)
    sums[...] = jnp.zeros_like(sums)
    sums[0:1, 0:C1P] = column_sum(grad_coarse)
    in_sum = jnp.zeros((1, C0P), jnp.float32)
    for s in range(4):
        d_down[s * C0 : (s + 1) * C0, :] = inner_rows(h_zero[s].astype(jnp.bfloat16), grad_coarse)[:C0]
        grad_h = product_t(grad_coarse, w_down[s]) + grad_summed[s]
        grad_a = (gelu_slope(a_zero[s]) * grad_h).astype(jnp.bfloat16)
        in_sum = in_sum + column_sum(grad_a)
        if s == 0:
            d_in[...] = inner_rows(taps[s], grad_a)
        else:
            d_in[...] += inner_rows(taps[s], grad_a)
    sums[1:2, 0:C0P] = in_sum


def outer_part(padded, grad_padded, grad_conv, grad_mixed, grad_summed, a_zero, h_zero, taps, w_dw, w_down):
    cells = grad_mixed.shape[0]
    batch, rows, breadth, _ = padded.shape
    vmem = pl.BlockSpec(memory_space=pltpu.VMEM)
    f32 = jnp.float32
    return pl.pallas_call(
        outer_kernel,
        out_shape=(
            jax.ShapeDtypeStruct((C1P // LANES, 56, LANES), f32),
            jax.ShapeDtypeStruct((C1, C1P), f32),
            jax.ShapeDtypeStruct((9 * CIP, C0P), f32),
            jax.ShapeDtypeStruct((8, C1P), f32),
        ),
        in_specs=[vmem] * 10,
        out_specs=tuple([vmem] * 4),
        scratch_shapes=[
            pltpu.VMEM((C1P // LANES, batch, rows, breadth, LANES), f32),
            pltpu.VMEM((cells, C1P), f32),
        ],
        compiler_params=pltpu.CompilerParams(vmem_limit_bytes=62 << 20),
    )(padded, grad_padded, grad_conv, grad_mixed, grad_summed, a_zero, h_zero, taps, w_dw, w_down)


def split_vector(vector):
    lengths = [C0, C1, C1, C1, C1, CH, C1, C0, CI]
    pieces = []
    start = 0
    for length in lengths:
        pieces.append(vector[start : start + length])
        start = start + length
    return pieces


def as_rows(piece, rows):
    flat = piece.reshape(-1)
    return jnp.pad(flat, (0, rows * LANES - flat.shape[0])).reshape(rows, LANES)


def widened(array, *shape):
    return jnp.pad(array, [(0, full - now) for full, now in zip(shape, array.shape)])


def on_device(
    inputs,
    targets,
    land_mask,
    volume,
    date_index,
    perm_narrow,
    perm_wide,
    w_in,
    w_down,
    w_dw,
    w_hidden,
    w_out,
    w_up,
    w_head,
    biases_gains,
    moment_first,
    moment_second,
):
    rows, cols = lax.axis_size("rows"), lax.axis_size("cols")
    b_in, b_down, b_dw, gain, shift, b_hidden, b_out, b_up, b_head = split_vector(biases_gains)
    weight = land_mask.astype(jnp.float32) * volume
    height, breadth = weight.shape
    half_h, half_w = (height // 2, breadth // 2)
    cells = MB * half_h * half_w
    matrices = (w_in, w_down, w_dw, w_hidden, w_out, w_up, w_head)

    def dates(field):
        picked = jnp.concatenate(
            [lax.dynamic_slice_in_dim(field, date_index[m], 1, 0) for m in range(MB)]
        )
        return widened(picked, MB, height, breadth, CIP)

    def by_subcell(field):
        chans = field.shape[-1]
        return (
            field.reshape(MB, half_h, 2, half_w, 2, chans)
            .transpose(2, 4, 0, 1, 3, 5)
            .reshape(4, cells, chans)
        )

    def line(vector, size):
        return widened(vector[None, :], 1, size)

    w_in_p = widened(w_in.reshape(9, CI, C0), 9, CIP, C0P).reshape(9 * CIP, C0P)
    w_down_p = widened(w_down.reshape(4, C0, C1), 4, C0P, C1P)
    w_up_p = widened(w_up.reshape(C1, 4, C0).transpose(1, 0, 2), 4, C1, C0P)
    w_dw_p = widened(w_dw.astype(jnp.float32), 56, C1P).reshape(56, C1P // LANES, LANES).transpose(1, 0, 2)
    target = by_subcell(dates(targets))
    weight_col = jnp.broadcast_to(weight[None, :, :, None], (MB, height, breadth, 1))
    weight_col = jnp.broadcast_to(by_subcell(weight_col), (4, cells, CIP))

    state = halo(rows, cols, 1, dates(inputs), 1)
    taps, a_zero, h_zero, coarse, coarse_low = input_part(
        state, w_in_p, line(b_in, C0P), w_down_p, line(b_down, C1P)
    )
    padded = halo(rows, cols, 3, coarse_low, 2)
    (
        normed, act, grad_pre, grad_mixed, grad_branch, grad_summed, grad_conv, d_up, d_head, sums
    ) = middle_part(
        padded, coarse, h_zero, target, weight_col, w_dw_p, w_hidden, w_out.T, w_up_p,
        widened(w_head, C0P, CIP), line(b_dw, C1P), line(gain, C1P), line(shift, C1P),
        line(b_hidden, CH), line(b_out, C1P), line(b_up, C0P), line(b_head, CIP),
    )
    space = Plan(rows, cols, PADDED).space
    grad, grad_padded = place_gradients(
        rows, cols, space, normed, grad_branch, grad_pre, act, perm_narrow, perm_wide, d_up, grad_conv
    )
    d_dw, d_down, d_in, sums_out = outer_part(
        padded, grad_padded, grad_conv, grad_mixed, grad_summed, a_zero, h_zero, taps, w_dw_p, w_down_p
    )
    d_in = d_in.reshape(9, CIP, C0P)[:, :CI, :C0].reshape(9 * CI, C0)
    d_dw = d_dw[:, :49].transpose(1, 0, 2).reshape(49, C1P)[:, :C1]
    d_vector = jnp.concatenate(
        [
            sums_out[1, :C0], sums_out[0, :C1], sums[7, :C1], sums[5, :C1], sums[6, :C1],
            sums[4], sums[3, :C1], sums[2, :C0], sums[1, :CI],
        ]
    )
    loss_local = jnp.sum(sums[0, :CIP])
    pieces = (
        jnp.pad(as_rows(d_in, ROW_AT[1] - ROW_AT[0]), ((ROW_AT[0], 0), (0, 0))),
        as_rows(d_dw, ROW_AT[3] - ROW_AT[2]),
        as_rows(d_head[:C0, :CI], ROW_AT[7] - ROW_AT[6]),
        as_rows(d_vector, space - ROW_AT[7]),
    )
    grad = complete_gradients(grad, d_down, pieces)
    lead = jnp.arange(8)[:, None]
    extra = jnp.where(lead == 0, loss_local, jnp.where(lead == 1, jnp.sum(weight), 0.0))
    extra = jnp.where(jnp.arange(LANES)[None, :] == 0, extra, 0.0)
    plan, (gathered, first, second, totals) = exchange(
        rows, cols, grad, moment_first, moment_second, extra
    )
    hidden_p, out_p, new_up, new_down, small_a, small_b, small_c = unpack(plan, gathered, w_up, w_down)
    small = {0: (small_a, 0), 2: (small_b, 1), 6: (small_c, 2), 7: (small_c, 2)}
    whole = {
        1: new_down,
        3: rebuild_hidden(hidden_p, perm_narrow, perm_wide, w_hidden),
        4: rebuild_out(out_p, perm_narrow, perm_wide, w_out),
        5: new_up,
    }
    olds = matrices + (biases_gains,)
    news = []
    for index, old in enumerate(olds):
        if index in whole:
            news.append(whole[index])
        else:
            source, which = small[index]
            start = FLAT_AT[index] - KEPT[which][0] * LANES
            piece = source.reshape(-1)[start : start + old.size].reshape(old.shape)
            news.append(moved(old, piece) if index < 7 else old - learn_rate * piece)
    return tuple(news) + (
        first.reshape(-1),
        second.reshape(-1),
        totals[0, 0],
        MB * CI * totals[1, 0],
        totals[8, 0],
    )


def solution(mesh):
    return jax.shard_map(
        on_device,
        mesh=mesh,
        in_specs=(
            P(None, "rows", "cols", None),
            P(None, "rows", "cols", None),
            P("rows", "cols"),
            P("rows", "cols"),
            P(),
            P(),
            P(),
            P(),
            P(),
            P(),
            P(),
            P(),
            P(),
            P(),
            P(),
            P(("rows", "cols")),
            P(("rows", "cols")),
        ),
        out_specs=(
            P(),
            P(),
            P(),
            P(),
            P(),
            P(),
            P(),
            P(),
            P(("rows", "cols")),
            P(("rows", "cols")),
            P(),
            P(),
            P(),
        ),
        check_vma=False,
    )
```

```python
import functools

import jax
import jax.numpy as jnp
from jax import lax
from jax.experimental import pallas as pl
from jax.experimental.pallas import tpu as pltpu
from jax.sharding import PartitionSpec as P

CI = 77
C0 = 200
C1 = 800
CH = 3200
MB = 2
STEP = 5
LANES = 128
MESH = pl.DeviceIdType.MESH
ROUNDER = 12582912.0

decay_first = 0.9
decay_second = 0.99
epsilon = 1e-08
learn_rate = 0.02
weight_decay = 0.1
clip_limit = 1.0

VEC = 4 * C1 + CH + C1 + 2 * C0 + CI
SIZES = (9 * CI * C0, 4 * C0 * C1, 49 * C1, C1 * CH, CH * C1, C1 * 4 * C0, C0 * CI, VEC)
PADDED = 6602752
FLAT_AT = []
ROW_AT = []
for size in SIZES:
    flat_here = FLAT_AT[-1] + SIZES[len(FLAT_AT) - 1] if FLAT_AT else PADDED - sum(SIZES)
    row_here = ROW_AT[-1] + -(-SIZES[len(ROW_AT) - 1] // 1024) * 8 if ROW_AT else 0
    row_here = max(row_here, -(-flat_here // 1024) * 8)
    FLAT_AT.append(flat_here)
    ROW_AT.append(row_here)
SHIFTS = []
for flat_here, row_here, size in zip(FLAT_AT, ROW_AT, SIZES):
    moved = divmod(row_here * LANES - flat_here, LANES)
    if SHIFTS and SHIFTS[-1][:2] == moved:
        SHIFTS[-1] = moved + (SHIFTS[-1][2], flat_here + size)
    else:
        SHIFTS.append(moved + (flat_here, flat_here + size))
MAX_SHIFT = max(s[0] for s in SHIFTS) + 1


def bit_masks(bits):
    masks = [()]
    for bit in bits:
        masks = masks + [m + (bit,) for m in masks]
    return sorted(masks, key=lambda m: -len(m))


class Plan:
    def __init__(self, rows, cols, total):
        self.rows, self.cols, self.count = rows, cols, rows * cols
        self.share = total // LANES // self.count
        self.bits = rows.bit_length() - 1
        need = 7 + self.share + MAX_SHIFT + 1
        self.block = 64 if need > 1024 else 32
        self.window = -(-need // (2 * self.block)) * 2 * self.block
        self.part = self.window // 2
        self.blocks = self.part // self.block
        self.scales = self.blocks
        upper = list(range(1, self.bits))
        self.orders = [upper, upper[1:] + upper[:1]]
        self.stages = len(upper)
        self.space = (self.share * (self.count - 1)) // 8 * 8 + self.window
        self.padded = -(-self.share // 16) * 16
        cut = -(-self.padded // 32) * 16
        self.cuts = [(0, cut), (cut, self.padded - cut)]
        self.local = self.count // 2


def exchange_kernel(
    plan, grad, m_first, m_second, extra, full, first, second, totals,
    acc, near, q_send, q_recv, s_send, s_recv, z_send, z_recv, zs_send, zs_recv,
    rolled, step, low, stats,
    sem_load, sem_near_s, sem_near_r, sem_qs, sem_qr, sem_ss, sem_sr,
    sem_zs, sem_zr, sem_zss, sem_zsr, sem_ts, sem_tr, sem_own,
    sem_gs, sem_gr, sem_hs, sem_hr, sem_cs, sem_cr,
):
    nr, nc, n = plan.rows, plan.cols, plan.count
    r = lax.axis_index("rows")
    c = lax.axis_index("cols")
    me = r * nc + c
    part, window, share = plan.part, plan.window, plan.share

    def flipped(mask):
        out = r
        for bit in mask:
            here = (r // (1 << bit)) % 2
            out = out + (1 - 2 * here) * (1 << bit)
        return out

    def remote(src, dst, send, recv, row, col):
        return pltpu.make_async_remote_copy(
            src_ref=src, dst_ref=dst, send_sem=send, recv_sem=recv,
            device_id=(row, col), device_id_type=MESH,
        )

    barrier = pltpu.get_barrier_semaphore()

    def greet(d, carry):
        k = lax.rem(me + d, n)
        pl.semaphore_signal(barrier, inc=1, device_id=(k // nc, k % nc), device_id_type=MESH)
        return carry

    lax.fori_loop(1, n, greet, 0)
    pl.semaphore_wait(barrier, n - 1)

    upper = list(range(1, plan.bits))
    masks = bit_masks(upper)

    def local_index(mask, col):
        return (flipped(mask) // 2) * nc + col

    def window_start(row, col):
        return pl.multiple_of((share * (row * nc + col)) // 8 * 8, 8)

    def near_copy(mask, col):
        row = flipped(mask + (0,))
        return remote(
            grad.at[pl.ds(window_start(row, col), window)],
            near.at[local_index(mask, col)],
            sem_near_s.at[local_index(mask, col)], sem_near_r.at[local_index(mask, col)],
            flipped((0,)), c,
        )

    def load_copy(mask, col):
        index = local_index(mask, col)
        return pltpu.make_async_copy(
            grad.at[pl.ds(window_start(flipped(mask), col), window)], acc.at[index], sem_load.at[index]
        )

    def begin(d, carry):
        for mask in masks:
            near_copy(mask, lax.rem(c + d, nc)).start()
            load_copy(mask, lax.rem(c + d, nc)).start()
        return carry

    lax.fori_loop(1, nc + 1, begin, 0)

    def encode(index, p, q_ref, s_ref):
        def body(b, carry):
            at = pl.ds(pl.multiple_of(b * plan.block, plan.block), plan.block)
            rows_at = pl.ds(pl.multiple_of(p * part + b * plan.block, 8), plan.block)
            values = acc[index, rows_at, :]
            top = jnp.maximum(jnp.max(jnp.abs(values), axis=0, keepdims=True), 1e-30)
            scaled = values * (32766.0 / top)
            scaled = (scaled + ROUNDER) - ROUNDER
            q_ref[at, :] = scaled.astype(jnp.int32).astype(jnp.int16)
            s_ref[pl.ds(b, 1), :] = top * (1.0 / 32766.0)
            return carry

        lax.fori_loop(0, plan.blocks, body, 0)

    def decode(index, p, q_ref, s_ref):
        def body(b, carry):
            at = pl.ds(pl.multiple_of(b * plan.block, plan.block), plan.block)
            rows_at = pl.ds(pl.multiple_of(p * part + b * plan.block, 8), plan.block)
            acc[index, rows_at, :] += q_ref[at, :].astype(jnp.float32) * s_ref[pl.ds(b, 1), :]
            return carry

        lax.fori_loop(0, plan.blocks, body, 0)

    def stage_base(stage):
        return sum((1 << (plan.stages - 1 - s)) for s in range(stage)) * nc

    def hop(p, stage, slot):
        row = flipped((plan.orders[p][stage],))
        at = stage_base(stage) + slot
        return (
            remote(q_send.at[p, at], q_recv.at[p, at], sem_qs.at[p, at], sem_qr.at[p, at], row, c),
            remote(s_send.at[p, at], s_recv.at[p, at], sem_ss.at[p, at], sem_sr.at[p, at], row, c),
        )

    def send_stage(p, stage, number, mask, col):
        bit = plan.orders[p][stage]
        index = local_index(mask + (bit,), col)
        slot = number * nc + col
        at = stage_base(stage) + slot
        encode(index, p, q_send.at[p, at], s_send.at[p, at])
        for copy in hop(p, stage, slot):
            copy.start()

    def take_stage(p, stage, number, mask, col):
        slot = number * nc + col
        for copy in hop(p, stage, slot):
            copy.wait_recv()
        at = stage_base(stage) + slot
        decode(local_index(mask, col), p, q_recv.at[p, at], s_recv.at[p, at])

    def free_masks(p, stage):
        rest = plan.orders[p][stage + 1 :]
        found = bit_masks(rest)
        if rest:
            found = [m for m in found if rest[0] in m] + [m for m in found if rest[0] not in m]
        return found

    def far_copy(p, d):
        col = lax.rem(c + d, nc)
        return (
            remote(z_send.at[p, d - 1], z_recv.at[p, d - 1], sem_zs.at[p, d - 1], sem_zr.at[p, d - 1], r, col),
            remote(zs_send.at[p, d - 1], zs_recv.at[p, d - 1], sem_zss.at[p, d - 1], sem_zsr.at[p, d - 1], r, col),
        )

    def join(d):
        col = lax.rem(c + d, nc)
        for mask in masks:
            index = local_index(mask, col)
            near_copy(mask, col).wait_recv()
            load_copy(mask, col).wait()

            def body(b, inner, index=index):
                at = pl.ds(pl.multiple_of(b * plan.block, plan.block), plan.block)
                acc[index, at, :] += near[index, at, :]
                return inner

            lax.fori_loop(0, 2 * plan.blocks, body, 0)
            for p in range(2):
                bit = plan.orders[p][0]
                if bit in mask:
                    rest = tuple(b for b in mask if b != bit)
                    options = free_masks(p, 0)
                    number = [sorted(o) for o in options].index(sorted(rest))
                    send_stage(p, 0, number, rest, col)

    def take(stage, d):
        col = lax.rem(c + d, nc)
        for number in range(1 << (plan.stages - 1 - stage)):
            for p in range(2):
                mask = free_masks(p, stage)[number]
                take_stage(p, stage, number, mask, col)
                if stage + 1 < plan.stages:
                    bit = plan.orders[p][stage + 1]
                    if bit in mask:
                        rest = tuple(b for b in mask if b != bit)
                        options = free_masks(p, stage + 1)
                        following = [sorted(o) for o in options].index(sorted(rest))
                        send_stage(p, stage + 1, following, rest, col)
                else:
                    @pl.when(d < nc)
                    def _(p=p):
                        encode(local_index((), col), p, z_send.at[p, d - 1], zs_send.at[p, d - 1])
                        for copy in far_copy(p, d):
                            copy.start()

    def turn_of(t, carry):
        @pl.when(t <= nc)
        def _():
            join(t)

        for stage in range(plan.stages):
            d = t - 1 - stage

            @pl.when((d >= 1) & (d <= nc))
            def _(stage=stage, d=d):
                take(stage, d)

        return carry

    lax.fori_loop(1, nc + plan.stages + 1, turn_of, 0)

    mine = local_index((), c)

    def gather_far(d, carry):
        for p in range(2):
            for copy in far_copy(p, d):
                copy.wait_recv()
            decode(mine, p, z_recv.at[p, d - 1], zs_recv.at[p, d - 1])
        return carry

    lax.fori_loop(1, nc, gather_far, 0)

    offset = lax.rem(share * me, 8)
    low_end, high_end = share * me * LANES, share * (me + 1) * LANES
    for number, (shift_rows, shift_lanes, begin, end) in enumerate(SHIFTS):
        def turn(b, carry, number=number, shift_lanes=shift_lanes):
            at = pl.ds(pl.multiple_of(b * plan.block, plan.block), plan.block)
            rolled[number, at, :] = pltpu.roll(acc[mine, at, :], LANES - shift_lanes, 1)
            return carry

        @pl.when((low_end < end) & (high_end > begin))
        def _(turn=turn):
            lax.fori_loop(0, 2 * plan.blocks, turn, 0)

    def share_rows(start, length, chosen):
        lane = lax.broadcasted_iota(jnp.int32, (length, LANES), 1)
        out = jnp.zeros((length, LANES), jnp.float32)
        if len(chosen) > 1:
            line = lax.broadcasted_iota(jnp.int32, (length, LANES), 0)
            flat = (share * me + start + line) * LANES + lane
        for number in chosen:
            shift_rows, shift_lanes, begin, end = SHIFTS[number]
            here = rolled[number, pl.ds(offset + start + shift_rows, length), :]
            after = rolled[number, pl.ds(offset + start + shift_rows + 1, length), :]
            value = jnp.where(lane < LANES - shift_lanes, here, after)
            if len(chosen) > 1:
                value = jnp.where((flat >= begin) & (flat < end), value, out)
            out = value
        return out

    chunk = 32
    whole, tail = share // chunk, share % chunk
    stats[me, 8:16, :] = extra[...]

    def squares(chosen):
        def square(b, total):
            start = pl.multiple_of(b * chunk, chunk)
            value = share_rows(start, chunk, chosen)
            step[pl.ds(start, chunk), :] = value
            return total + jnp.sum((value * value).reshape(chunk // 8, 8, LANES), axis=0)

        total = lax.fori_loop(0, whole, square, jnp.zeros((8, LANES), jnp.float32))
        stats[me, 0:8, :] = total
        if tail:
            value = share_rows(whole * chunk, tail, chosen)
            step[whole * chunk : share, :] = value
            stats[me, 0:1, :] += jnp.sum(value * value, axis=0, keepdims=True)

    largest = max(range(len(SHIFTS)), key=lambda i: SHIFTS[i][3] - SHIFTS[i][2])
    alone = (low_end >= SHIFTS[largest][2]) & (high_end <= SHIFTS[largest][3])

    @pl.when(alone)
    def _():
        squares((largest,))

    @pl.when(jnp.logical_not(alone))
    def _():
        squares(tuple(range(len(SHIFTS))))

    def stat_copy(target, source):
        return remote(
            stats.at[me], stats.at[me], sem_ts.at[target], sem_tr.at[me], target // nc, target % nc
        )

    def stat_wait(source):
        return remote(
            stats.at[source], stats.at[source], sem_ts.at[source], sem_tr.at[source],
            source // nc, source % nc,
        )

    def send_stat(d, carry):
        stat_copy(lax.rem(me + d, n), me).start()
        return carry

    lax.fori_loop(1, n, send_stat, 0)

    def wait_stat(d, carry):
        stat_wait(lax.rem(me + d, n)).wait_recv()
        return carry

    lax.fori_loop(1, n, wait_stat, 0)

    def add_stat(k, total):
        return total + stats[k]

    sums = lax.fori_loop(0, n, add_stat, jnp.zeros((16, LANES), jnp.float32))
    norm = jnp.sqrt(jnp.sum(sums[0:8], keepdims=True))
    totals[0:1, :] = jnp.broadcast_to(jnp.sum(sums[8:9], keepdims=True), (1, LANES))
    totals[1:2, :] = jnp.broadcast_to(jnp.sum(sums[9:10], keepdims=True), (1, LANES))
    totals[2:8, :] = jnp.zeros((6, LANES), jnp.float32)
    totals[8:16, :] = jnp.broadcast_to(norm, (8, LANES))
    clip = jnp.minimum(1.0, clip_limit / norm)

    def update(start, length):
        clipped = step[pl.ds(start, length), :] * clip
        one = decay_first * m_first[pl.ds(start, length), :] + (1.0 - decay_first) * clipped
        two = decay_second * m_second[pl.ds(start, length), :] + (1.0 - decay_second) * clipped * clipped
        first[pl.ds(start, length), :] = one
        second[pl.ds(start, length), :] = two
        step[pl.ds(start, length), :] = (
            one / (1.0 - decay_first**STEP) / (jnp.sqrt(two / (1.0 - decay_second**STEP)) + epsilon)
        )

    def update_chunk(b, carry):
        update(pl.multiple_of(b * chunk, chunk), chunk)
        return carry

    lax.fori_loop(0, whole, update_chunk, 0)
    if tail:
        update(whole * chunk, tail)
    if plan.padded > share:
        step[share : plan.padded, :] = jnp.zeros((plan.padded - share, LANES), jnp.float32)

    def narrow(b, carry):
        at = pl.ds(pl.multiple_of(b * 16, 16), 16)
        low[at, :] = step[at, :].astype(jnp.bfloat16)
        return carry

    lax.fori_loop(0, plan.padded // 16, narrow, 0)

    own = pltpu.make_async_copy(low, full.at[me], sem_own)
    own.start()
    own.wait()

    back = [list(reversed(order)) for order in plan.orders]

    def piece(mask, col, p):
        begin, length = plan.cuts[p]
        return full.at[flipped(mask) * nc + col, pl.ds(begin, length)]

    def along(direction, col, p, receive):
        step_col = 1 if direction == 0 else -1
        target = c - step_col if receive else c + step_col
        ref = piece((), col, p)
        return remote(ref, ref, sem_gs.at[direction, col, p], sem_gr.at[direction, col, p], r, target)

    def gather_masks(p, stage):
        return bit_masks(back[p][:stage])

    def gather_base(stage):
        return sum(1 << s for s in range(stage)) * nc

    def across(p, stage, number, mask, col):
        at = gather_base(stage) + number * nc + col
        ref = piece(mask, col, p)
        return remote(ref, ref, sem_hs.at[p, at], sem_hr.at[p, at], flipped((back[p][stage],)), c)

    def across_recv(p, stage, number, mask, col):
        at = gather_base(stage) + number * nc + col
        ref = piece(mask + (back[p][stage],), col, p)
        return remote(ref, ref, sem_hs.at[p, at], sem_hr.at[p, at], flipped((back[p][stage],)), c)

    def inward(p, mask, col):
        number = masks.index(tuple(sorted(mask)))
        at = number * nc + col
        ref = piece(mask, col, p)
        return remote(ref, ref, sem_cs.at[p, at], sem_cr.at[p, at], flipped((0,)), c)

    def inward_recv(p, mask, col):
        number = masks.index(tuple(sorted(mask)))
        at = number * nc + col
        ref = piece(mask + (0,), col, p)
        return remote(ref, ref, sem_cs.at[p, at], sem_cr.at[p, at], flipped((0,)), c)

    def spread(p, mask, col, stage):
        for later in range(stage, plan.stages):
            options = [sorted(o) for o in gather_masks(p, later)]
            if sorted(mask) in options:
                across(p, later, options.index(sorted(mask)), mask, col).start()
        inward(p, mask, col).start()

    def near_cols(t):
        if t == 0:
            return [(0, c)]
        return [(0, c - t), (1, c + t)]

    def inside(col):
        return (col >= 0) & (col < nc)

    for time in range(nc + plan.stages):
        for stage in range(plan.stages + 1):
            t = time - stage
            if not 0 <= t < nc:
                continue
            if stage == 0:
                if t == 0:
                    for p in range(2):
                        @pl.when(c < nc - 1)
                        def _(p=p):
                            along(0, c, p, False).start()

                        @pl.when(c > 0)
                        def _(p=p):
                            along(1, c, p, False).start()

                        spread(p, (), c, 0)
                else:
                    for direction, col in near_cols(t):
                        @pl.when(inside(col))
                        def _(direction=direction, col=col):
                            for p in range(2):
                                along(direction, col, p, True).wait_recv()
                                if direction == 0:
                                    @pl.when(c < nc - 1)
                                    def _():
                                        along(0, col, p, False).start()
                                else:
                                    @pl.when(c > 0)
                                    def _():
                                        along(1, col, p, False).start()
                                spread(p, (), col, 0)
            else:
                for direction, col in near_cols(t):
                    @pl.when(inside(col))
                    def _(col=col, stage=stage):
                        for number in range(1 << (stage - 1)):
                            for p in range(2):
                                mask = gather_masks(p, stage - 1)[number]
                                across_recv(p, stage - 1, number, mask, col).wait_recv()
                                spread(p, mask + (back[p][stage - 1],), col, stage)

    for mask in masks:
        def finish(col, carry, mask=mask):
            for p in range(2):
                inward_recv(p, mask, col).wait_recv()
                inward(p, mask, col).wait_send()
            near_copy(mask, col).wait_send()
            return carry

        lax.fori_loop(0, nc, finish, 0)
    for p in range(2):
        for stage in range(plan.stages):
            for number, mask in enumerate(gather_masks(p, stage)):
                def sent(col, carry, p=p, stage=stage, number=number, mask=mask):
                    across(p, stage, number, mask, col).wait_send()
                    return carry

                lax.fori_loop(0, nc, sent, 0)
            for number in range(1 << (plan.stages - 1 - stage)):
                def left(col, carry, p=p, stage=stage, number=number):
                    for copy in hop(p, stage, number * nc + col):
                        copy.wait_send()
                    return carry

                lax.fori_loop(0, nc, left, 0)

        def gone(col, carry, p=p):
            @pl.when((col <= c) & (c < nc - 1))
            def _():
                along(0, col, p, False).wait_send()

            @pl.when((col >= c) & (c > 0))
            def _():
                along(1, col, p, False).wait_send()

            return carry

        lax.fori_loop(0, nc, gone, 0)

        def far_gone(d, carry, p=p):
            for copy in far_copy(p, d):
                copy.wait_send()
            return carry

        lax.fori_loop(1, nc, far_gone, 0)

    def stat_gone(d, carry):
        stat_copy(lax.rem(me + d, n), me).wait_send()
        return carry

    lax.fori_loop(1, n, stat_gone, 0)


def exchange(rows, cols, grad, m_first, m_second, extra):
    plan = Plan(rows, cols, m_first.size * rows * cols)
    n, nc, share = plan.count, plan.cols, plan.share
    hops = sum(1 << s for s in range(plan.stages)) * nc
    dma = pltpu.SemaphoreType.DMA
    far = max(nc - 1, 1)
    vmem = pl.BlockSpec(memory_space=pltpu.VMEM)
    hbm = pl.BlockSpec(memory_space=pl.ANY)
    return plan, pl.pallas_call(
        functools.partial(exchange_kernel, plan),
        out_shape=(
            jax.ShapeDtypeStruct((n, plan.padded, LANES), jnp.bfloat16),
            jax.ShapeDtypeStruct((share, LANES), jnp.float32),
            jax.ShapeDtypeStruct((share, LANES), jnp.float32),
            jax.ShapeDtypeStruct((16, LANES), jnp.float32),
        ),
        in_specs=[hbm, vmem, vmem, vmem],
        out_specs=(hbm, vmem, vmem, vmem),
        scratch_shapes=[
            pltpu.VMEM((plan.local, plan.window, LANES), jnp.float32),
            pltpu.VMEM((plan.local, plan.window, LANES), jnp.float32),
            pltpu.VMEM((2, hops, plan.part, LANES), jnp.int16),
            pltpu.VMEM((2, hops, plan.part, LANES), jnp.int16),
            pltpu.VMEM((2, hops, plan.scales, LANES), jnp.float32),
            pltpu.VMEM((2, hops, plan.scales, LANES), jnp.float32),
            pltpu.VMEM((2, far, plan.part, LANES), jnp.int16),
            pltpu.VMEM((2, far, plan.part, LANES), jnp.int16),
            pltpu.VMEM((2, far, plan.scales, LANES), jnp.float32),
            pltpu.VMEM((2, far, plan.scales, LANES), jnp.float32),
            pltpu.VMEM((len(SHIFTS), plan.window, LANES), jnp.float32),
            pltpu.VMEM((plan.padded, LANES), jnp.float32),
            pltpu.VMEM((plan.padded, LANES), jnp.bfloat16),
            pltpu.VMEM((n, 16, LANES), jnp.float32),
            dma((plan.local,)), dma((plan.local,)), dma((plan.local,)),
            dma((2, hops)), dma((2, hops)), dma((2, hops)), dma((2, hops)),
            dma((2, far)), dma((2, far)), dma((2, far)), dma((2, far)),
            dma((n,)), dma((n,)), dma,
            dma((2, nc, 2)), dma((2, nc, 2)),
            dma((2, hops)), dma((2, hops)),
            dma((2, plan.local)), dma((2, plan.local)),
        ],
        compiler_params=pltpu.CompilerParams(
            collective_id=0, has_side_effects=True, vmem_limit_bytes=56 << 20
        ),
    )(grad, m_first.reshape(share, LANES), m_second.reshape(share, LANES), extra)


WIDE = CH + LANES
KEPT = ((8, 1104), (6096, 6408), (51400, 51584))
PLACES = tuple(divmod(FLAT_AT[i], LANES) for i in (3, 4, 5, 1))

SLOTS = 4
HALF = WIDE // 2
PITCH = 33


def unpack_kernel(
    plan, gathered, old_up, old_down, wide, hidden_out, rows_out, up_out, down_out, small_a, small_b, small_c,
    held, flat, woven, hidden, by_row, rows_low, up, down, sems, sem_out,
):
    n, share = plan.count, plan.share
    step = CH // LANES

    def fetch(k, slot):
        return pltpu.make_async_copy(gathered.at[k], held.at[slot], sems.at[slot])

    for k in range(SLOTS - 1):
        fetch(k, k).start()

    def widen(k, carry):
        slot = lax.rem(k, SLOTS)

        @pl.when(k + SLOTS - 1 < n)
        def _():
            fetch(k + SLOTS - 1, lax.rem(k + SLOTS - 1, SLOTS)).start()

        fetch(k, slot).wait()

        def body(b, inner):
            at = pl.ds(pl.multiple_of(b * 16, 16), 16)
            flat[pl.ds(share * k + b * 16, 16), :] = held[slot, at, :].astype(jnp.float32)
            return inner

        lax.fori_loop(0, plan.padded // 16, body, 0, unroll=4)
        return carry

    lax.fori_loop(0, n, widen, 0)

    copies = [
        pltpu.make_async_copy(source, target, sem_out.at[i])
        for i, (source, target) in enumerate(
            (
                (hidden, hidden_out.at[:, pl.ds(0, HALF)]), (rows_low, rows_out), (up, up_out),
                (down, down_out), (hidden, hidden_out.at[:, pl.ds(HALF, HALF)]),
            )
        )
    ]
    row, lane = PLACES[0]

    def columns(half):
        def column(t, carry):
            for begin in range(0, C1, 160):
                at = row + begin * step + half * (HALF // LANES) + t
                values = flat[pl.ds(at, 160, stride=step), :]
                at = pl.ds(pl.multiple_of(t * LANES, LANES), LANES)
                hidden[begin : begin + 160, at] = values.astype(jnp.bfloat16)
            return carry

        lax.fori_loop(0, HALF // LANES, column, 0)

    columns(0)
    copies[0].start()

    quarter = C1 // 4
    for number, (ref, old, (line, begin)) in enumerate(zip((up, down), (old_up, old_down), PLACES[2:])):
        for u in range(-(-C1 // LANES)):
            width = min(LANES, C1 - u * LANES)
            place = lax.broadcasted_iota(jnp.int32, (quarter, LANES), 1)
            for b in range(4):
                first, rest = divmod(C1 * b + begin, LANES)
                here = flat[pl.ds(line + first + u, quarter, stride=step), :]
                after = flat[pl.ds(line + first + u + 1, quarter, stride=step), :]
                value = pltpu.roll(jnp.where(place >= rest, here, after), LANES - rest, 1)
                woven[pl.ds(b, quarter, stride=4), :] = value
            at = slice(u * LANES, u * LANES + width)
            ref[:, at] = moved(old[:, at], woven[:, :width])
        copies[2 + number].start()

    for ref, (begin, end) in zip((small_a, small_b, small_c), KEPT):
        ref[...] = flat[begin:end, :]
    copies[0].wait()
    columns(1)
    copies[4].start()

    row, lane = PLACES[1]

    def align(part, carry):
        place = lax.broadcasted_iota(jnp.int32, (40, LANES), 1)
        for b in range(4):
            first, rest = divmod(C1 * b + lane, LANES)
            values = []
            for u in range(-(-C1 // LANES)):
                at = row + part * (40 * step) + first + u
                here = flat[pl.ds(at, 40, stride=step), :]
                after = flat[pl.ds(at + 1, 40, stride=step), :]
                values.append(pltpu.roll(jnp.where(place >= rest, here, after), LANES - rest, 1))
            for u, value in enumerate(values):
                flat[pl.ds(part * (40 * PITCH) + b * 8 + u, 40, stride=PITCH), :] = value
        return carry

    lax.fori_loop(0, C1 // 40, align, 0)

    def scatter(a, carry):
        for b in range(4):
            by_row[pl.ds(wide[a * 4 + b] * 9, 8), :] = flat[pl.ds(a * PITCH + b * 8, 8), :]
        return carry

    lax.fori_loop(0, CH // 4, scatter, 0, unroll=4)

    def by_lane(part, carry):
        for u in range(C1P // LANES):
            values = by_row[pl.ds(part * (160 * 9) + u, 160, stride=9), :]
            at = pl.ds(pl.multiple_of(part * 160, 160), 160)
            rows_low[at, u * LANES : (u + 1) * LANES] = values.astype(jnp.bfloat16)
        return carry

    lax.fori_loop(0, CH // 160, by_lane, 0)
    copies[1].start()
    for copy in copies[1:]:
        copy.wait()


def unpack(plan, gathered, old_up, old_down, wide):
    lines = PADDED // LANES
    vmem = pl.BlockSpec(memory_space=pltpu.VMEM)
    hbm = pl.BlockSpec(memory_space=pl.ANY)
    dma = pltpu.SemaphoreType.DMA
    f32, low = jnp.float32, jnp.bfloat16
    return pl.pallas_call(
        functools.partial(unpack_kernel, plan),
        out_shape=(
            jax.ShapeDtypeStruct((C1, WIDE), low),
            jax.ShapeDtypeStruct((CH, C1P), low),
            jax.ShapeDtypeStruct((C1, C1), f32),
            jax.ShapeDtypeStruct((C1, C1), f32),
        )
        + tuple(jax.ShapeDtypeStruct((end - begin, LANES), f32) for begin, end in KEPT),
        in_specs=[hbm, vmem, vmem, pl.BlockSpec(memory_space=pltpu.SMEM)],
        out_specs=(hbm, hbm, hbm, hbm, vmem, vmem, vmem),
        scratch_shapes=[
            pltpu.VMEM((SLOTS, plan.padded, LANES), low),
            pltpu.VMEM((-(-lines // 8) * 8 + 16, LANES), f32),
            pltpu.VMEM((C1, LANES), f32),
            pltpu.VMEM((C1, HALF), low),
            pltpu.VMEM((CH * 9, LANES), f32),
            pltpu.VMEM((CH, C1P), low),
            pltpu.VMEM((C1, C1), f32),
            pltpu.VMEM((C1, C1), f32),
            dma((SLOTS,)),
            dma((5,)),
        ],
        compiler_params=pltpu.CompilerParams(vmem_limit_bytes=63 << 20),
    )(gathered, old_up, old_down, wide)


def moved(old, direction):
    return old.astype(jnp.float32) * (1.0 - learn_rate * weight_decay) - learn_rate * direction


def one_hot(condition):
    return jnp.where(condition, 1.0, 0.0).astype(jnp.bfloat16)


def product(left, right):
    return jnp.dot(left, right, preferred_element_type=jnp.float32)


def product_t(left, right):
    return lax.dot_general(left, right, (((1,), (1,)), ((), ())), preferred_element_type=jnp.float32)


TILE = 640


DEEP = 256


def turn_kernel(prepare, packed, narrow, wide, old, new, lines):
    depth = lines.shape[1]

    @pl.when(pl.program_id(0) == 0)
    def _():
        prepare(packed, narrow, lines)

    base = pl.program_id(0) * TILE
    direction = None
    for begin in range(0, depth, DEEP):
        end = min(begin + DEEP, depth)
        place = wide[begin:end, :] - base
        lane = lax.broadcasted_iota(jnp.int32, (end - begin, LANES), 1)
        hot = jnp.concatenate([one_hot(lane + u == place) for u in range(0, TILE, LANES)], axis=1)
        term = product(lines[:, begin:end], hot)
        direction = term if direction is None else direction + term
    new[...] = moved(old[...], direction)


def prepare_hidden(packed, narrow, lines):
    turn = one_hot(lax.broadcasted_iota(jnp.int32, (C1, C1), 0) == narrow[...])
    for begin in range(0, WIDE, 832):
        lines[:, begin : begin + 832] = product(turn, packed[:, begin : begin + 832]).astype(jnp.bfloat16)


def turn_back(prepare, packed, narrow, wide, old):
    depth = wide.shape[0]
    return pl.pallas_call(
        functools.partial(turn_kernel, prepare),
        out_shape=jax.ShapeDtypeStruct((C1, CH), jnp.float32),
        grid=(CH // TILE,),
        in_specs=[
            pl.BlockSpec((C1, WIDE), lambda i: (0, 0)),
            pl.BlockSpec(narrow.shape, lambda i: (0, 0)),
            pl.BlockSpec((depth, LANES), lambda i: (0, 0)),
            pl.BlockSpec((C1, TILE), lambda i: (0, i)),
        ],
        out_specs=pl.BlockSpec((C1, TILE), lambda i: (0, i)),
        scratch_shapes=[pltpu.VMEM((C1, depth), jnp.bfloat16)],
        compiler_params=pltpu.CompilerParams(vmem_limit_bytes=48 << 20),
    )(packed, narrow, jnp.broadcast_to(wide[:, None], (depth, LANES)), old)


def rebuild_hidden(packed, narrow, wide, old):
    lane = PLACES[0][1]
    shifted = jnp.full((WIDE,), -1, jnp.int32).at[lane : lane + CH].set(wide)
    return turn_back(prepare_hidden, packed, narrow[None, :], shifted, old)


def out_kernel(rows, narrow, old, new, turn):
    @pl.when(pl.program_id(0) == 0)
    def _():
        turn[...] = one_hot(lax.broadcasted_iota(jnp.int32, (C1, C1), 0) == narrow[...])

    new[...] = moved(old[...], product_t(turn[...], rows[:, :C1]))


def rebuild_out(rows, narrow, old):
    return pl.pallas_call(
        out_kernel,
        out_shape=jax.ShapeDtypeStruct((C1, CH), jnp.float32),
        grid=(CH // TILE,),
        in_specs=[
            pl.BlockSpec((TILE, C1P), lambda i: (i, 0)),
            pl.BlockSpec((1, C1), lambda i: (0, 0)),
            pl.BlockSpec((C1, TILE), lambda i: (0, i)),
        ],
        out_specs=pl.BlockSpec((C1, TILE), lambda i: (0, i)),
        scratch_shapes=[pltpu.VMEM((C1, C1), jnp.bfloat16)],
        compiler_params=pltpu.CompilerParams(vmem_limit_bytes=48 << 20),
    )(rows, narrow[None, :], old.T).T


def weave(source, rows, put):
    for t in range(CH // LANES):
        b, begin = divmod(t * LANES, C1)
        u, rest = divmod(begin, LANES)
        place = lax.broadcasted_iota(jnp.int32, (rows, LANES), 1)
        value = source[u, pl.ds(b, rows, stride=4), :]
        if rest:
            if begin + LANES - rest < C1:
                after = source[u + 1, pl.ds(b, rows, stride=4), :]
                value = jnp.where(place >= rest, value, after)
            value = pltpu.roll(value, LANES - rest, 1)
        left = C1 - begin
        if left < LANES:
            following = source[0, pl.ds(b + 1, rows, stride=4), :]
            value = jnp.where(place < left, value, pltpu.roll(following, left, 1))
        put(t, value)


def place_kernel(
    nr, nc, normed, branch, pre, act, narrow_row, narrow_col, wide, up, cells,
    grad, padded, hidden, out, loose, up_rows, norm_t, branch_r, halo_cells,
    sem_out, sems, sem_halo_s, sem_halo_r,
):
    step = pl.program_id(0)
    steps = pl.num_programs(0)
    ratio = CH // LANES
    lines = TILE // 4
    tiles = TILE // LANES

    def out_copy(n):
        rows = lines * ratio
        return pltpu.make_async_copy(
            out.at[pl.ds(pl.multiple_of(n * rows, 8), rows)],
            grad.at[pl.ds(pl.multiple_of(ROW_AT[4] + n * rows, 8), rows)],
            sem_out.at[n],
        )

    copies = [
        pltpu.make_async_copy(ref, grad.at[pl.ds(row, ref.shape[0])], sems.at[i])
        for i, (ref, row) in enumerate(((up_rows, ROW_AT[5]), (hidden, ROW_AT[3])))
    ] + [pltpu.make_async_copy(halo_cells, padded, sems.at[2])]

    @pl.when(step == 0)
    def _():
        halo_start(nr, nc, 3, cells, halo_cells, sem_halo_s, sem_halo_r)
        line = lax.broadcasted_iota(jnp.int32, (C1, C1), 1)
        norm_t[...] = product_t(one_hot(line == narrow_col[:, 0:1]), normed[:, :C1]).astype(jnp.bfloat16)
        line = lax.broadcasted_iota(jnp.int32, (C1, C1P), 0)
        branch_r[...] = product(branch[:, :C1], one_hot(line == narrow_row[...])).astype(jnp.bfloat16)
        for u in range(-(-C1 // LANES)):
            width = min(LANES, C1 - u * LANES)
            loose[u, :, 0:width] = up[0:C1, u * LANES : u * LANES + width]

        def put(t, value):
            up_rows[pl.ds(t, C1 // 4, stride=ratio), :] = value

        weave(loose, C1 // 4, put)
        copies[0].start()

    turned_pre = turned_act = None
    for begin in range(0, CH, DEEP):
        end = min(begin + DEEP, CH)
        line = lax.broadcasted_iota(jnp.int32, (end - begin, TILE), 0) + begin
        hot = one_hot(line == wide[...])
        one = product(pre[:, begin:end], hot)
        two = product(act[:, begin:end], hot)
        turned_pre = one if turned_pre is None else turned_pre + one
        turned_act = two if turned_act is None else turned_act + two
    part = product(norm_t[...], turned_pre.astype(jnp.bfloat16))
    for t in range(tiles):
        hidden[pl.ds(step * tiles + t, C1, stride=ratio), :] = part[:, t * LANES : (t + 1) * LANES]
    part = inner_rows(turned_act.astype(jnp.bfloat16), branch_r[...])
    for u in range(-(-C1 // LANES)):
        loose[u, 0:TILE, :] = part[:, u * LANES : (u + 1) * LANES]

    def put_out(t, value):
        out[pl.ds(step * (lines * ratio) + t, lines, stride=ratio), :] = value

    weave(loose, lines, put_out)
    out_copy(step).start()

    @pl.when(step == steps - 1)
    def _():
        copies[1].start()
        halo_finish(nr, nc, 3, cells, halo_cells, sem_halo_s, sem_halo_r)
        copies[2].start()

        def finish(n, carry):
            out_copy(n).wait()
            return carry

        lax.fori_loop(0, steps, finish, 0)
        for copy in copies:
            copy.wait()


def place_gradients(nr, nc, space, normed, branch, pre, act, narrow, wide, up, cells):
    def whole(array):
        return pl.BlockSpec(
            array.shape, lambda i: (0,) * len(array.shape), pipeline_mode=pl.Buffered(1)
        )

    hbm = pl.BlockSpec(memory_space=pl.ANY)
    rows = pre.shape[0]
    batch, height, breadth, chans = cells.shape
    narrow_row = jnp.pad(narrow, (0, C1P - C1), constant_values=-1)[None, :]
    narrow_col = jnp.broadcast_to(narrow[:, None], (C1, LANES))
    framed = jax.ShapeDtypeStruct((batch, height + 6, breadth + 2 * EDGE, chans), cells.dtype)
    dma = pltpu.SemaphoreType.DMA
    return pl.pallas_call(
        functools.partial(place_kernel, nr, nc),
        out_shape=(jax.ShapeDtypeStruct((space, LANES), jnp.float32), framed),
        grid=(CH // TILE,),
        in_specs=[
            whole(normed), whole(branch), whole(pre), whole(act), whole(narrow_row), whole(narrow_col),
            pl.BlockSpec((1, TILE), lambda i: (0, i)),
            whole(up), whole(cells),
        ],
        out_specs=(hbm, hbm),
        scratch_shapes=[
            pltpu.VMEM((C1 * CH // LANES, LANES), jnp.float32),
            pltpu.VMEM((C1 * CH // LANES, LANES), jnp.float32),
            pltpu.VMEM((C1P // LANES, C1, LANES), jnp.float32),
            pltpu.VMEM((C1 * C1 // LANES, LANES), jnp.float32),
            pltpu.VMEM((C1, rows), jnp.bfloat16),
            pltpu.VMEM((rows, C1P), jnp.bfloat16),
            pltpu.VMEM(framed.shape, framed.dtype),
            dma((CH // TILE,)), dma((3,)), dma((8,)), dma((8,)),
        ],
        compiler_params=pltpu.CompilerParams(
            collective_id=3, has_side_effects=True, vmem_limit_bytes=60 << 20
        ),
    )(normed, branch, pre, act, narrow_row, narrow_col, wide[None, :], up, cells)


def complete_kernel(before, down, piece_in, piece_dw, piece_head, piece_vec, grad, loose, down_rows, sems):
    copies = [
        pltpu.make_async_copy(ref, grad.at[pl.ds(row, ref.shape[0])], sems.at[i])
        for i, (ref, row) in enumerate(
            (
                (piece_in, 0), (piece_dw, ROW_AT[2]), (piece_head, ROW_AT[6]), (piece_vec, ROW_AT[7]),
                (down_rows, ROW_AT[1]),
            )
        )
    ]
    for copy in copies[:4]:
        copy.start()
    for u in range(C1P // LANES):
        loose[u] = down[:, u * LANES : (u + 1) * LANES]

    def put(t, value):
        down_rows[pl.ds(t, C1 // 4, stride=CH // LANES), :] = value

    weave(loose, C1 // 4, put)
    copies[4].start()
    for copy in copies:
        copy.wait()


def complete_gradients(grad, down, pieces):
    vmem = pl.BlockSpec(memory_space=pltpu.VMEM)
    hbm = pl.BlockSpec(memory_space=pl.ANY)
    return pl.pallas_call(
        complete_kernel,
        out_shape=jax.ShapeDtypeStruct(grad.shape, grad.dtype),
        in_specs=[hbm, vmem, vmem, vmem, vmem, vmem],
        out_specs=hbm,
        input_output_aliases={0: 0},
        scratch_shapes=[
            pltpu.VMEM((C1P // LANES, C1, LANES), jnp.float32),
            pltpu.VMEM((C1 * C1 // LANES, LANES), jnp.float32),
            pltpu.SemaphoreType.DMA((5,)),
        ],
        compiler_params=pltpu.CompilerParams(vmem_limit_bytes=60 << 20),
    )(grad, down, *pieces)


C0P = 256
C1P = 896
CIP = 128
EDGE = 16
CURVE = 0.7978845608028654
CUBE = 0.044715


def inner_rows(left, right):
    return lax.dot_general(left, right, (((0,), (0,)), ((), ())), preferred_element_type=jnp.float32)


def column_sum(values):
    return jnp.sum(values.astype(jnp.float32), axis=0, keepdims=True)


def gelu(t):
    return 0.5 * t * (1.0 + jnp.tanh(CURVE * (t + CUBE * (t * t * t))))


def gelu_slope(t):
    bend = jnp.tanh(CURVE * (t + CUBE * (t * t * t)))
    return 0.5 * (1.0 + bend) + 0.5 * t * (1.0 - bend * bend) * (CURVE * (1.0 + 3.0 * CUBE * (t * t)))


WAYS = [(dr, dc) for dr in (-1, 0, 1) for dc in (-1, 0, 1) if (dr, dc) != (0, 0)]
ORDER = sorted(range(8), key=lambda i: (WAYS[i][1] != 0, WAYS[i][0] == 0))


def halo_place(nr, nc):
    r = lax.axis_index("rows")
    return r, lax.axis_index("cols"), lambda dr: (r + dr >= 0) & (r + dr < nr)


def halo_copy(nr, nc, width, cells, out, sem_s, sem_r, i, receive):
    r, c, there = halo_place(nr, nc)
    height, breadth = cells.shape[1], cells.shape[2]
    dr, dc = WAYS[i]
    rows_from = {-1: (0, width), 0: (0, height), 1: (height - width, width)}[dr]
    rows_to = {-1: height + width, 0: width, 1: 0}[dr]
    cols_from = {-1: (0, EDGE), 0: (0, breadth), 1: (breadth - EDGE, EDGE)}[dc]
    cols_to = {-1: EDGE + breadth, 0: EDGE, 1: 0}[dc]
    sign = -1 if receive else 1
    return pltpu.make_async_remote_copy(
        src_ref=cells.at[:, pl.ds(*rows_from), pl.ds(*cols_from)],
        dst_ref=out.at[:, pl.ds(rows_to, rows_from[1]), pl.ds(cols_to, cols_from[1])],
        send_sem=sem_s.at[i],
        recv_sem=sem_r.at[i],
        device_id=(r + sign * dr, lax.rem(c + sign * dc + nc, nc)),
        device_id_type=MESH,
    )


def halo_start(nr, nc, width, cells, out, sem_s, sem_r):
    r, c, there = halo_place(nr, nc)
    height, breadth = cells.shape[1], cells.shape[2]
    barrier = pltpu.get_barrier_semaphore()
    for dr, dc in WAYS:
        @pl.when(there(dr))
        def _(dr=dr, dc=dc):
            pl.semaphore_signal(
                barrier, inc=1, device_id=(r + dr, lax.rem(c + dc + nc, nc)), device_id_type=MESH
            )

    edge = (r == 0) | (r == nr - 1)

    @pl.when(edge)
    def _():
        pl.semaphore_wait(barrier, 5)

    @pl.when(jnp.logical_not(edge))
    def _():
        pl.semaphore_wait(barrier, 8)

    for i in ORDER:
        @pl.when(there(WAYS[i][0]))
        def _(i=i):
            halo_copy(nr, nc, width, cells, out, sem_s, sem_r, i, False).start()

    for m in range(cells.shape[0]):
        for row in range(height):
            out[m, width + row, EDGE : EDGE + breadth, :] = cells[m, row]

    @pl.when(r == 0)
    def _():
        out[:, 0:width] = jnp.zeros((out.shape[0], width) + out.shape[2:], out.dtype)

    @pl.when(r == nr - 1)
    def _():
        out[:, height + width :] = jnp.zeros((out.shape[0], width) + out.shape[2:], out.dtype)


def halo_finish(nr, nc, width, cells, out, sem_s, sem_r):
    r, c, there = halo_place(nr, nc)
    for i in ORDER:
        @pl.when(there(-WAYS[i][0]))
        def _(i=i):
            halo_copy(nr, nc, width, cells, out, sem_s, sem_r, i, True).wait_recv()

        @pl.when(there(WAYS[i][0]))
        def _(i=i):
            halo_copy(nr, nc, width, cells, out, sem_s, sem_r, i, False).wait_send()


def halo_kernel(nr, nc, width, cells, out, sem_s, sem_r):
    halo_start(nr, nc, width, cells, out, sem_s, sem_r)
    halo_finish(nr, nc, width, cells, out, sem_s, sem_r)


def halo(nr, nc, width, cells, identity):
    batch, height, breadth, chans = cells.shape
    vmem = pl.BlockSpec(memory_space=pltpu.VMEM)
    return pl.pallas_call(
        functools.partial(halo_kernel, nr, nc, width),
        out_shape=jax.ShapeDtypeStruct(
            (batch, height + 2 * width, breadth + 2 * EDGE, chans), cells.dtype
        ),
        in_specs=[vmem],
        out_specs=vmem,
        scratch_shapes=[pltpu.SemaphoreType.DMA((8,)), pltpu.SemaphoreType.DMA((8,))],
        compiler_params=pltpu.CompilerParams(
            collective_id=identity, has_side_effects=True, vmem_limit_bytes=24 << 20
        ),
    )(cells)


def input_kernel(state, w_in, w_down, lines, taps, a_zero, h_zero, coarse, coarse_low, wide):
    batch, rows, breadth, _ = state.shape
    half_h, half_w = (rows - 2) // 2, (breadth - 2 * EDGE) // 2
    for m in range(batch):
        for y in range(rows):
            wide[m, y] = state[m, y].astype(jnp.float32)
    for m in range(batch):
        for y in range(rows):
            for f in range(4):
                line = wide[m, y, pl.ds(EDGE - 1 + f, half_w, stride=2), :].astype(jnp.bfloat16)
                for dy in range(3):
                    i, sy = divmod(y - dy, 2)
                    if not 0 <= i < half_h:
                        continue
                    for dx in range(3):
                        if 0 <= f - dx < 2:
                            begin = (m * half_h + i) * half_w
                            tap = (dy * 3 + dx) * CIP
                            taps[sy * 2 + f - dx, begin : begin + half_w, tap : tap + CIP] = line
    coarse[...] = jnp.broadcast_to(lines[1:2, :C1P], coarse.shape)
    for s in range(4):
        value = product(taps[s], w_in[...]) + lines[0:1, :C0P]
        a_zero[s] = value
        value = gelu(value)
        h_zero[s] = value
        coarse[...] += product(value.astype(jnp.bfloat16), w_down[s])
    coarse_low[...] = coarse[...].astype(jnp.bfloat16).reshape(coarse_low.shape)


def input_part(state, w_in, w_down, lines):
    batch, rows, breadth, _ = state.shape
    half_h, half_w = (rows - 2) // 2, (breadth - 2 * EDGE) // 2
    cells = batch * half_h * half_w
    vmem = pl.BlockSpec(memory_space=pltpu.VMEM)
    return pl.pallas_call(
        input_kernel,
        out_shape=(
            jax.ShapeDtypeStruct((4, cells, 9 * CIP), jnp.bfloat16),
            jax.ShapeDtypeStruct((4, cells, C0P), jnp.float32),
            jax.ShapeDtypeStruct((4, cells, C0P), jnp.float32),
            jax.ShapeDtypeStruct((cells, C1P), jnp.float32),
            jax.ShapeDtypeStruct((batch, half_h, half_w, C1P), jnp.bfloat16),
        ),
        in_specs=[vmem] * 4,
        out_specs=tuple([vmem] * 5),
        scratch_shapes=[pltpu.VMEM(state.shape, jnp.float32)],
        compiler_params=pltpu.CompilerParams(vmem_limit_bytes=40 << 20),
    )(state, w_in, w_down, lines)


def spread_lanes(padded, held):
    for m in range(padded.shape[0]):
        def body(y, carry, m=m):
            for u in range(C1P // LANES):
                held[u, m, y] = padded[m, y, :, u * LANES : (u + 1) * LANES].astype(jnp.float32)
            return carry

        lax.fori_loop(0, padded.shape[1], body, 0)


def convolve(held, w_dw, put, back):
    tiles, batch, rows, breadth = held.shape[:4]
    height, half_w = rows - 6, breadth - 2 * EDGE

    def body(number, carry):
        u, m = number // batch, number % batch
        sums = [jnp.zeros((half_w, LANES), jnp.float32) for _ in range(height)]
        for x in range(7):
            for y in range(rows):
                window = held[u, m, y, pl.ds(EDGE - 3 + x, half_w), :]
                for i in range(height):
                    if 0 <= y - i < 7:
                        tap = (6 - (y - i)) * 7 + 6 - x if back else (y - i) * 7 + x
                        sums[i] = sums[i] + window * w_dw[pl.ds(tap, 1), lanes_at(u)]
        for i in range(height):
            put(u, m, i, sums[i])
        return carry

    lax.fori_loop(0, tiles * batch, body, 0)


def rows_at(m, i, height, half_w):
    return pl.ds(pl.multiple_of((m * height + i) * half_w, half_w), half_w)


def lanes_at(u):
    return pl.ds(pl.multiple_of(u * LANES, LANES), LANES)


PART = 640


LATE = ("coarse", "h_zero", "target", "weight", "w_hidden", "w_out_t", "w_up")
EARLY = ("normed", "act", "grad_mixed", "grad_branch", "grad_summed", "d_up")


def middle_kernel(names, *refs):
    ref = dict(zip(names, refs))
    batch, rows, breadth, _ = ref["padded"].shape
    cells = ref["coarse"].shape[0]
    height, half_w = rows - 6, breadth - 2 * EDGE
    fetch, store, held_in, held_out = {}, {}, {}, {}
    for i, name in enumerate(LATE):
        held_in[name] = ref["held_" + name]
        fetch[name] = pltpu.make_async_copy(ref[name], held_in[name], ref["sem_in"].at[i])
        fetch[name].start()
    for i, name in enumerate(EARLY):
        held_out[name] = ref["held_" + name]
        store[name] = pltpu.make_async_copy(held_out[name], ref[name], ref["sem_out"].at[i])
    conv = ref["conv"]

    def depthwise(held):
        spread_lanes(ref["padded"], held)

        def put(u, m, i, value):
            conv[rows_at(m, i, height, half_w), lanes_at(u)] = value

        convolve(held, ref["w_dw"], put, False)

    pl.run_scoped(depthwise, pltpu.VMEM((C1P // LANES, batch, rows, breadth, LANES), jnp.float32))
    pl.run_scoped(
        functools.partial(pointwise_part, ref, fetch, store, held_in, held_out),
        pltpu.VMEM((cells, CH), jnp.float32),
        pltpu.VMEM((cells, C1), jnp.bfloat16),
    )
    for name in EARLY:
        store[name].wait()


def pointwise_part(ref, fetch, store, held_in, held_out, pre, spread_all):
    conv, total, sums, extra = ref["conv"], ref["total"], ref["sums"], ref["extra"]
    gain, w_head = ref["lines"].at[3:4, 0:C1P], ref["w_head"]
    normed, act = held_out["normed"], held_out["act"]
    grad_mixed, grad_branch, grad_summed = (
        held_out[name] for name in ("grad_mixed", "grad_branch", "grad_summed")
    )
    w_hidden, w_out_t, w_up = (held_in[name] for name in ("w_hidden", "w_out_t", "w_up"))
    target, weight, h_zero = (held_in[name] for name in ("target", "weight", "h_zero"))
    batch, rows, breadth, _ = ref["padded"].shape
    height, half_w = rows - 6, breadth - 2 * EDGE

    inside = lax.broadcasted_iota(jnp.int32, (1, C1P), 1) < C1
    values = conv[...] + ref["lines"][2:3, :C1P]
    mean = jnp.sum(values, axis=1, keepdims=True) * (1.0 / C1)
    centered = jnp.where(inside, values - mean, 0.0)
    scale = lax.rsqrt(jnp.sum(centered * centered, axis=1, keepdims=True) * (1.0 / C1) + 1e-06)
    conv[...] = centered * scale
    normed[...] = (conv[...] * gain[...] + ref["lines"][4:5, :C1P]).astype(jnp.bfloat16)
    store["normed"].start()

    fetch["coarse"].wait()
    fetch["w_hidden"].wait()
    fetch["w_out_t"].wait()
    total[...] = held_in["coarse"][...]
    for begin in range(0, CH, PART):
        span = slice(begin, begin + PART)
        value = product(normed[:, :C1], w_hidden[:, span]) + ref["lines"][5:6, span]
        pre[:, span] = value
        act[:, span] = gelu(value).astype(jnp.bfloat16)
        total[:, :C1] += product_t(act[:, span], w_out_t[:, span])
    store["act"].start()
    mixed = (total[...] + ref["lines"][6:7, :C1P]).astype(jnp.bfloat16)

    for name in ("h_zero", "target", "weight", "w_up"):
        fetch[name].wait()
    grad_mixed[...] = jnp.zeros_like(grad_mixed)
    loss = jnp.zeros((1, CI), jnp.float32)
    head_sum = jnp.zeros((1, CI), jnp.float32)
    up_sum = jnp.zeros((1, C0), jnp.float32)
    for s in range(4):
        sub_y, sub_x = divmod(s, 2)
        for m in range(batch):
            for i in range(height):
                at = rows_at(m, i, height, half_w)
                line = pl.ds(sub_x, half_w, stride=2)
                ref["goal"][at, :] = target[m, 2 * i + sub_y, line, :]
                ref["load"][at, :] = weight[2 * i + sub_y, line, :]
        w_up_s = w_up[:, s * C0 : (s + 1) * C0]
        upper = product(mixed[:, :C1], w_up_s) + ref["lines"][7:8, :C0]
        summed = (upper + h_zero[s, :, :C0]).astype(jnp.bfloat16)
        error = product(summed, w_head[...]) + ref["lines"][8:9, :CI] - ref["goal"][:, :CI]
        weighted = ref["load"][:, :CI] * error
        loss = loss + column_sum(weighted * error)
        grad_out = (2.0 * weighted).astype(jnp.bfloat16)
        head_sum = head_sum + column_sum(grad_out)
        if s == 0:
            ref["d_head"][...] = inner_rows(summed, grad_out)
        else:
            ref["d_head"][...] += inner_rows(summed, grad_out)
        spread = product_t(grad_out, w_head[...])
        grad_summed[s] = spread
        grad_upper = spread.astype(jnp.bfloat16)
        up_sum = up_sum + column_sum(grad_upper)
        spread_all[:, s * C0 : (s + 1) * C0] = grad_upper
        grad_mixed[:, :C1] += product_t(grad_upper, w_up_s)
    store["grad_summed"].start()
    store["grad_mixed"].start()
    held_out["d_up"][...] = inner_rows(mixed[:, :C1], spread_all[...])
    store["d_up"].start()
    grad_branch[...] = grad_mixed[...].astype(jnp.bfloat16)
    store["grad_branch"].start()
    sums[...] = jnp.zeros_like(sums)
    extra[...] = jnp.zeros_like(extra)
    extra[0:1, 0:CI] = loss
    extra[1:2, :] = column_sum(ref["weight_map"][...])
    sums[1:2, 0:CI] = head_sum
    sums[2:3, 0:C0] = up_sum
    sums[3:4, 0:C1P] = column_sum(grad_branch[...])

    total[...] = jnp.zeros_like(total)
    for begin in range(0, CH, PART):
        span = slice(begin, begin + PART)
        value = product(grad_branch[:, :C1], w_out_t[:, span]) * gelu_slope(pre[:, span])
        low = value.astype(jnp.bfloat16)
        ref["grad_pre"][:, span] = low
        sums[4:5, span] = column_sum(low)
        total[:, :C1] += product_t(low, w_hidden[:, span])

    grad_normed = total[...]
    sums[5:6, 0:C1P] = column_sum(grad_normed * conv[...])
    sums[6:7, 0:C1P] = column_sum(grad_normed)
    inward = grad_normed * gain[...]
    first = jnp.sum(inward, axis=1, keepdims=True) * (1.0 / C1)
    second = jnp.sum(inward * conv[...], axis=1, keepdims=True) * (1.0 / C1)
    value = scale * jnp.where(inside, inward - first - conv[...] * second, 0.0)
    low = value.astype(jnp.bfloat16)
    sums[7:8, 0:C1P] = column_sum(low)
    ref["grad_conv"][...] = low.reshape(ref["grad_conv"].shape)


def middle_part(**given):
    cells = given["coarse"].shape[0]
    batch, rows, breadth, _ = given["padded"].shape
    half_h, half_w = rows - 6, breadth - 2 * EDGE
    vmem = pl.BlockSpec(memory_space=pltpu.VMEM)
    hbm = pl.BlockSpec(memory_space=pl.ANY)
    f32, low = jnp.float32, jnp.bfloat16
    outs = {
        "normed": ((cells, C1P), low),
        "act": ((cells, CH), low),
        "grad_pre": ((cells, CH), low),
        "grad_mixed": ((cells, C1P), f32),
        "grad_branch": ((cells, C1P), low),
        "grad_summed": ((4, cells, C0), f32),
        "grad_conv": ((batch, half_h, half_w, C1P), low),
        "d_up": ((C1, C1), f32),
        "d_head": ((C0, CI), f32),
        "sums": ((8, CH), f32),
        "extra": ((8, LANES), f32),
    }
    scratch = {
        "conv": pltpu.VMEM((cells, C1P), f32),
        "total": pltpu.VMEM((cells, C1P), f32),
        "goal": pltpu.VMEM((cells, LANES), f32),
        "load": pltpu.VMEM((cells, LANES), f32),
        "sem_in": pltpu.SemaphoreType.DMA((len(LATE),)),
        "sem_out": pltpu.SemaphoreType.DMA((len(EARLY),)),
    }
    for name in LATE:
        scratch["held_" + name] = pltpu.VMEM(given[name].shape, given[name].dtype)
    for name in EARLY:
        scratch["held_" + name] = pltpu.VMEM(*outs[name])
    found = pl.pallas_call(
        functools.partial(middle_kernel, tuple(given) + tuple(outs) + tuple(scratch)),
        out_shape=tuple(jax.ShapeDtypeStruct(*out) for out in outs.values()),
        in_specs=[hbm if name in LATE else vmem for name in given],
        out_specs=tuple(hbm if name in EARLY else vmem for name in outs),
        scratch_shapes=list(scratch.values()),
        compiler_params=pltpu.CompilerParams(vmem_limit_bytes=62 << 20),
    )(*given.values())
    return dict(zip(outs, found))


AFTER = ("grad_mixed", "grad_summed", "a_zero", "h_zero", "taps", "w_down")


def outer_kernel(names, *refs):
    ref = dict(zip(names, refs))
    fetch = {}
    for i, name in enumerate(AFTER):
        fetch[name] = pltpu.make_async_copy(ref[name], ref["held_" + name], ref["sem_in"].at[i])
        fetch[name].start()
    grad_mixed, grad_summed, a_zero, h_zero, taps, w_down = (ref["held_" + name] for name in AFTER)
    held, conv, sums, d_dw, d_in = (ref[name] for name in ("held", "conv", "sums", "d_dw", "d_in"))
    vector = ref["vector"]
    grad_conv = ref["grad_conv"]
    batch, height, half_w, _ = grad_conv.shape
    spread_lanes(ref["padded"], held)
    tiles = C1P // LANES
    d_dw[...] = jnp.zeros_like(d_dw)

    def taps_of(number, carry):
        u, m = number // batch, number % batch
        grads = [grad_conv[m, i, :, lanes_at(u)].astype(jnp.float32) for i in range(height)]
        for x in range(7):
            found = [jnp.zeros((8, LANES), jnp.float32) for _ in range(7)]
            for y in range(height + 6):
                window = held[u, m, y, pl.ds(EDGE - 3 + x, half_w), :]
                for i in range(height):
                    if 0 <= y - i < 7:
                        term = (window * grads[i]).reshape(half_w // 8, 8, LANES)
                        found[y - i] = found[y - i] + jnp.sum(term, axis=0)
            for dy in range(7):
                d_dw[pl.ds(dy * 7 + x, 1), lanes_at(u)] += jnp.sum(found[dy], axis=0, keepdims=True)
        return carry

    lax.fori_loop(0, tiles * batch, taps_of, 0)
    spread_lanes(ref["grad_padded"], held)

    def put(u, m, i, value):
        conv[rows_at(m, i, height, half_w), lanes_at(u)] = value

    convolve(held, ref["w_dw"], put, True)
    for name in AFTER:
        fetch[name].wait()
    grad_coarse = (conv[...] + grad_mixed[...]).astype(jnp.bfloat16)
    vector[...] = jnp.zeros_like(vector)
    pieces = [(column_sum(grad_coarse), C1)] + [(sums[i : i + 1, :], C1) for i in (7, 5, 6)]
    pieces += [(sums[4:5, :], CH), (sums[3:4, :], C1), (sums[2:3, :], C0), (sums[1:2, :], CI)]
    start = C0
    for piece, size in pieces:
        vector[:, start : start + size] = piece[:, :size]
        start = start + size
    in_sum = jnp.zeros((1, C0), jnp.float32)
    for s in range(4):
        ref["d_down"][s * C0 : (s + 1) * C0, :] = inner_rows(
            h_zero[s].astype(jnp.bfloat16), grad_coarse
        )[:C0]
        grad_h = product_t(grad_coarse, w_down[s])[:, :C0] + grad_summed[s]
        grad_a = (gelu_slope(a_zero[s, :, :C0]) * grad_h).astype(jnp.bfloat16)
        in_sum = in_sum + column_sum(grad_a)
        if s == 0:
            d_in[...] = inner_rows(taps[s], grad_a)
        else:
            d_in[...] += inner_rows(taps[s], grad_a)
    vector[:, 0:C0] = in_sum


def outer_part(length, **given):
    cells = given["grad_mixed"].shape[0]
    batch, rows, breadth, _ = given["padded"].shape
    vmem = pl.BlockSpec(memory_space=pltpu.VMEM)
    hbm = pl.BlockSpec(memory_space=pl.ANY)
    f32 = jnp.float32
    outs = {
        "d_dw": ((56, C1P), f32),
        "d_down": ((C1, C1P), f32),
        "d_in": ((9 * CIP, C0), f32),
        "vector": ((1, length), f32),
    }
    scratch = {
        "held": pltpu.VMEM((C1P // LANES, batch, rows, breadth, LANES), f32),
        "conv": pltpu.VMEM((cells, C1P), f32),
        "sem_in": pltpu.SemaphoreType.DMA((len(AFTER),)),
    }
    for name in AFTER:
        scratch["held_" + name] = pltpu.VMEM(given[name].shape, given[name].dtype)
    found = pl.pallas_call(
        functools.partial(outer_kernel, tuple(given) + tuple(outs) + tuple(scratch)),
        out_shape=tuple(jax.ShapeDtypeStruct(*out) for out in outs.values()),
        in_specs=[hbm if name in AFTER else vmem for name in given],
        out_specs=tuple([vmem] * len(outs)),
        scratch_shapes=list(scratch.values()),
        compiler_params=pltpu.CompilerParams(vmem_limit_bytes=60 << 20),
    )(*given.values())
    return dict(zip(outs, found))


def split_vector(vector):
    lengths = [C0, C1, C1, C1, C1, CH, C1, C0, CI]
    pieces = []
    start = 0
    for length in lengths:
        pieces.append(vector[start : start + length])
        start = start + length
    return pieces


def as_rows(piece, rows):
    flat = piece.reshape(-1)
    return jnp.pad(flat, (0, rows * LANES - flat.shape[0])).reshape(rows, LANES)


def widened(array, *shape):
    return jnp.pad(array, [(0, full - now) for full, now in zip(shape, array.shape)])


def on_device(
    inputs,
    targets,
    land_mask,
    volume,
    date_index,
    perm_narrow,
    perm_wide,
    w_in,
    w_down,
    w_dw,
    w_hidden,
    w_out,
    w_up,
    w_head,
    biases_gains,
    moment_first,
    moment_second,
):
    rows, cols = lax.axis_size("rows"), lax.axis_size("cols")
    weight = land_mask.astype(jnp.float32) * volume
    height, breadth = weight.shape
    half_h, half_w = (height // 2, breadth // 2)
    cells = MB * half_h * half_w
    matrices = (w_in, w_down, w_dw, w_hidden, w_out, w_up, w_head)

    def dates(field):
        picked = jnp.concatenate(
            [lax.dynamic_slice_in_dim(field, date_index[m], 1, 0) for m in range(MB)]
        )
        return widened(picked, MB, height, breadth, CIP)

    lines = jnp.stack([widened(piece, CH) for piece in split_vector(biases_gains)])
    w_in_p = widened(w_in.reshape(9, CI, C0), 9, CIP, C0P).reshape(9 * CIP, C0P)
    w_down_p = widened(w_down.reshape(4, C0, C1), 4, C0P, C1P)
    w_dw_p = widened(w_dw.astype(jnp.float32), 56, C1P)
    weight_map = jnp.broadcast_to(weight[:, :, None], (height, breadth, LANES))

    state = halo(rows, cols, 1, dates(inputs), 1)
    taps, a_zero, h_zero, coarse, coarse_low = input_part(
        state, w_in_p, w_down_p, lines
    )
    padded = halo(rows, cols, 3, coarse_low, 2)
    mid = middle_part(
        padded=padded, coarse=coarse, h_zero=h_zero, target=dates(targets).astype(jnp.float32),
        weight=weight_map, weight_map=weight, w_dw=w_dw_p, w_hidden=w_hidden, w_out_t=w_out.T,
        w_up=w_up, w_head=w_head, lines=lines,
    )
    space = Plan(rows, cols, PADDED).space
    grad, grad_padded = place_gradients(
        rows, cols, space, mid["normed"], mid["grad_branch"], mid["grad_pre"], mid["act"],
        perm_narrow, perm_wide, mid["d_up"], mid["grad_conv"],
    )
    out = outer_part(
        (space - ROW_AT[7]) * LANES,
        padded=padded, grad_padded=grad_padded, grad_conv=mid["grad_conv"],
        grad_mixed=mid["grad_mixed"], grad_summed=mid["grad_summed"], a_zero=a_zero, h_zero=h_zero,
        taps=taps, w_dw=w_dw_p, w_down=w_down_p, sums=mid["sums"],
    )
    d_in = out["d_in"].reshape(9, CIP, C0)[:, :CI].reshape(9 * CI, C0)
    pieces = (
        jnp.pad(as_rows(d_in, ROW_AT[1] - ROW_AT[0]), ((ROW_AT[0], 0), (0, 0))),
        as_rows(out["d_dw"][:49, :C1], ROW_AT[3] - ROW_AT[2]),
        as_rows(mid["d_head"], ROW_AT[7] - ROW_AT[6]),
        out["vector"].reshape(-1, LANES),
    )
    grad = complete_gradients(grad, out["d_down"], pieces)
    plan, (gathered, first, second, totals) = exchange(
        rows, cols, grad, moment_first, moment_second, mid["extra"]
    )
    hidden_p, out_p, new_up, new_down, small_a, small_b, small_c = unpack(plan, gathered, w_up, w_down, perm_wide)
    small = {0: (small_a, 0), 2: (small_b, 1), 6: (small_c, 2), 7: (small_c, 2)}
    whole = {
        1: new_down,
        3: rebuild_hidden(hidden_p, perm_narrow, perm_wide, w_hidden),
        4: rebuild_out(out_p, perm_narrow, w_out),
        5: new_up,
    }
    olds = matrices + (biases_gains,)
    news = []
    for index, old in enumerate(olds):
        if index in whole:
            news.append(whole[index])
        else:
            source, which = small[index]
            start = FLAT_AT[index] - KEPT[which][0] * LANES
            piece = source.reshape(-1)[start : start + old.size].reshape(old.shape)
            news.append(moved(old, piece) if index < 7 else old - learn_rate * piece)
    return tuple(news) + (
        first.reshape(-1),
        second.reshape(-1),
        totals[0, 0],
        MB * CI * totals[1, 0],
        totals[8, 0],
    )


def solution(mesh):
    return jax.shard_map(
        on_device,
        mesh=mesh,
        in_specs=(
            P(None, "rows", "cols", None),
            P(None, "rows", "cols", None),
            P("rows", "cols"),
            P("rows", "cols"),
            P(),
            P(),
            P(),
            P(),
            P(),
            P(),
            P(),
            P(),
            P(),
            P(),
            P(),
            P(("rows", "cols")),
            P(("rows", "cols")),
        ),
        out_specs=(
            P(),
            P(),
            P(),
            P(),
            P(),
            P(),
            P(),
            P(),
            P(("rows", "cols")),
            P(("rows", "cols")),
            P(),
            P(),
            P(),
        ),
        check_vma=False,
    )
```

```python
import functools

import jax
import jax.numpy as jnp
from jax import lax
from jax.experimental import pallas as pl
from jax.experimental.pallas import tpu as pltpu
from jax.sharding import PartitionSpec as P

CI = 77
C0 = 200
C1 = 800
CH = 3200
MB = 2
STEP = 5
LANES = 128
MESH = pl.DeviceIdType.MESH
ROUNDER = 12582912.0

decay_first = 0.9
decay_second = 0.99
epsilon = 1e-08
learn_rate = 0.02
weight_decay = 0.1
clip_limit = 1.0

VEC = 4 * C1 + CH + C1 + 2 * C0 + CI
SIZES = (9 * CI * C0, 4 * C0 * C1, 49 * C1, C1 * CH, CH * C1, C1 * 4 * C0, C0 * CI, VEC)
PADDED = 6602752
FLAT_AT = []
ROW_AT = []
for size in SIZES:
    flat_here = FLAT_AT[-1] + SIZES[len(FLAT_AT) - 1] if FLAT_AT else PADDED - sum(SIZES)
    row_here = ROW_AT[-1] + -(-SIZES[len(ROW_AT) - 1] // 1024) * 8 if ROW_AT else 0
    row_here = max(row_here, -(-flat_here // 1024) * 8)
    FLAT_AT.append(flat_here)
    ROW_AT.append(row_here)
SHIFTS = []
for flat_here, row_here, size in zip(FLAT_AT, ROW_AT, SIZES):
    moved = divmod(row_here * LANES - flat_here, LANES)
    if SHIFTS and SHIFTS[-1][:2] == moved:
        SHIFTS[-1] = moved + (SHIFTS[-1][2], flat_here + size)
    else:
        SHIFTS.append(moved + (flat_here, flat_here + size))
MAX_SHIFT = max(s[0] for s in SHIFTS) + 1


def bit_masks(bits):
    masks = [()]
    for bit in bits:
        masks = masks + [m + (bit,) for m in masks]
    return sorted(masks, key=lambda m: -len(m))


class Plan:
    def __init__(self, rows, cols, total):
        self.rows, self.cols, self.count = rows, cols, rows * cols
        self.share = total // LANES // self.count
        self.bits = rows.bit_length() - 1
        need = 7 + self.share + MAX_SHIFT + 1
        self.block = 64 if need > 1024 else 32
        self.window = -(-need // (2 * self.block)) * 2 * self.block
        self.part = self.window // 2
        self.blocks = self.part // self.block
        self.scales = self.blocks
        upper = list(range(1, self.bits))
        self.orders = [upper, upper[1:] + upper[:1]]
        self.stages = len(upper)
        self.space = (self.share * (self.count - 1)) // 8 * 8 + self.window
        self.padded = -(-self.share // 16) * 16
        cut = -(-self.padded // 32) * 16
        self.cuts = [(0, cut), (cut, self.padded - cut)]
        self.local = self.count // 2


def exchange_kernel(
    plan, grad, m_first, m_second, extra, full, first, second, totals,
    acc, near, q_send, q_recv, s_send, s_recv, z_send, z_recv, zs_send, zs_recv,
    rolled, step, low, stats,
    sem_load, sem_near_s, sem_near_r, sem_qs, sem_qr, sem_ss, sem_sr,
    sem_zs, sem_zr, sem_zss, sem_zsr, sem_ts, sem_tr, sem_own,
    sem_gs, sem_gr, sem_hs, sem_hr, sem_cs, sem_cr,
):
    nr, nc, n = plan.rows, plan.cols, plan.count
    r = lax.axis_index("rows")
    c = lax.axis_index("cols")
    me = r * nc + c
    part, window, share = plan.part, plan.window, plan.share

    def flipped(mask):
        out = r
        for bit in mask:
            here = (r // (1 << bit)) % 2
            out = out + (1 - 2 * here) * (1 << bit)
        return out

    def remote(src, dst, send, recv, row, col):
        return pltpu.make_async_remote_copy(
            src_ref=src, dst_ref=dst, send_sem=send, recv_sem=recv,
            device_id=(row, col), device_id_type=MESH,
        )

    barrier = pltpu.get_barrier_semaphore()

    def greet(d, carry):
        k = lax.rem(me + d, n)
        pl.semaphore_signal(barrier, inc=1, device_id=(k // nc, k % nc), device_id_type=MESH)
        return carry

    lax.fori_loop(1, n, greet, 0)
    pl.semaphore_wait(barrier, n - 1)

    upper = list(range(1, plan.bits))
    masks = bit_masks(upper)

    def local_index(mask, col):
        return (flipped(mask) // 2) * nc + col

    def window_start(row, col):
        return pl.multiple_of((share * (row * nc + col)) // 8 * 8, 8)

    def near_copy(mask, col):
        row = flipped(mask + (0,))
        return remote(
            grad.at[pl.ds(window_start(row, col), window)],
            near.at[local_index(mask, col)],
            sem_near_s.at[local_index(mask, col)], sem_near_r.at[local_index(mask, col)],
            flipped((0,)), c,
        )

    def load_copy(mask, col):
        index = local_index(mask, col)
        return pltpu.make_async_copy(
            grad.at[pl.ds(window_start(flipped(mask), col), window)], acc.at[index], sem_load.at[index]
        )

    half_way = nc // 2

    def column_of(t):
        return jnp.where(t == 1, half_way, jnp.where(t <= half_way, t - 1, t))

    def begin(t, carry):
        col = lax.rem(c + column_of(t), nc)
        for mask in masks:
            near_copy(mask, col).start()
            load_copy(mask, col).start()
        return carry

    lax.fori_loop(1, nc + 1, begin, 0)

    def encode(index, p, q_ref, s_ref):
        def body(b, carry):
            at = pl.ds(pl.multiple_of(b * plan.block, plan.block), plan.block)
            rows_at = pl.ds(pl.multiple_of(p * part + b * plan.block, 8), plan.block)
            values = acc[index, rows_at, :]
            top = jnp.maximum(jnp.max(jnp.abs(values), axis=0, keepdims=True), 1e-30)
            scaled = values * (32766.0 / top)
            scaled = (scaled + ROUNDER) - ROUNDER
            q_ref[at, :] = scaled.astype(jnp.int32).astype(jnp.int16)
            s_ref[pl.ds(b, 1), :] = top * (1.0 / 32766.0)
            return carry

        lax.fori_loop(0, plan.blocks, body, 0)

    def decode(index, p, q_ref, s_ref):
        def body(b, carry):
            at = pl.ds(pl.multiple_of(b * plan.block, plan.block), plan.block)
            rows_at = pl.ds(pl.multiple_of(p * part + b * plan.block, 8), plan.block)
            acc[index, rows_at, :] += q_ref[at, :].astype(jnp.float32) * s_ref[pl.ds(b, 1), :]
            return carry

        lax.fori_loop(0, plan.blocks, body, 0)

    def stage_base(stage):
        return sum((1 << (plan.stages - 1 - s)) for s in range(stage)) * nc

    def hop(p, stage, slot):
        row = flipped((plan.orders[p][stage],))
        at = stage_base(stage) + slot
        return (
            remote(q_send.at[p, at], q_recv.at[p, at], sem_qs.at[p, at], sem_qr.at[p, at], row, c),
            remote(s_send.at[p, at], s_recv.at[p, at], sem_ss.at[p, at], sem_sr.at[p, at], row, c),
        )

    def send_stage(p, stage, number, mask, col):
        bit = plan.orders[p][stage]
        index = local_index(mask + (bit,), col)
        slot = number * nc + col
        at = stage_base(stage) + slot
        encode(index, p, q_send.at[p, at], s_send.at[p, at])
        for copy in hop(p, stage, slot):
            copy.start()

    def take_stage(p, stage, number, mask, col):
        slot = number * nc + col
        for copy in hop(p, stage, slot):
            copy.wait_recv()
        at = stage_base(stage) + slot
        decode(local_index(mask, col), p, q_recv.at[p, at], s_recv.at[p, at])

    def free_masks(p, stage):
        rest = plan.orders[p][stage + 1 :]
        found = bit_masks(rest)
        if rest:
            found = [m for m in found if rest[0] in m] + [m for m in found if rest[0] not in m]
        return found

    def far_copy(p, d):
        col = lax.rem(c + d, nc)
        return (
            remote(z_send.at[p, d - 1], z_recv.at[p, d - 1], sem_zs.at[p, d - 1], sem_zr.at[p, d - 1], r, col),
            remote(zs_send.at[p, d - 1], zs_recv.at[p, d - 1], sem_zss.at[p, d - 1], sem_zsr.at[p, d - 1], r, col),
        )

    def join(t):
        d = column_of(t)
        col = lax.rem(c + d, nc)
        for mask in masks:
            index = local_index(mask, col)
            near_copy(mask, col).wait_recv()
            load_copy(mask, col).wait()

            def body(b, inner, index=index):
                at = pl.ds(pl.multiple_of(b * plan.block, plan.block), plan.block)
                acc[index, at, :] += near[index, at, :]
                return inner

            lax.fori_loop(0, 2 * plan.blocks, body, 0)
            for p in range(2):
                bit = plan.orders[p][0]
                if bit in mask:
                    rest = tuple(b for b in mask if b != bit)
                    options = free_masks(p, 0)
                    number = [sorted(o) for o in options].index(sorted(rest))
                    send_stage(p, 0, number, rest, col)

    def take(stage, t):
        d = column_of(t)
        col = lax.rem(c + d, nc)
        for number in range(1 << (plan.stages - 1 - stage)):
            for p in range(2):
                mask = free_masks(p, stage)[number]
                take_stage(p, stage, number, mask, col)
                if stage + 1 < plan.stages:
                    bit = plan.orders[p][stage + 1]
                    if bit in mask:
                        rest = tuple(b for b in mask if b != bit)
                        options = free_masks(p, stage + 1)
                        following = [sorted(o) for o in options].index(sorted(rest))
                        send_stage(p, stage + 1, following, rest, col)
                else:
                    @pl.when(d < nc)
                    def _(p=p):
                        encode(local_index((), col), p, z_send.at[p, d - 1], zs_send.at[p, d - 1])
                        for copy in far_copy(p, d):
                            copy.start()

    mine = local_index((), c)

    def gather_far(d, carry):
        for p in range(2):
            for copy in far_copy(p, d):
                copy.wait_recv()
            decode(mine, p, z_recv.at[p, d - 1], zs_recv.at[p, d - 1])
        return carry


    def turn_of(t, carry):
        @pl.when(t <= nc)
        def _():
            join(t)

        for stage in range(plan.stages):
            d = t - 1 - stage

            @pl.when((d >= 1) & (d <= nc))
            def _(stage=stage, d=d):
                take(stage, d)

        @pl.when((t > nc) & (t - nc < nc))
        def _():
            gather_far(column_of(t - nc), 0)

        return carry

    lax.fori_loop(1, nc + plan.stages + 1, turn_of, 0)

    def gather_rest(q, carry):
        return gather_far(column_of(q), carry)

    lax.fori_loop(min(plan.stages + 1, nc), nc, gather_rest, 0)

    offset = lax.rem(share * me, 8)
    low_end, high_end = share * me * LANES, share * (me + 1) * LANES
    for number, (shift_rows, shift_lanes, begin, end) in enumerate(SHIFTS):
        def turn(b, carry, number=number, shift_lanes=shift_lanes):
            at = pl.ds(pl.multiple_of(b * plan.block, plan.block), plan.block)
            rolled[number, at, :] = pltpu.roll(acc[mine, at, :], LANES - shift_lanes, 1)
            return carry

        @pl.when((low_end < end) & (high_end > begin))
        def _(turn=turn):
            lax.fori_loop(0, 2 * plan.blocks, turn, 0)

    def share_rows(start, length, chosen):
        lane = lax.broadcasted_iota(jnp.int32, (length, LANES), 1)
        out = jnp.zeros((length, LANES), jnp.float32)
        if len(chosen) > 1:
            line = lax.broadcasted_iota(jnp.int32, (length, LANES), 0)
            flat = (share * me + start + line) * LANES + lane
        for number in chosen:
            shift_rows, shift_lanes, begin, end = SHIFTS[number]
            here = rolled[number, pl.ds(offset + start + shift_rows, length), :]
            after = rolled[number, pl.ds(offset + start + shift_rows + 1, length), :]
            value = jnp.where(lane < LANES - shift_lanes, here, after)
            if len(chosen) > 1:
                value = jnp.where((flat >= begin) & (flat < end), value, out)
            out = value
        return out

    chunk = 32
    whole, tail = share // chunk, share % chunk
    stats[me, 8:16, :] = extra[...]

    def squares(chosen):
        def square(b, total):
            start = pl.multiple_of(b * chunk, chunk)
            value = share_rows(start, chunk, chosen)
            step[pl.ds(start, chunk), :] = value
            return total + jnp.sum((value * value).reshape(chunk // 8, 8, LANES), axis=0)

        total = lax.fori_loop(0, whole, square, jnp.zeros((8, LANES), jnp.float32))
        stats[me, 0:8, :] = total
        if tail:
            value = share_rows(whole * chunk, tail, chosen)
            step[whole * chunk : share, :] = value
            stats[me, 0:1, :] += jnp.sum(value * value, axis=0, keepdims=True)

    largest = max(range(len(SHIFTS)), key=lambda i: SHIFTS[i][3] - SHIFTS[i][2])
    alone = (low_end >= SHIFTS[largest][2]) & (high_end <= SHIFTS[largest][3])

    @pl.when(alone)
    def _():
        squares((largest,))

    @pl.when(jnp.logical_not(alone))
    def _():
        squares(tuple(range(len(SHIFTS))))

    def stat_copy(target, source):
        return remote(
            stats.at[me], stats.at[me], sem_ts.at[target], sem_tr.at[me], target // nc, target % nc
        )

    def stat_wait(source):
        return remote(
            stats.at[source], stats.at[source], sem_ts.at[source], sem_tr.at[source],
            source // nc, source % nc,
        )

    def send_stat(d, carry):
        stat_copy(lax.rem(me + d, n), me).start()
        return carry

    lax.fori_loop(1, n, send_stat, 0)

    def wait_stat(d, carry):
        stat_wait(lax.rem(me + d, n)).wait_recv()
        return carry

    lax.fori_loop(1, n, wait_stat, 0)

    def add_stat(k, total):
        return total + stats[k]

    sums = lax.fori_loop(0, n, add_stat, jnp.zeros((16, LANES), jnp.float32))
    norm = jnp.sqrt(jnp.sum(sums[0:8], keepdims=True))
    totals[0:1, :] = jnp.broadcast_to(jnp.sum(sums[8:9], keepdims=True), (1, LANES))
    totals[1:2, :] = jnp.broadcast_to(jnp.sum(sums[9:10], keepdims=True), (1, LANES))
    totals[2:8, :] = jnp.zeros((6, LANES), jnp.float32)
    totals[8:16, :] = jnp.broadcast_to(norm, (8, LANES))
    clip = jnp.minimum(1.0, clip_limit / norm)

    def update(start, length):
        clipped = step[pl.ds(start, length), :] * clip
        one = decay_first * m_first[pl.ds(start, length), :] + (1.0 - decay_first) * clipped
        two = decay_second * m_second[pl.ds(start, length), :] + (1.0 - decay_second) * clipped * clipped
        first[pl.ds(start, length), :] = one
        second[pl.ds(start, length), :] = two
        step[pl.ds(start, length), :] = (
            one / (1.0 - decay_first**STEP) / (jnp.sqrt(two / (1.0 - decay_second**STEP)) + epsilon)
        )

    def update_chunk(b, carry):
        update(pl.multiple_of(b * chunk, chunk), chunk)
        return carry

    lax.fori_loop(0, whole, update_chunk, 0)
    if tail:
        update(whole * chunk, tail)
    if plan.padded > share:
        step[share : plan.padded, :] = jnp.zeros((plan.padded - share, LANES), jnp.float32)

    def narrow(b, carry):
        at = pl.ds(pl.multiple_of(b * 16, 16), 16)
        low[at, :] = step[at, :].astype(jnp.bfloat16)
        return carry

    lax.fori_loop(0, plan.padded // 16, narrow, 0)

    own = pltpu.make_async_copy(low, full.at[me], sem_own)
    own.start()
    own.wait()

    back = [list(reversed(order)) for order in plan.orders]

    def piece(mask, col, p):
        begin, length = plan.cuts[p]
        return full.at[flipped(mask) * nc + col, pl.ds(begin, length)]

    def along(direction, col, p, receive):
        step_col = 1 if direction == 0 else -1
        target = c - step_col if receive else c + step_col
        ref = piece((), col, p)
        return remote(ref, ref, sem_gs.at[direction, col, p], sem_gr.at[direction, col, p], r, target)

    def gather_masks(p, stage):
        return bit_masks(back[p][:stage])

    def gather_base(stage):
        return sum(1 << s for s in range(stage)) * nc

    def across(p, stage, number, mask, col):
        at = gather_base(stage) + number * nc + col
        ref = piece(mask, col, p)
        return remote(ref, ref, sem_hs.at[p, at], sem_hr.at[p, at], flipped((back[p][stage],)), c)

    def across_recv(p, stage, number, mask, col):
        at = gather_base(stage) + number * nc + col
        ref = piece(mask + (back[p][stage],), col, p)
        return remote(ref, ref, sem_hs.at[p, at], sem_hr.at[p, at], flipped((back[p][stage],)), c)

    def inward(p, mask, col):
        number = masks.index(tuple(sorted(mask)))
        at = number * nc + col
        ref = piece(mask, col, p)
        return remote(ref, ref, sem_cs.at[p, at], sem_cr.at[p, at], flipped((0,)), c)

    def inward_recv(p, mask, col):
        number = masks.index(tuple(sorted(mask)))
        at = number * nc + col
        ref = piece(mask + (0,), col, p)
        return remote(ref, ref, sem_cs.at[p, at], sem_cr.at[p, at], flipped((0,)), c)

    def spread(p, mask, col, stage):
        for later in range(stage, plan.stages):
            options = [sorted(o) for o in gather_masks(p, later)]
            if sorted(mask) in options:
                across(p, later, options.index(sorted(mask)), mask, col).start()
        inward(p, mask, col).start()

    def near_cols(t):
        if t == 0:
            return [(0, c)]
        return [(0, c - t), (1, c + t)]

    def inside(col):
        return (col >= 0) & (col < nc)

    for time in range(nc + plan.stages):
        for stage in range(plan.stages + 1):
            t = time - stage
            if not 0 <= t < nc:
                continue
            if stage == 0:
                if t == 0:
                    for p in range(2):
                        @pl.when(c < nc - 1)
                        def _(p=p):
                            along(0, c, p, False).start()

                        @pl.when(c > 0)
                        def _(p=p):
                            along(1, c, p, False).start()

                        spread(p, (), c, 0)
                else:
                    for direction, col in near_cols(t):
                        @pl.when(inside(col))
                        def _(direction=direction, col=col):
                            for p in range(2):
                                along(direction, col, p, True).wait_recv()
                                if direction == 0:
                                    @pl.when(c < nc - 1)
                                    def _():
                                        along(0, col, p, False).start()
                                else:
                                    @pl.when(c > 0)
                                    def _():
                                        along(1, col, p, False).start()
                                spread(p, (), col, 0)
            else:
                for direction, col in near_cols(t):
                    @pl.when(inside(col))
                    def _(col=col, stage=stage):
                        for number in range(1 << (stage - 1)):
                            for p in range(2):
                                mask = gather_masks(p, stage - 1)[number]
                                across_recv(p, stage - 1, number, mask, col).wait_recv()
                                spread(p, mask + (back[p][stage - 1],), col, stage)

    for mask in masks:
        def finish(col, carry, mask=mask):
            for p in range(2):
                inward_recv(p, mask, col).wait_recv()
                inward(p, mask, col).wait_send()
            near_copy(mask, col).wait_send()
            return carry

        lax.fori_loop(0, nc, finish, 0)
    for p in range(2):
        for stage in range(plan.stages):
            for number, mask in enumerate(gather_masks(p, stage)):
                def sent(col, carry, p=p, stage=stage, number=number, mask=mask):
                    across(p, stage, number, mask, col).wait_send()
                    return carry

                lax.fori_loop(0, nc, sent, 0)
            for number in range(1 << (plan.stages - 1 - stage)):
                def left(col, carry, p=p, stage=stage, number=number):
                    for copy in hop(p, stage, number * nc + col):
                        copy.wait_send()
                    return carry

                lax.fori_loop(0, nc, left, 0)

        def gone(col, carry, p=p):
            @pl.when((col <= c) & (c < nc - 1))
            def _():
                along(0, col, p, False).wait_send()

            @pl.when((col >= c) & (c > 0))
            def _():
                along(1, col, p, False).wait_send()

            return carry

        lax.fori_loop(0, nc, gone, 0)

        def far_gone(d, carry, p=p):
            for copy in far_copy(p, d):
                copy.wait_send()
            return carry

        lax.fori_loop(1, nc, far_gone, 0)

    def stat_gone(d, carry):
        stat_copy(lax.rem(me + d, n), me).wait_send()
        return carry

    lax.fori_loop(1, n, stat_gone, 0)


def exchange(rows, cols, grad, m_first, m_second, extra):
    plan = Plan(rows, cols, m_first.size * rows * cols)
    n, nc, share = plan.count, plan.cols, plan.share
    hops = sum(1 << s for s in range(plan.stages)) * nc
    dma = pltpu.SemaphoreType.DMA
    far = max(nc - 1, 1)
    vmem = pl.BlockSpec(memory_space=pltpu.VMEM)
    hbm = pl.BlockSpec(memory_space=pl.ANY)
    return plan, pl.pallas_call(
        functools.partial(exchange_kernel, plan),
        out_shape=(
            jax.ShapeDtypeStruct((n, plan.padded, LANES), jnp.bfloat16),
            jax.ShapeDtypeStruct((share, LANES), jnp.float32),
            jax.ShapeDtypeStruct((share, LANES), jnp.float32),
            jax.ShapeDtypeStruct((16, LANES), jnp.float32),
        ),
        in_specs=[hbm, vmem, vmem, vmem],
        out_specs=(hbm, vmem, vmem, vmem),
        scratch_shapes=[
            pltpu.VMEM((plan.local, plan.window, LANES), jnp.float32),
            pltpu.VMEM((plan.local, plan.window, LANES), jnp.float32),
            pltpu.VMEM((2, hops, plan.part, LANES), jnp.int16),
            pltpu.VMEM((2, hops, plan.part, LANES), jnp.int16),
            pltpu.VMEM((2, hops, plan.scales, LANES), jnp.float32),
            pltpu.VMEM((2, hops, plan.scales, LANES), jnp.float32),
            pltpu.VMEM((2, far, plan.part, LANES), jnp.int16),
            pltpu.VMEM((2, far, plan.part, LANES), jnp.int16),
            pltpu.VMEM((2, far, plan.scales, LANES), jnp.float32),
            pltpu.VMEM((2, far, plan.scales, LANES), jnp.float32),
            pltpu.VMEM((len(SHIFTS), plan.window, LANES), jnp.float32),
            pltpu.VMEM((plan.padded, LANES), jnp.float32),
            pltpu.VMEM((plan.padded, LANES), jnp.bfloat16),
            pltpu.VMEM((n, 16, LANES), jnp.float32),
            dma((plan.local,)), dma((plan.local,)), dma((plan.local,)),
            dma((2, hops)), dma((2, hops)), dma((2, hops)), dma((2, hops)),
            dma((2, far)), dma((2, far)), dma((2, far)), dma((2, far)),
            dma((n,)), dma((n,)), dma,
            dma((2, nc, 2)), dma((2, nc, 2)),
            dma((2, hops)), dma((2, hops)),
            dma((2, plan.local)), dma((2, plan.local)),
        ],
        compiler_params=pltpu.CompilerParams(
            collective_id=0, has_side_effects=True, vmem_limit_bytes=56 << 20
        ),
    )(grad, m_first.reshape(share, LANES), m_second.reshape(share, LANES), extra)


WIDE = CH + LANES
KEPT = ((8, 1104), (6096, 6408), (51400, 51584))
PLACES = tuple(divmod(FLAT_AT[i], LANES) for i in (3, 4, 5, 1))

SLOTS = 4
HALF = WIDE // 2
PITCH = 33


def unpack_kernel(
    plan, gathered, old_up, old_down, narrow, wide, hidden_out, rows_out, up_out, down_out, small_a, small_b, small_c,
    held, flat, woven, hidden, by_row, rows_low, up, down, sems, sem_out,
):
    n, share = plan.count, plan.share
    step = CH // LANES

    def fetch(k, slot):
        return pltpu.make_async_copy(gathered.at[k], held.at[slot], sems.at[slot])

    for k in range(SLOTS - 1):
        fetch(k, k).start()

    def widen(k, carry):
        slot = lax.rem(k, SLOTS)

        @pl.when(k + SLOTS - 1 < n)
        def _():
            fetch(k + SLOTS - 1, lax.rem(k + SLOTS - 1, SLOTS)).start()

        fetch(k, slot).wait()

        def body(b, inner):
            at = pl.ds(pl.multiple_of(b * 16, 16), 16)
            flat[pl.ds(share * k + b * 16, 16), :] = held[slot, at, :].astype(jnp.float32)
            return inner

        lax.fori_loop(0, plan.padded // 16, body, 0, unroll=4)
        return carry

    lax.fori_loop(0, n, widen, 0)

    copies = [
        pltpu.make_async_copy(source, target, sem_out.at[i])
        for i, (source, target) in enumerate(
            (
                (hidden, hidden_out.at[:, pl.ds(0, HALF)]), (rows_low, rows_out), (up, up_out),
                (down, down_out), (hidden, hidden_out.at[:, pl.ds(HALF, HALF)]),
            )
        )
    ]
    row, lane = PLACES[0]

    def spread(a, carry):
        by_row[pl.ds(narrow[a] * PITCH, 32), :] = flat[pl.ds(row + a * step, 32), :]
        return carry

    lax.fori_loop(0, C1, spread, 0, unroll=4)

    def columns(half):
        def column(t, carry):
            for begin in range(0, C1, 160):
                at = begin * PITCH + half * (HALF // LANES) + t
                values = by_row[pl.ds(at, 160, stride=PITCH), :]
                at = pl.ds(pl.multiple_of(t * LANES, LANES), LANES)
                hidden[begin : begin + 160, at] = values.astype(jnp.bfloat16)
            return carry

        lax.fori_loop(0, HALF // LANES, column, 0)

    columns(0)
    copies[0].start()

    quarter = C1 // 4
    for number, (ref, old, (line, begin)) in enumerate(zip((up, down), (old_up, old_down), PLACES[2:])):
        for u in range(-(-C1 // LANES)):
            width = min(LANES, C1 - u * LANES)
            place = lax.broadcasted_iota(jnp.int32, (quarter, LANES), 1)
            for b in range(4):
                first, rest = divmod(C1 * b + begin, LANES)
                here = flat[pl.ds(line + first + u, quarter, stride=step), :]
                after = flat[pl.ds(line + first + u + 1, quarter, stride=step), :]
                value = pltpu.roll(jnp.where(place >= rest, here, after), LANES - rest, 1)
                woven[pl.ds(b, quarter, stride=4), :] = value
            at = slice(u * LANES, u * LANES + width)
            ref[:, at] = moved(old[:, at], woven[:, :width])
        copies[2 + number].start()

    for ref, (begin, end) in zip((small_a, small_b, small_c), KEPT):
        ref[...] = flat[begin:end, :]
    copies[0].wait()
    columns(1)
    copies[4].start()

    row, lane = PLACES[1]

    def align(part, carry):
        place = lax.broadcasted_iota(jnp.int32, (40, LANES), 1)
        for b in range(4):
            first, rest = divmod(C1 * b + lane, LANES)
            values = []
            for u in range(-(-C1 // LANES)):
                at = row + part * (40 * step) + first + u
                here = flat[pl.ds(at, 40, stride=step), :]
                after = flat[pl.ds(at + 1, 40, stride=step), :]
                values.append(pltpu.roll(jnp.where(place >= rest, here, after), LANES - rest, 1))
            for u, value in enumerate(values):
                flat[pl.ds(part * (40 * PITCH) + b * 8 + u, 40, stride=PITCH), :] = value
        return carry

    lax.fori_loop(0, C1 // 40, align, 0)

    def scatter(a, carry):
        for b in range(4):
            by_row[pl.ds(wide[a * 4 + b] * 9, 8), :] = flat[pl.ds(a * PITCH + b * 8, 8), :]
        return carry

    lax.fori_loop(0, CH // 4, scatter, 0, unroll=4)

    def by_lane(part, carry):
        for u in range(C1P // LANES):
            values = by_row[pl.ds(part * (160 * 9) + u, 160, stride=9), :]
            at = pl.ds(pl.multiple_of(part * 160, 160), 160)
            rows_low[at, u * LANES : (u + 1) * LANES] = values.astype(jnp.bfloat16)
        return carry

    lax.fori_loop(0, CH // 160, by_lane, 0)
    copies[1].start()
    for copy in copies[1:]:
        copy.wait()


def unpack(plan, gathered, old_up, old_down, narrow, wide):
    lines = PADDED // LANES
    vmem = pl.BlockSpec(memory_space=pltpu.VMEM)
    hbm = pl.BlockSpec(memory_space=pl.ANY)
    dma = pltpu.SemaphoreType.DMA
    f32, low = jnp.float32, jnp.bfloat16
    return pl.pallas_call(
        functools.partial(unpack_kernel, plan),
        out_shape=(
            jax.ShapeDtypeStruct((C1, WIDE), low),
            jax.ShapeDtypeStruct((CH, C1P), low),
            jax.ShapeDtypeStruct((C1, C1), f32),
            jax.ShapeDtypeStruct((C1, C1), f32),
        )
        + tuple(jax.ShapeDtypeStruct((end - begin, LANES), f32) for begin, end in KEPT),
        in_specs=[hbm, vmem, vmem] + [pl.BlockSpec(memory_space=pltpu.SMEM)] * 2,
        out_specs=(hbm, hbm, hbm, hbm, vmem, vmem, vmem),
        scratch_shapes=[
            pltpu.VMEM((SLOTS, plan.padded, LANES), low),
            pltpu.VMEM((-(-lines // 8) * 8 + 16, LANES), f32),
            pltpu.VMEM((C1, LANES), f32),
            pltpu.VMEM((C1, HALF), low),
            pltpu.VMEM((CH * 9, LANES), f32),
            pltpu.VMEM((CH, C1P), low),
            pltpu.VMEM((C1, C1), f32),
            pltpu.VMEM((C1, C1), f32),
            dma((SLOTS,)),
            dma((5,)),
        ],
        compiler_params=pltpu.CompilerParams(vmem_limit_bytes=63 << 20),
    )(gathered, old_up, old_down, narrow, wide)


def moved(old, direction):
    return old.astype(jnp.float32) * (1.0 - learn_rate * weight_decay) - learn_rate * direction


def one_hot(condition):
    return jnp.where(condition, 1.0, 0.0).astype(jnp.bfloat16)


def product(left, right):
    return jnp.dot(left, right, preferred_element_type=jnp.float32)


def product_t(left, right):
    return lax.dot_general(left, right, (((1,), (1,)), ((), ())), preferred_element_type=jnp.float32)


TILE = 640


DEEP = 256


def hidden_kernel(lines, wide, old, new):
    depth = lines.shape[1]
    base = pl.program_id(0) * TILE
    direction = None
    for begin in range(0, depth, DEEP):
        end = min(begin + DEEP, depth)
        place = wide[begin:end, :] - base
        lane = lax.broadcasted_iota(jnp.int32, (end - begin, LANES), 1)
        hot = jnp.concatenate([one_hot(lane + u == place) for u in range(0, TILE, LANES)], axis=1)
        term = product(lines[:, begin:end], hot)
        direction = term if direction is None else direction + term
    new[...] = moved(old[...], direction)


def rebuild_hidden(lines, wide, old):
    lane = PLACES[0][1]
    wide = jnp.full((WIDE,), -1, jnp.int32).at[lane : lane + CH].set(wide)
    return pl.pallas_call(
        hidden_kernel,
        out_shape=jax.ShapeDtypeStruct((C1, CH), jnp.float32),
        grid=(CH // TILE,),
        in_specs=[
            pl.BlockSpec((C1, WIDE), lambda i: (0, 0)),
            pl.BlockSpec((WIDE, LANES), lambda i: (0, 0)),
            pl.BlockSpec((C1, TILE), lambda i: (0, i)),
        ],
        out_specs=pl.BlockSpec((C1, TILE), lambda i: (0, i)),
        compiler_params=pltpu.CompilerParams(vmem_limit_bytes=48 << 20),
    )(lines, jnp.broadcast_to(wide[:, None], (WIDE, LANES)), old)


def out_kernel(rows, narrow, old, new, turn):
    @pl.when(pl.program_id(0) == 0)
    def _():
        turn[...] = one_hot(lax.broadcasted_iota(jnp.int32, (C1, C1), 0) == narrow[...])

    new[...] = moved(old[...], product_t(turn[...], rows[:, :C1]))


def rebuild_out(rows, narrow, old):
    return pl.pallas_call(
        out_kernel,
        out_shape=jax.ShapeDtypeStruct((C1, CH), jnp.float32),
        grid=(CH // TILE,),
        in_specs=[
            pl.BlockSpec((TILE, C1P), lambda i: (i, 0)),
            pl.BlockSpec((1, C1), lambda i: (0, 0)),
            pl.BlockSpec((C1, TILE), lambda i: (0, i)),
        ],
        out_specs=pl.BlockSpec((C1, TILE), lambda i: (0, i)),
        scratch_shapes=[pltpu.VMEM((C1, C1), jnp.bfloat16)],
        compiler_params=pltpu.CompilerParams(vmem_limit_bytes=48 << 20),
    )(rows, narrow[None, :], old.T).T


def weave(source, rows, put):
    for t in range(CH // LANES):
        b, begin = divmod(t * LANES, C1)
        u, rest = divmod(begin, LANES)
        place = lax.broadcasted_iota(jnp.int32, (rows, LANES), 1)
        value = source[u, pl.ds(b, rows, stride=4), :]
        if rest:
            if begin + LANES - rest < C1:
                after = source[u + 1, pl.ds(b, rows, stride=4), :]
                value = jnp.where(place >= rest, value, after)
            value = pltpu.roll(value, LANES - rest, 1)
        left = C1 - begin
        if left < LANES:
            following = source[0, pl.ds(b + 1, rows, stride=4), :]
            value = jnp.where(place < left, value, pltpu.roll(following, left, 1))
        put(t, value)


def place_kernel(
    nr, nc, normed, branch, pre, act, narrow_row, narrow_col, wide, up, cells,
    grad, padded, hidden, out, loose, up_rows, norm_t, branch_r, halo_cells,
    sem_out, sems, sem_halo_s, sem_halo_r,
):
    step = pl.program_id(0)
    steps = pl.num_programs(0)
    ratio = CH // LANES
    lines = TILE // 4
    tiles = TILE // LANES

    def out_copy(n):
        rows = lines * ratio
        return pltpu.make_async_copy(
            out.at[pl.ds(pl.multiple_of(n * rows, 8), rows)],
            grad.at[pl.ds(pl.multiple_of(ROW_AT[4] + n * rows, 8), rows)],
            sem_out.at[n],
        )

    copies = [
        pltpu.make_async_copy(ref, grad.at[pl.ds(row, ref.shape[0])], sems.at[i])
        for i, (ref, row) in enumerate(((up_rows, ROW_AT[5]), (hidden, ROW_AT[3])))
    ] + [pltpu.make_async_copy(halo_cells, padded, sems.at[2])]

    @pl.when(step == 0)
    def _():
        halo_start(nr, nc, 3, cells, halo_cells, sem_halo_s, sem_halo_r)
        line = lax.broadcasted_iota(jnp.int32, (C1, C1), 1)
        norm_t[...] = product_t(one_hot(line == narrow_col[:, 0:1]), normed[:, :C1]).astype(jnp.bfloat16)
        line = lax.broadcasted_iota(jnp.int32, (C1, C1P), 0)
        branch_r[...] = product(branch[:, :C1], one_hot(line == narrow_row[...])).astype(jnp.bfloat16)
        for u in range(-(-C1 // LANES)):
            width = min(LANES, C1 - u * LANES)
            loose[u, :, 0:width] = up[0:C1, u * LANES : u * LANES + width]

        def put(t, value):
            up_rows[pl.ds(t, C1 // 4, stride=ratio), :] = value

        weave(loose, C1 // 4, put)
        copies[0].start()

    turned_pre = turned_act = None
    for begin in range(0, CH, DEEP):
        end = min(begin + DEEP, CH)
        line = lax.broadcasted_iota(jnp.int32, (end - begin, TILE), 0) + begin
        hot = one_hot(line == wide[...])
        one = product(pre[:, begin:end], hot)
        two = product(act[:, begin:end], hot)
        turned_pre = one if turned_pre is None else turned_pre + one
        turned_act = two if turned_act is None else turned_act + two
    part = product(norm_t[...], turned_pre.astype(jnp.bfloat16))
    for t in range(tiles):
        hidden[pl.ds(step * tiles + t, C1, stride=ratio), :] = part[:, t * LANES : (t + 1) * LANES]
    part = inner_rows(turned_act.astype(jnp.bfloat16), branch_r[...])
    for u in range(-(-C1 // LANES)):
        loose[u, 0:TILE, :] = part[:, u * LANES : (u + 1) * LANES]

    def put_out(t, value):
        out[pl.ds(step * (lines * ratio) + t, lines, stride=ratio), :] = value

    weave(loose, lines, put_out)
    out_copy(step).start()

    @pl.when(step == steps - 1)
    def _():
        copies[1].start()
        halo_finish(nr, nc, 3, cells, halo_cells, sem_halo_s, sem_halo_r)
        copies[2].start()

        def finish(n, carry):
            out_copy(n).wait()
            return carry

        lax.fori_loop(0, steps, finish, 0)
        for copy in copies:
            copy.wait()


def place_gradients(nr, nc, space, normed, branch, pre, act, narrow, wide, up, cells):
    def whole(array):
        return pl.BlockSpec(
            array.shape, lambda i: (0,) * len(array.shape), pipeline_mode=pl.Buffered(1)
        )

    hbm = pl.BlockSpec(memory_space=pl.ANY)
    rows = pre.shape[0]
    batch, height, breadth, chans = cells.shape
    narrow_row = jnp.pad(narrow, (0, C1P - C1), constant_values=-1)[None, :]
    narrow_col = jnp.broadcast_to(narrow[:, None], (C1, LANES))
    framed = jax.ShapeDtypeStruct((batch, height + 6, breadth + 2 * EDGE, chans), cells.dtype)
    dma = pltpu.SemaphoreType.DMA
    return pl.pallas_call(
        functools.partial(place_kernel, nr, nc),
        out_shape=(jax.ShapeDtypeStruct((space, LANES), jnp.float32), framed),
        grid=(CH // TILE,),
        in_specs=[
            whole(normed), whole(branch), whole(pre), whole(act), whole(narrow_row), whole(narrow_col),
            pl.BlockSpec((1, TILE), lambda i: (0, i)),
            whole(up), whole(cells),
        ],
        out_specs=(hbm, hbm),
        scratch_shapes=[
            pltpu.VMEM((C1 * CH // LANES, LANES), jnp.float32),
            pltpu.VMEM((C1 * CH // LANES, LANES), jnp.float32),
            pltpu.VMEM((C1P // LANES, C1, LANES), jnp.float32),
            pltpu.VMEM((C1 * C1 // LANES, LANES), jnp.float32),
            pltpu.VMEM((C1, rows), jnp.bfloat16),
            pltpu.VMEM((rows, C1P), jnp.bfloat16),
            pltpu.VMEM(framed.shape, framed.dtype),
            dma((CH // TILE,)), dma((3,)), dma((8,)), dma((8,)),
        ],
        compiler_params=pltpu.CompilerParams(
            collective_id=3, has_side_effects=True, vmem_limit_bytes=60 << 20
        ),
    )(normed, branch, pre, act, narrow_row, narrow_col, wide[None, :], up, cells)


def complete_kernel(before, down, piece_in, piece_dw, piece_head, piece_vec, grad, loose, down_rows, sems):
    copies = [
        pltpu.make_async_copy(ref, grad.at[pl.ds(row, ref.shape[0])], sems.at[i])
        for i, (ref, row) in enumerate(
            (
                (piece_in, 0), (piece_dw, ROW_AT[2]), (piece_head, ROW_AT[6]), (piece_vec, ROW_AT[7]),
                (down_rows, ROW_AT[1]),
            )
        )
    ]
    for copy in copies[:4]:
        copy.start()
    for u in range(C1P // LANES):
        loose[u] = down[:, u * LANES : (u + 1) * LANES]

    def put(t, value):
        down_rows[pl.ds(t, C1 // 4, stride=CH // LANES), :] = value

    weave(loose, C1 // 4, put)
    copies[4].start()
    for copy in copies:
        copy.wait()


def complete_gradients(grad, down, pieces):
    vmem = pl.BlockSpec(memory_space=pltpu.VMEM)
    hbm = pl.BlockSpec(memory_space=pl.ANY)
    return pl.pallas_call(
        complete_kernel,
        out_shape=jax.ShapeDtypeStruct(grad.shape, grad.dtype),
        in_specs=[hbm, vmem, vmem, vmem, vmem, vmem],
        out_specs=hbm,
        input_output_aliases={0: 0},
        scratch_shapes=[
            pltpu.VMEM((C1P // LANES, C1, LANES), jnp.float32),
            pltpu.VMEM((C1 * C1 // LANES, LANES), jnp.float32),
            pltpu.SemaphoreType.DMA((5,)),
        ],
        compiler_params=pltpu.CompilerParams(vmem_limit_bytes=60 << 20),
    )(grad, down, *pieces)


C0P = 256
C1P = 896
CIP = 128
EDGE = 16
CURVE = 0.7978845608028654
CUBE = 0.044715


def inner_rows(left, right):
    return lax.dot_general(left, right, (((0,), (0,)), ((), ())), preferred_element_type=jnp.float32)


def column_sum(values):
    return jnp.sum(values.astype(jnp.float32), axis=0, keepdims=True)


def gelu(t):
    return 0.5 * t * (1.0 + jnp.tanh(CURVE * (t + CUBE * (t * t * t))))


def gelu_slope(t):
    bend = jnp.tanh(CURVE * (t + CUBE * (t * t * t)))
    return 0.5 * (1.0 + bend) + 0.5 * t * (1.0 - bend * bend) * (CURVE * (1.0 + 3.0 * CUBE * (t * t)))


WAYS = [(dr, dc) for dr in (-1, 0, 1) for dc in (-1, 0, 1) if (dr, dc) != (0, 0)]
ORDER = sorted(range(8), key=lambda i: (WAYS[i][1] != 0, WAYS[i][0] == 0))


def halo_place(nr, nc):
    r = lax.axis_index("rows")
    return r, lax.axis_index("cols"), lambda dr: (r + dr >= 0) & (r + dr < nr)


def halo_copy(nr, nc, width, cells, out, sem_s, sem_r, i, receive):
    r, c, there = halo_place(nr, nc)
    height, breadth = cells.shape[1], cells.shape[2]
    dr, dc = WAYS[i]
    rows_from = {-1: (0, width), 0: (0, height), 1: (height - width, width)}[dr]
    rows_to = {-1: height + width, 0: width, 1: 0}[dr]
    cols_from = {-1: (0, EDGE), 0: (0, breadth), 1: (breadth - EDGE, EDGE)}[dc]
    cols_to = {-1: EDGE + breadth, 0: EDGE, 1: 0}[dc]
    sign = -1 if receive else 1
    return pltpu.make_async_remote_copy(
        src_ref=cells.at[:, pl.ds(*rows_from), pl.ds(*cols_from)],
        dst_ref=out.at[:, pl.ds(rows_to, rows_from[1]), pl.ds(cols_to, cols_from[1])],
        send_sem=sem_s.at[i],
        recv_sem=sem_r.at[i],
        device_id=(r + sign * dr, lax.rem(c + sign * dc + nc, nc)),
        device_id_type=MESH,
    )


def halo_start(nr, nc, width, cells, out, sem_s, sem_r):
    r, c, there = halo_place(nr, nc)
    height, breadth = cells.shape[1], cells.shape[2]
    barrier = pltpu.get_barrier_semaphore()
    for dr, dc in WAYS:
        @pl.when(there(dr))
        def _(dr=dr, dc=dc):
            pl.semaphore_signal(
                barrier, inc=1, device_id=(r + dr, lax.rem(c + dc + nc, nc)), device_id_type=MESH
            )

    edge = (r == 0) | (r == nr - 1)

    @pl.when(edge)
    def _():
        pl.semaphore_wait(barrier, 5)

    @pl.when(jnp.logical_not(edge))
    def _():
        pl.semaphore_wait(barrier, 8)

    for i in ORDER:
        @pl.when(there(WAYS[i][0]))
        def _(i=i):
            halo_copy(nr, nc, width, cells, out, sem_s, sem_r, i, False).start()

    for m in range(cells.shape[0]):
        for row in range(height):
            out[m, width + row, EDGE : EDGE + breadth, :] = cells[m, row]

    @pl.when(r == 0)
    def _():
        out[:, 0:width] = jnp.zeros((out.shape[0], width) + out.shape[2:], out.dtype)

    @pl.when(r == nr - 1)
    def _():
        out[:, height + width :] = jnp.zeros((out.shape[0], width) + out.shape[2:], out.dtype)


def halo_finish(nr, nc, width, cells, out, sem_s, sem_r):
    r, c, there = halo_place(nr, nc)
    for i in ORDER:
        @pl.when(there(-WAYS[i][0]))
        def _(i=i):
            halo_copy(nr, nc, width, cells, out, sem_s, sem_r, i, True).wait_recv()

        @pl.when(there(WAYS[i][0]))
        def _(i=i):
            halo_copy(nr, nc, width, cells, out, sem_s, sem_r, i, False).wait_send()


def halo_kernel(nr, nc, width, cells, out, sem_s, sem_r):
    halo_start(nr, nc, width, cells, out, sem_s, sem_r)
    halo_finish(nr, nc, width, cells, out, sem_s, sem_r)


def halo(nr, nc, width, cells, identity):
    batch, height, breadth, chans = cells.shape
    vmem = pl.BlockSpec(memory_space=pltpu.VMEM)
    return pl.pallas_call(
        functools.partial(halo_kernel, nr, nc, width),
        out_shape=jax.ShapeDtypeStruct(
            (batch, height + 2 * width, breadth + 2 * EDGE, chans), cells.dtype
        ),
        in_specs=[vmem],
        out_specs=vmem,
        scratch_shapes=[pltpu.SemaphoreType.DMA((8,)), pltpu.SemaphoreType.DMA((8,))],
        compiler_params=pltpu.CompilerParams(
            collective_id=identity, has_side_effects=True, vmem_limit_bytes=24 << 20
        ),
    )(cells)


SIDE = 8
REACH = 3
FINE_REACH = 2 * REACH + 1


def input_kernel(
    nr, state, w_in, w_down, lines, taps, a_zero, h_zero, coarse, padded, wide, taps_all, coarse_all
):
    r = lax.axis_index("rows")
    batch, rows, breadth, _ = state.shape
    half_h, half_w = rows // 2 - FINE_REACH, breadth // 2 - EDGE
    all_h, all_w = half_h + 2 * REACH, half_w + 2 * SIDE
    for m in range(batch):
        for y in range(rows):
            wide[m, y, SIDE : SIDE + breadth, :] = state[m, y].astype(jnp.float32)
    for m in range(batch):
        for y in range(rows):
            for f in range(4):
                start = SIDE + EDGE - 2 * SIDE - 1 + f
                line = wide[m, y, pl.ds(start, all_w, stride=2), :]
                low = line.astype(jnp.bfloat16)
                inner = line[SIDE : SIDE + half_w].astype(jnp.bfloat16)
                for dy in range(3):
                    i, sy = divmod(y - dy, 2)
                    if not 0 <= i < all_h:
                        continue
                    for dx in range(3):
                        if not 0 <= f - dx < 2:
                            continue
                        s, tap = sy * 2 + f - dx, slice((dy * 3 + dx) * CIP, (dy * 3 + dx + 1) * CIP)
                        begin = (m * all_h + i) * all_w
                        taps_all[s, begin : begin + all_w, tap] = low
                        if REACH <= i < REACH + half_h:
                            begin = (m * half_h + i - REACH) * half_w
                            taps[s, begin : begin + half_w, tap] = inner
    size = all_h * all_w
    for m in range(batch):
        block = slice(m * size, (m + 1) * size)
        total = jnp.broadcast_to(lines[1:2, :C1P], (size, C1P))
        for s in range(4):
            value = product(taps_all[s, block, :], w_in[...]) + lines[0:1, :C0P]
            curved = gelu(value)
            for i in range(half_h):
                begin = (i + REACH) * all_w + SIDE
                at = slice((m * half_h + i) * half_w, (m * half_h + i + 1) * half_w)
                a_zero[s, at, :] = value[begin : begin + half_w]
                h_zero[s, at, :] = curved[begin : begin + half_w]
            total = total + product(curved.astype(jnp.bfloat16), w_down[s])
        coarse_all[...] = total
        for i in range(half_h):
            begin = (i + REACH) * all_w + SIDE
            at = slice((m * half_h + i) * half_w, (m * half_h + i + 1) * half_w)
            coarse[at, :] = coarse_all[begin : begin + half_w, :]
        padded[m] = coarse_all[...].astype(jnp.bfloat16).reshape(padded.shape[1:])

    @pl.when(r == 0)
    def _():
        padded[:, 0:REACH] = jnp.zeros((batch, REACH) + padded.shape[2:], padded.dtype)

    @pl.when(r == nr - 1)
    def _():
        padded[:, all_h - REACH :] = jnp.zeros((batch, REACH) + padded.shape[2:], padded.dtype)


def input_part(nr, state, w_in, w_down, lines):
    batch, rows, breadth, _ = state.shape
    half_h, half_w = rows // 2 - FINE_REACH, breadth // 2 - EDGE
    all_h, all_w = half_h + 2 * REACH, half_w + 2 * SIDE
    cells = batch * half_h * half_w
    vmem = pl.BlockSpec(memory_space=pltpu.VMEM)
    return pl.pallas_call(
        functools.partial(input_kernel, nr),
        out_shape=(
            jax.ShapeDtypeStruct((4, cells, 9 * CIP), jnp.bfloat16),
            jax.ShapeDtypeStruct((4, cells, C0P), jnp.float32),
            jax.ShapeDtypeStruct((4, cells, C0P), jnp.float32),
            jax.ShapeDtypeStruct((cells, C1P), jnp.float32),
            jax.ShapeDtypeStruct((batch, all_h, all_w, C1P), jnp.bfloat16),
        ),
        in_specs=[vmem] * 4,
        out_specs=tuple([vmem] * 5),
        scratch_shapes=[
            pltpu.VMEM((batch, rows, breadth + 2 * SIDE, CIP), jnp.float32),
            pltpu.VMEM((4, batch * all_h * all_w, 9 * CIP), jnp.bfloat16),
            pltpu.VMEM((all_h * all_w, C1P), jnp.float32),
        ],
        compiler_params=pltpu.CompilerParams(vmem_limit_bytes=56 << 20),
    )(state, w_in, w_down, lines)


def spread_lanes(padded, held):
    for m in range(padded.shape[0]):
        def body(y, carry, m=m):
            for u in range(C1P // LANES):
                held[u, m, y, 0 : padded.shape[2], :] = padded[m, y, :, u * LANES : (u + 1) * LANES].astype(jnp.float32)
            return carry

        lax.fori_loop(0, padded.shape[1], body, 0)


def convolve(held, w_dw, half_w, edge, put, back):
    tiles, batch, rows = held.shape[:3]
    height = rows - 2 * REACH

    def body(number, carry):
        u, m = number // batch, number % batch
        sums = [jnp.zeros((half_w, LANES), jnp.float32) for _ in range(height)]
        for x in range(7):
            for y in range(rows):
                window = held[u, m, y, pl.ds(edge - REACH + x, half_w), :]
                for i in range(height):
                    if 0 <= y - i < 7:
                        tap = (6 - (y - i)) * 7 + 6 - x if back else (y - i) * 7 + x
                        sums[i] = sums[i] + window * w_dw[pl.ds(tap, 1), lanes_at(u)]
        for i in range(height):
            put(u, m, i, sums[i])
        return carry

    lax.fori_loop(0, tiles * batch, body, 0)


def rows_at(m, i, height, half_w):
    return pl.ds(pl.multiple_of((m * height + i) * half_w, half_w), half_w)


def lanes_at(u):
    return pl.ds(pl.multiple_of(u * LANES, LANES), LANES)


PART = 640


LATE = ("coarse", "h_zero", "target", "weight", "w_hidden", "w_out_t", "w_up")
EARLY = ("normed", "act", "grad_mixed", "grad_branch", "grad_summed", "d_up")


def middle_kernel(names, *refs):
    ref = dict(zip(names, refs))
    batch, rows, breadth, _ = ref["padded"].shape
    cells = ref["coarse"].shape[0]
    height, half_w = rows - 2 * REACH, breadth - 2 * SIDE
    fetch, store, held_in, held_out = {}, {}, {}, {}
    for i, name in enumerate(LATE):
        held_in[name] = ref["held_" + name]
        fetch[name] = pltpu.make_async_copy(ref[name], held_in[name], ref["sem_in"].at[i])
        fetch[name].start()
    for i, name in enumerate(EARLY):
        held_out[name] = ref["held_" + name]
        store[name] = pltpu.make_async_copy(held_out[name], ref[name], ref["sem_out"].at[i])
    conv = ref["conv"]

    def depthwise(held):
        spread_lanes(ref["padded"], held)

        def put(u, m, i, value):
            conv[rows_at(m, i, height, half_w), lanes_at(u)] = value

        convolve(held, ref["w_dw"], half_w, SIDE, put, False)

    pl.run_scoped(depthwise, pltpu.VMEM((C1P // LANES, batch, rows, breadth, LANES), jnp.float32))
    pl.run_scoped(
        functools.partial(pointwise_part, ref, fetch, store, held_in, held_out),
        pltpu.VMEM((cells, CH), jnp.float32),
        pltpu.VMEM((cells, C1), jnp.bfloat16),
    )
    for name in EARLY:
        store[name].wait()


def pointwise_part(ref, fetch, store, held_in, held_out, pre, spread_all):
    conv, total, sums, extra = ref["conv"], ref["total"], ref["sums"], ref["extra"]
    gain, w_head = ref["lines"].at[3:4, 0:C1P], ref["w_head"]
    normed, act = held_out["normed"], held_out["act"]
    grad_mixed, grad_branch, grad_summed = (
        held_out[name] for name in ("grad_mixed", "grad_branch", "grad_summed")
    )
    w_hidden, w_out_t, w_up = (held_in[name] for name in ("w_hidden", "w_out_t", "w_up"))
    target, weight, h_zero = (held_in[name] for name in ("target", "weight", "h_zero"))
    batch, rows, breadth, _ = ref["padded"].shape
    height, half_w = rows - 2 * REACH, breadth - 2 * SIDE

    inside = lax.broadcasted_iota(jnp.int32, (1, C1P), 1) < C1
    values = conv[...] + ref["lines"][2:3, :C1P]
    mean = jnp.sum(values, axis=1, keepdims=True) * (1.0 / C1)
    centered = jnp.where(inside, values - mean, 0.0)
    scale = lax.rsqrt(jnp.sum(centered * centered, axis=1, keepdims=True) * (1.0 / C1) + 1e-06)
    conv[...] = centered * scale
    normed[...] = (conv[...] * gain[...] + ref["lines"][4:5, :C1P]).astype(jnp.bfloat16)
    store["normed"].start()

    fetch["coarse"].wait()
    fetch["w_hidden"].wait()
    fetch["w_out_t"].wait()
    total[...] = held_in["coarse"][...]
    for begin in range(0, CH, PART):
        span = slice(begin, begin + PART)
        value = product(normed[:, :C1], w_hidden[:, span]) + ref["lines"][5:6, span]
        pre[:, span] = value
        act[:, span] = gelu(value).astype(jnp.bfloat16)
        total[:, :C1] += product_t(act[:, span], w_out_t[:, span])
    store["act"].start()
    mixed = (total[...] + ref["lines"][6:7, :C1P]).astype(jnp.bfloat16)

    for name in ("h_zero", "target", "weight", "w_up"):
        fetch[name].wait()
    grad_mixed[...] = jnp.zeros_like(grad_mixed)
    loss = jnp.zeros((1, CI), jnp.float32)
    head_sum = jnp.zeros((1, CI), jnp.float32)
    up_sum = jnp.zeros((1, C0), jnp.float32)
    for s in range(4):
        sub_y, sub_x = divmod(s, 2)
        for m in range(batch):
            for i in range(height):
                at = rows_at(m, i, height, half_w)
                line = pl.ds(sub_x, half_w, stride=2)
                ref["goal"][at, :] = target[m, 2 * i + sub_y, line, :]
                ref["load"][at, :] = weight[2 * i + sub_y, line, :]
        w_up_s = w_up[:, s * C0 : (s + 1) * C0]
        upper = product(mixed[:, :C1], w_up_s) + ref["lines"][7:8, :C0]
        summed = (upper + h_zero[s, :, :C0]).astype(jnp.bfloat16)
        error = product(summed, w_head[...]) + ref["lines"][8:9, :CI] - ref["goal"][:, :CI]
        weighted = ref["load"][:, :CI] * error
        loss = loss + column_sum(weighted * error)
        grad_out = (2.0 * weighted).astype(jnp.bfloat16)
        head_sum = head_sum + column_sum(grad_out)
        if s == 0:
            ref["d_head"][...] = inner_rows(summed, grad_out)
        else:
            ref["d_head"][...] += inner_rows(summed, grad_out)
        spread = product_t(grad_out, w_head[...])
        grad_summed[s] = spread
        grad_upper = spread.astype(jnp.bfloat16)
        up_sum = up_sum + column_sum(grad_upper)
        spread_all[:, s * C0 : (s + 1) * C0] = grad_upper
        grad_mixed[:, :C1] += product_t(grad_upper, w_up_s)
    store["grad_summed"].start()
    store["grad_mixed"].start()
    held_out["d_up"][...] = inner_rows(mixed[:, :C1], spread_all[...])
    store["d_up"].start()
    grad_branch[...] = grad_mixed[...].astype(jnp.bfloat16)
    store["grad_branch"].start()
    sums[...] = jnp.zeros_like(sums)
    extra[...] = jnp.zeros_like(extra)
    extra[0:1, 0:CI] = loss
    extra[1:2, :] = column_sum(ref["weight_map"][...])
    sums[1:2, 0:CI] = head_sum
    sums[2:3, 0:C0] = up_sum
    sums[3:4, 0:C1P] = column_sum(grad_branch[...])

    total[...] = jnp.zeros_like(total)
    for begin in range(0, CH, PART):
        span = slice(begin, begin + PART)
        value = product(grad_branch[:, :C1], w_out_t[:, span]) * gelu_slope(pre[:, span])
        low = value.astype(jnp.bfloat16)
        ref["grad_pre"][:, span] = low
        sums[4:5, span] = column_sum(low)
        total[:, :C1] += product_t(low, w_hidden[:, span])

    grad_normed = total[...]
    sums[5:6, 0:C1P] = column_sum(grad_normed * conv[...])
    sums[6:7, 0:C1P] = column_sum(grad_normed)
    inward = grad_normed * gain[...]
    first = jnp.sum(inward, axis=1, keepdims=True) * (1.0 / C1)
    second = jnp.sum(inward * conv[...], axis=1, keepdims=True) * (1.0 / C1)
    value = scale * jnp.where(inside, inward - first - conv[...] * second, 0.0)
    low = value.astype(jnp.bfloat16)
    sums[7:8, 0:C1P] = column_sum(low)
    ref["grad_conv"][...] = low.reshape(ref["grad_conv"].shape)


def middle_part(**given):
    cells = given["coarse"].shape[0]
    batch, rows, breadth, _ = given["padded"].shape
    half_h, half_w = rows - 2 * REACH, breadth - 2 * SIDE
    vmem = pl.BlockSpec(memory_space=pltpu.VMEM)
    hbm = pl.BlockSpec(memory_space=pl.ANY)
    f32, low = jnp.float32, jnp.bfloat16
    outs = {
        "normed": ((cells, C1P), low),
        "act": ((cells, CH), low),
        "grad_pre": ((cells, CH), low),
        "grad_mixed": ((cells, C1P), f32),
        "grad_branch": ((cells, C1P), low),
        "grad_summed": ((4, cells, C0), f32),
        "grad_conv": ((batch, half_h, half_w, C1P), low),
        "d_up": ((C1, C1), f32),
        "d_head": ((C0, CI), f32),
        "sums": ((8, CH), f32),
        "extra": ((8, LANES), f32),
    }
    scratch = {
        "conv": pltpu.VMEM((cells, C1P), f32),
        "total": pltpu.VMEM((cells, C1P), f32),
        "goal": pltpu.VMEM((cells, LANES), f32),
        "load": pltpu.VMEM((cells, LANES), f32),
        "sem_in": pltpu.SemaphoreType.DMA((len(LATE),)),
        "sem_out": pltpu.SemaphoreType.DMA((len(EARLY),)),
    }
    for name in LATE:
        scratch["held_" + name] = pltpu.VMEM(given[name].shape, given[name].dtype)
    for name in EARLY:
        scratch["held_" + name] = pltpu.VMEM(*outs[name])
    found = pl.pallas_call(
        functools.partial(middle_kernel, tuple(given) + tuple(outs) + tuple(scratch)),
        out_shape=tuple(jax.ShapeDtypeStruct(*out) for out in outs.values()),
        in_specs=[hbm if name in LATE else vmem for name in given],
        out_specs=tuple(hbm if name in EARLY else vmem for name in outs),
        scratch_shapes=list(scratch.values()),
        compiler_params=pltpu.CompilerParams(vmem_limit_bytes=62 << 20),
    )(*given.values())
    return dict(zip(outs, found))


AFTER = ("grad_mixed", "grad_summed", "a_zero", "h_zero", "taps", "w_down")


def outer_kernel(names, *refs):
    ref = dict(zip(names, refs))
    fetch = {}
    for i, name in enumerate(AFTER):
        fetch[name] = pltpu.make_async_copy(ref[name], ref["held_" + name], ref["sem_in"].at[i])
        fetch[name].start()
    grad_mixed, grad_summed, a_zero, h_zero, taps, w_down = (ref["held_" + name] for name in AFTER)
    held, conv, sums, d_dw, d_in = (ref[name] for name in ("held", "conv", "sums", "d_dw", "d_in"))
    vector = ref["vector"]
    grad_conv = ref["grad_conv"]
    batch, height, half_w, _ = grad_conv.shape
    spread_lanes(ref["padded"], held)
    tiles = C1P // LANES
    d_dw[...] = jnp.zeros_like(d_dw)

    def taps_of(number, carry):
        u, m = number // batch, number % batch
        grads = [grad_conv[m, i, :, lanes_at(u)].astype(jnp.float32) for i in range(height)]
        for x in range(7):
            found = [jnp.zeros((8, LANES), jnp.float32) for _ in range(7)]
            for y in range(height + 6):
                window = held[u, m, y, pl.ds(SIDE - REACH + x, half_w), :]
                for i in range(height):
                    if 0 <= y - i < 7:
                        term = (window * grads[i]).reshape(half_w // 8, 8, LANES)
                        found[y - i] = found[y - i] + jnp.sum(term, axis=0)
            for dy in range(7):
                d_dw[pl.ds(dy * 7 + x, 1), lanes_at(u)] += jnp.sum(found[dy], axis=0, keepdims=True)
        return carry

    lax.fori_loop(0, tiles * batch, taps_of, 0)
    spread_lanes(ref["grad_padded"], held)

    def put(u, m, i, value):
        conv[rows_at(m, i, height, half_w), lanes_at(u)] = value

    convolve(held, ref["w_dw"], half_w, EDGE, put, True)
    for name in AFTER:
        fetch[name].wait()
    grad_coarse = (conv[...] + grad_mixed[...]).astype(jnp.bfloat16)
    vector[...] = jnp.zeros_like(vector)
    pieces = [(column_sum(grad_coarse), C1)] + [(sums[i : i + 1, :], C1) for i in (7, 5, 6)]
    pieces += [(sums[4:5, :], CH), (sums[3:4, :], C1), (sums[2:3, :], C0), (sums[1:2, :], CI)]
    start = C0
    for piece, size in pieces:
        vector[:, start : start + size] = piece[:, :size]
        start = start + size
    in_sum = jnp.zeros((1, C0), jnp.float32)
    for s in range(4):
        ref["d_down"][s * C0 : (s + 1) * C0, :] = inner_rows(
            h_zero[s].astype(jnp.bfloat16), grad_coarse
        )[:C0]
        grad_h = product_t(grad_coarse, w_down[s])[:, :C0] + grad_summed[s]
        grad_a = (gelu_slope(a_zero[s, :, :C0]) * grad_h).astype(jnp.bfloat16)
        in_sum = in_sum + column_sum(grad_a)
        if s == 0:
            d_in[...] = inner_rows(taps[s], grad_a)
        else:
            d_in[...] += inner_rows(taps[s], grad_a)
    vector[:, 0:C0] = in_sum


def outer_part(length, **given):
    cells = given["grad_mixed"].shape[0]
    batch, rows, breadth, _ = given["grad_padded"].shape
    vmem = pl.BlockSpec(memory_space=pltpu.VMEM)
    hbm = pl.BlockSpec(memory_space=pl.ANY)
    f32 = jnp.float32
    outs = {
        "d_dw": ((56, C1P), f32),
        "d_down": ((C1, C1P), f32),
        "d_in": ((9 * CIP, C0), f32),
        "vector": ((1, length), f32),
    }
    scratch = {
        "held": pltpu.VMEM((C1P // LANES, batch, rows, breadth, LANES), f32),
        "conv": pltpu.VMEM((cells, C1P), f32),
        "sem_in": pltpu.SemaphoreType.DMA((len(AFTER),)),
    }
    for name in AFTER:
        scratch["held_" + name] = pltpu.VMEM(given[name].shape, given[name].dtype)
    found = pl.pallas_call(
        functools.partial(outer_kernel, tuple(given) + tuple(outs) + tuple(scratch)),
        out_shape=tuple(jax.ShapeDtypeStruct(*out) for out in outs.values()),
        in_specs=[hbm if name in AFTER else vmem for name in given],
        out_specs=tuple([vmem] * len(outs)),
        scratch_shapes=list(scratch.values()),
        compiler_params=pltpu.CompilerParams(vmem_limit_bytes=60 << 20),
    )(*given.values())
    return dict(zip(outs, found))


def split_vector(vector):
    lengths = [C0, C1, C1, C1, C1, CH, C1, C0, CI]
    pieces = []
    start = 0
    for length in lengths:
        pieces.append(vector[start : start + length])
        start = start + length
    return pieces


def as_rows(piece, rows):
    flat = piece.reshape(-1)
    return jnp.pad(flat, (0, rows * LANES - flat.shape[0])).reshape(rows, LANES)


def widened(array, *shape):
    return jnp.pad(array, [(0, full - now) for full, now in zip(shape, array.shape)])


def on_device(
    inputs,
    targets,
    land_mask,
    volume,
    date_index,
    perm_narrow,
    perm_wide,
    w_in,
    w_down,
    w_dw,
    w_hidden,
    w_out,
    w_up,
    w_head,
    biases_gains,
    moment_first,
    moment_second,
):
    rows, cols = lax.axis_size("rows"), lax.axis_size("cols")
    weight = land_mask.astype(jnp.float32) * volume
    height, breadth = weight.shape
    half_h, half_w = (height // 2, breadth // 2)
    cells = MB * half_h * half_w
    matrices = (w_in, w_down, w_dw, w_hidden, w_out, w_up, w_head)

    def dates(field):
        picked = jnp.concatenate(
            [lax.dynamic_slice_in_dim(field, date_index[m], 1, 0, allow_negative_indices=False) for m in range(MB)]
        )
        return widened(picked, MB, height, breadth, CIP)

    lines = jnp.stack([widened(piece, CH) for piece in split_vector(biases_gains)])
    w_in_p = widened(w_in.reshape(9, CI, C0), 9, CIP, C0P).reshape(9 * CIP, C0P)
    w_down_p = widened(w_down.reshape(4, C0, C1), 4, C0P, C1P)
    w_dw_p = widened(w_dw.astype(jnp.float32), 56, C1P)
    weight_map = jnp.broadcast_to(weight[:, :, None], (height, breadth, LANES))

    state = halo(rows, cols, FINE_REACH, dates(inputs), 1)
    taps, a_zero, h_zero, coarse, padded = input_part(rows, state, w_in_p, w_down_p, lines)
    mid = middle_part(
        padded=padded, coarse=coarse, h_zero=h_zero, target=dates(targets).astype(jnp.float32),
        weight=weight_map, weight_map=weight, w_dw=w_dw_p, w_hidden=w_hidden, w_out_t=w_out.T,
        w_up=w_up, w_head=w_head, lines=lines,
    )
    space = Plan(rows, cols, PADDED).space
    grad, grad_padded = place_gradients(
        rows, cols, space, mid["normed"], mid["grad_branch"], mid["grad_pre"], mid["act"],
        perm_narrow, perm_wide, mid["d_up"], mid["grad_conv"],
    )
    out = outer_part(
        (space - ROW_AT[7]) * LANES,
        padded=padded, grad_padded=grad_padded, grad_conv=mid["grad_conv"],
        grad_mixed=mid["grad_mixed"], grad_summed=mid["grad_summed"], a_zero=a_zero, h_zero=h_zero,
        taps=taps, w_dw=w_dw_p, w_down=w_down_p, sums=mid["sums"],
    )
    d_in = out["d_in"].reshape(9, CIP, C0)[:, :CI].reshape(9 * CI, C0)
    pieces = (
        jnp.pad(as_rows(d_in, ROW_AT[1] - ROW_AT[0]), ((ROW_AT[0], 0), (0, 0))),
        as_rows(out["d_dw"][:49, :C1], ROW_AT[3] - ROW_AT[2]),
        as_rows(mid["d_head"], ROW_AT[7] - ROW_AT[6]),
        out["vector"].reshape(-1, LANES),
    )
    grad = complete_gradients(grad, out["d_down"], pieces)
    plan, (gathered, first, second, totals) = exchange(
        rows, cols, grad, moment_first, moment_second, mid["extra"]
    )
    hidden_p, out_p, new_up, new_down, small_a, small_b, small_c = unpack(plan, gathered, w_up, w_down, perm_narrow, perm_wide)
    small = {0: (small_a, 0), 2: (small_b, 1), 6: (small_c, 2), 7: (small_c, 2)}
    whole = {
        1: new_down,
        3: rebuild_hidden(hidden_p, perm_wide, w_hidden),
        4: rebuild_out(out_p, perm_narrow, w_out),
        5: new_up,
    }
    olds = matrices + (biases_gains,)
    news = []
    for index, old in enumerate(olds):
        if index in whole:
            news.append(whole[index])
        else:
            source, which = small[index]
            start = FLAT_AT[index] - KEPT[which][0] * LANES
            piece = source.reshape(-1)[start : start + old.size].reshape(old.shape)
            news.append(moved(old, piece) if index < 7 else old - learn_rate * piece)
    return tuple(news) + (
        first.reshape(-1),
        second.reshape(-1),
        totals[0, 0],
        MB * CI * totals[1, 0],
        totals[8, 0],
    )


def solution(mesh):
    return jax.shard_map(
        on_device,
        mesh=mesh,
        in_specs=(
            P(None, "rows", "cols", None),
            P(None, "rows", "cols", None),
            P("rows", "cols"),
            P("rows", "cols"),
            P(),
            P(),
            P(),
            P(),
            P(),
            P(),
            P(),
            P(),
            P(),
            P(),
            P(),
            P(("rows", "cols")),
            P(("rows", "cols")),
        ),
        out_specs=(
            P(),
            P(),
            P(),
            P(),
            P(),
            P(),
            P(),
            P(),
            P(("rows", "cols")),
            P(("rows", "cols")),
            P(),
            P(),
            P(),
        ),
        check_vma=False,
    )
```

```python
import functools

import jax
import jax.numpy as jnp
from jax import lax
from jax.experimental import pallas as pl
from jax.experimental.pallas import tpu as pltpu
from jax.sharding import PartitionSpec as P

CI = 77
C0 = 200
C1 = 800
CH = 3200
MB = 2
STEP = 5
LANES = 128
MESH = pl.DeviceIdType.MESH
ROUNDER = 12582912.0

decay_first = 0.9
decay_second = 0.99
epsilon = 1e-08
learn_rate = 0.02
weight_decay = 0.1
clip_limit = 1.0

VEC = 4 * C1 + CH + C1 + 2 * C0 + CI
SIZES = (9 * CI * C0, 4 * C0 * C1, 49 * C1, C1 * CH, CH * C1, C1 * 4 * C0, C0 * CI, VEC)
PADDED = 6602752
FLAT_AT = []
ROW_AT = []
for size in SIZES:
    flat_here = FLAT_AT[-1] + SIZES[len(FLAT_AT) - 1] if FLAT_AT else PADDED - sum(SIZES)
    row_here = ROW_AT[-1] + -(-SIZES[len(ROW_AT) - 1] // 1024) * 8 if ROW_AT else 0
    row_here = max(row_here, -(-flat_here // 1024) * 8)
    FLAT_AT.append(flat_here)
    ROW_AT.append(row_here)
SHIFTS = []
for flat_here, row_here, size in zip(FLAT_AT, ROW_AT, SIZES):
    moved = divmod(row_here * LANES - flat_here, LANES)
    if SHIFTS and SHIFTS[-1][:2] == moved:
        SHIFTS[-1] = moved + (SHIFTS[-1][2], flat_here + size)
    else:
        SHIFTS.append(moved + (flat_here, flat_here + size))
MAX_SHIFT = max(s[0] for s in SHIFTS) + 1


def bit_masks(bits):
    masks = [()]
    for bit in bits:
        masks = masks + [m + (bit,) for m in masks]
    return sorted(masks, key=lambda m: -len(m))


class Plan:
    def __init__(self, rows, cols, total):
        self.rows, self.cols, self.count = rows, cols, rows * cols
        self.share = total // LANES // self.count
        self.bits = rows.bit_length() - 1
        need = 7 + self.share + MAX_SHIFT + 1
        self.block = 64 if need > 1024 else 32
        self.window = -(-need // (2 * self.block)) * 2 * self.block
        self.part = self.window // 2
        self.blocks = self.part // self.block
        self.scales = self.blocks
        upper = list(range(1, self.bits))
        self.orders = [upper, upper[1:] + upper[:1]]
        self.stages = len(upper)
        self.space = (self.share * (self.count - 1)) // 8 * 8 + self.window
        self.padded = -(-self.share // 16) * 16
        cut = -(-self.padded // 32) * 16
        self.cuts = [(0, cut), (cut, self.padded - cut)]
        self.local = self.count // 2


def exchange_kernel(
    plan, grad, m_first, m_second, extra, full, first, second, totals,
    acc, near, q_send, q_recv, s_send, s_recv, z_send, z_recv, zs_send, zs_recv,
    rolled, step, low, stats,
    sem_load, sem_near_s, sem_near_r, sem_qs, sem_qr, sem_ss, sem_sr,
    sem_zs, sem_zr, sem_zss, sem_zsr, sem_ts, sem_tr, sem_own,
    sem_gs, sem_gr, sem_hs, sem_hr, sem_cs, sem_cr,
):
    nr, nc, n = plan.rows, plan.cols, plan.count
    r = lax.axis_index("rows")
    c = lax.axis_index("cols")
    me = r * nc + c
    part, window, share = plan.part, plan.window, plan.share

    def flipped(mask):
        out = r
        for bit in mask:
            here = (r // (1 << bit)) % 2
            out = out + (1 - 2 * here) * (1 << bit)
        return out

    def remote(src, dst, send, recv, row, col):
        return pltpu.make_async_remote_copy(
            src_ref=src, dst_ref=dst, send_sem=send, recv_sem=recv,
            device_id=(row, col), device_id_type=MESH,
        )

    barrier = pltpu.get_barrier_semaphore()

    def greet(d, carry):
        k = lax.rem(me + d, n)
        pl.semaphore_signal(barrier, inc=1, device_id=(k // nc, k % nc), device_id_type=MESH)
        return carry

    lax.fori_loop(1, n, greet, 0)
    pl.semaphore_wait(barrier, n - 1)

    upper = list(range(1, plan.bits))
    masks = bit_masks(upper)

    def local_index(mask, col):
        return (flipped(mask) // 2) * nc + col

    def window_start(row, col):
        return pl.multiple_of((share * (row * nc + col)) // 8 * 8, 8)

    def near_copy(mask, col):
        row = flipped(mask + (0,))
        return remote(
            grad.at[pl.ds(window_start(row, col), window)],
            near.at[local_index(mask, col)],
            sem_near_s.at[local_index(mask, col)], sem_near_r.at[local_index(mask, col)],
            flipped((0,)), c,
        )

    def load_copy(mask, col):
        index = local_index(mask, col)
        return pltpu.make_async_copy(
            grad.at[pl.ds(window_start(flipped(mask), col), window)], acc.at[index], sem_load.at[index]
        )

    half_way = nc // 2

    def column_of(t):
        return jnp.where(t == 1, half_way, jnp.where(t <= half_way, t - 1, t))

    def begin(t, carry):
        col = lax.rem(c + column_of(t), nc)
        for mask in masks:
            near_copy(mask, col).start()
            load_copy(mask, col).start()
        return carry

    lax.fori_loop(1, nc + 1, begin, 0)

    def encode(index, p, q_ref, s_ref):
        def body(b, carry):
            at = pl.ds(pl.multiple_of(b * plan.block, plan.block), plan.block)
            rows_at = pl.ds(pl.multiple_of(p * part + b * plan.block, 8), plan.block)
            values = acc[index, rows_at, :]
            top = jnp.maximum(jnp.max(jnp.abs(values), axis=0, keepdims=True), 1e-30)
            scaled = values * (32766.0 / top)
            scaled = (scaled + ROUNDER) - ROUNDER
            q_ref[at, :] = scaled.astype(jnp.int32).astype(jnp.int16)
            s_ref[pl.ds(b, 1), :] = top * (1.0 / 32766.0)
            return carry

        lax.fori_loop(0, plan.blocks, body, 0)

    def decode(index, p, q_ref, s_ref):
        def body(b, carry):
            at = pl.ds(pl.multiple_of(b * plan.block, plan.block), plan.block)
            rows_at = pl.ds(pl.multiple_of(p * part + b * plan.block, 8), plan.block)
            acc[index, rows_at, :] += q_ref[at, :].astype(jnp.float32) * s_ref[pl.ds(b, 1), :]
            return carry

        lax.fori_loop(0, plan.blocks, body, 0)

    def stage_base(stage):
        return sum((1 << (plan.stages - 1 - s)) for s in range(stage)) * nc

    def hop(p, stage, slot):
        row = flipped((plan.orders[p][stage],))
        at = stage_base(stage) + slot
        return (
            remote(q_send.at[p, at], q_recv.at[p, at], sem_qs.at[p, at], sem_qr.at[p, at], row, c),
            remote(s_send.at[p, at], s_recv.at[p, at], sem_ss.at[p, at], sem_sr.at[p, at], row, c),
        )

    def send_stage(p, stage, number, mask, col):
        bit = plan.orders[p][stage]
        index = local_index(mask + (bit,), col)
        slot = number * nc + col
        at = stage_base(stage) + slot
        encode(index, p, q_send.at[p, at], s_send.at[p, at])
        for copy in hop(p, stage, slot):
            copy.start()

    def take_stage(p, stage, number, mask, col):
        slot = number * nc + col
        for copy in hop(p, stage, slot):
            copy.wait_recv()
        at = stage_base(stage) + slot
        decode(local_index(mask, col), p, q_recv.at[p, at], s_recv.at[p, at])

    def free_masks(p, stage):
        rest = plan.orders[p][stage + 1 :]
        found = bit_masks(rest)
        if rest:
            found = [m for m in found if rest[0] in m] + [m for m in found if rest[0] not in m]
        return found

    def far_copy(p, d):
        col = lax.rem(c + d, nc)
        return (
            remote(z_send.at[p, d - 1], z_recv.at[p, d - 1], sem_zs.at[p, d - 1], sem_zr.at[p, d - 1], r, col),
            remote(zs_send.at[p, d - 1], zs_recv.at[p, d - 1], sem_zss.at[p, d - 1], sem_zsr.at[p, d - 1], r, col),
        )

    def join(t):
        d = column_of(t)
        col = lax.rem(c + d, nc)
        for mask in masks:
            index = local_index(mask, col)
            near_copy(mask, col).wait_recv()
            load_copy(mask, col).wait()

            def body(b, inner, index=index):
                at = pl.ds(pl.multiple_of(b * plan.block, plan.block), plan.block)
                acc[index, at, :] += near[index, at, :]
                return inner

            lax.fori_loop(0, 2 * plan.blocks, body, 0)
            for p in range(2):
                bit = plan.orders[p][0]
                if bit in mask:
                    rest = tuple(b for b in mask if b != bit)
                    options = free_masks(p, 0)
                    number = [sorted(o) for o in options].index(sorted(rest))
                    send_stage(p, 0, number, rest, col)

    def take(stage, t):
        d = column_of(t)
        col = lax.rem(c + d, nc)
        for number in range(1 << (plan.stages - 1 - stage)):
            for p in range(2):
                mask = free_masks(p, stage)[number]
                take_stage(p, stage, number, mask, col)
                if stage + 1 < plan.stages:
                    bit = plan.orders[p][stage + 1]
                    if bit in mask:
                        rest = tuple(b for b in mask if b != bit)
                        options = free_masks(p, stage + 1)
                        following = [sorted(o) for o in options].index(sorted(rest))
                        send_stage(p, stage + 1, following, rest, col)
                else:
                    @pl.when(d < nc)
                    def _(p=p):
                        encode(local_index((), col), p, z_send.at[p, d - 1], zs_send.at[p, d - 1])
                        for copy in far_copy(p, d):
                            copy.start()

    mine = local_index((), c)

    def gather_far(d, carry):
        for p in range(2):
            for copy in far_copy(p, d):
                copy.wait_recv()
            decode(mine, p, z_recv.at[p, d - 1], zs_recv.at[p, d - 1])
        return carry


    def turn_of(t, carry):
        @pl.when(t <= nc)
        def _():
            join(t)

        for stage in range(plan.stages):
            d = t - 1 - stage

            @pl.when((d >= 1) & (d <= nc))
            def _(stage=stage, d=d):
                take(stage, d)

        @pl.when((t > nc) & (t - nc < nc))
        def _():
            gather_far(column_of(t - nc), 0)

        return carry

    lax.fori_loop(1, nc + plan.stages + 1, turn_of, 0)

    def gather_rest(q, carry):
        return gather_far(column_of(q), carry)

    lax.fori_loop(min(plan.stages + 1, nc), nc, gather_rest, 0)

    offset = lax.rem(share * me, 8)
    low_end, high_end = share * me * LANES, share * (me + 1) * LANES
    for number, (shift_rows, shift_lanes, begin, end) in enumerate(SHIFTS):
        def turn(b, carry, number=number, shift_lanes=shift_lanes):
            at = pl.ds(pl.multiple_of(b * plan.block, plan.block), plan.block)
            rolled[number, at, :] = pltpu.roll(acc[mine, at, :], LANES - shift_lanes, 1)
            return carry

        @pl.when((low_end < end) & (high_end > begin))
        def _(turn=turn):
            lax.fori_loop(0, 2 * plan.blocks, turn, 0)

    def share_rows(start, length, chosen):
        lane = lax.broadcasted_iota(jnp.int32, (length, LANES), 1)
        out = jnp.zeros((length, LANES), jnp.float32)
        if len(chosen) > 1:
            line = lax.broadcasted_iota(jnp.int32, (length, LANES), 0)
            flat = (share * me + start + line) * LANES + lane
        for number in chosen:
            shift_rows, shift_lanes, begin, end = SHIFTS[number]
            here = rolled[number, pl.ds(offset + start + shift_rows, length), :]
            after = rolled[number, pl.ds(offset + start + shift_rows + 1, length), :]
            value = jnp.where(lane < LANES - shift_lanes, here, after)
            if len(chosen) > 1:
                value = jnp.where((flat >= begin) & (flat < end), value, out)
            out = value
        return out

    chunk = 32
    whole, tail = share // chunk, share % chunk
    stats[me, 8:16, :] = extra[...]

    def squares(chosen):
        def square(b, total):
            start = pl.multiple_of(b * chunk, chunk)
            value = share_rows(start, chunk, chosen)
            step[pl.ds(start, chunk), :] = value
            return total + jnp.sum((value * value).reshape(chunk // 8, 8, LANES), axis=0)

        total = lax.fori_loop(0, whole, square, jnp.zeros((8, LANES), jnp.float32))
        stats[me, 0:8, :] = total
        if tail:
            value = share_rows(whole * chunk, tail, chosen)
            step[whole * chunk : share, :] = value
            stats[me, 0:1, :] += jnp.sum(value * value, axis=0, keepdims=True)

    largest = max(range(len(SHIFTS)), key=lambda i: SHIFTS[i][3] - SHIFTS[i][2])
    alone = (low_end >= SHIFTS[largest][2]) & (high_end <= SHIFTS[largest][3])

    @pl.when(alone)
    def _():
        squares((largest,))

    @pl.when(jnp.logical_not(alone))
    def _():
        squares(tuple(range(len(SHIFTS))))

    def stat_copy(target, source):
        return remote(
            stats.at[me], stats.at[me], sem_ts.at[target], sem_tr.at[me], target // nc, target % nc
        )

    def stat_wait(source):
        return remote(
            stats.at[source], stats.at[source], sem_ts.at[source], sem_tr.at[source],
            source // nc, source % nc,
        )

    def send_stat(d, carry):
        stat_copy(lax.rem(me + d, n), me).start()
        return carry

    lax.fori_loop(1, n, send_stat, 0)

    def wait_stat(d, carry):
        stat_wait(lax.rem(me + d, n)).wait_recv()
        return carry

    lax.fori_loop(1, n, wait_stat, 0)

    def add_stat(k, total):
        return total + stats[k]

    sums = lax.fori_loop(0, n, add_stat, jnp.zeros((16, LANES), jnp.float32))
    norm = jnp.sqrt(jnp.sum(sums[0:8], keepdims=True))
    totals[0:1, :] = jnp.broadcast_to(jnp.sum(sums[8:9], keepdims=True), (1, LANES))
    totals[1:2, :] = jnp.broadcast_to(jnp.sum(sums[9:10], keepdims=True), (1, LANES))
    totals[2:8, :] = jnp.zeros((6, LANES), jnp.float32)
    totals[8:16, :] = jnp.broadcast_to(norm, (8, LANES))
    clip = jnp.minimum(1.0, clip_limit / norm)

    def update(start, length):
        clipped = step[pl.ds(start, length), :] * clip
        one = decay_first * m_first[pl.ds(start, length), :] + (1.0 - decay_first) * clipped
        two = decay_second * m_second[pl.ds(start, length), :] + (1.0 - decay_second) * clipped * clipped
        first[pl.ds(start, length), :] = one
        second[pl.ds(start, length), :] = two
        step[pl.ds(start, length), :] = (
            one / (1.0 - decay_first**STEP) / (jnp.sqrt(two / (1.0 - decay_second**STEP)) + epsilon)
        )

    def update_chunk(b, carry):
        update(pl.multiple_of(b * chunk, chunk), chunk)
        return carry

    lax.fori_loop(0, whole, update_chunk, 0)
    if tail:
        update(whole * chunk, tail)
    if plan.padded > share:
        step[share : plan.padded, :] = jnp.zeros((plan.padded - share, LANES), jnp.float32)

    def narrow(b, carry):
        at = pl.ds(pl.multiple_of(b * 16, 16), 16)
        low[at, :] = step[at, :].astype(jnp.bfloat16)
        return carry

    lax.fori_loop(0, plan.padded // 16, narrow, 0)

    own = pltpu.make_async_copy(low, full.at[me], sem_own)
    own.start()
    own.wait()

    back = [list(reversed(order)) for order in plan.orders]

    def piece(mask, col, p):
        begin, length = plan.cuts[p]
        return full.at[flipped(mask) * nc + col, pl.ds(begin, length)]

    def along(direction, col, p, receive):
        step_col = 1 if direction == 0 else -1
        target = c - step_col if receive else c + step_col
        ref = piece((), col, p)
        return remote(ref, ref, sem_gs.at[direction, col, p], sem_gr.at[direction, col, p], r, target)

    def gather_masks(p, stage):
        return bit_masks(back[p][:stage])

    def gather_base(stage):
        return sum(1 << s for s in range(stage)) * nc

    def across(p, stage, number, mask, col):
        at = gather_base(stage) + number * nc + col
        ref = piece(mask, col, p)
        return remote(ref, ref, sem_hs.at[p, at], sem_hr.at[p, at], flipped((back[p][stage],)), c)

    def across_recv(p, stage, number, mask, col):
        at = gather_base(stage) + number * nc + col
        ref = piece(mask + (back[p][stage],), col, p)
        return remote(ref, ref, sem_hs.at[p, at], sem_hr.at[p, at], flipped((back[p][stage],)), c)

    def inward(p, mask, col):
        number = masks.index(tuple(sorted(mask)))
        at = number * nc + col
        ref = piece(mask, col, p)
        return remote(ref, ref, sem_cs.at[p, at], sem_cr.at[p, at], flipped((0,)), c)

    def inward_recv(p, mask, col):
        number = masks.index(tuple(sorted(mask)))
        at = number * nc + col
        ref = piece(mask + (0,), col, p)
        return remote(ref, ref, sem_cs.at[p, at], sem_cr.at[p, at], flipped((0,)), c)

    def spread(p, mask, col, stage):
        for later in range(stage, plan.stages):
            options = [sorted(o) for o in gather_masks(p, later)]
            if sorted(mask) in options:
                across(p, later, options.index(sorted(mask)), mask, col).start()
        inward(p, mask, col).start()

    def near_cols(t):
        if t == 0:
            return [(0, c)]
        return [(0, c - t), (1, c + t)]

    def inside(col):
        return (col >= 0) & (col < nc)

    for time in range(nc + plan.stages):
        for stage in range(plan.stages + 1):
            t = time - stage
            if not 0 <= t < nc:
                continue
            if stage == 0:
                if t == 0:
                    for p in range(2):
                        @pl.when(c < nc - 1)
                        def _(p=p):
                            along(0, c, p, False).start()

                        @pl.when(c > 0)
                        def _(p=p):
                            along(1, c, p, False).start()

                        spread(p, (), c, 0)
                else:
                    for direction, col in near_cols(t):
                        @pl.when(inside(col))
                        def _(direction=direction, col=col):
                            for p in range(2):
                                along(direction, col, p, True).wait_recv()
                                if direction == 0:
                                    @pl.when(c < nc - 1)
                                    def _():
                                        along(0, col, p, False).start()
                                else:
                                    @pl.when(c > 0)
                                    def _():
                                        along(1, col, p, False).start()
                                spread(p, (), col, 0)
            else:
                for direction, col in near_cols(t):
                    @pl.when(inside(col))
                    def _(col=col, stage=stage):
                        for number in range(1 << (stage - 1)):
                            for p in range(2):
                                mask = gather_masks(p, stage - 1)[number]
                                across_recv(p, stage - 1, number, mask, col).wait_recv()
                                spread(p, mask + (back[p][stage - 1],), col, stage)

    for mask in masks:
        def finish(col, carry, mask=mask):
            for p in range(2):
                inward_recv(p, mask, col).wait_recv()
                inward(p, mask, col).wait_send()
            near_copy(mask, col).wait_send()
            return carry

        lax.fori_loop(0, nc, finish, 0)
    for p in range(2):
        for stage in range(plan.stages):
            for number, mask in enumerate(gather_masks(p, stage)):
                def sent(col, carry, p=p, stage=stage, number=number, mask=mask):
                    across(p, stage, number, mask, col).wait_send()
                    return carry

                lax.fori_loop(0, nc, sent, 0)
            for number in range(1 << (plan.stages - 1 - stage)):
                def left(col, carry, p=p, stage=stage, number=number):
                    for copy in hop(p, stage, number * nc + col):
                        copy.wait_send()
                    return carry

                lax.fori_loop(0, nc, left, 0)

        def gone(col, carry, p=p):
            @pl.when((col <= c) & (c < nc - 1))
            def _():
                along(0, col, p, False).wait_send()

            @pl.when((col >= c) & (c > 0))
            def _():
                along(1, col, p, False).wait_send()

            return carry

        lax.fori_loop(0, nc, gone, 0)

        def far_gone(d, carry, p=p):
            for copy in far_copy(p, d):
                copy.wait_send()
            return carry

        lax.fori_loop(1, nc, far_gone, 0)

    def stat_gone(d, carry):
        stat_copy(lax.rem(me + d, n), me).wait_send()
        return carry

    lax.fori_loop(1, n, stat_gone, 0)


def exchange(rows, cols, grad, m_first, m_second, extra):
    plan = Plan(rows, cols, m_first.size * rows * cols)
    n, nc, share = plan.count, plan.cols, plan.share
    hops = sum(1 << s for s in range(plan.stages)) * nc
    dma = pltpu.SemaphoreType.DMA
    far = max(nc - 1, 1)
    vmem = pl.BlockSpec(memory_space=pltpu.VMEM)
    hbm = pl.BlockSpec(memory_space=pl.ANY)
    return plan, pl.pallas_call(
        functools.partial(exchange_kernel, plan),
        out_shape=(
            jax.ShapeDtypeStruct((n, plan.padded, LANES), jnp.bfloat16),
            jax.ShapeDtypeStruct((share, LANES), jnp.float32),
            jax.ShapeDtypeStruct((share, LANES), jnp.float32),
            jax.ShapeDtypeStruct((16, LANES), jnp.float32),
        ),
        in_specs=[hbm, vmem, vmem, vmem],
        out_specs=(hbm, vmem, vmem, vmem),
        scratch_shapes=[
            pltpu.VMEM((plan.local, plan.window, LANES), jnp.float32),
            pltpu.VMEM((plan.local, plan.window, LANES), jnp.float32),
            pltpu.VMEM((2, hops, plan.part, LANES), jnp.int16),
            pltpu.VMEM((2, hops, plan.part, LANES), jnp.int16),
            pltpu.VMEM((2, hops, plan.scales, LANES), jnp.float32),
            pltpu.VMEM((2, hops, plan.scales, LANES), jnp.float32),
            pltpu.VMEM((2, far, plan.part, LANES), jnp.int16),
            pltpu.VMEM((2, far, plan.part, LANES), jnp.int16),
            pltpu.VMEM((2, far, plan.scales, LANES), jnp.float32),
            pltpu.VMEM((2, far, plan.scales, LANES), jnp.float32),
            pltpu.VMEM((len(SHIFTS), plan.window, LANES), jnp.float32),
            pltpu.VMEM((plan.padded, LANES), jnp.float32),
            pltpu.VMEM((plan.padded, LANES), jnp.bfloat16),
            pltpu.VMEM((n, 16, LANES), jnp.float32),
            dma((plan.local,)), dma((plan.local,)), dma((plan.local,)),
            dma((2, hops)), dma((2, hops)), dma((2, hops)), dma((2, hops)),
            dma((2, far)), dma((2, far)), dma((2, far)), dma((2, far)),
            dma((n,)), dma((n,)), dma,
            dma((2, nc, 2)), dma((2, nc, 2)),
            dma((2, hops)), dma((2, hops)),
            dma((2, plan.local)), dma((2, plan.local)),
        ],
        compiler_params=pltpu.CompilerParams(
            collective_id=0, has_side_effects=True, vmem_limit_bytes=56 << 20
        ),
    )(grad, m_first.reshape(share, LANES), m_second.reshape(share, LANES), extra)


WIDE = CH + LANES
KEPT = ((8, 1104), (6096, 6408), (51400, 51584))
PLACES = tuple(divmod(FLAT_AT[i], LANES) for i in (3, 4, 5, 1))

SLOTS = 6
HALF = WIDE // 2
PITCH = 33


def unpack_kernel(
    plan, gathered, old_up, old_down, narrow, wide, hidden_out, rows_out, up_out, down_out, small_a, small_b, small_c,
    held, flat, woven, hidden, by_row, rows_low, up, down, sems, sem_out,
):
    n, share = plan.count, plan.share
    step = CH // LANES

    def fetch(k, slot):
        return pltpu.make_async_copy(gathered.at[k], held.at[slot], sems.at[slot])

    for k in range(SLOTS - 1):
        fetch(k, k).start()

    def widen(k, carry):
        slot = lax.rem(k, SLOTS)

        @pl.when(k + SLOTS - 1 < n)
        def _():
            fetch(k + SLOTS - 1, lax.rem(k + SLOTS - 1, SLOTS)).start()

        fetch(k, slot).wait()

        def body(b, inner):
            at = pl.ds(pl.multiple_of(b * 16, 16), 16)
            flat[pl.ds(share * k + b * 16, 16), :] = held[slot, at, :].astype(jnp.float32)
            return inner

        lax.fori_loop(0, plan.padded // 16, body, 0, unroll=4)
        return carry

    lax.fori_loop(0, n, widen, 0)

    copies = [
        pltpu.make_async_copy(source, target, sem_out.at[i])
        for i, (source, target) in enumerate(
            (
                (hidden, hidden_out.at[:, pl.ds(0, HALF)]), (rows_low, rows_out), (up, up_out),
                (down, down_out), (hidden, hidden_out.at[:, pl.ds(HALF, HALF)]),
            )
        )
    ]
    row, lane = PLACES[0]

    def spread(a, carry):
        by_row[pl.ds(narrow[a] * PITCH, 32), :] = flat[pl.ds(row + a * step, 32), :]
        return carry

    lax.fori_loop(0, C1, spread, 0, unroll=4)

    def columns(half):
        def column(t, carry):
            for begin in range(0, C1, 160):
                at = begin * PITCH + half * (HALF // LANES) + t
                values = by_row[pl.ds(at, 160, stride=PITCH), :]
                at = pl.ds(pl.multiple_of(t * LANES, LANES), LANES)
                hidden[begin : begin + 160, at] = values.astype(jnp.bfloat16)
            return carry

        lax.fori_loop(0, HALF // LANES, column, 0)

    columns(0)
    copies[0].start()

    quarter = C1 // 4
    for number, (ref, old, (line, begin)) in enumerate(zip((up, down), (old_up, old_down), PLACES[2:])):
        for u in range(-(-C1 // LANES)):
            width = min(LANES, C1 - u * LANES)
            place = lax.broadcasted_iota(jnp.int32, (quarter, LANES), 1)
            for b in range(4):
                first, rest = divmod(C1 * b + begin, LANES)
                here = flat[pl.ds(line + first + u, quarter, stride=step), :]
                after = flat[pl.ds(line + first + u + 1, quarter, stride=step), :]
                value = pltpu.roll(jnp.where(place >= rest, here, after), LANES - rest, 1)
                woven[pl.ds(b, quarter, stride=4), :] = value
            at = slice(u * LANES, u * LANES + width)
            ref[:, at] = moved(old[:, at], woven[:, :width])
        copies[2 + number].start()

    for ref, (begin, end) in zip((small_a, small_b, small_c), KEPT):
        ref[...] = flat[begin:end, :]
    copies[0].wait()
    columns(1)
    copies[4].start()

    row, lane = PLACES[1]

    def align(part, carry):
        place = lax.broadcasted_iota(jnp.int32, (40, LANES), 1)
        for b in range(4):
            first, rest = divmod(C1 * b + lane, LANES)
            tiles = [
                flat[pl.ds(row + part * (40 * step) + first + u, 40, stride=step), :]
                for u in range(C1P // LANES + 1)
            ]
            values = [
                pltpu.roll(jnp.where(place >= rest, here, after), LANES - rest, 1)
                for here, after in zip(tiles, tiles[1:])
            ]
            for u, value in enumerate(values):
                flat[pl.ds(part * (40 * PITCH) + b * 8 + u, 40, stride=PITCH), :] = value
        return carry

    lax.fori_loop(0, C1 // 40, align, 0)

    def scatter(a, carry):
        for b in range(4):
            by_row[pl.ds(wide[a * 4 + b] * 9, 8), :] = flat[pl.ds(a * PITCH + b * 8, 8), :]
        return carry

    lax.fori_loop(0, CH // 4, scatter, 0, unroll=4)

    def by_lane(part, carry):
        for u in range(C1P // LANES):
            values = by_row[pl.ds(part * (160 * 9) + u, 160, stride=9), :]
            at = pl.ds(pl.multiple_of(part * 160, 160), 160)
            rows_low[at, u * LANES : (u + 1) * LANES] = values.astype(jnp.bfloat16)
        return carry

    lax.fori_loop(0, CH // 160, by_lane, 0)
    copies[1].start()
    for copy in copies[1:]:
        copy.wait()


def unpack(plan, gathered, old_up, old_down, narrow, wide):
    lines = PADDED // LANES
    vmem = pl.BlockSpec(memory_space=pltpu.VMEM)
    hbm = pl.BlockSpec(memory_space=pl.ANY)
    dma = pltpu.SemaphoreType.DMA
    f32, low = jnp.float32, jnp.bfloat16
    return pl.pallas_call(
        functools.partial(unpack_kernel, plan),
        out_shape=(
            jax.ShapeDtypeStruct((C1, WIDE), low),
            jax.ShapeDtypeStruct((CH, C1P), low),
            jax.ShapeDtypeStruct((C1, C1), f32),
            jax.ShapeDtypeStruct((C1, C1), f32),
        )
        + tuple(jax.ShapeDtypeStruct((end - begin, LANES), f32) for begin, end in KEPT),
        in_specs=[hbm, vmem, vmem] + [pl.BlockSpec(memory_space=pltpu.SMEM)] * 2,
        out_specs=(hbm, hbm, hbm, hbm, vmem, vmem, vmem),
        scratch_shapes=[
            pltpu.VMEM((SLOTS, plan.padded, LANES), low),
            pltpu.VMEM((-(-lines // 8) * 8 + 16, LANES), f32),
            pltpu.VMEM((C1, LANES), f32),
            pltpu.VMEM((C1, HALF), low),
            pltpu.VMEM((CH * 9, LANES), f32),
            pltpu.VMEM((CH, C1P), low),
            pltpu.VMEM((C1, C1), f32),
            pltpu.VMEM((C1, C1), f32),
            dma((SLOTS,)),
            dma((5,)),
        ],
        compiler_params=pltpu.CompilerParams(vmem_limit_bytes=63 << 20),
    )(gathered, old_up, old_down, narrow, wide)


def moved(old, direction):
    return old.astype(jnp.float32) * (1.0 - learn_rate * weight_decay) - learn_rate * direction


def one_hot(condition):
    return jnp.where(condition, 1.0, 0.0).astype(jnp.bfloat16)


def product(left, right):
    return jnp.dot(left, right, preferred_element_type=jnp.float32)


def product_t(left, right):
    return lax.dot_general(left, right, (((1,), (1,)), ((), ())), preferred_element_type=jnp.float32)


TILE = 640


DEEP = 256


def hidden_kernel(lines, wide, old, new):
    depth = lines.shape[1]
    base = pl.program_id(0) * TILE
    direction = None
    for begin in range(0, depth, DEEP):
        end = min(begin + DEEP, depth)
        place = wide[begin:end, :] - base
        lane = lax.broadcasted_iota(jnp.int32, (end - begin, LANES), 1)
        hot = jnp.concatenate([one_hot(lane + u == place) for u in range(0, TILE, LANES)], axis=1)
        term = product(lines[:, begin:end], hot)
        direction = term if direction is None else direction + term
    new[...] = moved(old[...], direction)


def rebuild_hidden(lines, wide, old):
    lane = PLACES[0][1]
    wide = jnp.full((WIDE,), -1, jnp.int32).at[lane : lane + CH].set(wide)
    return pl.pallas_call(
        hidden_kernel,
        out_shape=jax.ShapeDtypeStruct((C1, CH), jnp.float32),
        grid=(CH // TILE,),
        in_specs=[
            pl.BlockSpec((C1, WIDE), lambda i: (0, 0)),
            pl.BlockSpec((WIDE, LANES), lambda i: (0, 0)),
            pl.BlockSpec((C1, TILE), lambda i: (0, i)),
        ],
        out_specs=pl.BlockSpec((C1, TILE), lambda i: (0, i)),
        compiler_params=pltpu.CompilerParams(vmem_limit_bytes=48 << 20),
    )(lines, jnp.broadcast_to(wide[:, None], (WIDE, LANES)), old)


def out_kernel(rows, narrow, old, new, turn):
    @pl.when(pl.program_id(0) == 0)
    def _():
        turn[...] = one_hot(lax.broadcasted_iota(jnp.int32, (C1, C1), 0) == narrow[...])

    new[...] = moved(old[...], product_t(turn[...], rows[:, :C1]))


def rebuild_out(rows, narrow, old):
    return pl.pallas_call(
        out_kernel,
        out_shape=jax.ShapeDtypeStruct((C1, CH), jnp.float32),
        grid=(CH // TILE,),
        in_specs=[
            pl.BlockSpec((TILE, C1P), lambda i: (i, 0)),
            pl.BlockSpec((1, C1), lambda i: (0, 0)),
            pl.BlockSpec((C1, TILE), lambda i: (0, i)),
        ],
        out_specs=pl.BlockSpec((C1, TILE), lambda i: (0, i)),
        scratch_shapes=[pltpu.VMEM((C1, C1), jnp.bfloat16)],
        compiler_params=pltpu.CompilerParams(vmem_limit_bytes=48 << 20),
    )(rows, narrow[None, :], old.T).T


def weave(source, rows, put):
    for t in range(CH // LANES):
        b, begin = divmod(t * LANES, C1)
        u, rest = divmod(begin, LANES)
        place = lax.broadcasted_iota(jnp.int32, (rows, LANES), 1)
        value = source[u, pl.ds(b, rows, stride=4), :]
        if rest:
            if begin + LANES - rest < C1:
                after = source[u + 1, pl.ds(b, rows, stride=4), :]
                value = jnp.where(place >= rest, value, after)
            value = pltpu.roll(value, LANES - rest, 1)
        left = C1 - begin
        if left < LANES:
            following = source[0, pl.ds(b + 1, rows, stride=4), :]
            value = jnp.where(place < left, value, pltpu.roll(following, left, 1))
        put(t, value)


def place_kernel(
    nr, nc, normed, branch, pre, act, narrow_row, narrow_col, wide, up, cells,
    grad, padded, hidden, out, loose, up_rows, norm_t, branch_r, halo_cells, held_pre, held_act,
    sem_out, sems, sem_halo_s, sem_halo_r, sem_in,
):
    step = pl.program_id(0)
    steps = pl.num_programs(0)
    ratio = CH // LANES
    lines = TILE // 4
    tiles = TILE // LANES

    def out_copy(n):
        rows = lines * ratio
        return pltpu.make_async_copy(
            out.at[pl.ds(pl.multiple_of(n * rows, 8), rows)],
            grad.at[pl.ds(pl.multiple_of(ROW_AT[4] + n * rows, 8), rows)],
            sem_out.at[n],
        )

    copies = [
        pltpu.make_async_copy(ref, grad.at[pl.ds(row, ref.shape[0])], sems.at[i])
        for i, (ref, row) in enumerate(((up_rows, ROW_AT[5]), (hidden, ROW_AT[3])))
    ] + [pltpu.make_async_copy(halo_cells, padded, sems.at[2])]

    fetch_pre = pltpu.make_async_copy(pre, held_pre, sem_in.at[0])
    fetch_act = pltpu.make_async_copy(act, held_act, sem_in.at[1])

    @pl.when(step == 0)
    def _():
        fetch_pre.start()
        fetch_act.start()
        halo_start(nr, nc, 3, cells, halo_cells, sem_halo_s, sem_halo_r)
        line = lax.broadcasted_iota(jnp.int32, (C1, C1), 1)
        norm_t[...] = product_t(one_hot(line == narrow_col[:, 0:1]), normed[:, :C1]).astype(jnp.bfloat16)
        line = lax.broadcasted_iota(jnp.int32, (C1, C1P), 0)
        branch_r[...] = product(branch[:, :C1], one_hot(line == narrow_row[...])).astype(jnp.bfloat16)
        for u in range(-(-C1 // LANES)):
            width = min(LANES, C1 - u * LANES)
            loose[u, :, 0:width] = up[0:C1, u * LANES : u * LANES + width]

        def put(t, value):
            up_rows[pl.ds(t, C1 // 4, stride=ratio), :] = value

        weave(loose, C1 // 4, put)
        copies[0].start()
        fetch_pre.wait()
        fetch_act.wait()

    turned_pre = turned_act = None
    for begin in range(0, CH, DEEP):
        end = min(begin + DEEP, CH)
        line = lax.broadcasted_iota(jnp.int32, (end - begin, TILE), 0) + begin
        hot = one_hot(line == wide[...])
        one = product(held_pre[:, begin:end], hot)
        two = product(held_act[:, begin:end], hot)
        turned_pre = one if turned_pre is None else turned_pre + one
        turned_act = two if turned_act is None else turned_act + two
    part = product(norm_t[...], turned_pre.astype(jnp.bfloat16))
    for t in range(tiles):
        hidden[pl.ds(step * tiles + t, C1, stride=ratio), :] = part[:, t * LANES : (t + 1) * LANES]
    part = inner_rows(turned_act.astype(jnp.bfloat16), branch_r[...])
    for u in range(-(-C1 // LANES)):
        loose[u, 0:TILE, :] = part[:, u * LANES : (u + 1) * LANES]

    def put_out(t, value):
        out[pl.ds(step * (lines * ratio) + t, lines, stride=ratio), :] = value

    weave(loose, lines, put_out)
    out_copy(step).start()

    @pl.when(step == steps - 1)
    def _():
        copies[1].start()
        halo_finish(nr, nc, 3, cells, halo_cells, sem_halo_s, sem_halo_r)
        copies[2].start()

        def finish(n, carry):
            out_copy(n).wait()
            return carry

        lax.fori_loop(0, steps, finish, 0)
        for copy in copies:
            copy.wait()


def place_gradients(nr, nc, space, normed, branch, pre, act, narrow, wide, up, cells):
    def whole(array):
        return pl.BlockSpec(
            array.shape, lambda i: (0,) * len(array.shape), pipeline_mode=pl.Buffered(1)
        )

    hbm = pl.BlockSpec(memory_space=pl.ANY)
    rows = pre.shape[0]
    batch, height, breadth, chans = cells.shape
    narrow_row = jnp.pad(narrow, (0, C1P - C1), constant_values=-1)[None, :]
    narrow_col = jnp.broadcast_to(narrow[:, None], (C1, LANES))
    framed = jax.ShapeDtypeStruct((batch, height + 6, breadth + 2 * EDGE, chans), cells.dtype)
    dma = pltpu.SemaphoreType.DMA
    return pl.pallas_call(
        functools.partial(place_kernel, nr, nc),
        out_shape=(jax.ShapeDtypeStruct((space, LANES), jnp.float32), framed),
        grid=(CH // TILE,),
        in_specs=[
            whole(normed), whole(branch), hbm, hbm, whole(narrow_row), whole(narrow_col),
            pl.BlockSpec((1, TILE), lambda i: (0, i)),
            whole(up), whole(cells),
        ],
        out_specs=(hbm, hbm),
        scratch_shapes=[
            pltpu.VMEM((C1 * CH // LANES, LANES), jnp.float32),
            pltpu.VMEM((C1 * CH // LANES, LANES), jnp.float32),
            pltpu.VMEM((C1P // LANES, C1, LANES), jnp.float32),
            pltpu.VMEM((C1 * C1 // LANES, LANES), jnp.float32),
            pltpu.VMEM((C1, rows), jnp.bfloat16),
            pltpu.VMEM((rows, C1P), jnp.bfloat16),
            pltpu.VMEM(framed.shape, framed.dtype),
            pltpu.VMEM(pre.shape, pre.dtype),
            pltpu.VMEM(act.shape, act.dtype),
            dma((CH // TILE,)), dma((3,)), dma((8,)), dma((8,)), dma((2,)),
        ],
        compiler_params=pltpu.CompilerParams(
            collective_id=3, has_side_effects=True, vmem_limit_bytes=60 << 20
        ),
    )(normed, branch, pre, act, narrow_row, narrow_col, wide[None, :], up, cells)


def complete_kernel(before, down, piece_in, piece_dw, piece_head, piece_vec, grad, loose, down_rows, sems):
    copies = [
        pltpu.make_async_copy(ref, grad.at[pl.ds(row, ref.shape[0])], sems.at[i])
        for i, (ref, row) in enumerate(
            (
                (piece_in, 0), (piece_dw, ROW_AT[2]), (piece_head, ROW_AT[6]), (piece_vec, ROW_AT[7]),
                (down_rows, ROW_AT[1]),
            )
        )
    ]
    for copy in copies[:4]:
        copy.start()
    for u in range(C1P // LANES):
        loose[u] = down[:, u * LANES : (u + 1) * LANES]

    def put(t, value):
        down_rows[pl.ds(t, C1 // 4, stride=CH // LANES), :] = value

    weave(loose, C1 // 4, put)
    copies[4].start()
    for copy in copies:
        copy.wait()


def complete_gradients(grad, down, pieces):
    vmem = pl.BlockSpec(memory_space=pltpu.VMEM)
    hbm = pl.BlockSpec(memory_space=pl.ANY)
    return pl.pallas_call(
        complete_kernel,
        out_shape=jax.ShapeDtypeStruct(grad.shape, grad.dtype),
        in_specs=[hbm, vmem, vmem, vmem, vmem, vmem],
        out_specs=hbm,
        input_output_aliases={0: 0},
        scratch_shapes=[
            pltpu.VMEM((C1P // LANES, C1, LANES), jnp.float32),
            pltpu.VMEM((C1 * C1 // LANES, LANES), jnp.float32),
            pltpu.SemaphoreType.DMA((5,)),
        ],
        compiler_params=pltpu.CompilerParams(vmem_limit_bytes=60 << 20),
    )(grad, down, *pieces)


C0P = 256
C1P = 896
CIP = 128
EDGE = 16
CURVE = 0.7978845608028654
CUBE = 0.044715


def inner_rows(left, right):
    return lax.dot_general(left, right, (((0,), (0,)), ((), ())), preferred_element_type=jnp.float32)


def column_sum(values):
    return jnp.sum(values.astype(jnp.float32), axis=0, keepdims=True)


def gelu(t):
    return 0.5 * t * (1.0 + jnp.tanh(CURVE * (t + CUBE * (t * t * t))))


def gelu_slope(t):
    bend = jnp.tanh(CURVE * (t + CUBE * (t * t * t)))
    return 0.5 * (1.0 + bend) + 0.5 * t * (1.0 - bend * bend) * (CURVE * (1.0 + 3.0 * CUBE * (t * t)))


WAYS = [(dr, dc) for dr in (-1, 0, 1) for dc in (-1, 0, 1) if (dr, dc) != (0, 0)]
ORDER = sorted(range(8), key=lambda i: (WAYS[i][1] != 0, WAYS[i][0] == 0))


def halo_place(nr, nc):
    r = lax.axis_index("rows")
    return r, lax.axis_index("cols"), lambda dr: (r + dr >= 0) & (r + dr < nr)


def halo_copy(nr, nc, width, cells, out, sem_s, sem_r, i, receive):
    r, c, there = halo_place(nr, nc)
    height, breadth = cells.shape[1], cells.shape[2]
    dr, dc = WAYS[i]
    rows_from = {-1: (0, width), 0: (0, height), 1: (height - width, width)}[dr]
    rows_to = {-1: height + width, 0: width, 1: 0}[dr]
    cols_from = {-1: (0, EDGE), 0: (0, breadth), 1: (breadth - EDGE, EDGE)}[dc]
    cols_to = {-1: EDGE + breadth, 0: EDGE, 1: 0}[dc]
    sign = -1 if receive else 1
    return pltpu.make_async_remote_copy(
        src_ref=cells.at[:, pl.ds(*rows_from), pl.ds(*cols_from)],
        dst_ref=out.at[:, pl.ds(rows_to, rows_from[1]), pl.ds(cols_to, cols_from[1])],
        send_sem=sem_s.at[i],
        recv_sem=sem_r.at[i],
        device_id=(r + sign * dr, lax.rem(c + sign * dc + nc, nc)),
        device_id_type=MESH,
    )


def halo_start(nr, nc, width, cells, out, sem_s, sem_r):
    r, c, there = halo_place(nr, nc)
    height, breadth = cells.shape[1], cells.shape[2]
    barrier = pltpu.get_barrier_semaphore()
    for dr, dc in WAYS:
        @pl.when(there(dr))
        def _(dr=dr, dc=dc):
            pl.semaphore_signal(
                barrier, inc=1, device_id=(r + dr, lax.rem(c + dc + nc, nc)), device_id_type=MESH
            )

    edge = (r == 0) | (r == nr - 1)

    @pl.when(edge)
    def _():
        pl.semaphore_wait(barrier, 5)

    @pl.when(jnp.logical_not(edge))
    def _():
        pl.semaphore_wait(barrier, 8)

    for i in ORDER:
        @pl.when(there(WAYS[i][0]))
        def _(i=i):
            halo_copy(nr, nc, width, cells, out, sem_s, sem_r, i, False).start()

    for m in range(cells.shape[0]):
        for row in range(height):
            out[m, width + row, EDGE : EDGE + breadth, :] = cells[m, row]

    @pl.when(r == 0)
    def _():
        out[:, 0:width] = jnp.zeros((out.shape[0], width) + out.shape[2:], out.dtype)

    @pl.when(r == nr - 1)
    def _():
        out[:, height + width :] = jnp.zeros((out.shape[0], width) + out.shape[2:], out.dtype)


def halo_finish(nr, nc, width, cells, out, sem_s, sem_r):
    r, c, there = halo_place(nr, nc)
    for i in ORDER:
        @pl.when(there(-WAYS[i][0]))
        def _(i=i):
            halo_copy(nr, nc, width, cells, out, sem_s, sem_r, i, True).wait_recv()

        @pl.when(there(WAYS[i][0]))
        def _(i=i):
            halo_copy(nr, nc, width, cells, out, sem_s, sem_r, i, False).wait_send()


def halo_kernel(nr, nc, width, cells, out, sem_s, sem_r):
    halo_start(nr, nc, width, cells, out, sem_s, sem_r)
    halo_finish(nr, nc, width, cells, out, sem_s, sem_r)


def halo(nr, nc, width, cells, identity):
    batch, height, breadth, chans = cells.shape
    vmem = pl.BlockSpec(memory_space=pltpu.VMEM)
    return pl.pallas_call(
        functools.partial(halo_kernel, nr, nc, width),
        out_shape=jax.ShapeDtypeStruct(
            (batch, height + 2 * width, breadth + 2 * EDGE, chans), cells.dtype
        ),
        in_specs=[vmem],
        out_specs=vmem,
        scratch_shapes=[pltpu.SemaphoreType.DMA((8,)), pltpu.SemaphoreType.DMA((8,))],
        compiler_params=pltpu.CompilerParams(
            collective_id=identity, has_side_effects=True, vmem_limit_bytes=24 << 20
        ),
    )(cells)


SIDE = 8
REACH = 3
FINE_REACH = 2 * REACH + 1


def input_kernel(
    nr, state, w_in, w_down, vector, taps_out, a_zero_out, h_zero_out, coarse, padded, lines,
    wide, taps_all, coarse_all, taps, a_zero, h_zero, sems,
):
    r = lax.axis_index("rows")
    copies = [
        pltpu.make_async_copy(source, target, sems.at[i])
        for i, (source, target) in enumerate(((taps, taps_out), (a_zero, a_zero_out), (h_zero, h_zero_out)))
    ]
    lines[...] = jnp.zeros_like(lines)
    start = 0
    for number, size in enumerate((C0, C1, C1, C1, C1, CH, C1, C0, CI)):
        lines[number : number + 1, 0:size] = vector[:, start : start + size]
        start = start + size
    batch, rows, breadth, _ = state.shape
    half_h, half_w = rows // 2 - FINE_REACH, breadth // 2 - EDGE
    all_h, all_w = half_h + 2 * REACH, half_w + 2 * SIDE
    for m in range(batch):
        for y in range(rows):
            wide[m, y, SIDE : SIDE + breadth, :] = state[m, y].astype(jnp.float32)
    for m in range(batch):
        for y in range(rows):
            for f in range(4):
                start = SIDE + EDGE - 2 * SIDE - 1 + f
                line = wide[m, y, pl.ds(start, all_w, stride=2), :]
                low = line.astype(jnp.bfloat16)
                inner = line[SIDE : SIDE + half_w].astype(jnp.bfloat16)
                for dy in range(3):
                    i, sy = divmod(y - dy, 2)
                    if not 0 <= i < all_h:
                        continue
                    for dx in range(3):
                        if not 0 <= f - dx < 2:
                            continue
                        s, tap = sy * 2 + f - dx, slice((dy * 3 + dx) * CIP, (dy * 3 + dx + 1) * CIP)
                        begin = (m * all_h + i) * all_w
                        taps_all[s, begin : begin + all_w, tap] = low
                        if REACH <= i < REACH + half_h:
                            begin = (m * half_h + i - REACH) * half_w
                            taps[s, begin : begin + half_w, tap] = inner
    copies[0].start()
    size = all_h * all_w
    for m in range(batch):
        block = slice(m * size, (m + 1) * size)
        total = jnp.broadcast_to(lines[1:2, :C1P], (size, C1P))
        for s in range(4):
            value = product(taps_all[s, block, :], w_in[...]) + lines[0:1, :C0P]
            curved = gelu(value)
            for i in range(half_h):
                begin = (i + REACH) * all_w + SIDE
                at = slice((m * half_h + i) * half_w, (m * half_h + i + 1) * half_w)
                a_zero[s, at, :] = value[begin : begin + half_w]
                h_zero[s, at, :] = curved[begin : begin + half_w]
            total = total + product(curved.astype(jnp.bfloat16), w_down[s])
        coarse_all[...] = total
        for i in range(half_h):
            begin = (i + REACH) * all_w + SIDE
            at = slice((m * half_h + i) * half_w, (m * half_h + i + 1) * half_w)
            coarse[at, :] = coarse_all[begin : begin + half_w, :]
        if m == batch - 1:
            copies[1].start()
            copies[2].start()
        padded[m] = coarse_all[...].astype(jnp.bfloat16).reshape(padded.shape[1:])

    @pl.when(r == 0)
    def _():
        padded[:, 0:REACH] = jnp.zeros((batch, REACH) + padded.shape[2:], padded.dtype)

    @pl.when(r == nr - 1)
    def _():
        padded[:, all_h - REACH :] = jnp.zeros((batch, REACH) + padded.shape[2:], padded.dtype)

    for copy in copies:
        copy.wait()


def input_part(nr, state, w_in, w_down, vector):
    batch, rows, breadth, _ = state.shape
    half_h, half_w = rows // 2 - FINE_REACH, breadth // 2 - EDGE
    all_h, all_w = half_h + 2 * REACH, half_w + 2 * SIDE
    cells = batch * half_h * half_w
    vmem = pl.BlockSpec(memory_space=pltpu.VMEM)
    hbm = pl.BlockSpec(memory_space=pl.ANY)
    large = (
        jax.ShapeDtypeStruct((4, cells, 9 * CIP), jnp.bfloat16),
        jax.ShapeDtypeStruct((4, cells, C0P), jnp.float32),
        jax.ShapeDtypeStruct((4, cells, C0P), jnp.float32),
    )
    return pl.pallas_call(
        functools.partial(input_kernel, nr),
        out_shape=large
        + (
            jax.ShapeDtypeStruct((cells, C1P), jnp.float32),
            jax.ShapeDtypeStruct((batch, all_h, all_w, C1P), jnp.bfloat16),
            jax.ShapeDtypeStruct((16, CH), jnp.float32),
        ),
        in_specs=[vmem] * 4,
        out_specs=(hbm, hbm, hbm, vmem, vmem, vmem),
        scratch_shapes=[
            pltpu.VMEM((batch, rows, breadth + 2 * SIDE, CIP), jnp.float32),
            pltpu.VMEM((4, batch * all_h * all_w, 9 * CIP), jnp.bfloat16),
            pltpu.VMEM((all_h * all_w, C1P), jnp.float32),
        ]
        + [pltpu.VMEM(shape.shape, shape.dtype) for shape in large]
        + [pltpu.SemaphoreType.DMA((3,))],
        compiler_params=pltpu.CompilerParams(vmem_limit_bytes=60 << 20),
    )(state, w_in, w_down, vector)


def spread_lanes(padded, held):
    for m in range(padded.shape[0]):
        def body(y, carry, m=m):
            for u in range(C1P // LANES):
                held[u, m, y, 0 : padded.shape[2], :] = padded[m, y, :, u * LANES : (u + 1) * LANES].astype(jnp.float32)
            return carry

        lax.fori_loop(0, padded.shape[1], body, 0)


def convolve(held, w_dw, half_w, edge, put, back):
    tiles, batch, rows = held.shape[:3]
    height = rows - 2 * REACH

    def body(number, carry):
        u, m = number // batch, number % batch
        sums = [jnp.zeros((half_w, LANES), jnp.float32) for _ in range(height)]
        for x in range(7):
            for y in range(rows):
                window = held[u, m, y, pl.ds(edge - REACH + x, half_w), :]
                for i in range(height):
                    if 0 <= y - i < 7:
                        tap = (6 - (y - i)) * 7 + 6 - x if back else (y - i) * 7 + x
                        sums[i] = sums[i] + window * w_dw[pl.ds(tap, 1), lanes_at(u)]
        for i in range(height):
            put(u, m, i, sums[i])
        return carry

    lax.fori_loop(0, tiles * batch, body, 0)


def rows_at(m, i, height, half_w):
    return pl.ds(pl.multiple_of((m * height + i) * half_w, half_w), half_w)


def lanes_at(u):
    return pl.ds(pl.multiple_of(u * LANES, LANES), LANES)


PART = 640


LATE = ("coarse", "h_zero", "target", "weight", "w_hidden", "w_out_t", "w_up")
EARLY = ("normed", "act", "grad_mixed", "grad_branch", "grad_summed", "d_up")


def middle_kernel(names, *refs):
    ref = dict(zip(names, refs))
    batch, rows, breadth, _ = ref["padded"].shape
    cells = ref["coarse"].shape[0]
    height, half_w = rows - 2 * REACH, breadth - 2 * SIDE
    fetch, store, held_in, held_out = {}, {}, {}, {}
    for i, name in enumerate(LATE):
        held_in[name] = ref["held_" + name]
        fetch[name] = pltpu.make_async_copy(ref[name], held_in[name], ref["sem_in"].at[i])
        fetch[name].start()
    for i, name in enumerate(EARLY):
        held_out[name] = ref["held_" + name]
        store[name] = pltpu.make_async_copy(held_out[name], ref[name], ref["sem_out"].at[i])
    conv = ref["conv"]

    def depthwise(held):
        spread_lanes(ref["padded"], held)

        def put(u, m, i, value):
            conv[rows_at(m, i, height, half_w), lanes_at(u)] = value

        convolve(held, ref["w_dw"], half_w, SIDE, put, False)

    pl.run_scoped(depthwise, pltpu.VMEM((C1P // LANES, batch, rows, breadth, LANES), jnp.float32))
    pl.run_scoped(
        functools.partial(pointwise_part, ref, fetch, store, held_in, held_out),
        pltpu.VMEM((cells, CH), jnp.float32),
        pltpu.VMEM((cells, C1), jnp.bfloat16),
    )
    for name in EARLY:
        store[name].wait()


def pointwise_part(ref, fetch, store, held_in, held_out, pre, spread_all):
    conv, total, sums, extra = ref["conv"], ref["total"], ref["sums"], ref["extra"]
    gain, w_head = ref["lines"].at[3:4, 0:C1P], ref["w_head"]
    normed, act = held_out["normed"], held_out["act"]
    grad_mixed, grad_branch, grad_summed = (
        held_out[name] for name in ("grad_mixed", "grad_branch", "grad_summed")
    )
    w_hidden, w_out_t, w_up = (held_in[name] for name in ("w_hidden", "w_out_t", "w_up"))
    target, weight, h_zero = (held_in[name] for name in ("target", "weight", "h_zero"))
    batch, rows, breadth, _ = ref["padded"].shape
    height, half_w = rows - 2 * REACH, breadth - 2 * SIDE

    inside = lax.broadcasted_iota(jnp.int32, (1, C1P), 1) < C1
    values = conv[...] + ref["lines"][2:3, :C1P]
    mean = jnp.sum(values, axis=1, keepdims=True) * (1.0 / C1)
    centered = jnp.where(inside, values - mean, 0.0)
    scale = lax.rsqrt(jnp.sum(centered * centered, axis=1, keepdims=True) * (1.0 / C1) + 1e-06)
    conv[...] = centered * scale
    normed[...] = (conv[...] * gain[...] + ref["lines"][4:5, :C1P]).astype(jnp.bfloat16)
    store["normed"].start()

    fetch["coarse"].wait()
    fetch["w_hidden"].wait()
    fetch["w_out_t"].wait()
    total[...] = held_in["coarse"][...]
    for begin in range(0, CH, PART):
        span = slice(begin, begin + PART)
        value = product(normed[:, :C1], w_hidden[:, span]) + ref["lines"][5:6, span]
        pre[:, span] = value
        act[:, span] = gelu(value).astype(jnp.bfloat16)
        total[:, :C1] += product_t(act[:, span], w_out_t[:, span])
    store["act"].start()
    mixed = (total[...] + ref["lines"][6:7, :C1P]).astype(jnp.bfloat16)

    for name in ("h_zero", "target", "weight", "w_up"):
        fetch[name].wait()
    grad_mixed[...] = jnp.zeros_like(grad_mixed)
    loss = jnp.zeros((1, CI), jnp.float32)
    head_sum = jnp.zeros((1, CI), jnp.float32)
    up_sum = jnp.zeros((1, C0), jnp.float32)
    for s in range(4):
        sub_y, sub_x = divmod(s, 2)
        for m in range(batch):
            for i in range(height):
                at = rows_at(m, i, height, half_w)
                line = pl.ds(sub_x, half_w, stride=2)
                ref["goal"][at, :] = target[m, 2 * i + sub_y, line, :]
                ref["load"][at, :] = weight[2 * i + sub_y, line, :]
        w_up_s = w_up[:, s * C0 : (s + 1) * C0]
        upper = product(mixed[:, :C1], w_up_s) + ref["lines"][7:8, :C0]
        summed = (upper + h_zero[s, :, :C0]).astype(jnp.bfloat16)
        error = product(summed, w_head[...]) + ref["lines"][8:9, :CI] - ref["goal"][:, :CI]
        weighted = ref["load"][:, :CI] * error
        loss = loss + column_sum(weighted * error)
        grad_out = (2.0 * weighted).astype(jnp.bfloat16)
        head_sum = head_sum + column_sum(grad_out)
        if s == 0:
            ref["d_head"][...] = inner_rows(summed, grad_out)
        else:
            ref["d_head"][...] += inner_rows(summed, grad_out)
        spread = product_t(grad_out, w_head[...])
        grad_summed[s] = spread
        grad_upper = spread.astype(jnp.bfloat16)
        up_sum = up_sum + column_sum(grad_upper)
        spread_all[:, s * C0 : (s + 1) * C0] = grad_upper
        grad_mixed[:, :C1] += product_t(grad_upper, w_up_s)
    store["grad_summed"].start()
    store["grad_mixed"].start()
    held_out["d_up"][...] = inner_rows(mixed[:, :C1], spread_all[...])
    store["d_up"].start()
    grad_branch[...] = grad_mixed[...].astype(jnp.bfloat16)
    store["grad_branch"].start()
    sums[...] = jnp.zeros_like(sums)
    extra[...] = jnp.zeros_like(extra)
    extra[0:1, 0:CI] = loss
    extra[1:2, :] = column_sum(ref["weight_map"][...])
    sums[1:2, 0:CI] = head_sum
    sums[2:3, 0:C0] = up_sum
    sums[3:4, 0:C1P] = column_sum(grad_branch[...])

    total[...] = jnp.zeros_like(total)
    for begin in range(0, CH, PART):
        span = slice(begin, begin + PART)
        value = product(grad_branch[:, :C1], w_out_t[:, span]) * gelu_slope(pre[:, span])
        low = value.astype(jnp.bfloat16)
        ref["grad_pre"][:, span] = low
        sums[4:5, span] = column_sum(low)
        total[:, :C1] += product_t(low, w_hidden[:, span])

    grad_normed = total[...]
    sums[5:6, 0:C1P] = column_sum(grad_normed * conv[...])
    sums[6:7, 0:C1P] = column_sum(grad_normed)
    inward = grad_normed * gain[...]
    first = jnp.sum(inward, axis=1, keepdims=True) * (1.0 / C1)
    second = jnp.sum(inward * conv[...], axis=1, keepdims=True) * (1.0 / C1)
    value = scale * jnp.where(inside, inward - first - conv[...] * second, 0.0)
    low = value.astype(jnp.bfloat16)
    sums[7:8, 0:C1P] = column_sum(low)
    ref["grad_conv"][...] = low.reshape(ref["grad_conv"].shape)


def middle_part(**given):
    cells = given["coarse"].shape[0]
    batch, rows, breadth, _ = given["padded"].shape
    half_h, half_w = rows - 2 * REACH, breadth - 2 * SIDE
    vmem = pl.BlockSpec(memory_space=pltpu.VMEM)
    hbm = pl.BlockSpec(memory_space=pl.ANY)
    f32, low = jnp.float32, jnp.bfloat16
    outs = {
        "normed": ((cells, C1P), low),
        "act": ((cells, CH), low),
        "grad_pre": ((cells, CH), low),
        "grad_mixed": ((cells, C1P), f32),
        "grad_branch": ((cells, C1P), low),
        "grad_summed": ((4, cells, C0), f32),
        "grad_conv": ((batch, half_h, half_w, C1P), low),
        "d_up": ((C1, C1), f32),
        "d_head": ((C0, CI), f32),
        "sums": ((8, CH), f32),
        "extra": ((8, LANES), f32),
    }
    scratch = {
        "conv": pltpu.VMEM((cells, C1P), f32),
        "total": pltpu.VMEM((cells, C1P), f32),
        "goal": pltpu.VMEM((cells, LANES), f32),
        "load": pltpu.VMEM((cells, LANES), f32),
        "sem_in": pltpu.SemaphoreType.DMA((len(LATE),)),
        "sem_out": pltpu.SemaphoreType.DMA((len(EARLY),)),
    }
    for name in LATE:
        scratch["held_" + name] = pltpu.VMEM(given[name].shape, given[name].dtype)
    for name in EARLY:
        scratch["held_" + name] = pltpu.VMEM(*outs[name])
    found = pl.pallas_call(
        functools.partial(middle_kernel, tuple(given) + tuple(outs) + tuple(scratch)),
        out_shape=tuple(jax.ShapeDtypeStruct(*out) for out in outs.values()),
        in_specs=[hbm if name in LATE else vmem for name in given],
        out_specs=tuple(hbm if name in EARLY else vmem for name in outs),
        scratch_shapes=list(scratch.values()),
        compiler_params=pltpu.CompilerParams(vmem_limit_bytes=62 << 20),
    )(*given.values())
    return dict(zip(outs, found))


AFTER = ("grad_mixed", "grad_summed", "a_zero", "h_zero", "taps", "w_down")


def outer_kernel(names, *refs):
    ref = dict(zip(names, refs))
    fetch = {}
    for i, name in enumerate(AFTER):
        fetch[name] = pltpu.make_async_copy(ref[name], ref["held_" + name], ref["sem_in"].at[i])
        fetch[name].start()
    grad_mixed, grad_summed, a_zero, h_zero, taps, w_down = (ref["held_" + name] for name in AFTER)
    held, conv, sums, d_dw, d_in = (ref[name] for name in ("held", "conv", "sums", "d_dw", "d_in"))
    vector = ref["vector"]
    grad_conv = ref["grad_conv"]
    batch, height, half_w, _ = grad_conv.shape
    spread_lanes(ref["padded"], held)
    tiles = C1P // LANES
    d_dw[...] = jnp.zeros_like(d_dw)

    def taps_of(number, carry):
        u, m = number // batch, number % batch
        grads = [grad_conv[m, i, :, lanes_at(u)].astype(jnp.float32) for i in range(height)]
        for x in range(7):
            found = [jnp.zeros((8, LANES), jnp.float32) for _ in range(7)]
            for y in range(height + 6):
                window = held[u, m, y, pl.ds(SIDE - REACH + x, half_w), :]
                for i in range(height):
                    if 0 <= y - i < 7:
                        term = (window * grads[i]).reshape(half_w // 8, 8, LANES)
                        found[y - i] = found[y - i] + jnp.sum(term, axis=0)
            for dy in range(7):
                d_dw[pl.ds(dy * 7 + x, 1), lanes_at(u)] += jnp.sum(found[dy], axis=0, keepdims=True)
        return carry

    lax.fori_loop(0, tiles * batch, taps_of, 0)
    spread_lanes(ref["grad_padded"], held)

    def put(u, m, i, value):
        conv[rows_at(m, i, height, half_w), lanes_at(u)] = value

    convolve(held, ref["w_dw"], half_w, EDGE, put, True)
    for name in AFTER:
        fetch[name].wait()
    grad_coarse = (conv[...] + grad_mixed[...]).astype(jnp.bfloat16)
    vector[...] = jnp.zeros_like(vector)
    pieces = [(column_sum(grad_coarse), C1)] + [(sums[i : i + 1, :], C1) for i in (7, 5, 6)]
    pieces += [(sums[4:5, :], CH), (sums[3:4, :], C1), (sums[2:3, :], C0), (sums[1:2, :], CI)]
    start = C0
    for piece, size in pieces:
        vector[:, start : start + size] = piece[:, :size]
        start = start + size
    in_sum = jnp.zeros((1, C0), jnp.float32)
    for s in range(4):
        ref["d_down"][s * C0 : (s + 1) * C0, :] = inner_rows(
            h_zero[s].astype(jnp.bfloat16), grad_coarse
        )[:C0]
        grad_h = product_t(grad_coarse, w_down[s])[:, :C0] + grad_summed[s]
        grad_a = (gelu_slope(a_zero[s, :, :C0]) * grad_h).astype(jnp.bfloat16)
        in_sum = in_sum + column_sum(grad_a)
        if s == 0:
            d_in[...] = inner_rows(taps[s], grad_a)
        else:
            d_in[...] += inner_rows(taps[s], grad_a)
    vector[:, 0:C0] = in_sum


def outer_part(length, **given):
    cells = given["grad_mixed"].shape[0]
    batch, rows, breadth, _ = given["grad_padded"].shape
    vmem = pl.BlockSpec(memory_space=pltpu.VMEM)
    hbm = pl.BlockSpec(memory_space=pl.ANY)
    f32 = jnp.float32
    outs = {
        "d_dw": ((56, C1P), f32),
        "d_down": ((C1, C1P), f32),
        "d_in": ((9 * CIP, C0), f32),
        "vector": ((1, length), f32),
    }
    scratch = {
        "held": pltpu.VMEM((C1P // LANES, batch, rows, breadth, LANES), f32),
        "conv": pltpu.VMEM((cells, C1P), f32),
        "sem_in": pltpu.SemaphoreType.DMA((len(AFTER),)),
    }
    for name in AFTER:
        scratch["held_" + name] = pltpu.VMEM(given[name].shape, given[name].dtype)
    found = pl.pallas_call(
        functools.partial(outer_kernel, tuple(given) + tuple(outs) + tuple(scratch)),
        out_shape=tuple(jax.ShapeDtypeStruct(*out) for out in outs.values()),
        in_specs=[hbm if name in AFTER else vmem for name in given],
        out_specs=tuple([vmem] * len(outs)),
        scratch_shapes=list(scratch.values()),
        compiler_params=pltpu.CompilerParams(vmem_limit_bytes=60 << 20),
    )(*given.values())
    return dict(zip(outs, found))


def as_rows(piece, rows):
    flat = piece.reshape(-1)
    return jnp.pad(flat, (0, rows * LANES - flat.shape[0])).reshape(rows, LANES)


def widened(array, *shape):
    return jnp.pad(array, [(0, full - now) for full, now in zip(shape, array.shape)])


def on_device(
    inputs,
    targets,
    land_mask,
    volume,
    date_index,
    perm_narrow,
    perm_wide,
    w_in,
    w_down,
    w_dw,
    w_hidden,
    w_out,
    w_up,
    w_head,
    biases_gains,
    moment_first,
    moment_second,
):
    rows, cols = lax.axis_size("rows"), lax.axis_size("cols")
    weight = land_mask.astype(jnp.float32) * volume
    height, breadth = weight.shape
    half_h, half_w = (height // 2, breadth // 2)
    cells = MB * half_h * half_w
    matrices = (w_in, w_down, w_dw, w_hidden, w_out, w_up, w_head)

    def dates(field):
        picked = jnp.concatenate(
            [lax.dynamic_slice_in_dim(field, date_index[m], 1, 0, allow_negative_indices=False) for m in range(MB)]
        )
        return widened(picked, MB, height, breadth, CIP)

    w_in_p = widened(w_in.reshape(9, CI, C0), 9, CIP, C0P).reshape(9 * CIP, C0P)
    w_down_p = widened(w_down.reshape(4, C0, C1), 4, C0P, C1P)
    w_dw_p = widened(w_dw.astype(jnp.float32), 56, C1P)
    weight_map = jnp.broadcast_to(weight[:, :, None], (height, breadth, LANES))

    state = halo(rows, cols, FINE_REACH, dates(inputs), 1)
    taps, a_zero, h_zero, coarse, padded, lines = input_part(
        rows, state, w_in_p, w_down_p, biases_gains[None, :]
    )
    mid = middle_part(
        padded=padded, coarse=coarse, h_zero=h_zero, target=dates(targets).astype(jnp.float32),
        weight=weight_map, weight_map=weight, w_dw=w_dw_p, w_hidden=w_hidden, w_out_t=w_out.T,
        w_up=w_up, w_head=w_head, lines=lines,
    )
    space = Plan(rows, cols, PADDED).space
    grad, grad_padded = place_gradients(
        rows, cols, space, mid["normed"], mid["grad_branch"], mid["grad_pre"], mid["act"],
        perm_narrow, perm_wide, mid["d_up"], mid["grad_conv"],
    )
    out = outer_part(
        (space - ROW_AT[7]) * LANES,
        padded=padded, grad_padded=grad_padded, grad_conv=mid["grad_conv"],
        grad_mixed=mid["grad_mixed"], grad_summed=mid["grad_summed"], a_zero=a_zero, h_zero=h_zero,
        taps=taps, w_dw=w_dw_p, w_down=w_down_p, sums=mid["sums"],
    )
    d_in = out["d_in"].reshape(9, CIP, C0)[:, :CI].reshape(9 * CI, C0)
    pieces = (
        jnp.pad(as_rows(d_in, ROW_AT[1] - ROW_AT[0]), ((ROW_AT[0], 0), (0, 0))),
        as_rows(out["d_dw"][:49, :C1], ROW_AT[3] - ROW_AT[2]),
        as_rows(mid["d_head"], ROW_AT[7] - ROW_AT[6]),
        out["vector"].reshape(-1, LANES),
    )
    grad = complete_gradients(grad, out["d_down"], pieces)
    plan, (gathered, first, second, totals) = exchange(
        rows, cols, grad, moment_first, moment_second, mid["extra"]
    )
    hidden_p, out_p, new_up, new_down, small_a, small_b, small_c = unpack(plan, gathered, w_up, w_down, perm_narrow, perm_wide)
    small = {0: (small_a, 0), 2: (small_b, 1), 6: (small_c, 2), 7: (small_c, 2)}
    whole = {
        1: new_down,
        3: rebuild_hidden(hidden_p, perm_wide, w_hidden),
        4: rebuild_out(out_p, perm_narrow, w_out),
        5: new_up,
    }
    olds = matrices + (biases_gains,)
    news = []
    for index, old in enumerate(olds):
        if index in whole:
            news.append(whole[index])
        else:
            source, which = small[index]
            start = FLAT_AT[index] - KEPT[which][0] * LANES
            piece = source.reshape(-1)[start : start + old.size].reshape(old.shape)
            news.append(moved(old, piece) if index < 7 else old - learn_rate * piece)
    return tuple(news) + (
        first.reshape(-1),
        second.reshape(-1),
        totals[0, 0],
        MB * CI * totals[1, 0],
        totals[8, 0],
    )


def solution(mesh):
    return jax.shard_map(
        on_device,
        mesh=mesh,
        in_specs=(
            P(None, "rows", "cols", None),
            P(None, "rows", "cols", None),
            P("rows", "cols"),
            P("rows", "cols"),
            P(),
            P(),
            P(),
            P(),
            P(),
            P(),
            P(),
            P(),
            P(),
            P(),
            P(),
            P(("rows", "cols")),
            P(("rows", "cols")),
        ),
        out_specs=(
            P(),
            P(),
            P(),
            P(),
            P(),
            P(),
            P(),
            P(),
            P(("rows", "cols")),
            P(("rows", "cols")),
            P(),
            P(),
            P(),
        ),
        check_vma=False,
    )
```

```python
import functools

import jax
import jax.numpy as jnp
from jax import lax
from jax.experimental import pallas as pl
from jax.experimental.pallas import tpu as pltpu
from jax.sharding import PartitionSpec as P

CI = 77
C0 = 200
C1 = 800
CH = 3200
MB = 2
STEP = 5
LANES = 128
MESH = pl.DeviceIdType.MESH
ROUNDER = 12582912.0

decay_first = 0.9
decay_second = 0.99
epsilon = 1e-08
learn_rate = 0.02
weight_decay = 0.1
clip_limit = 1.0

VEC = 4 * C1 + CH + C1 + 2 * C0 + CI
SIZES = (9 * CI * C0, 4 * C0 * C1, 49 * C1, C1 * CH, CH * C1, C1 * 4 * C0, C0 * CI, VEC)
PADDED = 6602752
FLAT_AT = []
ROW_AT = []
for size in SIZES:
    flat_here = FLAT_AT[-1] + SIZES[len(FLAT_AT) - 1] if FLAT_AT else PADDED - sum(SIZES)
    row_here = ROW_AT[-1] + -(-SIZES[len(ROW_AT) - 1] // 1024) * 8 if ROW_AT else 0
    row_here = max(row_here, -(-flat_here // 1024) * 8)
    FLAT_AT.append(flat_here)
    ROW_AT.append(row_here)
SHIFTS = []
for flat_here, row_here, size in zip(FLAT_AT, ROW_AT, SIZES):
    moved = divmod(row_here * LANES - flat_here, LANES)
    if SHIFTS and SHIFTS[-1][:2] == moved:
        SHIFTS[-1] = moved + (SHIFTS[-1][2], flat_here + size)
    else:
        SHIFTS.append(moved + (flat_here, flat_here + size))
MAX_SHIFT = max(s[0] for s in SHIFTS) + 1


def bit_masks(bits):
    masks = [()]
    for bit in bits:
        masks = masks + [m + (bit,) for m in masks]
    return sorted(masks, key=lambda m: -len(m))


class Plan:
    def __init__(self, rows, cols, total):
        self.rows, self.cols, self.count = rows, cols, rows * cols
        self.share = total // LANES // self.count
        self.bits = rows.bit_length() - 1
        need = 7 + self.share + MAX_SHIFT + 1
        self.block = 64 if need > 1024 else 32
        self.window = -(-need // (2 * self.block)) * 2 * self.block
        self.part = self.window // 2
        self.blocks = self.part // self.block
        self.scales = self.blocks
        upper = list(range(1, self.bits))
        self.orders = [upper, upper[1:] + upper[:1]]
        self.stages = len(upper)
        self.space = (self.share * (self.count - 1)) // 8 * 8 + self.window
        self.padded = -(-self.share // 16) * 16
        cut = -(-self.padded // 32) * 16
        self.cuts = [(0, cut), (cut, self.padded - cut)]
        self.local = self.count // 2


def exchange_kernel(
    plan, grad, m_first, m_second, extra, full, first, second, totals,
    acc, near, q_send, q_recv, s_send, s_recv, z_send, z_recv, zs_send, zs_recv,
    rolled, step, low, stats,
    sem_load, sem_near_s, sem_near_r, sem_qs, sem_qr, sem_ss, sem_sr,
    sem_zs, sem_zr, sem_zss, sem_zsr, sem_ts, sem_tr, sem_own,
    sem_gs, sem_gr, sem_hs, sem_hr, sem_cs, sem_cr,
):
    nr, nc, n = plan.rows, plan.cols, plan.count
    r = lax.axis_index("rows")
    c = lax.axis_index("cols")
    me = r * nc + c
    part, window, share = plan.part, plan.window, plan.share

    def flipped(mask):
        out = r
        for bit in mask:
            here = (r // (1 << bit)) % 2
            out = out + (1 - 2 * here) * (1 << bit)
        return out

    def remote(src, dst, send, recv, row, col):
        return pltpu.make_async_remote_copy(
            src_ref=src, dst_ref=dst, send_sem=send, recv_sem=recv,
            device_id=(row, col), device_id_type=MESH,
        )

    barrier = pltpu.get_barrier_semaphore()

    def greet(d, carry):
        k = lax.rem(me + d, n)
        pl.semaphore_signal(barrier, inc=1, device_id=(k // nc, k % nc), device_id_type=MESH)
        return carry

    lax.fori_loop(1, n, greet, 0)
    pl.semaphore_wait(barrier, n - 1)

    upper = list(range(1, plan.bits))
    masks = bit_masks(upper)

    def local_index(mask, col):
        return (flipped(mask) // 2) * nc + col

    def window_start(row, col):
        return pl.multiple_of((share * (row * nc + col)) // 8 * 8, 8)

    def near_copy(mask, col):
        row = flipped(mask + (0,))
        return remote(
            grad.at[pl.ds(window_start(row, col), window)],
            near.at[local_index(mask, col)],
            sem_near_s.at[local_index(mask, col)], sem_near_r.at[local_index(mask, col)],
            flipped((0,)), c,
        )

    def load_copy(mask, col):
        index = local_index(mask, col)
        return pltpu.make_async_copy(
            grad.at[pl.ds(window_start(flipped(mask), col), window)], acc.at[index], sem_load.at[index]
        )

    half_way = nc // 2

    def column_of(t):
        return jnp.where(t == 1, half_way, jnp.where(t <= half_way, t - 1, t))

    def begin(t, carry):
        col = lax.rem(c + column_of(t), nc)
        for mask in masks:
            near_copy(mask, col).start()
            load_copy(mask, col).start()
        return carry

    lax.fori_loop(1, nc + 1, begin, 0)

    def encode(index, p, q_ref, s_ref):
        def body(b, carry):
            at = pl.ds(pl.multiple_of(b * plan.block, plan.block), plan.block)
            rows_at = pl.ds(pl.multiple_of(p * part + b * plan.block, 8), plan.block)
            values = acc[index, rows_at, :]
            top = jnp.maximum(jnp.max(jnp.abs(values), axis=0, keepdims=True), 1e-30)
            scaled = values * (32766.0 / top)
            scaled = (scaled + ROUNDER) - ROUNDER
            q_ref[at, :] = scaled.astype(jnp.int32).astype(jnp.int16)
            s_ref[pl.ds(b, 1), :] = top * (1.0 / 32766.0)
            return carry

        lax.fori_loop(0, plan.blocks, body, 0)

    def decode(index, p, q_ref, s_ref):
        def body(b, carry):
            at = pl.ds(pl.multiple_of(b * plan.block, plan.block), plan.block)
            rows_at = pl.ds(pl.multiple_of(p * part + b * plan.block, 8), plan.block)
            acc[index, rows_at, :] += q_ref[at, :].astype(jnp.float32) * s_ref[pl.ds(b, 1), :]
            return carry

        lax.fori_loop(0, plan.blocks, body, 0)

    def stage_base(stage):
        return sum((1 << (plan.stages - 1 - s)) for s in range(stage)) * nc

    def hop(p, stage, slot):
        row = flipped((plan.orders[p][stage],))
        at = stage_base(stage) + slot
        return (
            remote(q_send.at[p, at], q_recv.at[p, at], sem_qs.at[p, at], sem_qr.at[p, at], row, c),
            remote(s_send.at[p, at], s_recv.at[p, at], sem_ss.at[p, at], sem_sr.at[p, at], row, c),
        )

    def send_stage(p, stage, number, mask, col):
        bit = plan.orders[p][stage]
        index = local_index(mask + (bit,), col)
        slot = number * nc + col
        at = stage_base(stage) + slot
        encode(index, p, q_send.at[p, at], s_send.at[p, at])
        for copy in hop(p, stage, slot):
            copy.start()

    def take_stage(p, stage, number, mask, col):
        slot = number * nc + col
        for copy in hop(p, stage, slot):
            copy.wait_recv()
        at = stage_base(stage) + slot
        decode(local_index(mask, col), p, q_recv.at[p, at], s_recv.at[p, at])

    def free_masks(p, stage):
        rest = plan.orders[p][stage + 1 :]
        found = bit_masks(rest)
        if rest:
            found = [m for m in found if rest[0] in m] + [m for m in found if rest[0] not in m]
        return found

    def far_copy(p, d):
        col = lax.rem(c + d, nc)
        return (
            remote(z_send.at[p, d - 1], z_recv.at[p, d - 1], sem_zs.at[p, d - 1], sem_zr.at[p, d - 1], r, col),
            remote(zs_send.at[p, d - 1], zs_recv.at[p, d - 1], sem_zss.at[p, d - 1], sem_zsr.at[p, d - 1], r, col),
        )

    def join(t):
        d = column_of(t)
        col = lax.rem(c + d, nc)
        for mask in masks:
            index = local_index(mask, col)
            near_copy(mask, col).wait_recv()
            load_copy(mask, col).wait()

            def body(b, inner, index=index):
                at = pl.ds(pl.multiple_of(b * plan.block, plan.block), plan.block)
                acc[index, at, :] += near[index, at, :]
                return inner

            lax.fori_loop(0, 2 * plan.blocks, body, 0)
            for p in range(2):
                bit = plan.orders[p][0]
                if bit in mask:
                    rest = tuple(b for b in mask if b != bit)
                    options = free_masks(p, 0)
                    number = [sorted(o) for o in options].index(sorted(rest))
                    send_stage(p, 0, number, rest, col)

    def take(stage, t):
        d = column_of(t)
        col = lax.rem(c + d, nc)
        for number in range(1 << (plan.stages - 1 - stage)):
            for p in range(2):
                mask = free_masks(p, stage)[number]
                take_stage(p, stage, number, mask, col)
                if stage + 1 < plan.stages:
                    bit = plan.orders[p][stage + 1]
                    if bit in mask:
                        rest = tuple(b for b in mask if b != bit)
                        options = free_masks(p, stage + 1)
                        following = [sorted(o) for o in options].index(sorted(rest))
                        send_stage(p, stage + 1, following, rest, col)
                else:
                    @pl.when(d < nc)
                    def _(p=p):
                        encode(local_index((), col), p, z_send.at[p, d - 1], zs_send.at[p, d - 1])
                        for copy in far_copy(p, d):
                            copy.start()

    mine = local_index((), c)

    def gather_far(d, carry):
        for p in range(2):
            for copy in far_copy(p, d):
                copy.wait_recv()
            decode(mine, p, z_recv.at[p, d - 1], zs_recv.at[p, d - 1])
        return carry


    def turn_of(t, carry):
        @pl.when(t <= nc)
        def _():
            join(t)

        for stage in range(plan.stages):
            d = t - 1 - stage

            @pl.when((d >= 1) & (d <= nc))
            def _(stage=stage, d=d):
                take(stage, d)

        @pl.when((t > nc) & (t - nc < nc))
        def _():
            gather_far(column_of(t - nc), 0)

        return carry

    lax.fori_loop(1, nc + plan.stages + 1, turn_of, 0)

    def gather_rest(q, carry):
        return gather_far(column_of(q), carry)

    lax.fori_loop(min(plan.stages + 1, nc), nc, gather_rest, 0)

    offset = lax.rem(share * me, 8)
    low_end, high_end = share * me * LANES, share * (me + 1) * LANES
    for number, (shift_rows, shift_lanes, begin, end) in enumerate(SHIFTS):
        def turn(b, carry, number=number, shift_lanes=shift_lanes):
            at = pl.ds(pl.multiple_of(b * plan.block, plan.block), plan.block)
            rolled[number, at, :] = pltpu.roll(acc[mine, at, :], LANES - shift_lanes, 1)
            return carry

        @pl.when((low_end < end) & (high_end > begin))
        def _(turn=turn):
            lax.fori_loop(0, 2 * plan.blocks, turn, 0)

    def share_rows(start, length, chosen):
        lane = lax.broadcasted_iota(jnp.int32, (length, LANES), 1)
        out = jnp.zeros((length, LANES), jnp.float32)
        if len(chosen) > 1:
            line = lax.broadcasted_iota(jnp.int32, (length, LANES), 0)
            flat = (share * me + start + line) * LANES + lane
        for number in chosen:
            shift_rows, shift_lanes, begin, end = SHIFTS[number]
            here = rolled[number, pl.ds(offset + start + shift_rows, length), :]
            after = rolled[number, pl.ds(offset + start + shift_rows + 1, length), :]
            value = jnp.where(lane < LANES - shift_lanes, here, after)
            if len(chosen) > 1:
                value = jnp.where((flat >= begin) & (flat < end), value, out)
            out = value
        return out

    chunk = 32
    whole, tail = share // chunk, share % chunk
    stats[me, 8:16, :] = extra[...]

    def squares(chosen):
        def square(b, total):
            start = pl.multiple_of(b * chunk, chunk)
            value = share_rows(start, chunk, chosen)
            step[pl.ds(start, chunk), :] = value
            return total + jnp.sum((value * value).reshape(chunk // 8, 8, LANES), axis=0)

        total = lax.fori_loop(0, whole, square, jnp.zeros((8, LANES), jnp.float32))
        stats[me, 0:8, :] = total
        if tail:
            value = share_rows(whole * chunk, tail, chosen)
            step[whole * chunk : share, :] = value
            stats[me, 0:1, :] += jnp.sum(value * value, axis=0, keepdims=True)

    largest = max(range(len(SHIFTS)), key=lambda i: SHIFTS[i][3] - SHIFTS[i][2])
    alone = (low_end >= SHIFTS[largest][2]) & (high_end <= SHIFTS[largest][3])

    @pl.when(alone)
    def _():
        squares((largest,))

    @pl.when(jnp.logical_not(alone))
    def _():
        squares(tuple(range(len(SHIFTS))))

    def stat_copy(target, source):
        return remote(
            stats.at[me], stats.at[me], sem_ts.at[target], sem_tr.at[me], target // nc, target % nc
        )

    def stat_wait(source):
        return remote(
            stats.at[source], stats.at[source], sem_ts.at[source], sem_tr.at[source],
            source // nc, source % nc,
        )

    def send_stat(d, carry):
        stat_copy(lax.rem(me + d, n), me).start()
        return carry

    lax.fori_loop(1, n, send_stat, 0)

    def wait_stat(d, carry):
        stat_wait(lax.rem(me + d, n)).wait_recv()
        return carry

    lax.fori_loop(1, n, wait_stat, 0)

    def add_stat(k, total):
        return total + stats[k]

    sums = lax.fori_loop(0, n, add_stat, jnp.zeros((16, LANES), jnp.float32))
    norm = jnp.sqrt(jnp.sum(sums[0:8], keepdims=True))
    totals[0:1, :] = jnp.broadcast_to(jnp.sum(sums[8:9], keepdims=True), (1, LANES))
    totals[1:2, :] = jnp.broadcast_to(jnp.sum(sums[9:10], keepdims=True), (1, LANES))
    totals[2:8, :] = jnp.zeros((6, LANES), jnp.float32)
    totals[8:16, :] = jnp.broadcast_to(norm, (8, LANES))
    clip = jnp.minimum(1.0, clip_limit / norm)

    def update(start, length):
        clipped = step[pl.ds(start, length), :] * clip
        one = decay_first * m_first[pl.ds(start, length), :] + (1.0 - decay_first) * clipped
        two = decay_second * m_second[pl.ds(start, length), :] + (1.0 - decay_second) * clipped * clipped
        first[pl.ds(start, length), :] = one
        second[pl.ds(start, length), :] = two
        step[pl.ds(start, length), :] = (
            one / (1.0 - decay_first**STEP) / (jnp.sqrt(two / (1.0 - decay_second**STEP)) + epsilon)
        )

    def update_chunk(b, carry):
        update(pl.multiple_of(b * chunk, chunk), chunk)
        return carry

    lax.fori_loop(0, whole, update_chunk, 0)
    if tail:
        update(whole * chunk, tail)
    if plan.padded > share:
        step[share : plan.padded, :] = jnp.zeros((plan.padded - share, LANES), jnp.float32)

    def narrow(b, carry):
        at = pl.ds(pl.multiple_of(b * 16, 16), 16)
        low[at, :] = step[at, :].astype(jnp.bfloat16)
        return carry

    lax.fori_loop(0, plan.padded // 16, narrow, 0)

    own = pltpu.make_async_copy(low, full.at[me], sem_own)
    own.start()
    own.wait()

    back = [list(reversed(order)) for order in plan.orders]

    def piece(mask, col, p):
        begin, length = plan.cuts[p]
        return full.at[flipped(mask) * nc + col, pl.ds(begin, length)]

    def along(direction, col, p, receive):
        step_col = 1 if direction == 0 else -1
        target = c - step_col if receive else c + step_col
        ref = piece((), col, p)
        return remote(ref, ref, sem_gs.at[direction, col, p], sem_gr.at[direction, col, p], r, target)

    def gather_masks(p, stage):
        return bit_masks(back[p][:stage])

    def gather_base(stage):
        return sum(1 << s for s in range(stage)) * nc

    def across(p, stage, number, mask, col):
        at = gather_base(stage) + number * nc + col
        ref = piece(mask, col, p)
        return remote(ref, ref, sem_hs.at[p, at], sem_hr.at[p, at], flipped((back[p][stage],)), c)

    def across_recv(p, stage, number, mask, col):
        at = gather_base(stage) + number * nc + col
        ref = piece(mask + (back[p][stage],), col, p)
        return remote(ref, ref, sem_hs.at[p, at], sem_hr.at[p, at], flipped((back[p][stage],)), c)

    def inward(p, mask, col):
        number = masks.index(tuple(sorted(mask)))
        at = number * nc + col
        ref = piece(mask, col, p)
        return remote(ref, ref, sem_cs.at[p, at], sem_cr.at[p, at], flipped((0,)), c)

    def inward_recv(p, mask, col):
        number = masks.index(tuple(sorted(mask)))
        at = number * nc + col
        ref = piece(mask + (0,), col, p)
        return remote(ref, ref, sem_cs.at[p, at], sem_cr.at[p, at], flipped((0,)), c)

    def spread(p, mask, col, stage):
        for later in range(stage, plan.stages):
            options = [sorted(o) for o in gather_masks(p, later)]
            if sorted(mask) in options:
                across(p, later, options.index(sorted(mask)), mask, col).start()
        inward(p, mask, col).start()

    def near_cols(t):
        if t == 0:
            return [(0, c)]
        return [(0, c - t), (1, c + t)]

    def inside(col):
        return (col >= 0) & (col < nc)

    for time in range(nc + plan.stages):
        for stage in range(plan.stages + 1):
            t = time - stage
            if not 0 <= t < nc:
                continue
            if stage == 0:
                if t == 0:
                    for p in range(2):
                        @pl.when(c < nc - 1)
                        def _(p=p):
                            along(0, c, p, False).start()

                        @pl.when(c > 0)
                        def _(p=p):
                            along(1, c, p, False).start()

                        spread(p, (), c, 0)
                else:
                    for direction, col in near_cols(t):
                        @pl.when(inside(col))
                        def _(direction=direction, col=col):
                            for p in range(2):
                                along(direction, col, p, True).wait_recv()
                                if direction == 0:
                                    @pl.when(c < nc - 1)
                                    def _():
                                        along(0, col, p, False).start()
                                else:
                                    @pl.when(c > 0)
                                    def _():
                                        along(1, col, p, False).start()
                                spread(p, (), col, 0)
            else:
                for direction, col in near_cols(t):
                    @pl.when(inside(col))
                    def _(col=col, stage=stage):
                        for number in range(1 << (stage - 1)):
                            for p in range(2):
                                mask = gather_masks(p, stage - 1)[number]
                                across_recv(p, stage - 1, number, mask, col).wait_recv()
                                spread(p, mask + (back[p][stage - 1],), col, stage)

    for mask in masks:
        def finish(col, carry, mask=mask):
            for p in range(2):
                inward_recv(p, mask, col).wait_recv()
                inward(p, mask, col).wait_send()
            near_copy(mask, col).wait_send()
            return carry

        lax.fori_loop(0, nc, finish, 0)
    for p in range(2):
        for stage in range(plan.stages):
            for number, mask in enumerate(gather_masks(p, stage)):
                def sent(col, carry, p=p, stage=stage, number=number, mask=mask):
                    across(p, stage, number, mask, col).wait_send()
                    return carry

                lax.fori_loop(0, nc, sent, 0)
            for number in range(1 << (plan.stages - 1 - stage)):
                def left(col, carry, p=p, stage=stage, number=number):
                    for copy in hop(p, stage, number * nc + col):
                        copy.wait_send()
                    return carry

                lax.fori_loop(0, nc, left, 0)

        def gone(col, carry, p=p):
            @pl.when((col <= c) & (c < nc - 1))
            def _():
                along(0, col, p, False).wait_send()

            @pl.when((col >= c) & (c > 0))
            def _():
                along(1, col, p, False).wait_send()

            return carry

        lax.fori_loop(0, nc, gone, 0)

        def far_gone(d, carry, p=p):
            for copy in far_copy(p, d):
                copy.wait_send()
            return carry

        lax.fori_loop(1, nc, far_gone, 0)

    def stat_gone(d, carry):
        stat_copy(lax.rem(me + d, n), me).wait_send()
        return carry

    lax.fori_loop(1, n, stat_gone, 0)


def exchange(rows, cols, grad, m_first, m_second, extra):
    plan = Plan(rows, cols, m_first.size * rows * cols)
    n, nc, share = plan.count, plan.cols, plan.share
    hops = sum(1 << s for s in range(plan.stages)) * nc
    dma = pltpu.SemaphoreType.DMA
    far = max(nc - 1, 1)
    vmem = pl.BlockSpec(memory_space=pltpu.VMEM)
    hbm = pl.BlockSpec(memory_space=pl.ANY)
    return plan, pl.pallas_call(
        functools.partial(exchange_kernel, plan),
        out_shape=(
            jax.ShapeDtypeStruct((n, plan.padded, LANES), jnp.bfloat16),
            jax.ShapeDtypeStruct((share, LANES), jnp.float32),
            jax.ShapeDtypeStruct((share, LANES), jnp.float32),
            jax.ShapeDtypeStruct((16, LANES), jnp.float32),
        ),
        in_specs=[hbm, vmem, vmem, vmem],
        out_specs=(hbm, vmem, vmem, vmem),
        scratch_shapes=[
            pltpu.VMEM((plan.local, plan.window, LANES), jnp.float32),
            pltpu.VMEM((plan.local, plan.window, LANES), jnp.float32),
            pltpu.VMEM((2, hops, plan.part, LANES), jnp.int16),
            pltpu.VMEM((2, hops, plan.part, LANES), jnp.int16),
            pltpu.VMEM((2, hops, plan.scales, LANES), jnp.float32),
            pltpu.VMEM((2, hops, plan.scales, LANES), jnp.float32),
            pltpu.VMEM((2, far, plan.part, LANES), jnp.int16),
            pltpu.VMEM((2, far, plan.part, LANES), jnp.int16),
            pltpu.VMEM((2, far, plan.scales, LANES), jnp.float32),
            pltpu.VMEM((2, far, plan.scales, LANES), jnp.float32),
            pltpu.VMEM((len(SHIFTS), plan.window, LANES), jnp.float32),
            pltpu.VMEM((plan.padded, LANES), jnp.float32),
            pltpu.VMEM((plan.padded, LANES), jnp.bfloat16),
            pltpu.VMEM((n, 16, LANES), jnp.float32),
            dma((plan.local,)), dma((plan.local,)), dma((plan.local,)),
            dma((2, hops)), dma((2, hops)), dma((2, hops)), dma((2, hops)),
            dma((2, far)), dma((2, far)), dma((2, far)), dma((2, far)),
            dma((n,)), dma((n,)), dma,
            dma((2, nc, 2)), dma((2, nc, 2)),
            dma((2, hops)), dma((2, hops)),
            dma((2, plan.local)), dma((2, plan.local)),
        ],
        compiler_params=pltpu.CompilerParams(
            collective_id=0, has_side_effects=True, vmem_limit_bytes=56 << 20
        ),
    )(grad, m_first.reshape(share, LANES), m_second.reshape(share, LANES), extra)


WIDE = CH + LANES
KEPT = ((8, 1104), (6096, 6408), (51400, 51584))
PLACES = tuple(divmod(FLAT_AT[i], LANES) for i in (3, 4, 5, 1))

SLOTS = 6
HALF = WIDE // 2
PITCH = 33


def unpack_kernel(
    plan, gathered, old_up, old_down, narrow, wide, hidden_out, rows_out, up_out, down_out, small_a, small_b, small_c,
    held, flat, woven, hidden, by_row, rows_low, up, down, sems, sem_out,
):
    n, share = plan.count, plan.share
    step = CH // LANES

    def fetch(k, slot):
        return pltpu.make_async_copy(gathered.at[k], held.at[slot], sems.at[slot])

    for k in range(SLOTS - 1):
        fetch(k, k).start()

    def widen(k, carry):
        slot = lax.rem(k, SLOTS)

        @pl.when(k + SLOTS - 1 < n)
        def _():
            fetch(k + SLOTS - 1, lax.rem(k + SLOTS - 1, SLOTS)).start()

        fetch(k, slot).wait()

        def body(b, inner):
            at = pl.ds(pl.multiple_of(b * 16, 16), 16)
            flat[pl.ds(share * k + b * 16, 16), :] = held[slot, at, :].astype(jnp.float32)
            return inner

        lax.fori_loop(0, plan.padded // 16, body, 0, unroll=4)
        return carry

    lax.fori_loop(0, n, widen, 0)

    copies = [
        pltpu.make_async_copy(source, target, sem_out.at[i])
        for i, (source, target) in enumerate(
            (
                (hidden, hidden_out.at[:, pl.ds(0, HALF)]), (rows_low, rows_out), (up, up_out),
                (down, down_out), (hidden, hidden_out.at[:, pl.ds(HALF, HALF)]),
            )
        )
    ]
    row, lane = PLACES[0]

    def spread(a, carry):
        by_row[pl.ds(narrow[a] * PITCH, 32), :] = flat[pl.ds(row + a * step, 32), :]
        return carry

    lax.fori_loop(0, C1, spread, 0, unroll=4)

    def columns(half):
        def column(t, carry):
            for begin in range(0, C1, 160):
                at = begin * PITCH + half * (HALF // LANES) + t
                values = by_row[pl.ds(at, 160, stride=PITCH), :]
                at = pl.ds(pl.multiple_of(t * LANES, LANES), LANES)
                hidden[begin : begin + 160, at] = values.astype(jnp.bfloat16)
            return carry

        lax.fori_loop(0, HALF // LANES, column, 0)

    columns(0)
    copies[0].start()

    quarter = C1 // 4
    for number, (ref, old, (line, begin)) in enumerate(zip((up, down), (old_up, old_down), PLACES[2:])):
        for u in range(-(-C1 // LANES)):
            width = min(LANES, C1 - u * LANES)
            place = lax.broadcasted_iota(jnp.int32, (quarter, LANES), 1)
            for b in range(4):
                first, rest = divmod(C1 * b + begin, LANES)
                here = flat[pl.ds(line + first + u, quarter, stride=step), :]
                after = flat[pl.ds(line + first + u + 1, quarter, stride=step), :]
                value = pltpu.roll(jnp.where(place >= rest, here, after), LANES - rest, 1)
                woven[pl.ds(b, quarter, stride=4), :] = value
            at = slice(u * LANES, u * LANES + width)
            ref[:, at] = moved(old[:, at], woven[:, :width])
        copies[2 + number].start()

    for ref, (begin, end) in zip((small_a, small_b, small_c), KEPT):
        ref[...] = flat[begin:end, :]
    copies[0].wait()
    columns(1)
    copies[4].start()

    row, lane = PLACES[1]

    def align(part, carry):
        place = lax.broadcasted_iota(jnp.int32, (40, LANES), 1)
        for b in range(4):
            first, rest = divmod(C1 * b + lane, LANES)
            tiles = [
                flat[pl.ds(row + part * (40 * step) + first + u, 40, stride=step), :]
                for u in range(C1P // LANES + 1)
            ]
            values = [
                pltpu.roll(jnp.where(place >= rest, here, after), LANES - rest, 1)
                for here, after in zip(tiles, tiles[1:])
            ]
            for u, value in enumerate(values):
                flat[pl.ds(part * (40 * PITCH) + b * 8 + u, 40, stride=PITCH), :] = value
        return carry

    lax.fori_loop(0, C1 // 40, align, 0)

    def scatter(a, carry):
        for b in range(4):
            by_row[pl.ds(wide[a * 4 + b] * 9, 8), :] = flat[pl.ds(a * PITCH + b * 8, 8), :]
        return carry

    lax.fori_loop(0, CH // 4, scatter, 0, unroll=4)

    def by_lane(part, carry):
        for u in range(C1P // LANES):
            values = by_row[pl.ds(part * (160 * 9) + u, 160, stride=9), :]
            at = pl.ds(pl.multiple_of(part * 160, 160), 160)
            rows_low[at, u * LANES : (u + 1) * LANES] = values.astype(jnp.bfloat16)
        return carry

    lax.fori_loop(0, CH // 160, by_lane, 0)
    copies[1].start()
    for copy in copies[1:]:
        copy.wait()


def unpack(plan, gathered, old_up, old_down, narrow, wide):
    lines = PADDED // LANES
    vmem = pl.BlockSpec(memory_space=pltpu.VMEM)
    hbm = pl.BlockSpec(memory_space=pl.ANY)
    dma = pltpu.SemaphoreType.DMA
    f32, low = jnp.float32, jnp.bfloat16
    return pl.pallas_call(
        functools.partial(unpack_kernel, plan),
        out_shape=(
            jax.ShapeDtypeStruct((C1, WIDE), low),
            jax.ShapeDtypeStruct((CH, C1P), low),
            jax.ShapeDtypeStruct((C1, C1), f32),
            jax.ShapeDtypeStruct((C1, C1), f32),
        )
        + tuple(jax.ShapeDtypeStruct((end - begin, LANES), f32) for begin, end in KEPT),
        in_specs=[hbm, vmem, vmem] + [pl.BlockSpec(memory_space=pltpu.SMEM)] * 2,
        out_specs=(hbm, hbm, hbm, hbm, vmem, vmem, vmem),
        scratch_shapes=[
            pltpu.VMEM((SLOTS, plan.padded, LANES), low),
            pltpu.VMEM((-(-lines // 8) * 8 + 16, LANES), f32),
            pltpu.VMEM((C1, LANES), f32),
            pltpu.VMEM((C1, HALF), low),
            pltpu.VMEM((CH * 9, LANES), f32),
            pltpu.VMEM((CH, C1P), low),
            pltpu.VMEM((C1, C1), f32),
            pltpu.VMEM((C1, C1), f32),
            dma((SLOTS,)),
            dma((5,)),
        ],
        compiler_params=pltpu.CompilerParams(vmem_limit_bytes=63 << 20),
    )(gathered, old_up, old_down, narrow, wide)


def moved(old, direction):
    return old.astype(jnp.float32) * (1.0 - learn_rate * weight_decay) - learn_rate * direction


def one_hot(condition):
    return jnp.where(condition, 1.0, 0.0).astype(jnp.bfloat16)


def product(left, right):
    return jnp.dot(left, right, preferred_element_type=jnp.float32)


def product_t(left, right):
    return lax.dot_general(left, right, (((1,), (1,)), ((), ())), preferred_element_type=jnp.float32)


TILE = 512
STEPS = -(-CH // TILE)
LAST = CH - (STEPS - 1) * TILE


DEEP = 256


def by_width(body):
    final = pl.program_id(0) == STEPS - 1

    @pl.when(jnp.logical_not(final))
    def _():
        body(TILE)

    @pl.when(final)
    def _():
        body(LAST)


def hidden_kernel(lines, wide, old, new):
    depth = lines.shape[1]
    base = pl.program_id(0) * TILE

    def body(width):
        direction = None
        for begin in range(0, depth, DEEP):
            end = min(begin + DEEP, depth)
            place = wide[begin:end, :] - base
            lane = lax.broadcasted_iota(jnp.int32, (end - begin, LANES), 1)
            hot = jnp.concatenate([one_hot(lane + u == place) for u in range(0, width, LANES)], axis=1)
            term = product(lines[:, begin:end], hot)
            direction = term if direction is None else direction + term
        new[:, :width] = moved(old[:, :width], direction)

    by_width(body)


def rebuild_hidden(lines, wide, old):
    lane = PLACES[0][1]
    wide = jnp.full((WIDE,), -1, jnp.int32).at[lane : lane + CH].set(wide)
    return pl.pallas_call(
        hidden_kernel,
        out_shape=jax.ShapeDtypeStruct((C1, CH), jnp.float32),
        grid=(STEPS,),
        in_specs=[
            pl.BlockSpec((C1, WIDE), lambda i: (0, 0)),
            pl.BlockSpec((WIDE, LANES), lambda i: (0, 0)),
            pl.BlockSpec((C1, TILE), lambda i: (0, i)),
        ],
        out_specs=pl.BlockSpec((C1, TILE), lambda i: (0, i)),
        compiler_params=pltpu.CompilerParams(vmem_limit_bytes=48 << 20),
    )(lines, jnp.broadcast_to(wide[:, None], (WIDE, LANES)), old)


def out_kernel(rows, narrow, old, new, turn):
    @pl.when(pl.program_id(0) == 0)
    def _():
        turn[...] = one_hot(lax.broadcasted_iota(jnp.int32, (C1, C1), 0) == narrow[...])

    def body(width):
        new[:, :width] = moved(old[:, :width], product_t(turn[...], rows[:width, :C1]))

    by_width(body)


def rebuild_out(rows, narrow, old):
    return pl.pallas_call(
        out_kernel,
        out_shape=jax.ShapeDtypeStruct((C1, CH), jnp.float32),
        grid=(STEPS,),
        in_specs=[
            pl.BlockSpec((TILE, C1P), lambda i: (i, 0)),
            pl.BlockSpec((1, C1), lambda i: (0, 0)),
            pl.BlockSpec((C1, TILE), lambda i: (0, i)),
        ],
        out_specs=pl.BlockSpec((C1, TILE), lambda i: (0, i)),
        scratch_shapes=[pltpu.VMEM((C1, C1), jnp.bfloat16)],
        compiler_params=pltpu.CompilerParams(vmem_limit_bytes=48 << 20),
    )(rows, narrow[None, :], old.T).T


def weave(source, rows, put):
    for t in range(CH // LANES):
        b, begin = divmod(t * LANES, C1)
        u, rest = divmod(begin, LANES)
        place = lax.broadcasted_iota(jnp.int32, (rows, LANES), 1)
        value = source[u, pl.ds(b, rows, stride=4), :]
        if rest:
            if begin + LANES - rest < C1:
                after = source[u + 1, pl.ds(b, rows, stride=4), :]
                value = jnp.where(place >= rest, value, after)
            value = pltpu.roll(value, LANES - rest, 1)
        left = C1 - begin
        if left < LANES:
            following = source[0, pl.ds(b + 1, rows, stride=4), :]
            value = jnp.where(place < left, value, pltpu.roll(following, left, 1))
        put(t, value)


def place_kernel(
    nr, nc, normed, branch, pre, act, narrow_row, narrow_col, wide, up, cells,
    grad, padded, hidden, out, loose, up_rows, norm_t, branch_r, halo_cells, held_pre, held_act,
    sem_out, sems, sem_halo_s, sem_halo_r, sem_in,
):
    step = pl.program_id(0)
    steps = STEPS
    ratio = CH // LANES

    def out_copy(n, width):
        begin = n * (TILE // 4 * ratio)
        rows = width // 4 * ratio
        return pltpu.make_async_copy(
            out.at[pl.ds(pl.multiple_of(begin, 8), rows)],
            grad.at[pl.ds(pl.multiple_of(ROW_AT[4] + begin, 8), rows)],
            sem_out.at[n],
        )

    copies = [
        pltpu.make_async_copy(ref, grad.at[pl.ds(row, ref.shape[0])], sems.at[i])
        for i, (ref, row) in enumerate(((up_rows, ROW_AT[5]), (hidden, ROW_AT[3])))
    ] + [pltpu.make_async_copy(halo_cells, padded, sems.at[2])]

    fetch_pre = pltpu.make_async_copy(pre, held_pre, sem_in.at[0])
    fetch_act = pltpu.make_async_copy(act, held_act, sem_in.at[1])

    @pl.when(step == 0)
    def _():
        fetch_pre.start()
        fetch_act.start()
        halo_start(nr, nc, 3, cells, halo_cells, sem_halo_s, sem_halo_r)
        line = lax.broadcasted_iota(jnp.int32, (C1, C1), 1)
        norm_t[...] = product_t(one_hot(line == narrow_col[:, 0:1]), normed[:, :C1]).astype(jnp.bfloat16)
        line = lax.broadcasted_iota(jnp.int32, (C1, C1P), 0)
        branch_r[...] = product(branch[:, :C1], one_hot(line == narrow_row[...])).astype(jnp.bfloat16)
        for u in range(-(-C1 // LANES)):
            width = min(LANES, C1 - u * LANES)
            loose[u, :, 0:width] = up[0:C1, u * LANES : u * LANES + width]

        def put(t, value):
            up_rows[pl.ds(t, C1 // 4, stride=ratio), :] = value

        weave(loose, C1 // 4, put)
        copies[0].start()
        fetch_pre.wait()
        fetch_act.wait()

    def body(width):
        turned_pre = turned_act = None
        for begin in range(0, CH, DEEP):
            end = min(begin + DEEP, CH)
            line = lax.broadcasted_iota(jnp.int32, (end - begin, width), 0) + begin
            hot = one_hot(line == wide[:, :width])
            one = product(held_pre[:, begin:end], hot)
            two = product(held_act[:, begin:end], hot)
            turned_pre = one if turned_pre is None else turned_pre + one
            turned_act = two if turned_act is None else turned_act + two
        part = product(norm_t[...], turned_pre.astype(jnp.bfloat16))
        for t in range(width // LANES):
            at = pl.ds(step * (TILE // LANES) + t, C1, stride=ratio)
            hidden[at, :] = part[:, t * LANES : (t + 1) * LANES]
        part = inner_rows(turned_act.astype(jnp.bfloat16), branch_r[...])
        for u in range(-(-C1 // LANES)):
            loose[u, 0:width, :] = part[:, u * LANES : (u + 1) * LANES]

        def put_out(t, value):
            out[pl.ds(step * (TILE // 4 * ratio) + t, width // 4, stride=ratio), :] = value

        weave(loose, width // 4, put_out)
        out_copy(step, width).start()

    by_width(body)

    @pl.when(step == steps - 1)
    def _():
        copies[1].start()
        halo_finish(nr, nc, 3, cells, halo_cells, sem_halo_s, sem_halo_r)
        copies[2].start()

        def finish(n, carry):
            out_copy(n, TILE).wait()
            return carry

        lax.fori_loop(0, steps - 1, finish, 0)
        out_copy(steps - 1, LAST).wait()
        for copy in copies:
            copy.wait()


def place_gradients(nr, nc, space, normed, branch, pre, act, narrow, wide, up, cells):
    def whole(array):
        return pl.BlockSpec(
            array.shape, lambda i: (0,) * len(array.shape), pipeline_mode=pl.Buffered(1)
        )

    hbm = pl.BlockSpec(memory_space=pl.ANY)
    rows = pre.shape[0]
    batch, height, breadth, chans = cells.shape
    narrow_row = jnp.pad(narrow, (0, C1P - C1), constant_values=-1)[None, :]
    narrow_col = jnp.broadcast_to(narrow[:, None], (C1, LANES))
    framed = jax.ShapeDtypeStruct((batch, height + 6, breadth + 2 * EDGE, chans), cells.dtype)
    dma = pltpu.SemaphoreType.DMA
    return pl.pallas_call(
        functools.partial(place_kernel, nr, nc),
        out_shape=(jax.ShapeDtypeStruct((space, LANES), jnp.float32), framed),
        grid=(STEPS,),
        in_specs=[
            whole(normed), whole(branch), hbm, hbm, whole(narrow_row), whole(narrow_col),
            pl.BlockSpec((1, TILE), lambda i: (0, i)),
            whole(up), whole(cells),
        ],
        out_specs=(hbm, hbm),
        scratch_shapes=[
            pltpu.VMEM((C1 * CH // LANES, LANES), jnp.float32),
            pltpu.VMEM((C1 * CH // LANES, LANES), jnp.float32),
            pltpu.VMEM((C1P // LANES, C1, LANES), jnp.float32),
            pltpu.VMEM((C1 * C1 // LANES, LANES), jnp.float32),
            pltpu.VMEM((C1, rows), jnp.bfloat16),
            pltpu.VMEM((rows, C1P), jnp.bfloat16),
            pltpu.VMEM(framed.shape, framed.dtype),
            pltpu.VMEM(pre.shape, pre.dtype),
            pltpu.VMEM(act.shape, act.dtype),
            dma((STEPS,)), dma((3,)), dma((8,)), dma((8,)), dma((2,)),
        ],
        compiler_params=pltpu.CompilerParams(
            collective_id=3, has_side_effects=True, vmem_limit_bytes=60 << 20
        ),
    )(normed, branch, pre, act, narrow_row, narrow_col, wide[None, :], up, cells)


def complete_kernel(before, down, piece_in, piece_dw, piece_head, piece_vec, grad, loose, down_rows, sems):
    copies = [
        pltpu.make_async_copy(ref, grad.at[pl.ds(row, ref.shape[0])], sems.at[i])
        for i, (ref, row) in enumerate(
            (
                (piece_in, 0), (piece_dw, ROW_AT[2]), (piece_head, ROW_AT[6]), (piece_vec, ROW_AT[7]),
                (down_rows, ROW_AT[1]),
            )
        )
    ]
    for copy in copies[:4]:
        copy.start()
    for u in range(C1P // LANES):
        loose[u] = down[:, u * LANES : (u + 1) * LANES]

    def put(t, value):
        down_rows[pl.ds(t, C1 // 4, stride=CH // LANES), :] = value

    weave(loose, C1 // 4, put)
    copies[4].start()
    for copy in copies:
        copy.wait()


def complete_gradients(grad, down, pieces):
    vmem = pl.BlockSpec(memory_space=pltpu.VMEM)
    hbm = pl.BlockSpec(memory_space=pl.ANY)
    return pl.pallas_call(
        complete_kernel,
        out_shape=jax.ShapeDtypeStruct(grad.shape, grad.dtype),
        in_specs=[hbm, vmem, vmem, vmem, vmem, vmem],
        out_specs=hbm,
        input_output_aliases={0: 0},
        scratch_shapes=[
            pltpu.VMEM((C1P // LANES, C1, LANES), jnp.float32),
            pltpu.VMEM((C1 * C1 // LANES, LANES), jnp.float32),
            pltpu.SemaphoreType.DMA((5,)),
        ],
        compiler_params=pltpu.CompilerParams(vmem_limit_bytes=60 << 20),
    )(grad, down, *pieces)


C0P = 256
C1P = 896
CIP = 128
EDGE = 16
CURVE = 0.7978845608028654
CUBE = 0.044715


def inner_rows(left, right):
    return lax.dot_general(left, right, (((0,), (0,)), ((), ())), preferred_element_type=jnp.float32)


def column_sum(values):
    return jnp.sum(values.astype(jnp.float32), axis=0, keepdims=True)


def gelu_and_slope(t):
    square = t * t
    bend = jnp.tanh(CURVE * (t + CUBE * (square * t)))
    half = 0.5 * (1.0 + bend)
    return t * half, half + 0.5 * t * (1.0 - bend * bend) * (CURVE * (1.0 + 3.0 * CUBE * square))


WAYS = [(dr, dc) for dr in (-1, 0, 1) for dc in (-1, 0, 1) if (dr, dc) != (0, 0)]
ORDER = sorted(range(8), key=lambda i: (WAYS[i][1] != 0, WAYS[i][0] == 0))


def halo_place(nr, nc):
    r = lax.axis_index("rows")
    return r, lax.axis_index("cols"), lambda dr: (r + dr >= 0) & (r + dr < nr)


def halo_copy(nr, nc, width, cells, out, sem_s, sem_r, i, receive):
    r, c, there = halo_place(nr, nc)
    height, breadth = cells.shape[1], cells.shape[2]
    dr, dc = WAYS[i]
    rows_from = {-1: (0, width), 0: (0, height), 1: (height - width, width)}[dr]
    rows_to = {-1: height + width, 0: width, 1: 0}[dr]
    cols_from = {-1: (0, EDGE), 0: (0, breadth), 1: (breadth - EDGE, EDGE)}[dc]
    cols_to = {-1: EDGE + breadth, 0: EDGE, 1: 0}[dc]
    sign = -1 if receive else 1
    return pltpu.make_async_remote_copy(
        src_ref=cells.at[:, pl.ds(*rows_from), pl.ds(*cols_from)],
        dst_ref=out.at[:, pl.ds(rows_to, rows_from[1]), pl.ds(cols_to, cols_from[1])],
        send_sem=sem_s.at[i],
        recv_sem=sem_r.at[i],
        device_id=(r + sign * dr, lax.rem(c + sign * dc + nc, nc)),
        device_id_type=MESH,
    )


def halo_start(nr, nc, width, cells, out, sem_s, sem_r):
    r, c, there = halo_place(nr, nc)
    height, breadth = cells.shape[1], cells.shape[2]
    barrier = pltpu.get_barrier_semaphore()
    for dr, dc in WAYS:
        @pl.when(there(dr))
        def _(dr=dr, dc=dc):
            pl.semaphore_signal(
                barrier, inc=1, device_id=(r + dr, lax.rem(c + dc + nc, nc)), device_id_type=MESH
            )

    edge = (r == 0) | (r == nr - 1)

    @pl.when(edge)
    def _():
        pl.semaphore_wait(barrier, 5)

    @pl.when(jnp.logical_not(edge))
    def _():
        pl.semaphore_wait(barrier, 8)

    for i in ORDER:
        @pl.when(there(WAYS[i][0]))
        def _(i=i):
            halo_copy(nr, nc, width, cells, out, sem_s, sem_r, i, False).start()

    for m in range(cells.shape[0]):
        for row in range(height):
            out[m, width + row, EDGE : EDGE + breadth, :] = cells[m, row]

    @pl.when(r == 0)
    def _():
        out[:, 0:width] = jnp.zeros((out.shape[0], width) + out.shape[2:], out.dtype)

    @pl.when(r == nr - 1)
    def _():
        out[:, height + width :] = jnp.zeros((out.shape[0], width) + out.shape[2:], out.dtype)


def halo_finish(nr, nc, width, cells, out, sem_s, sem_r):
    r, c, there = halo_place(nr, nc)
    for i in ORDER:
        @pl.when(there(-WAYS[i][0]))
        def _(i=i):
            halo_copy(nr, nc, width, cells, out, sem_s, sem_r, i, True).wait_recv()

        @pl.when(there(WAYS[i][0]))
        def _(i=i):
            halo_copy(nr, nc, width, cells, out, sem_s, sem_r, i, False).wait_send()


def halo_kernel(nr, nc, width, cells, out, sem_s, sem_r):
    halo_start(nr, nc, width, cells, out, sem_s, sem_r)
    halo_finish(nr, nc, width, cells, out, sem_s, sem_r)


def halo(nr, nc, width, cells, identity):
    batch, height, breadth, chans = cells.shape
    vmem = pl.BlockSpec(memory_space=pltpu.VMEM)
    return pl.pallas_call(
        functools.partial(halo_kernel, nr, nc, width),
        out_shape=jax.ShapeDtypeStruct(
            (batch, height + 2 * width, breadth + 2 * EDGE, chans), cells.dtype
        ),
        in_specs=[vmem],
        out_specs=vmem,
        scratch_shapes=[pltpu.SemaphoreType.DMA((8,)), pltpu.SemaphoreType.DMA((8,))],
        compiler_params=pltpu.CompilerParams(
            collective_id=identity, has_side_effects=True, vmem_limit_bytes=24 << 20
        ),
    )(cells)


SIDE = 8
REACH = 3
FINE_REACH = 2 * REACH + 1


def input_kernel(
    nr, state, w_in, w_down, vector, taps_out, slope_zero_out, h_zero_out, coarse, padded, lines,
    wide, taps_all, coarse_all, taps, slope_zero, h_zero, sems,
):
    r = lax.axis_index("rows")
    copies = [
        pltpu.make_async_copy(source, target, sems.at[i])
        for i, (source, target) in enumerate(((taps, taps_out), (slope_zero, slope_zero_out), (h_zero, h_zero_out)))
    ]
    lines[...] = jnp.zeros_like(lines)
    start = 0
    for number, size in enumerate((C0, C1, C1, C1, C1, CH, C1, C0, CI)):
        lines[number : number + 1, 0:size] = vector[:, start : start + size]
        start = start + size
    batch, rows, breadth, _ = state.shape
    half_h, half_w = rows // 2 - FINE_REACH, breadth // 2 - EDGE
    all_h, all_w = half_h + 2 * REACH, half_w + 2 * SIDE
    for m in range(batch):
        for y in range(rows):
            wide[m, y, SIDE : SIDE + breadth, :] = state[m, y].astype(jnp.float32)
    for m in range(batch):
        for y in range(rows):
            for f in range(4):
                start = SIDE + EDGE - 2 * SIDE - 1 + f
                line = wide[m, y, pl.ds(start, all_w, stride=2), :]
                low = line.astype(jnp.bfloat16)
                inner = line[SIDE : SIDE + half_w].astype(jnp.bfloat16)
                for dy in range(3):
                    i, sy = divmod(y - dy, 2)
                    if not 0 <= i < all_h:
                        continue
                    for dx in range(3):
                        if not 0 <= f - dx < 2:
                            continue
                        s, tap = sy * 2 + f - dx, slice((dy * 3 + dx) * CIP, (dy * 3 + dx + 1) * CIP)
                        begin = (m * all_h + i) * all_w
                        taps_all[s, begin : begin + all_w, tap] = low
                        if REACH <= i < REACH + half_h:
                            begin = (m * half_h + i - REACH) * half_w
                            taps[s, begin : begin + half_w, tap] = inner
    copies[0].start()
    size = all_h * all_w
    for m in range(batch):
        block = slice(m * size, (m + 1) * size)
        total = jnp.broadcast_to(lines[1:2, :C1P], (size, C1P))
        for s in range(4):
            value = product(taps_all[s, block, :], w_in[...]) + lines[0:1, :C0P]
            curved, slope = gelu_and_slope(value)
            for i in range(half_h):
                begin = (i + REACH) * all_w + SIDE
                at = slice((m * half_h + i) * half_w, (m * half_h + i + 1) * half_w)
                slope_zero[s, at, :] = slope[begin : begin + half_w]
                h_zero[s, at, :] = curved[begin : begin + half_w]
            total = total + product(curved.astype(jnp.bfloat16), w_down[s])
        coarse_all[...] = total
        for i in range(half_h):
            begin = (i + REACH) * all_w + SIDE
            at = slice((m * half_h + i) * half_w, (m * half_h + i + 1) * half_w)
            coarse[at, :] = coarse_all[begin : begin + half_w, :]
        if m == batch - 1:
            copies[1].start()
            copies[2].start()
        padded[m] = coarse_all[...].astype(jnp.bfloat16).reshape(padded.shape[1:])

    @pl.when(r == 0)
    def _():
        padded[:, 0:REACH] = jnp.zeros((batch, REACH) + padded.shape[2:], padded.dtype)

    @pl.when(r == nr - 1)
    def _():
        padded[:, all_h - REACH :] = jnp.zeros((batch, REACH) + padded.shape[2:], padded.dtype)

    for copy in copies:
        copy.wait()


def input_part(nr, state, w_in, w_down, vector):
    batch, rows, breadth, _ = state.shape
    half_h, half_w = rows // 2 - FINE_REACH, breadth // 2 - EDGE
    all_h, all_w = half_h + 2 * REACH, half_w + 2 * SIDE
    cells = batch * half_h * half_w
    vmem = pl.BlockSpec(memory_space=pltpu.VMEM)
    hbm = pl.BlockSpec(memory_space=pl.ANY)
    large = (
        jax.ShapeDtypeStruct((4, cells, 9 * CIP), jnp.bfloat16),
        jax.ShapeDtypeStruct((4, cells, C0P), jnp.float32),
        jax.ShapeDtypeStruct((4, cells, C0P), jnp.float32),
    )
    return pl.pallas_call(
        functools.partial(input_kernel, nr),
        out_shape=large
        + (
            jax.ShapeDtypeStruct((cells, C1P), jnp.float32),
            jax.ShapeDtypeStruct((batch, all_h, all_w, C1P), jnp.bfloat16),
            jax.ShapeDtypeStruct((16, CH), jnp.float32),
        ),
        in_specs=[vmem] * 4,
        out_specs=(hbm, hbm, hbm, vmem, vmem, vmem),
        scratch_shapes=[
            pltpu.VMEM((batch, rows, breadth + 2 * SIDE, CIP), jnp.float32),
            pltpu.VMEM((4, batch * all_h * all_w, 9 * CIP), jnp.bfloat16),
            pltpu.VMEM((all_h * all_w, C1P), jnp.float32),
        ]
        + [pltpu.VMEM(shape.shape, shape.dtype) for shape in large]
        + [pltpu.SemaphoreType.DMA((3,))],
        compiler_params=pltpu.CompilerParams(vmem_limit_bytes=60 << 20),
    )(state, w_in, w_down, vector)


def spread_lanes(padded, held):
    for m in range(padded.shape[0]):
        def body(y, carry, m=m):
            for u in range(C1P // LANES):
                held[u, m, y, 0 : padded.shape[2], :] = padded[m, y, :, u * LANES : (u + 1) * LANES].astype(jnp.float32)
            return carry

        lax.fori_loop(0, padded.shape[1], body, 0)


def convolve(held, w_dw, half_w, edge, put, back):
    tiles, batch, rows = held.shape[:3]
    height = rows - 2 * REACH

    def body(number, carry):
        u, m = number // batch, number % batch
        sums = [jnp.zeros((half_w, LANES), jnp.float32) for _ in range(height)]
        for x in range(7):
            for y in range(rows):
                window = held[u, m, y, pl.ds(edge - REACH + x, half_w), :]
                for i in range(height):
                    if 0 <= y - i < 7:
                        tap = (6 - (y - i)) * 7 + 6 - x if back else (y - i) * 7 + x
                        sums[i] = sums[i] + window * w_dw[pl.ds(tap, 1), lanes_at(u)]
        for i in range(height):
            put(u, m, i, sums[i])
        return carry

    lax.fori_loop(0, tiles * batch, body, 0)


def rows_at(m, i, height, half_w):
    return pl.ds(pl.multiple_of((m * height + i) * half_w, half_w), half_w)


def lanes_at(u):
    return pl.ds(pl.multiple_of(u * LANES, LANES), LANES)


PART = 640


LATE = ("coarse", "h_zero", "target", "weight", "w_hidden", "w_out_t", "w_up")
EARLY = ("normed", "act", "grad_mixed", "grad_branch", "grad_summed", "d_up")


def middle_kernel(names, *refs):
    ref = dict(zip(names, refs))
    batch, rows, breadth, _ = ref["padded"].shape
    cells = ref["coarse"].shape[0]
    height, half_w = rows - 2 * REACH, breadth - 2 * SIDE
    fetch, store, held_in, held_out = {}, {}, {}, {}
    for i, name in enumerate(LATE):
        held_in[name] = ref["held_" + name]
        fetch[name] = pltpu.make_async_copy(ref[name], held_in[name], ref["sem_in"].at[i])
        fetch[name].start()
    for i, name in enumerate(EARLY):
        held_out[name] = ref["held_" + name]
        store[name] = pltpu.make_async_copy(held_out[name], ref[name], ref["sem_out"].at[i])
    conv = ref["conv"]

    def depthwise(held):
        spread_lanes(ref["padded"], held)

        def put(u, m, i, value):
            conv[rows_at(m, i, height, half_w), lanes_at(u)] = value

        convolve(held, ref["w_dw"], half_w, SIDE, put, False)

    pl.run_scoped(depthwise, pltpu.VMEM((C1P // LANES, batch, rows, breadth, LANES), jnp.float32))
    pl.run_scoped(
        functools.partial(pointwise_part, ref, fetch, store, held_in, held_out),
        pltpu.VMEM((cells, CH), jnp.float32),
        pltpu.VMEM((cells, C1), jnp.bfloat16),
    )
    for name in EARLY:
        store[name].wait()


def pointwise_part(ref, fetch, store, held_in, held_out, slopes, spread_all):
    conv, total, sums, extra = ref["conv"], ref["total"], ref["sums"], ref["extra"]
    gain, w_head = ref["lines"].at[3:4, 0:C1P], ref["w_head"]
    normed, act = held_out["normed"], held_out["act"]
    grad_mixed, grad_branch, grad_summed = (
        held_out[name] for name in ("grad_mixed", "grad_branch", "grad_summed")
    )
    w_hidden, w_out_t, w_up = (held_in[name] for name in ("w_hidden", "w_out_t", "w_up"))
    target, weight, h_zero = (held_in[name] for name in ("target", "weight", "h_zero"))
    batch, rows, breadth, _ = ref["padded"].shape
    height, half_w = rows - 2 * REACH, breadth - 2 * SIDE

    inside = lax.broadcasted_iota(jnp.int32, (1, C1P), 1) < C1
    values = conv[...] + ref["lines"][2:3, :C1P]
    mean = jnp.sum(values, axis=1, keepdims=True) * (1.0 / C1)
    centered = jnp.where(inside, values - mean, 0.0)
    scale = lax.rsqrt(jnp.sum(centered * centered, axis=1, keepdims=True) * (1.0 / C1) + 1e-06)
    conv[...] = centered * scale
    normed[...] = (conv[...] * gain[...] + ref["lines"][4:5, :C1P]).astype(jnp.bfloat16)
    store["normed"].start()

    fetch["coarse"].wait()
    fetch["w_hidden"].wait()
    fetch["w_out_t"].wait()
    total[...] = held_in["coarse"][...]
    for begin in range(0, CH, PART):
        span = slice(begin, min(begin + PART, CH))
        value = product(normed[:, :C1], w_hidden[:, span]) + ref["lines"][5:6, span]
        curved, slope = gelu_and_slope(value)
        slopes[:, span] = slope
        act[:, span] = curved.astype(jnp.bfloat16)
        total[:, :C1] += product_t(act[:, span], w_out_t[:, span])
    store["act"].start()
    mixed = (total[...] + ref["lines"][6:7, :C1P]).astype(jnp.bfloat16)

    for name in ("h_zero", "target", "weight", "w_up"):
        fetch[name].wait()
    grad_mixed[...] = jnp.zeros_like(grad_mixed)
    loss = jnp.zeros((1, CI), jnp.float32)
    head_sum = jnp.zeros((1, CI), jnp.float32)
    up_sum = jnp.zeros((1, C0), jnp.float32)
    for s in range(4):
        sub_y, sub_x = divmod(s, 2)
        for m in range(batch):
            for i in range(height):
                at = rows_at(m, i, height, half_w)
                line = pl.ds(sub_x, half_w, stride=2)
                ref["goal"][at, :] = target[m, 2 * i + sub_y, line, :]
                ref["load"][at, :] = weight[2 * i + sub_y, line, :]
        w_up_s = w_up[:, s * C0 : (s + 1) * C0]
        upper = product(mixed[:, :C1], w_up_s) + ref["lines"][7:8, :C0]
        summed = (upper + h_zero[s, :, :C0]).astype(jnp.bfloat16)
        error = product(summed, w_head[...]) + ref["lines"][8:9, :CI] - ref["goal"][:, :CI]
        weighted = ref["load"][:, :CI] * error
        loss = loss + column_sum(weighted * error)
        grad_out = (2.0 * weighted).astype(jnp.bfloat16)
        head_sum = head_sum + column_sum(grad_out)
        if s == 0:
            ref["d_head"][...] = inner_rows(summed, grad_out)
        else:
            ref["d_head"][...] += inner_rows(summed, grad_out)
        spread = product_t(grad_out, w_head[...])
        grad_summed[s] = spread
        grad_upper = spread.astype(jnp.bfloat16)
        up_sum = up_sum + column_sum(grad_upper)
        spread_all[:, s * C0 : (s + 1) * C0] = grad_upper
        grad_mixed[:, :C1] += product_t(grad_upper, w_up_s)
    store["grad_summed"].start()
    store["grad_mixed"].start()
    held_out["d_up"][...] = inner_rows(mixed[:, :C1], spread_all[...])
    store["d_up"].start()
    grad_branch[...] = grad_mixed[...].astype(jnp.bfloat16)
    store["grad_branch"].start()
    sums[...] = jnp.zeros_like(sums)
    extra[...] = jnp.zeros_like(extra)
    extra[0:1, 0:CI] = loss
    extra[1:2, :] = column_sum(ref["weight_map"][...])
    sums[1:2, 0:CI] = head_sum
    sums[2:3, 0:C0] = up_sum
    sums[3:4, 0:C1P] = column_sum(grad_branch[...])

    total[...] = jnp.zeros_like(total)
    for begin in range(0, CH, PART):
        span = slice(begin, min(begin + PART, CH))
        value = product(grad_branch[:, :C1], w_out_t[:, span]) * slopes[:, span]
        low = value.astype(jnp.bfloat16)
        ref["grad_pre"][:, span] = low
        sums[4:5, span] = column_sum(low)
        total[:, :C1] += product_t(low, w_hidden[:, span])

    grad_normed = total[...]
    sums[5:6, 0:C1P] = column_sum(grad_normed * conv[...])
    sums[6:7, 0:C1P] = column_sum(grad_normed)
    inward = grad_normed * gain[...]
    first = jnp.sum(inward, axis=1, keepdims=True) * (1.0 / C1)
    second = jnp.sum(inward * conv[...], axis=1, keepdims=True) * (1.0 / C1)
    value = scale * jnp.where(inside, inward - first - conv[...] * second, 0.0)
    low = value.astype(jnp.bfloat16)
    sums[7:8, 0:C1P] = column_sum(low)
    ref["grad_conv"][...] = low.reshape(ref["grad_conv"].shape)


def middle_part(**given):
    cells = given["coarse"].shape[0]
    batch, rows, breadth, _ = given["padded"].shape
    half_h, half_w = rows - 2 * REACH, breadth - 2 * SIDE
    vmem = pl.BlockSpec(memory_space=pltpu.VMEM)
    hbm = pl.BlockSpec(memory_space=pl.ANY)
    f32, low = jnp.float32, jnp.bfloat16
    outs = {
        "normed": ((cells, C1P), low),
        "act": ((cells, CH), low),
        "grad_pre": ((cells, CH), low),
        "grad_mixed": ((cells, C1P), f32),
        "grad_branch": ((cells, C1P), low),
        "grad_summed": ((4, cells, C0), f32),
        "grad_conv": ((batch, half_h, half_w, C1P), low),
        "d_up": ((C1, C1), f32),
        "d_head": ((C0, CI), f32),
        "sums": ((8, CH), f32),
        "extra": ((8, LANES), f32),
    }
    scratch = {
        "conv": pltpu.VMEM((cells, C1P), f32),
        "total": pltpu.VMEM((cells, C1P), f32),
        "goal": pltpu.VMEM((cells, LANES), f32),
        "load": pltpu.VMEM((cells, LANES), f32),
        "sem_in": pltpu.SemaphoreType.DMA((len(LATE),)),
        "sem_out": pltpu.SemaphoreType.DMA((len(EARLY),)),
    }
    for name in LATE:
        scratch["held_" + name] = pltpu.VMEM(given[name].shape, given[name].dtype)
    for name in EARLY:
        scratch["held_" + name] = pltpu.VMEM(*outs[name])
    found = pl.pallas_call(
        functools.partial(middle_kernel, tuple(given) + tuple(outs) + tuple(scratch)),
        out_shape=tuple(jax.ShapeDtypeStruct(*out) for out in outs.values()),
        in_specs=[hbm if name in LATE else vmem for name in given],
        out_specs=tuple(hbm if name in EARLY else vmem for name in outs),
        scratch_shapes=list(scratch.values()),
        compiler_params=pltpu.CompilerParams(vmem_limit_bytes=62 << 20),
    )(*given.values())
    return dict(zip(outs, found))


AFTER = ("grad_mixed", "grad_summed", "slope_zero", "h_zero", "taps", "w_down")


def outer_kernel(names, *refs):
    ref = dict(zip(names, refs))
    fetch = {}
    for i, name in enumerate(AFTER):
        fetch[name] = pltpu.make_async_copy(ref[name], ref["held_" + name], ref["sem_in"].at[i])
        fetch[name].start()
    grad_mixed, grad_summed, slope_zero, h_zero, taps, w_down = (ref["held_" + name] for name in AFTER)
    held, conv, sums, d_dw, d_in = (ref[name] for name in ("held", "conv", "sums", "d_dw", "d_in"))
    vector = ref["vector"]
    grad_conv = ref["grad_conv"]
    batch, height, half_w, _ = grad_conv.shape
    spread_lanes(ref["padded"], held)
    tiles = C1P // LANES
    d_dw[...] = jnp.zeros_like(d_dw)

    def taps_of(number, carry):
        u, m = number // batch, number % batch
        grads = [grad_conv[m, i, :, lanes_at(u)].astype(jnp.float32) for i in range(height)]
        for x in range(7):
            found = [jnp.zeros((8, LANES), jnp.float32) for _ in range(7)]
            for y in range(height + 6):
                window = held[u, m, y, pl.ds(SIDE - REACH + x, half_w), :]
                for i in range(height):
                    if 0 <= y - i < 7:
                        term = (window * grads[i]).reshape(half_w // 8, 8, LANES)
                        found[y - i] = found[y - i] + jnp.sum(term, axis=0)
            for dy in range(7):
                d_dw[pl.ds(dy * 7 + x, 1), lanes_at(u)] += jnp.sum(found[dy], axis=0, keepdims=True)
        return carry

    lax.fori_loop(0, tiles * batch, taps_of, 0)
    spread_lanes(ref["grad_padded"], held)

    def put(u, m, i, value):
        conv[rows_at(m, i, height, half_w), lanes_at(u)] = value

    convolve(held, ref["w_dw"], half_w, EDGE, put, True)
    for name in AFTER:
        fetch[name].wait()
    grad_coarse = (conv[...] + grad_mixed[...]).astype(jnp.bfloat16)
    vector[...] = jnp.zeros_like(vector)
    pieces = [(column_sum(grad_coarse), C1)] + [(sums[i : i + 1, :], C1) for i in (7, 5, 6)]
    pieces += [(sums[4:5, :], CH), (sums[3:4, :], C1), (sums[2:3, :], C0), (sums[1:2, :], CI)]
    start = C0
    for piece, size in pieces:
        vector[:, start : start + size] = piece[:, :size]
        start = start + size
    in_sum = jnp.zeros((1, C0), jnp.float32)
    for s in range(4):
        ref["d_down"][s * C0 : (s + 1) * C0, :] = inner_rows(
            h_zero[s].astype(jnp.bfloat16), grad_coarse
        )[:C0]
        grad_h = product_t(grad_coarse, w_down[s])[:, :C0] + grad_summed[s]
        grad_a = (slope_zero[s, :, :C0] * grad_h).astype(jnp.bfloat16)
        in_sum = in_sum + column_sum(grad_a)
        if s == 0:
            d_in[...] = inner_rows(taps[s], grad_a)
        else:
            d_in[...] += inner_rows(taps[s], grad_a)
    vector[:, 0:C0] = in_sum


def outer_part(length, **given):
    cells = given["grad_mixed"].shape[0]
    batch, rows, breadth, _ = given["grad_padded"].shape
    vmem = pl.BlockSpec(memory_space=pltpu.VMEM)
    hbm = pl.BlockSpec(memory_space=pl.ANY)
    f32 = jnp.float32
    outs = {
        "d_dw": ((56, C1P), f32),
        "d_down": ((C1, C1P), f32),
        "d_in": ((9 * CIP, C0), f32),
        "vector": ((1, length), f32),
    }
    scratch = {
        "held": pltpu.VMEM((C1P // LANES, batch, rows, breadth, LANES), f32),
        "conv": pltpu.VMEM((cells, C1P), f32),
        "sem_in": pltpu.SemaphoreType.DMA((len(AFTER),)),
    }
    for name in AFTER:
        scratch["held_" + name] = pltpu.VMEM(given[name].shape, given[name].dtype)
    found = pl.pallas_call(
        functools.partial(outer_kernel, tuple(given) + tuple(outs) + tuple(scratch)),
        out_shape=tuple(jax.ShapeDtypeStruct(*out) for out in outs.values()),
        in_specs=[hbm if name in AFTER else vmem for name in given],
        out_specs=tuple([vmem] * len(outs)),
        scratch_shapes=list(scratch.values()),
        compiler_params=pltpu.CompilerParams(vmem_limit_bytes=60 << 20),
    )(*given.values())
    return dict(zip(outs, found))


def as_rows(piece, rows):
    flat = piece.reshape(-1)
    return jnp.pad(flat, (0, rows * LANES - flat.shape[0])).reshape(rows, LANES)


def widened(array, *shape):
    return jnp.pad(array, [(0, full - now) for full, now in zip(shape, array.shape)])


def on_device(
    inputs,
    targets,
    land_mask,
    volume,
    date_index,
    perm_narrow,
    perm_wide,
    w_in,
    w_down,
    w_dw,
    w_hidden,
    w_out,
    w_up,
    w_head,
    biases_gains,
    moment_first,
    moment_second,
):
    rows, cols = lax.axis_size("rows"), lax.axis_size("cols")
    weight = land_mask.astype(jnp.float32) * volume
    height, breadth = weight.shape
    half_h, half_w = (height // 2, breadth // 2)
    cells = MB * half_h * half_w
    matrices = (w_in, w_down, w_dw, w_hidden, w_out, w_up, w_head)

    def dates(field):
        picked = jnp.concatenate(
            [lax.dynamic_slice_in_dim(field, date_index[m], 1, 0, allow_negative_indices=False) for m in range(MB)]
        )
        return widened(picked, MB, height, breadth, CIP)

    w_in_p = widened(w_in.reshape(9, CI, C0), 9, CIP, C0P).reshape(9 * CIP, C0P)
    w_down_p = widened(w_down.reshape(4, C0, C1), 4, C0P, C1P)
    w_dw_p = widened(w_dw.astype(jnp.float32), 56, C1P)
    weight_map = jnp.broadcast_to(weight[:, :, None], (height, breadth, LANES))

    state = halo(rows, cols, FINE_REACH, dates(inputs), 1)
    taps, slope_zero, h_zero, coarse, padded, lines = input_part(
        rows, state, w_in_p, w_down_p, biases_gains[None, :]
    )
    mid = middle_part(
        padded=padded, coarse=coarse, h_zero=h_zero, target=dates(targets).astype(jnp.float32),
        weight=weight_map, weight_map=weight, w_dw=w_dw_p, w_hidden=w_hidden, w_out_t=w_out.T,
        w_up=w_up, w_head=w_head, lines=lines,
    )
    space = Plan(rows, cols, PADDED).space
    grad, grad_padded = place_gradients(
        rows, cols, space, mid["normed"], mid["grad_branch"], mid["grad_pre"], mid["act"],
        perm_narrow, perm_wide, mid["d_up"], mid["grad_conv"],
    )
    out = outer_part(
        (space - ROW_AT[7]) * LANES,
        padded=padded, grad_padded=grad_padded, grad_conv=mid["grad_conv"],
        grad_mixed=mid["grad_mixed"], grad_summed=mid["grad_summed"], slope_zero=slope_zero, h_zero=h_zero,
        taps=taps, w_dw=w_dw_p, w_down=w_down_p, sums=mid["sums"],
    )
    d_in = out["d_in"].reshape(9, CIP, C0)[:, :CI].reshape(9 * CI, C0)
    pieces = (
        jnp.pad(as_rows(d_in, ROW_AT[1] - ROW_AT[0]), ((ROW_AT[0], 0), (0, 0))),
        as_rows(out["d_dw"][:49, :C1], ROW_AT[3] - ROW_AT[2]),
        as_rows(mid["d_head"], ROW_AT[7] - ROW_AT[6]),
        out["vector"].reshape(-1, LANES),
    )
    grad = complete_gradients(grad, out["d_down"], pieces)
    plan, (gathered, first, second, totals) = exchange(
        rows, cols, grad, moment_first, moment_second, mid["extra"]
    )
    hidden_p, out_p, new_up, new_down, small_a, small_b, small_c = unpack(plan, gathered, w_up, w_down, perm_narrow, perm_wide)
    small = {0: (small_a, 0), 2: (small_b, 1), 6: (small_c, 2), 7: (small_c, 2)}
    whole = {
        1: new_down,
        3: rebuild_hidden(hidden_p, perm_wide, w_hidden),
        4: rebuild_out(out_p, perm_narrow, w_out),
        5: new_up,
    }
    olds = matrices + (biases_gains,)
    news = []
    for index, old in enumerate(olds):
        if index in whole:
            news.append(whole[index])
        else:
            source, which = small[index]
            start = FLAT_AT[index] - KEPT[which][0] * LANES
            piece = source.reshape(-1)[start : start + old.size].reshape(old.shape)
            news.append(moved(old, piece) if index < 7 else old - learn_rate * piece)
    return tuple(news) + (
        first.reshape(-1),
        second.reshape(-1),
        totals[0, 0],
        MB * CI * totals[1, 0],
        totals[8, 0],
    )


def solution(mesh):
    return jax.shard_map(
        on_device,
        mesh=mesh,
        in_specs=(
            P(None, "rows", "cols", None),
            P(None, "rows", "cols", None),
            P("rows", "cols"),
            P("rows", "cols"),
            P(),
            P(),
            P(),
            P(),
            P(),
            P(),
            P(),
            P(),
            P(),
            P(),
            P(),
            P(("rows", "cols")),
            P(("rows", "cols")),
        ),
        out_specs=(
            P(),
            P(),
            P(),
            P(),
            P(),
            P(),
            P(),
            P(),
            P(("rows", "cols")),
            P(("rows", "cols")),
            P(),
            P(),
            P(),
        ),
        check_vma=False,
    )
```

```python
import functools

import jax
import jax.numpy as jnp
from jax import lax
from jax.experimental import pallas as pl
from jax.experimental.pallas import tpu as pltpu
from jax.sharding import PartitionSpec as P

CI = 77
C0 = 200
C1 = 800
CH = 3200
MB = 2
STEP = 5
LANES = 128
MESH = pl.DeviceIdType.MESH
ROUNDER = 12582912.0

decay_first = 0.9
decay_second = 0.99
epsilon = 1e-08
learn_rate = 0.02
weight_decay = 0.1
clip_limit = 1.0

VEC = 4 * C1 + CH + C1 + 2 * C0 + CI
SIZES = (9 * CI * C0, 4 * C0 * C1, 49 * C1, C1 * CH, CH * C1, C1 * 4 * C0, C0 * CI, VEC)
PADDED = 6602752
FLAT_AT = []
ROW_AT = []
for size in SIZES:
    flat_here = FLAT_AT[-1] + SIZES[len(FLAT_AT) - 1] if FLAT_AT else PADDED - sum(SIZES)
    row_here = ROW_AT[-1] + -(-SIZES[len(ROW_AT) - 1] // 1024) * 8 if ROW_AT else 0
    row_here = max(row_here, -(-flat_here // 1024) * 8)
    FLAT_AT.append(flat_here)
    ROW_AT.append(row_here)
SHIFTS = []
for flat_here, row_here, size in zip(FLAT_AT, ROW_AT, SIZES):
    moved = divmod(row_here * LANES - flat_here, LANES)
    if SHIFTS and SHIFTS[-1][:2] == moved:
        SHIFTS[-1] = moved + (SHIFTS[-1][2], flat_here + size)
    else:
        SHIFTS.append(moved + (flat_here, flat_here + size))
MAX_SHIFT = max(s[0] for s in SHIFTS) + 1


def bit_masks(bits):
    masks = [()]
    for bit in bits:
        masks = masks + [m + (bit,) for m in masks]
    return sorted(masks, key=lambda m: -len(m))


class Plan:
    def __init__(self, rows, cols, total):
        self.rows, self.cols, self.count = rows, cols, rows * cols
        self.share = total // LANES // self.count
        self.bits = rows.bit_length() - 1
        need = 7 + self.share + MAX_SHIFT + 1
        self.block = 64 if need > 1024 else 32
        self.window = -(-need // (2 * self.block)) * 2 * self.block
        self.part = self.window // 2
        self.blocks = self.part // self.block
        self.scales = self.blocks
        upper = list(range(1, self.bits))
        self.orders = [upper, upper[1:] + upper[:1]]
        self.stages = len(upper)
        self.space = (self.share * (self.count - 1)) // 8 * 8 + self.window
        self.padded = -(-self.share // 16) * 16
        cut = -(-self.padded // 32) * 16
        self.cuts = [(0, cut), (cut, self.padded - cut)]
        self.local = self.count // 2


def exchange_kernel(
    plan, grad, m_first, m_second, extra, full, first, second, totals,
    acc, near, q_send, q_recv, s_send, s_recv, z_send, z_recv, zs_send, zs_recv,
    rolled, step, low, stats,
    sem_load, sem_near_s, sem_near_r, sem_qs, sem_qr, sem_ss, sem_sr,
    sem_zs, sem_zr, sem_zss, sem_zsr, sem_ts, sem_tr, sem_own,
    sem_gs, sem_gr, sem_hs, sem_hr, sem_cs, sem_cr,
):
    nr, nc, n = plan.rows, plan.cols, plan.count
    r = lax.axis_index("rows")
    c = lax.axis_index("cols")
    me = r * nc + c
    part, window, share = plan.part, plan.window, plan.share

    def flipped(mask):
        out = r
        for bit in mask:
            here = (r // (1 << bit)) % 2
            out = out + (1 - 2 * here) * (1 << bit)
        return out

    def remote(src, dst, send, recv, row, col):
        return pltpu.make_async_remote_copy(
            src_ref=src, dst_ref=dst, send_sem=send, recv_sem=recv,
            device_id=(row, col), device_id_type=MESH,
        )

    barrier = pltpu.get_barrier_semaphore()

    def greet(d, carry):
        k = lax.rem(me + d, n)
        pl.semaphore_signal(barrier, inc=1, device_id=(k // nc, k % nc), device_id_type=MESH)
        return carry

    lax.fori_loop(1, n, greet, 0)
    pl.semaphore_wait(barrier, n - 1)

    upper = list(range(1, plan.bits))
    masks = bit_masks(upper)

    def local_index(mask, col):
        return (flipped(mask) // 2) * nc + col

    def window_start(row, col):
        return pl.multiple_of((share * (row * nc + col)) // 8 * 8, 8)

    def near_copy(mask, col):
        row = flipped(mask + (0,))
        return remote(
            grad.at[pl.ds(window_start(row, col), window)],
            near.at[local_index(mask, col)],
            sem_near_s.at[local_index(mask, col)], sem_near_r.at[local_index(mask, col)],
            flipped((0,)), c,
        )

    def load_copy(mask, col):
        index = local_index(mask, col)
        return pltpu.make_async_copy(
            grad.at[pl.ds(window_start(flipped(mask), col), window)], acc.at[index], sem_load.at[index]
        )

    half_way = nc // 2

    def column_of(t):
        return jnp.where(t == 1, half_way, jnp.where(t <= half_way, t - 1, t))

    def begin(t, carry):
        col = lax.rem(c + column_of(t), nc)
        for mask in masks:
            near_copy(mask, col).start()
            load_copy(mask, col).start()
        return carry

    lax.fori_loop(1, nc + 1, begin, 0)

    def encode(index, p, q_ref, s_ref):
        def body(b, carry):
            at = pl.ds(pl.multiple_of(b * plan.block, plan.block), plan.block)
            rows_at = pl.ds(pl.multiple_of(p * part + b * plan.block, 8), plan.block)
            values = acc[index, rows_at, :]
            top = jnp.maximum(jnp.max(jnp.abs(values), axis=0, keepdims=True), 1e-30)
            scaled = values * (32766.0 / top)
            scaled = (scaled + ROUNDER) - ROUNDER
            q_ref[at, :] = scaled.astype(jnp.int32).astype(jnp.int16)
            s_ref[pl.ds(b, 1), :] = top * (1.0 / 32766.0)
            return carry

        lax.fori_loop(0, plan.blocks, body, 0)

    def decode(index, p, q_ref, s_ref):
        def body(b, carry):
            at = pl.ds(pl.multiple_of(b * plan.block, plan.block), plan.block)
            rows_at = pl.ds(pl.multiple_of(p * part + b * plan.block, 8), plan.block)
            acc[index, rows_at, :] += q_ref[at, :].astype(jnp.float32) * s_ref[pl.ds(b, 1), :]
            return carry

        lax.fori_loop(0, plan.blocks, body, 0)

    def stage_base(stage):
        return sum((1 << (plan.stages - 1 - s)) for s in range(stage)) * nc

    def hop(p, stage, slot):
        row = flipped((plan.orders[p][stage],))
        at = stage_base(stage) + slot
        return (
            remote(q_send.at[p, at], q_recv.at[p, at], sem_qs.at[p, at], sem_qr.at[p, at], row, c),
            remote(s_send.at[p, at], s_recv.at[p, at], sem_ss.at[p, at], sem_sr.at[p, at], row, c),
        )

    def send_stage(p, stage, number, mask, col):
        bit = plan.orders[p][stage]
        index = local_index(mask + (bit,), col)
        slot = number * nc + col
        at = stage_base(stage) + slot
        encode(index, p, q_send.at[p, at], s_send.at[p, at])
        for copy in hop(p, stage, slot):
            copy.start()

    def take_stage(p, stage, number, mask, col):
        slot = number * nc + col
        for copy in hop(p, stage, slot):
            copy.wait_recv()
        at = stage_base(stage) + slot
        decode(local_index(mask, col), p, q_recv.at[p, at], s_recv.at[p, at])

    def free_masks(p, stage):
        rest = plan.orders[p][stage + 1 :]
        found = bit_masks(rest)
        if rest:
            found = [m for m in found if rest[0] in m] + [m for m in found if rest[0] not in m]
        return found

    def far_copy(p, d):
        col = lax.rem(c + d, nc)
        return (
            remote(z_send.at[p, d - 1], z_recv.at[p, d - 1], sem_zs.at[p, d - 1], sem_zr.at[p, d - 1], r, col),
            remote(zs_send.at[p, d - 1], zs_recv.at[p, d - 1], sem_zss.at[p, d - 1], sem_zsr.at[p, d - 1], r, col),
        )

    def join(t):
        d = column_of(t)
        col = lax.rem(c + d, nc)
        for mask in masks:
            index = local_index(mask, col)
            near_copy(mask, col).wait_recv()
            load_copy(mask, col).wait()

            def body(b, inner, index=index):
                at = pl.ds(pl.multiple_of(b * plan.block, plan.block), plan.block)
                acc[index, at, :] += near[index, at, :]
                return inner

            lax.fori_loop(0, 2 * plan.blocks, body, 0)
            for p in range(2):
                bit = plan.orders[p][0]
                if bit in mask:
                    rest = tuple(b for b in mask if b != bit)
                    options = free_masks(p, 0)
                    number = [sorted(o) for o in options].index(sorted(rest))
                    send_stage(p, 0, number, rest, col)

    def take(stage, t):
        d = column_of(t)
        col = lax.rem(c + d, nc)
        for number in range(1 << (plan.stages - 1 - stage)):
            for p in range(2):
                mask = free_masks(p, stage)[number]
                take_stage(p, stage, number, mask, col)
                if stage + 1 < plan.stages:
                    bit = plan.orders[p][stage + 1]
                    if bit in mask:
                        rest = tuple(b for b in mask if b != bit)
                        options = free_masks(p, stage + 1)
                        following = [sorted(o) for o in options].index(sorted(rest))
                        send_stage(p, stage + 1, following, rest, col)
                else:
                    @pl.when(d < nc)
                    def _(p=p):
                        encode(local_index((), col), p, z_send.at[p, d - 1], zs_send.at[p, d - 1])
                        for copy in far_copy(p, d):
                            copy.start()

    mine = local_index((), c)

    def gather_far(d, carry):
        for p in range(2):
            for copy in far_copy(p, d):
                copy.wait_recv()
            decode(mine, p, z_recv.at[p, d - 1], zs_recv.at[p, d - 1])
        return carry


    def turn_of(t, carry):
        @pl.when(t <= nc)
        def _():
            join(t)

        for stage in range(plan.stages):
            d = t - 1 - stage

            @pl.when((d >= 1) & (d <= nc))
            def _(stage=stage, d=d):
                take(stage, d)

        @pl.when((t > nc) & (t - nc < nc))
        def _():
            gather_far(column_of(t - nc), 0)

        return carry

    lax.fori_loop(1, nc + plan.stages + 1, turn_of, 0)

    def gather_rest(q, carry):
        return gather_far(column_of(q), carry)

    lax.fori_loop(min(plan.stages + 1, nc), nc, gather_rest, 0)

    offset = lax.rem(share * me, 8)
    low_end, high_end = share * me * LANES, share * (me + 1) * LANES
    for number, (shift_rows, shift_lanes, begin, end) in enumerate(SHIFTS):
        def turn(b, carry, number=number, shift_lanes=shift_lanes):
            at = pl.ds(pl.multiple_of(b * plan.block, plan.block), plan.block)
            rolled[number, at, :] = pltpu.roll(acc[mine, at, :], LANES - shift_lanes, 1)
            return carry

        @pl.when((low_end < end) & (high_end > begin))
        def _(turn=turn):
            lax.fori_loop(0, 2 * plan.blocks, turn, 0)

    def share_rows(start, length, chosen):
        lane = lax.broadcasted_iota(jnp.int32, (length, LANES), 1)
        out = jnp.zeros((length, LANES), jnp.float32)
        if len(chosen) > 1:
            line = lax.broadcasted_iota(jnp.int32, (length, LANES), 0)
            flat = (share * me + start + line) * LANES + lane
        for number in chosen:
            shift_rows, shift_lanes, begin, end = SHIFTS[number]
            here = rolled[number, pl.ds(offset + start + shift_rows, length), :]
            after = rolled[number, pl.ds(offset + start + shift_rows + 1, length), :]
            value = jnp.where(lane < LANES - shift_lanes, here, after)
            if len(chosen) > 1:
                value = jnp.where((flat >= begin) & (flat < end), value, out)
            out = value
        return out

    chunk = 32
    whole, tail = share // chunk, share % chunk
    stats[me, 8:16, :] = extra[...]

    def squares(chosen):
        def square(b, total):
            start = pl.multiple_of(b * chunk, chunk)
            value = share_rows(start, chunk, chosen)
            step[pl.ds(start, chunk), :] = value
            return total + jnp.sum((value * value).reshape(chunk // 8, 8, LANES), axis=0)

        total = lax.fori_loop(0, whole, square, jnp.zeros((8, LANES), jnp.float32))
        stats[me, 0:8, :] = total
        if tail:
            value = share_rows(whole * chunk, tail, chosen)
            step[whole * chunk : share, :] = value
            stats[me, 0:1, :] += jnp.sum(value * value, axis=0, keepdims=True)

    largest = max(range(len(SHIFTS)), key=lambda i: SHIFTS[i][3] - SHIFTS[i][2])
    alone = (low_end >= SHIFTS[largest][2]) & (high_end <= SHIFTS[largest][3])

    @pl.when(alone)
    def _():
        squares((largest,))

    @pl.when(jnp.logical_not(alone))
    def _():
        squares(tuple(range(len(SHIFTS))))

    def stat_copy(target, source):
        return remote(
            stats.at[me], stats.at[me], sem_ts.at[target], sem_tr.at[me], target // nc, target % nc
        )

    def stat_wait(source):
        return remote(
            stats.at[source], stats.at[source], sem_ts.at[source], sem_tr.at[source],
            source // nc, source % nc,
        )

    def send_stat(d, carry):
        stat_copy(lax.rem(me + d, n), me).start()
        return carry

    lax.fori_loop(1, n, send_stat, 0)

    def wait_stat(d, carry):
        stat_wait(lax.rem(me + d, n)).wait_recv()
        return carry

    lax.fori_loop(1, n, wait_stat, 0)

    def add_stat(k, total):
        return total + stats[k]

    sums = lax.fori_loop(0, n, add_stat, jnp.zeros((16, LANES), jnp.float32))
    norm = jnp.sqrt(jnp.sum(sums[0:8], keepdims=True))
    totals[0:1, :] = jnp.broadcast_to(jnp.sum(sums[8:9], keepdims=True), (1, LANES))
    totals[1:2, :] = jnp.broadcast_to(jnp.sum(sums[9:10], keepdims=True), (1, LANES))
    totals[2:8, :] = jnp.zeros((6, LANES), jnp.float32)
    totals[8:16, :] = jnp.broadcast_to(norm, (8, LANES))
    clip = jnp.minimum(1.0, clip_limit / norm)

    def update(start, length):
        clipped = step[pl.ds(start, length), :] * clip
        one = decay_first * m_first[pl.ds(start, length), :] + (1.0 - decay_first) * clipped
        two = decay_second * m_second[pl.ds(start, length), :] + (1.0 - decay_second) * clipped * clipped
        first[pl.ds(start, length), :] = one
        second[pl.ds(start, length), :] = two
        step[pl.ds(start, length), :] = (
            one / (1.0 - decay_first**STEP) / (jnp.sqrt(two / (1.0 - decay_second**STEP)) + epsilon)
        )

    def update_chunk(b, carry):
        update(pl.multiple_of(b * chunk, chunk), chunk)
        return carry

    lax.fori_loop(0, whole, update_chunk, 0)
    if tail:
        update(whole * chunk, tail)
    if plan.padded > share:
        step[share : plan.padded, :] = jnp.zeros((plan.padded - share, LANES), jnp.float32)

    def narrow(b, carry):
        at = pl.ds(pl.multiple_of(b * 16, 16), 16)
        low[at, :] = step[at, :].astype(jnp.bfloat16)
        return carry

    lax.fori_loop(0, plan.padded // 16, narrow, 0)

    own = pltpu.make_async_copy(low, full.at[me], sem_own)
    own.start()
    own.wait()

    back = [list(reversed(order)) for order in plan.orders]

    def piece(mask, col, p):
        begin, length = plan.cuts[p]
        return full.at[flipped(mask) * nc + col, pl.ds(begin, length)]

    def along(direction, col, p, receive):
        step_col = 1 if direction == 0 else -1
        target = c - step_col if receive else c + step_col
        ref = piece((), col, p)
        return remote(ref, ref, sem_gs.at[direction, col, p], sem_gr.at[direction, col, p], r, target)

    def gather_masks(p, stage):
        return bit_masks(back[p][:stage])

    def gather_base(stage):
        return sum(1 << s for s in range(stage)) * nc

    def across(p, stage, number, mask, col):
        at = gather_base(stage) + number * nc + col
        ref = piece(mask, col, p)
        return remote(ref, ref, sem_hs.at[p, at], sem_hr.at[p, at], flipped((back[p][stage],)), c)

    def across_recv(p, stage, number, mask, col):
        at = gather_base(stage) + number * nc + col
        ref = piece(mask + (back[p][stage],), col, p)
        return remote(ref, ref, sem_hs.at[p, at], sem_hr.at[p, at], flipped((back[p][stage],)), c)

    def inward(p, mask, col):
        number = masks.index(tuple(sorted(mask)))
        at = number * nc + col
        ref = piece(mask, col, p)
        return remote(ref, ref, sem_cs.at[p, at], sem_cr.at[p, at], flipped((0,)), c)

    def inward_recv(p, mask, col):
        number = masks.index(tuple(sorted(mask)))
        at = number * nc + col
        ref = piece(mask + (0,), col, p)
        return remote(ref, ref, sem_cs.at[p, at], sem_cr.at[p, at], flipped((0,)), c)

    def spread(p, mask, col, stage):
        for later in range(stage, plan.stages):
            options = [sorted(o) for o in gather_masks(p, later)]
            if sorted(mask) in options:
                across(p, later, options.index(sorted(mask)), mask, col).start()
        inward(p, mask, col).start()

    def near_cols(t):
        if t == 0:
            return [(0, c)]
        return [(0, c - t), (1, c + t)]

    def inside(col):
        return (col >= 0) & (col < nc)

    for time in range(nc + plan.stages):
        for stage in range(plan.stages + 1):
            t = time - stage
            if not 0 <= t < nc:
                continue
            if stage == 0:
                if t == 0:
                    for p in range(2):
                        @pl.when(c < nc - 1)
                        def _(p=p):
                            along(0, c, p, False).start()

                        @pl.when(c > 0)
                        def _(p=p):
                            along(1, c, p, False).start()

                        spread(p, (), c, 0)
                else:
                    for direction, col in near_cols(t):
                        @pl.when(inside(col))
                        def _(direction=direction, col=col):
                            for p in range(2):
                                along(direction, col, p, True).wait_recv()
                                if direction == 0:
                                    @pl.when(c < nc - 1)
                                    def _():
                                        along(0, col, p, False).start()
                                else:
                                    @pl.when(c > 0)
                                    def _():
                                        along(1, col, p, False).start()
                                spread(p, (), col, 0)
            else:
                for direction, col in near_cols(t):
                    @pl.when(inside(col))
                    def _(col=col, stage=stage):
                        for number in range(1 << (stage - 1)):
                            for p in range(2):
                                mask = gather_masks(p, stage - 1)[number]
                                across_recv(p, stage - 1, number, mask, col).wait_recv()
                                spread(p, mask + (back[p][stage - 1],), col, stage)

    for mask in masks:
        def finish(col, carry, mask=mask):
            for p in range(2):
                inward_recv(p, mask, col).wait_recv()
                inward(p, mask, col).wait_send()
            near_copy(mask, col).wait_send()
            return carry

        lax.fori_loop(0, nc, finish, 0)
    for p in range(2):
        for stage in range(plan.stages):
            for number, mask in enumerate(gather_masks(p, stage)):
                def sent(col, carry, p=p, stage=stage, number=number, mask=mask):
                    across(p, stage, number, mask, col).wait_send()
                    return carry

                lax.fori_loop(0, nc, sent, 0)
            for number in range(1 << (plan.stages - 1 - stage)):
                def left(col, carry, p=p, stage=stage, number=number):
                    for copy in hop(p, stage, number * nc + col):
                        copy.wait_send()
                    return carry

                lax.fori_loop(0, nc, left, 0)

        def gone(col, carry, p=p):
            @pl.when((col <= c) & (c < nc - 1))
            def _():
                along(0, col, p, False).wait_send()

            @pl.when((col >= c) & (c > 0))
            def _():
                along(1, col, p, False).wait_send()

            return carry

        lax.fori_loop(0, nc, gone, 0)

        def far_gone(d, carry, p=p):
            for copy in far_copy(p, d):
                copy.wait_send()
            return carry

        lax.fori_loop(1, nc, far_gone, 0)

    def stat_gone(d, carry):
        stat_copy(lax.rem(me + d, n), me).wait_send()
        return carry

    lax.fori_loop(1, n, stat_gone, 0)


def exchange(rows, cols, grad, m_first, m_second, extra):
    plan = Plan(rows, cols, m_first.size * rows * cols)
    n, nc, share = plan.count, plan.cols, plan.share
    hops = sum(1 << s for s in range(plan.stages)) * nc
    dma = pltpu.SemaphoreType.DMA
    far = max(nc - 1, 1)
    vmem = pl.BlockSpec(memory_space=pltpu.VMEM)
    hbm = pl.BlockSpec(memory_space=pl.ANY)
    return plan, pl.pallas_call(
        functools.partial(exchange_kernel, plan),
        out_shape=(
            jax.ShapeDtypeStruct((n, plan.padded, LANES), jnp.bfloat16),
            jax.ShapeDtypeStruct((share, LANES), jnp.float32),
            jax.ShapeDtypeStruct((share, LANES), jnp.float32),
            jax.ShapeDtypeStruct((16, LANES), jnp.float32),
        ),
        in_specs=[hbm, vmem, vmem, vmem],
        out_specs=(hbm, vmem, vmem, vmem),
        scratch_shapes=[
            pltpu.VMEM((plan.local, plan.window, LANES), jnp.float32),
            pltpu.VMEM((plan.local, plan.window, LANES), jnp.float32),
            pltpu.VMEM((2, hops, plan.part, LANES), jnp.int16),
            pltpu.VMEM((2, hops, plan.part, LANES), jnp.int16),
            pltpu.VMEM((2, hops, plan.scales, LANES), jnp.float32),
            pltpu.VMEM((2, hops, plan.scales, LANES), jnp.float32),
            pltpu.VMEM((2, far, plan.part, LANES), jnp.int16),
            pltpu.VMEM((2, far, plan.part, LANES), jnp.int16),
            pltpu.VMEM((2, far, plan.scales, LANES), jnp.float32),
            pltpu.VMEM((2, far, plan.scales, LANES), jnp.float32),
            pltpu.VMEM((len(SHIFTS), plan.window, LANES), jnp.float32),
            pltpu.VMEM((plan.padded, LANES), jnp.float32),
            pltpu.VMEM((plan.padded, LANES), jnp.bfloat16),
            pltpu.VMEM((n, 16, LANES), jnp.float32),
            dma((plan.local,)), dma((plan.local,)), dma((plan.local,)),
            dma((2, hops)), dma((2, hops)), dma((2, hops)), dma((2, hops)),
            dma((2, far)), dma((2, far)), dma((2, far)), dma((2, far)),
            dma((n,)), dma((n,)), dma,
            dma((2, nc, 2)), dma((2, nc, 2)),
            dma((2, hops)), dma((2, hops)),
            dma((2, plan.local)), dma((2, plan.local)),
        ],
        compiler_params=pltpu.CompilerParams(
            collective_id=0, has_side_effects=True, vmem_limit_bytes=56 << 20
        ),
    )(grad, m_first.reshape(share, LANES), m_second.reshape(share, LANES), extra)


WIDE = CH + LANES
KEPT = ((8, 1104), (6096, 6408), (51400, 51584))
PLACES = tuple(divmod(FLAT_AT[i], LANES) for i in (3, 4, 5, 1))

SLOTS = 6
HALF = WIDE // 2
PITCH = 33


def unpack_kernel(
    plan, gathered, old_up, old_down, narrow, wide, hidden_out, rows_out, up_out, down_out, small_a, small_b, small_c,
    held, flat, woven, hidden, by_row, rows_low, up, down, sems, sem_out,
):
    n, share = plan.count, plan.share
    step = CH // LANES

    def fetch(k, slot):
        return pltpu.make_async_copy(gathered.at[k], held.at[slot], sems.at[slot])

    for k in range(SLOTS - 1):
        fetch(k, k).start()

    def widen(k, carry):
        slot = lax.rem(k, SLOTS)

        @pl.when(k + SLOTS - 1 < n)
        def _():
            fetch(k + SLOTS - 1, lax.rem(k + SLOTS - 1, SLOTS)).start()

        fetch(k, slot).wait()

        def body(b, inner):
            at = pl.ds(pl.multiple_of(b * 16, 16), 16)
            flat[pl.ds(share * k + b * 16, 16), :] = held[slot, at, :].astype(jnp.float32)
            return inner

        lax.fori_loop(0, plan.padded // 16, body, 0, unroll=4)
        return carry

    lax.fori_loop(0, n, widen, 0)

    copies = [
        pltpu.make_async_copy(source, target, sem_out.at[i])
        for i, (source, target) in enumerate(
            (
                (hidden, hidden_out.at[:, pl.ds(0, HALF)]), (rows_low, rows_out), (up, up_out),
                (down, down_out), (hidden, hidden_out.at[:, pl.ds(HALF, HALF)]),
            )
        )
    ]
    row, lane = PLACES[0]

    def spread(a, carry):
        by_row[pl.ds(narrow[a] * PITCH, 32), :] = flat[pl.ds(row + a * step, 32), :]
        return carry

    lax.fori_loop(0, C1, spread, 0, unroll=4)

    def columns(half):
        def column(t, carry):
            for begin in range(0, C1, 160):
                at = begin * PITCH + half * (HALF // LANES) + t
                values = by_row[pl.ds(at, 160, stride=PITCH), :]
                at = pl.ds(pl.multiple_of(t * LANES, LANES), LANES)
                hidden[begin : begin + 160, at] = values.astype(jnp.bfloat16)
            return carry

        lax.fori_loop(0, HALF // LANES, column, 0)

    columns(0)
    copies[0].start()

    quarter = C1 // 4
    for number, (ref, old, (line, begin)) in enumerate(zip((up, down), (old_up, old_down), PLACES[2:])):
        for u in range(-(-C1 // LANES)):
            width = min(LANES, C1 - u * LANES)
            place = lax.broadcasted_iota(jnp.int32, (quarter, LANES), 1)
            for b in range(4):
                first, rest = divmod(C1 * b + begin, LANES)
                here = flat[pl.ds(line + first + u, quarter, stride=step), :]
                after = flat[pl.ds(line + first + u + 1, quarter, stride=step), :]
                value = pltpu.roll(jnp.where(place >= rest, here, after), LANES - rest, 1)
                woven[pl.ds(b, quarter, stride=4), :] = value
            at = slice(u * LANES, u * LANES + width)
            ref[:, at] = moved(old[:, at], woven[:, :width])
        copies[2 + number].start()

    for ref, (begin, end) in zip((small_a, small_b, small_c), KEPT):
        ref[...] = flat[begin:end, :]
    copies[0].wait()
    columns(1)
    copies[4].start()

    row, lane = PLACES[1]

    def align(part, carry):
        place = lax.broadcasted_iota(jnp.int32, (40, LANES), 1)
        for b in range(4):
            first, rest = divmod(C1 * b + lane, LANES)
            tiles = [
                flat[pl.ds(row + part * (40 * step) + first + u, 40, stride=step), :]
                for u in range(C1P // LANES + 1)
            ]
            values = [
                pltpu.roll(jnp.where(place >= rest, here, after), LANES - rest, 1)
                for here, after in zip(tiles, tiles[1:])
            ]
            for u, value in enumerate(values):
                flat[pl.ds(part * (40 * PITCH) + b * 8 + u, 40, stride=PITCH), :] = value
        return carry

    lax.fori_loop(0, C1 // 40, align, 0)

    def scatter(a, carry):
        for b in range(4):
            by_row[pl.ds(wide[a * 4 + b] * 9, 8), :] = flat[pl.ds(a * PITCH + b * 8, 8), :]
        return carry

    lax.fori_loop(0, CH // 4, scatter, 0, unroll=4)

    def by_lane(part, carry):
        for u in range(C1P // LANES):
            values = by_row[pl.ds(part * (160 * 9) + u, 160, stride=9), :]
            at = pl.ds(pl.multiple_of(part * 160, 160), 160)
            rows_low[at, u * LANES : (u + 1) * LANES] = values.astype(jnp.bfloat16)
        return carry

    lax.fori_loop(0, CH // 160, by_lane, 0)
    copies[1].start()
    for copy in copies[1:]:
        copy.wait()


def unpack(plan, gathered, old_up, old_down, narrow, wide):
    lines = PADDED // LANES
    vmem = pl.BlockSpec(memory_space=pltpu.VMEM)
    hbm = pl.BlockSpec(memory_space=pl.ANY)
    dma = pltpu.SemaphoreType.DMA
    f32, low = jnp.float32, jnp.bfloat16
    return pl.pallas_call(
        functools.partial(unpack_kernel, plan),
        out_shape=(
            jax.ShapeDtypeStruct((C1, WIDE), low),
            jax.ShapeDtypeStruct((CH, C1P), low),
            jax.ShapeDtypeStruct((C1, C1), f32),
            jax.ShapeDtypeStruct((C1, C1), f32),
        )
        + tuple(jax.ShapeDtypeStruct((end - begin, LANES), f32) for begin, end in KEPT),
        in_specs=[hbm, vmem, vmem] + [pl.BlockSpec(memory_space=pltpu.SMEM)] * 2,
        out_specs=(hbm, hbm, hbm, hbm, vmem, vmem, vmem),
        scratch_shapes=[
            pltpu.VMEM((SLOTS, plan.padded, LANES), low),
            pltpu.VMEM((-(-lines // 8) * 8 + 16, LANES), f32),
            pltpu.VMEM((C1, LANES), f32),
            pltpu.VMEM((C1, HALF), low),
            pltpu.VMEM((CH * 9, LANES), f32),
            pltpu.VMEM((CH, C1P), low),
            pltpu.VMEM((C1, C1), f32),
            pltpu.VMEM((C1, C1), f32),
            dma((SLOTS,)),
            dma((5,)),
        ],
        compiler_params=pltpu.CompilerParams(vmem_limit_bytes=63 << 20),
    )(gathered, old_up, old_down, narrow, wide)


def moved(old, direction):
    return old.astype(jnp.float32) * (1.0 - learn_rate * weight_decay) - learn_rate * direction


def one_hot(condition):
    return jnp.where(condition, 1.0, 0.0).astype(jnp.bfloat16)


def product(left, right):
    return jnp.dot(left, right, preferred_element_type=jnp.float32)


def product_t(left, right):
    return lax.dot_general(left, right, (((1,), (1,)), ((), ())), preferred_element_type=jnp.float32)


TILE = 512
STEPS = -(-CH // TILE)
LAST = CH - (STEPS - 1) * TILE


DEEP = 256


def by_width(body):
    final = pl.program_id(0) == STEPS - 1

    @pl.when(jnp.logical_not(final))
    def _():
        body(TILE)

    @pl.when(final)
    def _():
        body(LAST)


def hidden_kernel(lines, wide, old, new):
    depth = lines.shape[1]
    base = pl.program_id(0) * TILE

    def body(width):
        direction = None
        for begin in range(0, depth, DEEP):
            end = min(begin + DEEP, depth)
            place = wide[begin:end, :] - base
            lane = lax.broadcasted_iota(jnp.int32, (end - begin, LANES), 1)
            hot = jnp.concatenate([one_hot(lane + u == place) for u in range(0, width, LANES)], axis=1)
            term = product(lines[:, begin:end], hot)
            direction = term if direction is None else direction + term
        new[:, :width] = moved(old[:, :width], direction)

    by_width(body)


def rebuild_hidden(lines, wide, old):
    lane = PLACES[0][1]
    wide = jnp.full((WIDE,), -1, jnp.int32).at[lane : lane + CH].set(wide)
    return pl.pallas_call(
        hidden_kernel,
        out_shape=jax.ShapeDtypeStruct((C1, CH), jnp.float32),
        grid=(STEPS,),
        in_specs=[
            pl.BlockSpec((C1, WIDE), lambda i: (0, 0)),
            pl.BlockSpec((WIDE, LANES), lambda i: (0, 0)),
            pl.BlockSpec((C1, TILE), lambda i: (0, i)),
        ],
        out_specs=pl.BlockSpec((C1, TILE), lambda i: (0, i)),
        compiler_params=pltpu.CompilerParams(vmem_limit_bytes=48 << 20),
    )(lines, jnp.broadcast_to(wide[:, None], (WIDE, LANES)), old)


def out_kernel(rows, narrow, old, new, turn):
    @pl.when(pl.program_id(0) == 0)
    def _():
        turn[...] = one_hot(lax.broadcasted_iota(jnp.int32, (C1, C1), 0) == narrow[...])

    def body(width):
        new[:, :width] = moved(old[:, :width], product_t(turn[...], rows[:width, :C1]))

    by_width(body)


def rebuild_out(rows, narrow, old):
    return pl.pallas_call(
        out_kernel,
        out_shape=jax.ShapeDtypeStruct((C1, CH), jnp.float32),
        grid=(STEPS,),
        in_specs=[
            pl.BlockSpec((TILE, C1P), lambda i: (i, 0)),
            pl.BlockSpec((1, C1), lambda i: (0, 0)),
            pl.BlockSpec((C1, TILE), lambda i: (0, i)),
        ],
        out_specs=pl.BlockSpec((C1, TILE), lambda i: (0, i)),
        scratch_shapes=[pltpu.VMEM((C1, C1), jnp.bfloat16)],
        compiler_params=pltpu.CompilerParams(vmem_limit_bytes=48 << 20),
    )(rows, narrow[None, :], old.T).T


def weave(source, rows, put, width=C1):
    group = CH // width
    for t in range(CH // LANES):
        b, begin = divmod(t * LANES, width)
        u, rest = divmod(begin, LANES)
        place = lax.broadcasted_iota(jnp.int32, (rows, LANES), 1)
        value = source[u, pl.ds(b, rows, stride=group), :]
        if rest:
            if begin + LANES - rest < width:
                after = source[u + 1, pl.ds(b, rows, stride=group), :]
                value = jnp.where(place >= rest, value, after)
            value = pltpu.roll(value, LANES - rest, 1)
        left = width - begin
        if left < LANES:
            following = source[0, pl.ds(b + 1, rows, stride=group), :]
            value = jnp.where(place < left, value, pltpu.roll(following, left, 1))
        put(t, value)


def place_kernel(
    nr, nc, normed, branch, pre, act, narrow_row, narrow_col, wide, up, cells,
    grad, padded, hidden, out, loose, up_rows, norm_t, branch_r, halo_cells, held_pre, held_act,
    sem_out, sems, sem_halo_s, sem_halo_r, sem_in,
):
    step = pl.program_id(0)
    steps = STEPS
    ratio = CH // LANES

    def out_copy(n, width):
        begin = n * (TILE // 4 * ratio)
        rows = width // 4 * ratio
        return pltpu.make_async_copy(
            out.at[pl.ds(pl.multiple_of(begin, 8), rows)],
            grad.at[pl.ds(pl.multiple_of(ROW_AT[4] + begin, 8), rows)],
            sem_out.at[n],
        )

    copies = [
        pltpu.make_async_copy(ref, grad.at[pl.ds(row, ref.shape[0])], sems.at[i])
        for i, (ref, row) in enumerate(((up_rows, ROW_AT[5]), (hidden, ROW_AT[3])))
    ] + [pltpu.make_async_copy(halo_cells, padded, sems.at[2])]

    fetch_pre = pltpu.make_async_copy(pre, held_pre, sem_in.at[0])
    fetch_act = pltpu.make_async_copy(act, held_act, sem_in.at[1])

    @pl.when(step == 0)
    def _():
        fetch_pre.start()
        fetch_act.start()
        halo_start(nr, nc, 3, cells, halo_cells, sem_halo_s, sem_halo_r)
        line = lax.broadcasted_iota(jnp.int32, (C1, C1), 1)
        norm_t[...] = product_t(one_hot(line == narrow_col[:, 0:1]), normed[:, :C1]).astype(jnp.bfloat16)
        line = lax.broadcasted_iota(jnp.int32, (C1, C1P), 0)
        branch_r[...] = product(branch[:, :C1], one_hot(line == narrow_row[...])).astype(jnp.bfloat16)
        for u in range(-(-C1 // LANES)):
            width = min(LANES, C1 - u * LANES)
            loose[u, :, 0:width] = up[0:C1, u * LANES : u * LANES + width]

        def put(t, value):
            up_rows[pl.ds(t, C1 // 4, stride=ratio), :] = value

        weave(loose, C1 // 4, put)
        copies[0].start()
        fetch_pre.wait()
        fetch_act.wait()

    def body(width):
        turned_pre = turned_act = None
        for begin in range(0, CH, DEEP):
            end = min(begin + DEEP, CH)
            line = lax.broadcasted_iota(jnp.int32, (end - begin, width), 0) + begin
            hot = one_hot(line == wide[:, :width])
            one = product(held_pre[:, begin:end], hot)
            two = product(held_act[:, begin:end], hot)
            turned_pre = one if turned_pre is None else turned_pre + one
            turned_act = two if turned_act is None else turned_act + two
        part = product(norm_t[...], turned_pre.astype(jnp.bfloat16))
        for t in range(width // LANES):
            at = pl.ds(step * (TILE // LANES) + t, C1, stride=ratio)
            hidden[at, :] = part[:, t * LANES : (t + 1) * LANES]
        part = inner_rows(turned_act.astype(jnp.bfloat16), branch_r[...])
        for u in range(-(-C1 // LANES)):
            loose[u, 0:width, :] = part[:, u * LANES : (u + 1) * LANES]

        def put_out(t, value):
            out[pl.ds(step * (TILE // 4 * ratio) + t, width // 4, stride=ratio), :] = value

        weave(loose, width // 4, put_out)
        out_copy(step, width).start()

    by_width(body)

    @pl.when(step == steps - 1)
    def _():
        copies[1].start()
        halo_finish(nr, nc, 3, cells, halo_cells, sem_halo_s, sem_halo_r)
        copies[2].start()

        def finish(n, carry):
            out_copy(n, TILE).wait()
            return carry

        lax.fori_loop(0, steps - 1, finish, 0)
        out_copy(steps - 1, LAST).wait()
        for copy in copies:
            copy.wait()


def place_gradients(nr, nc, space, normed, branch, pre, act, narrow, wide, up, cells):
    def whole(array):
        return pl.BlockSpec(
            array.shape, lambda i: (0,) * len(array.shape), pipeline_mode=pl.Buffered(1)
        )

    hbm = pl.BlockSpec(memory_space=pl.ANY)
    rows = pre.shape[0]
    batch, height, breadth, chans = cells.shape
    narrow_row = jnp.pad(narrow, (0, C1P - C1), constant_values=-1)[None, :]
    narrow_col = jnp.broadcast_to(narrow[:, None], (C1, LANES))
    framed = jax.ShapeDtypeStruct((batch, height + 6, breadth + 2 * EDGE, chans), cells.dtype)
    dma = pltpu.SemaphoreType.DMA
    return pl.pallas_call(
        functools.partial(place_kernel, nr, nc),
        out_shape=(jax.ShapeDtypeStruct((space, LANES), jnp.float32), framed),
        grid=(STEPS,),
        in_specs=[
            whole(normed), whole(branch), hbm, hbm, whole(narrow_row), whole(narrow_col),
            pl.BlockSpec((1, TILE), lambda i: (0, i)),
            whole(up), whole(cells),
        ],
        out_specs=(hbm, hbm),
        scratch_shapes=[
            pltpu.VMEM((C1 * CH // LANES, LANES), jnp.float32),
            pltpu.VMEM((C1 * CH // LANES, LANES), jnp.float32),
            pltpu.VMEM((C1P // LANES, C1, LANES), jnp.float32),
            pltpu.VMEM((C1 * C1 // LANES, LANES), jnp.float32),
            pltpu.VMEM((C1, rows), jnp.bfloat16),
            pltpu.VMEM((rows, C1P), jnp.bfloat16),
            pltpu.VMEM(framed.shape, framed.dtype),
            pltpu.VMEM(pre.shape, pre.dtype),
            pltpu.VMEM(act.shape, act.dtype),
            dma((STEPS,)), dma((3,)), dma((8,)), dma((8,)), dma((2,)),
        ],
        compiler_params=pltpu.CompilerParams(
            collective_id=3, has_side_effects=True, vmem_limit_bytes=60 << 20
        ),
    )(normed, branch, pre, act, narrow_row, narrow_col, wide[None, :], up, cells)


C0P = 256
C1P = 896
CIP = 128
EDGE = 16
CURVE = 0.7978845608028654
CUBE = 0.044715


def inner_rows(left, right):
    return lax.dot_general(left, right, (((0,), (0,)), ((), ())), preferred_element_type=jnp.float32)


def column_sum(values):
    return jnp.sum(values.astype(jnp.float32), axis=0, keepdims=True)


def gelu_and_slope(t):
    square = t * t
    bend = jnp.tanh(CURVE * (t + CUBE * (square * t)))
    half = 0.5 * (1.0 + bend)
    return t * half, half + 0.5 * t * (1.0 - bend * bend) * (CURVE * (1.0 + 3.0 * CUBE * square))


WAYS = [(dr, dc) for dr in (-1, 0, 1) for dc in (-1, 0, 1) if (dr, dc) != (0, 0)]
ORDER = sorted(range(8), key=lambda i: (WAYS[i][1] != 0, WAYS[i][0] == 0))


def halo_place(nr, nc):
    r = lax.axis_index("rows")
    return r, lax.axis_index("cols"), lambda dr: (r + dr >= 0) & (r + dr < nr)


def halo_copy(nr, nc, width, cells, out, sem_s, sem_r, i, receive):
    r, c, there = halo_place(nr, nc)
    height, breadth = cells.shape[1], cells.shape[2]
    dr, dc = WAYS[i]
    rows_from = {-1: (0, width), 0: (0, height), 1: (height - width, width)}[dr]
    rows_to = {-1: height + width, 0: width, 1: 0}[dr]
    cols_from = {-1: (0, EDGE), 0: (0, breadth), 1: (breadth - EDGE, EDGE)}[dc]
    cols_to = {-1: EDGE + breadth, 0: EDGE, 1: 0}[dc]
    sign = -1 if receive else 1
    return pltpu.make_async_remote_copy(
        src_ref=cells.at[:, pl.ds(*rows_from), pl.ds(*cols_from)],
        dst_ref=out.at[:, pl.ds(rows_to, rows_from[1]), pl.ds(cols_to, cols_from[1])],
        send_sem=sem_s.at[i],
        recv_sem=sem_r.at[i],
        device_id=(r + sign * dr, lax.rem(c + sign * dc + nc, nc)),
        device_id_type=MESH,
    )


def halo_start(nr, nc, width, cells, out, sem_s, sem_r):
    r, c, there = halo_place(nr, nc)
    height, breadth = cells.shape[1], cells.shape[2]
    barrier = pltpu.get_barrier_semaphore()
    for dr, dc in WAYS:
        @pl.when(there(dr))
        def _(dr=dr, dc=dc):
            pl.semaphore_signal(
                barrier, inc=1, device_id=(r + dr, lax.rem(c + dc + nc, nc)), device_id_type=MESH
            )

    edge = (r == 0) | (r == nr - 1)

    @pl.when(edge)
    def _():
        pl.semaphore_wait(barrier, 5)

    @pl.when(jnp.logical_not(edge))
    def _():
        pl.semaphore_wait(barrier, 8)

    for i in ORDER:
        @pl.when(there(WAYS[i][0]))
        def _(i=i):
            halo_copy(nr, nc, width, cells, out, sem_s, sem_r, i, False).start()

    for m in range(cells.shape[0]):
        for row in range(height):
            out[m, width + row, EDGE : EDGE + breadth, :] = cells[m, row]

    @pl.when(r == 0)
    def _():
        out[:, 0:width] = jnp.zeros((out.shape[0], width) + out.shape[2:], out.dtype)

    @pl.when(r == nr - 1)
    def _():
        out[:, height + width :] = jnp.zeros((out.shape[0], width) + out.shape[2:], out.dtype)


def halo_finish(nr, nc, width, cells, out, sem_s, sem_r):
    r, c, there = halo_place(nr, nc)
    for i in ORDER:
        @pl.when(there(-WAYS[i][0]))
        def _(i=i):
            halo_copy(nr, nc, width, cells, out, sem_s, sem_r, i, True).wait_recv()

        @pl.when(there(WAYS[i][0]))
        def _(i=i):
            halo_copy(nr, nc, width, cells, out, sem_s, sem_r, i, False).wait_send()


def halo_kernel(nr, nc, width, cells, out, sem_s, sem_r):
    halo_start(nr, nc, width, cells, out, sem_s, sem_r)
    halo_finish(nr, nc, width, cells, out, sem_s, sem_r)


def halo(nr, nc, width, cells, identity):
    batch, height, breadth, chans = cells.shape
    vmem = pl.BlockSpec(memory_space=pltpu.VMEM)
    return pl.pallas_call(
        functools.partial(halo_kernel, nr, nc, width),
        out_shape=jax.ShapeDtypeStruct(
            (batch, height + 2 * width, breadth + 2 * EDGE, chans), cells.dtype
        ),
        in_specs=[vmem],
        out_specs=vmem,
        scratch_shapes=[pltpu.SemaphoreType.DMA((8,)), pltpu.SemaphoreType.DMA((8,))],
        compiler_params=pltpu.CompilerParams(
            collective_id=identity, has_side_effects=True, vmem_limit_bytes=24 << 20
        ),
    )(cells)


SIDE = 8
REACH = 3
FINE_REACH = 2 * REACH + 1


def input_kernel(
    nr, state, w_in, w_down, vector, taps_out, slope_zero_out, h_zero_out, coarse, padded, lines,
    wide, taps_all, coarse_all, taps, slope_zero, h_zero, sems,
):
    r = lax.axis_index("rows")
    copies = [
        pltpu.make_async_copy(source, target, sems.at[i])
        for i, (source, target) in enumerate(((taps, taps_out), (slope_zero, slope_zero_out), (h_zero, h_zero_out)))
    ]
    lines[...] = jnp.zeros_like(lines)
    start = 0
    for number, size in enumerate((C0, C1, C1, C1, C1, CH, C1, C0, CI)):
        lines[number : number + 1, 0:size] = vector[:, start : start + size]
        start = start + size
    batch, rows, breadth, _ = state.shape
    half_h, half_w = rows // 2 - FINE_REACH, breadth // 2 - EDGE
    all_h, all_w = half_h + 2 * REACH, half_w + 2 * SIDE
    for m in range(batch):
        for y in range(rows):
            wide[m, y, SIDE : SIDE + breadth, :] = state[m, y].astype(jnp.float32)
    for m in range(batch):
        for y in range(rows):
            for f in range(4):
                start = SIDE + EDGE - 2 * SIDE - 1 + f
                line = wide[m, y, pl.ds(start, all_w, stride=2), :]
                low = line.astype(jnp.bfloat16)
                inner = line[SIDE : SIDE + half_w].astype(jnp.bfloat16)
                for dy in range(3):
                    i, sy = divmod(y - dy, 2)
                    if not 0 <= i < all_h:
                        continue
                    for dx in range(3):
                        if not 0 <= f - dx < 2:
                            continue
                        s, tap = sy * 2 + f - dx, slice((dy * 3 + dx) * CIP, (dy * 3 + dx + 1) * CIP)
                        begin = (m * all_h + i) * all_w
                        taps_all[s, begin : begin + all_w, tap] = low
                        if REACH <= i < REACH + half_h:
                            begin = (m * half_h + i - REACH) * half_w
                            taps[s, begin : begin + half_w, tap] = inner
    copies[0].start()
    size = all_h * all_w
    for m in range(batch):
        block = slice(m * size, (m + 1) * size)
        total = jnp.broadcast_to(lines[1:2, :C1P], (size, C1P))
        for s in range(4):
            value = product(taps_all[s, block, :], w_in[...]) + lines[0:1, :C0P]
            curved, slope = gelu_and_slope(value)
            for i in range(half_h):
                begin = (i + REACH) * all_w + SIDE
                at = slice((m * half_h + i) * half_w, (m * half_h + i + 1) * half_w)
                slope_zero[s, at, :] = slope[begin : begin + half_w]
                h_zero[s, at, :] = curved[begin : begin + half_w]
            total = total + product(curved.astype(jnp.bfloat16), w_down[s])
        coarse_all[...] = total
        for i in range(half_h):
            begin = (i + REACH) * all_w + SIDE
            at = slice((m * half_h + i) * half_w, (m * half_h + i + 1) * half_w)
            coarse[at, :] = coarse_all[begin : begin + half_w, :]
        if m == batch - 1:
            copies[1].start()
            copies[2].start()
        padded[m] = coarse_all[...].astype(jnp.bfloat16).reshape(padded.shape[1:])

    @pl.when(r == 0)
    def _():
        padded[:, 0:REACH] = jnp.zeros((batch, REACH) + padded.shape[2:], padded.dtype)

    @pl.when(r == nr - 1)
    def _():
        padded[:, all_h - REACH :] = jnp.zeros((batch, REACH) + padded.shape[2:], padded.dtype)

    for copy in copies:
        copy.wait()


def input_part(nr, state, w_in, w_down, vector):
    batch, rows, breadth, _ = state.shape
    half_h, half_w = rows // 2 - FINE_REACH, breadth // 2 - EDGE
    all_h, all_w = half_h + 2 * REACH, half_w + 2 * SIDE
    cells = batch * half_h * half_w
    vmem = pl.BlockSpec(memory_space=pltpu.VMEM)
    hbm = pl.BlockSpec(memory_space=pl.ANY)
    large = (
        jax.ShapeDtypeStruct((4, cells, 9 * CIP), jnp.bfloat16),
        jax.ShapeDtypeStruct((4, cells, C0P), jnp.float32),
        jax.ShapeDtypeStruct((4, cells, C0P), jnp.float32),
    )
    return pl.pallas_call(
        functools.partial(input_kernel, nr),
        out_shape=large
        + (
            jax.ShapeDtypeStruct((cells, C1P), jnp.float32),
            jax.ShapeDtypeStruct((batch, all_h, all_w, C1P), jnp.bfloat16),
            jax.ShapeDtypeStruct((16, CH), jnp.float32),
        ),
        in_specs=[vmem] * 4,
        out_specs=(hbm, hbm, hbm, vmem, vmem, vmem),
        scratch_shapes=[
            pltpu.VMEM((batch, rows, breadth + 2 * SIDE, CIP), jnp.float32),
            pltpu.VMEM((4, batch * all_h * all_w, 9 * CIP), jnp.bfloat16),
            pltpu.VMEM((all_h * all_w, C1P), jnp.float32),
        ]
        + [pltpu.VMEM(shape.shape, shape.dtype) for shape in large]
        + [pltpu.SemaphoreType.DMA((3,))],
        compiler_params=pltpu.CompilerParams(vmem_limit_bytes=60 << 20),
    )(state, w_in, w_down, vector)


def spread_lanes(padded, held):
    for m in range(padded.shape[0]):
        def body(y, carry, m=m):
            for u in range(C1P // LANES):
                held[u, m, y, 0 : padded.shape[2], :] = padded[m, y, :, u * LANES : (u + 1) * LANES].astype(jnp.float32)
            return carry

        lax.fori_loop(0, padded.shape[1], body, 0)


def convolve(held, w_dw, half_w, edge, put, back):
    tiles, batch, rows = held.shape[:3]
    height = rows - 2 * REACH

    def body(number, carry):
        u, m = number // batch, number % batch
        sums = [jnp.zeros((half_w, LANES), jnp.float32) for _ in range(height)]
        for x in range(7):
            for y in range(rows):
                window = held[u, m, y, pl.ds(edge - REACH + x, half_w), :]
                for i in range(height):
                    if 0 <= y - i < 7:
                        tap = (6 - (y - i)) * 7 + 6 - x if back else (y - i) * 7 + x
                        sums[i] = sums[i] + window * w_dw[pl.ds(tap, 1), lanes_at(u)]
        for i in range(height):
            put(u, m, i, sums[i])
        return carry

    lax.fori_loop(0, tiles * batch, body, 0)


def rows_at(m, i, height, half_w):
    return pl.ds(pl.multiple_of((m * height + i) * half_w, half_w), half_w)


def lanes_at(u):
    return pl.ds(pl.multiple_of(u * LANES, LANES), LANES)


PART = 640


LATE = ("coarse", "h_zero", "target", "weight", "w_hidden", "w_out_t", "w_up")
EARLY = ("normed", "act", "grad_mixed", "grad_branch", "grad_summed", "d_up")


def middle_kernel(names, *refs):
    ref = dict(zip(names, refs))
    batch, rows, breadth, _ = ref["padded"].shape
    cells = ref["coarse"].shape[0]
    height, half_w = rows - 2 * REACH, breadth - 2 * SIDE
    fetch, store, held_in, held_out = {}, {}, {}, {}
    for i, name in enumerate(LATE):
        held_in[name] = ref["held_" + name]
        fetch[name] = pltpu.make_async_copy(ref[name], held_in[name], ref["sem_in"].at[i])
        fetch[name].start()
    for i, name in enumerate(EARLY):
        held_out[name] = ref["held_" + name]
        store[name] = pltpu.make_async_copy(held_out[name], ref[name], ref["sem_out"].at[i])
    conv = ref["conv"]

    def depthwise(held):
        spread_lanes(ref["padded"], held)

        def put(u, m, i, value):
            conv[rows_at(m, i, height, half_w), lanes_at(u)] = value

        convolve(held, ref["w_dw"], half_w, SIDE, put, False)

    pl.run_scoped(depthwise, pltpu.VMEM((C1P // LANES, batch, rows, breadth, LANES), jnp.float32))
    pl.run_scoped(
        functools.partial(pointwise_part, ref, fetch, store, held_in, held_out),
        pltpu.VMEM((cells, CH), jnp.float32),
        pltpu.VMEM((cells, C1), jnp.bfloat16),
    )
    for name in EARLY:
        store[name].wait()


def pointwise_part(ref, fetch, store, held_in, held_out, slopes, spread_all):
    conv, total, sums, extra = ref["conv"], ref["total"], ref["sums"], ref["extra"]
    gain, w_head = ref["lines"].at[3:4, 0:C1P], ref["w_head"]
    normed, act = held_out["normed"], held_out["act"]
    grad_mixed, grad_branch, grad_summed = (
        held_out[name] for name in ("grad_mixed", "grad_branch", "grad_summed")
    )
    w_hidden, w_out_t, w_up = (held_in[name] for name in ("w_hidden", "w_out_t", "w_up"))
    target, weight, h_zero = (held_in[name] for name in ("target", "weight", "h_zero"))
    batch, rows, breadth, _ = ref["padded"].shape
    height, half_w = rows - 2 * REACH, breadth - 2 * SIDE

    inside = lax.broadcasted_iota(jnp.int32, (1, C1P), 1) < C1
    values = conv[...] + ref["lines"][2:3, :C1P]
    mean = jnp.sum(values, axis=1, keepdims=True) * (1.0 / C1)
    centered = jnp.where(inside, values - mean, 0.0)
    scale = lax.rsqrt(jnp.sum(centered * centered, axis=1, keepdims=True) * (1.0 / C1) + 1e-06)
    conv[...] = centered * scale
    normed[...] = (conv[...] * gain[...] + ref["lines"][4:5, :C1P]).astype(jnp.bfloat16)
    store["normed"].start()

    fetch["coarse"].wait()
    fetch["w_hidden"].wait()
    fetch["w_out_t"].wait()
    total[...] = held_in["coarse"][...]
    for begin in range(0, CH, PART):
        span = slice(begin, min(begin + PART, CH))
        value = product(normed[:, :C1], w_hidden[:, span]) + ref["lines"][5:6, span]
        curved, slope = gelu_and_slope(value)
        slopes[:, span] = slope
        act[:, span] = curved.astype(jnp.bfloat16)
        total[:, :C1] += product_t(act[:, span], w_out_t[:, span])
    store["act"].start()
    mixed = (total[...] + ref["lines"][6:7, :C1P]).astype(jnp.bfloat16)

    for name in ("h_zero", "target", "weight", "w_up"):
        fetch[name].wait()
    grad_mixed[...] = jnp.zeros_like(grad_mixed)
    loss = jnp.zeros((1, CI), jnp.float32)
    head_sum = jnp.zeros((1, CI), jnp.float32)
    up_sum = jnp.zeros((1, C0), jnp.float32)
    for s in range(4):
        sub_y, sub_x = divmod(s, 2)
        for m in range(batch):
            for i in range(height):
                at = rows_at(m, i, height, half_w)
                line = pl.ds(sub_x, half_w, stride=2)
                ref["goal"][at, :] = target[m, 2 * i + sub_y, line, :]
                ref["load"][at, :] = weight[2 * i + sub_y, line, :]
        w_up_s = w_up[:, s * C0 : (s + 1) * C0]
        upper = product(mixed[:, :C1], w_up_s) + ref["lines"][7:8, :C0]
        summed = (upper + h_zero[s, :, :C0]).astype(jnp.bfloat16)
        error = product(summed, w_head[...]) + ref["lines"][8:9, :CI] - ref["goal"][:, :CI]
        weighted = ref["load"][:, :CI] * error
        loss = loss + column_sum(weighted * error)
        grad_out = (2.0 * weighted).astype(jnp.bfloat16)
        head_sum = head_sum + column_sum(grad_out)
        if s == 0:
            ref["d_head"][...] = inner_rows(summed, grad_out)
        else:
            ref["d_head"][...] += inner_rows(summed, grad_out)
        spread = product_t(grad_out, w_head[...])
        grad_summed[s] = spread
        grad_upper = spread.astype(jnp.bfloat16)
        up_sum = up_sum + column_sum(grad_upper)
        spread_all[:, s * C0 : (s + 1) * C0] = grad_upper
        grad_mixed[:, :C1] += product_t(grad_upper, w_up_s)
    store["grad_summed"].start()
    store["grad_mixed"].start()
    held_out["d_up"][...] = inner_rows(mixed[:, :C1], spread_all[...])
    store["d_up"].start()
    grad_branch[...] = grad_mixed[...].astype(jnp.bfloat16)
    store["grad_branch"].start()
    sums[...] = jnp.zeros_like(sums)
    extra[...] = jnp.zeros_like(extra)
    extra[0:1, 0:CI] = loss
    extra[1:2, :] = column_sum(ref["weight_map"][...])
    sums[1:2, 0:CI] = head_sum
    sums[2:3, 0:C0] = up_sum
    sums[3:4, 0:C1P] = column_sum(grad_branch[...])

    total[...] = jnp.zeros_like(total)
    for begin in range(0, CH, PART):
        span = slice(begin, min(begin + PART, CH))
        value = product(grad_branch[:, :C1], w_out_t[:, span]) * slopes[:, span]
        low = value.astype(jnp.bfloat16)
        ref["grad_pre"][:, span] = low
        sums[4:5, span] = column_sum(low)
        total[:, :C1] += product_t(low, w_hidden[:, span])

    grad_normed = total[...]
    sums[5:6, 0:C1P] = column_sum(grad_normed * conv[...])
    sums[6:7, 0:C1P] = column_sum(grad_normed)
    inward = grad_normed * gain[...]
    first = jnp.sum(inward, axis=1, keepdims=True) * (1.0 / C1)
    second = jnp.sum(inward * conv[...], axis=1, keepdims=True) * (1.0 / C1)
    value = scale * jnp.where(inside, inward - first - conv[...] * second, 0.0)
    low = value.astype(jnp.bfloat16)
    sums[7:8, 0:C1P] = column_sum(low)
    ref["grad_conv"][...] = low.reshape(ref["grad_conv"].shape)


def middle_part(**given):
    cells = given["coarse"].shape[0]
    batch, rows, breadth, _ = given["padded"].shape
    half_h, half_w = rows - 2 * REACH, breadth - 2 * SIDE
    vmem = pl.BlockSpec(memory_space=pltpu.VMEM)
    hbm = pl.BlockSpec(memory_space=pl.ANY)
    f32, low = jnp.float32, jnp.bfloat16
    outs = {
        "normed": ((cells, C1P), low),
        "act": ((cells, CH), low),
        "grad_pre": ((cells, CH), low),
        "grad_mixed": ((cells, C1P), f32),
        "grad_branch": ((cells, C1P), low),
        "grad_summed": ((4, cells, C0), f32),
        "grad_conv": ((batch, half_h, half_w, C1P), low),
        "d_up": ((C1, C1), f32),
        "d_head": ((C0, CI), f32),
        "sums": ((8, CH), f32),
        "extra": ((8, LANES), f32),
    }
    scratch = {
        "conv": pltpu.VMEM((cells, C1P), f32),
        "total": pltpu.VMEM((cells, C1P), f32),
        "goal": pltpu.VMEM((cells, LANES), f32),
        "load": pltpu.VMEM((cells, LANES), f32),
        "sem_in": pltpu.SemaphoreType.DMA((len(LATE),)),
        "sem_out": pltpu.SemaphoreType.DMA((len(EARLY),)),
    }
    for name in LATE:
        scratch["held_" + name] = pltpu.VMEM(given[name].shape, given[name].dtype)
    for name in EARLY:
        scratch["held_" + name] = pltpu.VMEM(*outs[name])
    found = pl.pallas_call(
        functools.partial(middle_kernel, tuple(given) + tuple(outs) + tuple(scratch)),
        out_shape=tuple(jax.ShapeDtypeStruct(*out) for out in outs.values()),
        in_specs=[hbm if name in LATE else vmem for name in given],
        out_specs=tuple(hbm if name in EARLY else vmem for name in outs),
        scratch_shapes=list(scratch.values()),
        compiler_params=pltpu.CompilerParams(vmem_limit_bytes=62 << 20),
    )(*given.values())
    return dict(zip(outs, found))


AFTER = ("grad_mixed", "grad_summed", "slope_zero", "h_zero", "taps", "w_down")


def place_rows(source, rows, start, target, width=C1):
    def put(t, value):
        target[pl.ds(start + t, rows, stride=CH // LANES), :] = value

    weave(source, rows, put, width)


def outer_kernel(names, *refs):
    ref = dict(zip(names, refs))
    fetch = {}
    for i, name in enumerate(AFTER):
        fetch[name] = pltpu.make_async_copy(ref[name], ref["held_" + name], ref["sem_in"].at[i])
        fetch[name].start()
    stores = [
        pltpu.make_async_copy(
            source.at[pl.ds(0, count)], ref["grad"].at[pl.ds(row, count)], ref["sem_out"].at[i]
        )
        for i, (source, row, count) in enumerate(
            (
                (ref["piece_head"], ROW_AT[6], ROW_AT[7] - ROW_AT[6]),
                (ref["dw_rows"], ROW_AT[2], ROW_AT[3] - ROW_AT[2]),
                (ref["down_rows"], ROW_AT[1], ROW_AT[2] - ROW_AT[1]),
                (ref["in_rows"], 0, ROW_AT[1]),
                (ref["vector_rows"], ROW_AT[7], ref["vector_rows"].shape[0]),
            )
        )
    ]
    stores[0].start()
    grad_mixed, grad_summed, slope_zero, h_zero, taps, w_down = (ref["held_" + name] for name in AFTER)
    held, conv, sums, d_dw, d_in = (ref[name] for name in ("held", "conv", "sums", "d_dw", "d_in"))
    vector, loose = ref["vector"], ref["loose"]
    grad_conv = ref["grad_conv"]
    batch, height, half_w, _ = grad_conv.shape
    spread_lanes(ref["padded"], held)
    tiles = C1P // LANES
    d_dw[...] = jnp.zeros_like(d_dw)

    def taps_of(number, carry):
        u, m = number // batch, number % batch
        grads = [grad_conv[m, i, :, lanes_at(u)].astype(jnp.float32) for i in range(height)]
        for x in range(7):
            found = [jnp.zeros((8, LANES), jnp.float32) for _ in range(7)]
            for y in range(height + 6):
                window = held[u, m, y, pl.ds(SIDE - REACH + x, half_w), :]
                for i in range(height):
                    if 0 <= y - i < 7:
                        term = (window * grads[i]).reshape(half_w // 8, 8, LANES)
                        found[y - i] = found[y - i] + jnp.sum(term, axis=0)
            for dy in range(7):
                d_dw[u, pl.ds(dy * 7 + x, 1), :] += jnp.sum(found[dy], axis=0, keepdims=True)
        return carry

    lax.fori_loop(0, tiles * batch, taps_of, 0)
    place_rows(d_dw, 13, 0, ref["dw_rows"])
    stores[1].start()
    spread_lanes(ref["grad_padded"], held)

    def put(u, m, i, value):
        conv[rows_at(m, i, height, half_w), lanes_at(u)] = value

    convolve(held, ref["w_dw"], half_w, EDGE, put, True)
    for name in AFTER:
        fetch[name].wait()
    grad_coarse = (conv[...] + grad_mixed[...]).astype(jnp.bfloat16)
    vector[...] = jnp.zeros_like(vector)
    pieces = [(column_sum(grad_coarse), C1)] + [(sums[i : i + 1, :], C1) for i in (7, 5, 6)]
    pieces += [(sums[4:5, :], CH), (sums[3:4, :], C1), (sums[2:3, :], C0), (sums[1:2, :], CI)]
    start = C0
    for piece, size in pieces:
        vector[:, start : start + size] = piece[:, :size]
        start = start + size
    for s in range(4):
        part = inner_rows(h_zero[s].astype(jnp.bfloat16), grad_coarse)
        for u in range(tiles):
            loose[u, s * C0 : (s + 1) * C0, :] = part[:C0, u * LANES : (u + 1) * LANES]
    place_rows(loose, C1 // 4, 0, ref["down_rows"])
    stores[2].start()
    in_sum = jnp.zeros((1, C0), jnp.float32)
    for s in range(4):
        grad_h = product_t(grad_coarse, w_down[s])[:, :C0] + grad_summed[s]
        grad_a = (slope_zero[s, :, :C0] * grad_h).astype(jnp.bfloat16)
        in_sum = in_sum + column_sum(grad_a)
        if s == 0:
            d_in[...] = inner_rows(taps[s], grad_a)
        else:
            d_in[...] += inner_rows(taps[s], grad_a)
    vector[:, 0:C0] = in_sum
    for row in range(ref["vector_rows"].shape[0]):
        ref["vector_rows"][row : row + 1, :] = vector[:, row * LANES : (row + 1) * LANES]
    stores[4].start()

    close = ref["close"]
    used = 9 * CI
    close[:, used:, :] = jnp.zeros((2, close.shape[1] - used, LANES), jnp.float32)
    for tap in range(9):
        at = slice(tap * CI, (tap + 1) * CI)
        close[0, at, :] = d_in[tap * CIP : tap * CIP + CI, 0:LANES]
        close[1, at, 0 : C0 - LANES] = d_in[tap * CIP : tap * CIP + CI, LANES:C0]
    ref["in_rows"][0 : ROW_AT[0], :] = jnp.zeros((ROW_AT[0], LANES), jnp.float32)
    place_rows(close, close.shape[1] * C0 // CH, ROW_AT[0], ref["in_rows"], C0)
    stores[3].start()
    for store in stores:
        store.wait()


def outer_part(grad, **given):
    cells = given["grad_mixed"].shape[0]
    batch, rows, breadth, _ = given["grad_padded"].shape
    vmem = pl.BlockSpec(memory_space=pltpu.VMEM)
    hbm = pl.BlockSpec(memory_space=pl.ANY)
    f32 = jnp.float32
    groups = -(-9 * CI * C0 // CH)
    scratch = {
        "held": pltpu.VMEM((C1P // LANES, batch, rows, breadth, LANES), f32),
        "conv": pltpu.VMEM((cells, C1P), f32),
        "d_dw": pltpu.VMEM((C1P // LANES, 56, LANES), f32),
        "d_in": pltpu.VMEM((9 * CIP, C0), f32),
        "vector": pltpu.VMEM((1, (grad.shape[0] - ROW_AT[7]) * LANES), f32),
        "vector_rows": pltpu.VMEM((grad.shape[0] - ROW_AT[7], LANES), f32),
        "loose": pltpu.VMEM((C1P // LANES, C1, LANES), f32),
        "close": pltpu.VMEM((2, groups * CH // C0, LANES), f32),
        "dw_rows": pltpu.VMEM((13 * CH // LANES + 3, LANES), f32),
        "down_rows": pltpu.VMEM((ROW_AT[2] - ROW_AT[1], LANES), f32),
        "in_rows": pltpu.VMEM((ROW_AT[0] + groups * CH // LANES + 4, LANES), f32),
        "sem_in": pltpu.SemaphoreType.DMA((len(AFTER),)),
        "sem_out": pltpu.SemaphoreType.DMA((5,)),
    }
    for name in AFTER:
        scratch["held_" + name] = pltpu.VMEM(given[name].shape, given[name].dtype)
    return pl.pallas_call(
        functools.partial(outer_kernel, ("before",) + tuple(given) + ("grad",) + tuple(scratch)),
        out_shape=jax.ShapeDtypeStruct(grad.shape, grad.dtype),
        in_specs=[hbm] + [hbm if name in AFTER + ("piece_head",) else vmem for name in given],
        out_specs=hbm,
        input_output_aliases={0: 0},
        scratch_shapes=list(scratch.values()),
        compiler_params=pltpu.CompilerParams(vmem_limit_bytes=62 << 20),
    )(grad, *given.values())


def as_rows(piece, rows):
    flat = piece.reshape(-1)
    return jnp.pad(flat, (0, rows * LANES - flat.shape[0])).reshape(rows, LANES)


def widened(array, *shape):
    return jnp.pad(array, [(0, full - now) for full, now in zip(shape, array.shape)])


def on_device(
    inputs,
    targets,
    land_mask,
    volume,
    date_index,
    perm_narrow,
    perm_wide,
    w_in,
    w_down,
    w_dw,
    w_hidden,
    w_out,
    w_up,
    w_head,
    biases_gains,
    moment_first,
    moment_second,
):
    rows, cols = lax.axis_size("rows"), lax.axis_size("cols")
    weight = land_mask.astype(jnp.float32) * volume
    height, breadth = weight.shape
    half_h, half_w = (height // 2, breadth // 2)
    cells = MB * half_h * half_w
    matrices = (w_in, w_down, w_dw, w_hidden, w_out, w_up, w_head)

    def dates(field):
        picked = jnp.concatenate(
            [lax.dynamic_slice_in_dim(field, date_index[m], 1, 0, allow_negative_indices=False) for m in range(MB)]
        )
        return widened(picked, MB, height, breadth, CIP)

    w_in_p = widened(w_in.reshape(9, CI, C0), 9, CIP, C0P).reshape(9 * CIP, C0P)
    w_down_p = widened(w_down.reshape(4, C0, C1), 4, C0P, C1P)
    w_dw_p = widened(w_dw.astype(jnp.float32), 56, C1P)
    weight_map = jnp.broadcast_to(weight[:, :, None], (height, breadth, LANES))

    state = halo(rows, cols, FINE_REACH, dates(inputs), 1)
    taps, slope_zero, h_zero, coarse, padded, lines = input_part(
        rows, state, w_in_p, w_down_p, biases_gains[None, :]
    )
    mid = middle_part(
        padded=padded, coarse=coarse, h_zero=h_zero, target=dates(targets).astype(jnp.float32),
        weight=weight_map, weight_map=weight, w_dw=w_dw_p, w_hidden=w_hidden, w_out_t=w_out.T,
        w_up=w_up, w_head=w_head, lines=lines,
    )
    space = Plan(rows, cols, PADDED).space
    grad, grad_padded = place_gradients(
        rows, cols, space, mid["normed"], mid["grad_branch"], mid["grad_pre"], mid["act"],
        perm_narrow, perm_wide, mid["d_up"], mid["grad_conv"],
    )
    grad = outer_part(
        grad, padded=padded, grad_padded=grad_padded, grad_conv=mid["grad_conv"],
        grad_mixed=mid["grad_mixed"], grad_summed=mid["grad_summed"], slope_zero=slope_zero,
        h_zero=h_zero, taps=taps, w_dw=w_dw_p, w_down=w_down_p, sums=mid["sums"],
        piece_head=as_rows(mid["d_head"], ROW_AT[7] - ROW_AT[6]),
    )
    plan, (gathered, first, second, totals) = exchange(
        rows, cols, grad, moment_first, moment_second, mid["extra"]
    )
    hidden_p, out_p, new_up, new_down, small_a, small_b, small_c = unpack(plan, gathered, w_up, w_down, perm_narrow, perm_wide)
    small = {0: (small_a, 0), 2: (small_b, 1), 6: (small_c, 2), 7: (small_c, 2)}
    whole = {
        1: new_down,
        3: rebuild_hidden(hidden_p, perm_wide, w_hidden),
        4: rebuild_out(out_p, perm_narrow, w_out),
        5: new_up,
    }
    olds = matrices + (biases_gains,)
    news = []
    for index, old in enumerate(olds):
        if index in whole:
            news.append(whole[index])
        else:
            source, which = small[index]
            start = FLAT_AT[index] - KEPT[which][0] * LANES
            piece = source.reshape(-1)[start : start + old.size].reshape(old.shape)
            news.append(moved(old, piece) if index < 7 else old - learn_rate * piece)
    return tuple(news) + (
        first.reshape(-1),
        second.reshape(-1),
        totals[0, 0],
        MB * CI * totals[1, 0],
        totals[8, 0],
    )


def solution(mesh):
    return jax.shard_map(
        on_device,
        mesh=mesh,
        in_specs=(
            P(None, "rows", "cols", None),
            P(None, "rows", "cols", None),
            P("rows", "cols"),
            P("rows", "cols"),
            P(),
            P(),
            P(),
            P(),
            P(),
            P(),
            P(),
            P(),
            P(),
            P(),
            P(),
            P(("rows", "cols")),
            P(("rows", "cols")),
        ),
        out_specs=(
            P(),
            P(),
            P(),
            P(),
            P(),
            P(),
            P(),
            P(),
            P(("rows", "cols")),
            P(("rows", "cols")),
            P(),
            P(),
            P(),
        ),
        check_vma=False,
    )
```

```python
import functools
import types

import jax
import jax.numpy as jnp
from jax import lax
from jax.experimental import pallas as pl
from jax.experimental.pallas import tpu as pltpu
from jax.sharding import PartitionSpec as P

CI = 77
C0 = 200
C1 = 800
CH = 3200
MB = 2
STEP = 5
LANES = 128
MESH = pl.DeviceIdType.MESH
ROUNDER = 12582912.0

decay_first = 0.9
decay_second = 0.99
epsilon = 1e-08
learn_rate = 0.02
weight_decay = 0.1
clip_limit = 1.0

VEC = 4 * C1 + CH + C1 + 2 * C0 + CI
SIZES = (9 * CI * C0, 4 * C0 * C1, 49 * C1, C1 * CH, CH * C1, C1 * 4 * C0, C0 * CI, VEC)
PADDED = 6602752
FLAT_AT = []
ROW_AT = []
for size in SIZES:
    flat_here = FLAT_AT[-1] + SIZES[len(FLAT_AT) - 1] if FLAT_AT else PADDED - sum(SIZES)
    row_here = ROW_AT[-1] + -(-SIZES[len(ROW_AT) - 1] // 1024) * 8 if ROW_AT else 0
    row_here = max(row_here, -(-flat_here // 1024) * 8)
    FLAT_AT.append(flat_here)
    ROW_AT.append(row_here)
SHIFTS = []
for flat_here, row_here, size in zip(FLAT_AT, ROW_AT, SIZES):
    moved = divmod(row_here * LANES - flat_here, LANES)
    if SHIFTS and SHIFTS[-1][:2] == moved:
        SHIFTS[-1] = moved + (SHIFTS[-1][2], flat_here + size)
    else:
        SHIFTS.append(moved + (flat_here, flat_here + size))
MAX_SHIFT = max(s[0] for s in SHIFTS) + 1


def bit_masks(bits):
    masks = [()]
    for bit in bits:
        masks = masks + [m + (bit,) for m in masks]
    return sorted(masks, key=lambda m: -len(m))


class Plan:
    def __init__(self, rows, cols, total):
        self.rows, self.cols, self.count = rows, cols, rows * cols
        self.share = total // LANES // self.count
        self.bits = rows.bit_length() - 1
        need = 7 + self.share + MAX_SHIFT + 1
        self.block = 64 if need > 1024 else 32
        self.window = -(-need // (2 * self.block)) * 2 * self.block
        self.part = self.window // 2
        self.blocks = self.part // self.block
        self.scales = self.blocks
        upper = list(range(1, self.bits))
        self.orders = [upper, upper[1:] + upper[:1]]
        self.stages = len(upper)
        self.space = (self.share * (self.count - 1)) // 8 * 8 + self.window
        self.padded = -(-self.share // 16) * 16
        cut = -(-self.padded // 32) * 16
        self.cuts = [(0, cut), (cut, self.padded - cut)]
        self.local = self.count // 2


def exchange_kernel(
    plan, grad, m_first, m_second, extra, full, first, second, totals,
    acc, near, q_send, q_recv, s_send, s_recv, z_send, z_recv, zs_send, zs_recv,
    rolled, step, low, stats,
    sem_load, sem_near_s, sem_near_r, sem_qs, sem_qr, sem_ss, sem_sr,
    sem_zs, sem_zr, sem_zss, sem_zsr, sem_ts, sem_tr, sem_own,
    sem_gs, sem_gr, sem_hs, sem_hr, sem_cs, sem_cr,
):
    nr, nc, n = plan.rows, plan.cols, plan.count
    r = lax.axis_index("rows")
    c = lax.axis_index("cols")
    me = r * nc + c
    part, window, share = plan.part, plan.window, plan.share

    def flipped(mask):
        out = r
        for bit in mask:
            here = (r // (1 << bit)) % 2
            out = out + (1 - 2 * here) * (1 << bit)
        return out

    def remote(src, dst, send, recv, row, col):
        return pltpu.make_async_remote_copy(
            src_ref=src, dst_ref=dst, send_sem=send, recv_sem=recv,
            device_id=(row, col), device_id_type=MESH,
        )

    barrier = pltpu.get_barrier_semaphore()

    def greet(d, carry):
        k = lax.rem(me + d, n)
        pl.semaphore_signal(barrier, inc=1, device_id=(k // nc, k % nc), device_id_type=MESH)
        return carry

    lax.fori_loop(1, n, greet, 0)
    pl.semaphore_wait(barrier, n - 1)

    upper = list(range(1, plan.bits))
    masks = bit_masks(upper)

    def local_index(mask, col):
        return (flipped(mask) // 2) * nc + col

    def window_start(row, col):
        return pl.multiple_of((share * (row * nc + col)) // 8 * 8, 8)

    def near_copy(mask, col):
        row = flipped(mask + (0,))
        return remote(
            grad.at[pl.ds(window_start(row, col), window)],
            near.at[local_index(mask, col)],
            sem_near_s.at[local_index(mask, col)], sem_near_r.at[local_index(mask, col)],
            flipped((0,)), c,
        )

    def load_copy(mask, col):
        index = local_index(mask, col)
        return pltpu.make_async_copy(
            grad.at[pl.ds(window_start(flipped(mask), col), window)], acc.at[index], sem_load.at[index]
        )

    half_way = nc // 2

    def column_of(t):
        return jnp.where(t == 1, half_way, jnp.where(t <= half_way, t - 1, t))

    def begin(t, carry):
        col = lax.rem(c + column_of(t), nc)
        for mask in masks:
            near_copy(mask, col).start()
            load_copy(mask, col).start()
        return carry

    lax.fori_loop(1, nc + 1, begin, 0)

    def encode(index, p, q_ref, s_ref):
        def body(b, carry):
            at = pl.ds(pl.multiple_of(b * plan.block, plan.block), plan.block)
            rows_at = pl.ds(pl.multiple_of(p * part + b * plan.block, 8), plan.block)
            values = acc[index, rows_at, :]
            top = jnp.maximum(jnp.max(jnp.abs(values), axis=0, keepdims=True), 1e-30)
            scaled = values * (32766.0 / top)
            scaled = (scaled + ROUNDER) - ROUNDER
            q_ref[at, :] = scaled.astype(jnp.int32).astype(jnp.int16)
            s_ref[pl.ds(b, 1), :] = top * (1.0 / 32766.0)
            return carry

        lax.fori_loop(0, plan.blocks, body, 0)

    def decode(index, p, q_ref, s_ref):
        def body(b, carry):
            at = pl.ds(pl.multiple_of(b * plan.block, plan.block), plan.block)
            rows_at = pl.ds(pl.multiple_of(p * part + b * plan.block, 8), plan.block)
            acc[index, rows_at, :] += q_ref[at, :].astype(jnp.float32) * s_ref[pl.ds(b, 1), :]
            return carry

        lax.fori_loop(0, plan.blocks, body, 0)

    def stage_base(stage):
        return sum((1 << (plan.stages - 1 - s)) for s in range(stage)) * nc

    def hop(p, stage, slot):
        row = flipped((plan.orders[p][stage],))
        at = stage_base(stage) + slot
        return (
            remote(q_send.at[p, at], q_recv.at[p, at], sem_qs.at[p, at], sem_qr.at[p, at], row, c),
            remote(s_send.at[p, at], s_recv.at[p, at], sem_ss.at[p, at], sem_sr.at[p, at], row, c),
        )

    def send_stage(p, stage, number, mask, col):
        bit = plan.orders[p][stage]
        index = local_index(mask + (bit,), col)
        slot = number * nc + col
        at = stage_base(stage) + slot
        encode(index, p, q_send.at[p, at], s_send.at[p, at])
        for copy in hop(p, stage, slot):
            copy.start()

    def take_stage(p, stage, number, mask, col):
        slot = number * nc + col
        for copy in hop(p, stage, slot):
            copy.wait_recv()
        at = stage_base(stage) + slot
        decode(local_index(mask, col), p, q_recv.at[p, at], s_recv.at[p, at])

    def free_masks(p, stage):
        rest = plan.orders[p][stage + 1 :]
        found = bit_masks(rest)
        if rest:
            found = [m for m in found if rest[0] in m] + [m for m in found if rest[0] not in m]
        return found

    def far_copy(p, d):
        col = lax.rem(c + d, nc)
        return (
            remote(z_send.at[p, d - 1], z_recv.at[p, d - 1], sem_zs.at[p, d - 1], sem_zr.at[p, d - 1], r, col),
            remote(zs_send.at[p, d - 1], zs_recv.at[p, d - 1], sem_zss.at[p, d - 1], sem_zsr.at[p, d - 1], r, col),
        )

    def join(t):
        d = column_of(t)
        col = lax.rem(c + d, nc)
        for mask in masks:
            index = local_index(mask, col)
            near_copy(mask, col).wait_recv()
            load_copy(mask, col).wait()

            def body(b, inner, index=index):
                at = pl.ds(pl.multiple_of(b * plan.block, plan.block), plan.block)
                acc[index, at, :] += near[index, at, :]
                return inner

            lax.fori_loop(0, 2 * plan.blocks, body, 0)
            for p in range(2):
                bit = plan.orders[p][0]
                if bit in mask:
                    rest = tuple(b for b in mask if b != bit)
                    options = free_masks(p, 0)
                    number = [sorted(o) for o in options].index(sorted(rest))
                    send_stage(p, 0, number, rest, col)

    def take(stage, t):
        d = column_of(t)
        col = lax.rem(c + d, nc)
        for number in range(1 << (plan.stages - 1 - stage)):
            for p in range(2):
                mask = free_masks(p, stage)[number]
                take_stage(p, stage, number, mask, col)
                if stage + 1 < plan.stages:
                    bit = plan.orders[p][stage + 1]
                    if bit in mask:
                        rest = tuple(b for b in mask if b != bit)
                        options = free_masks(p, stage + 1)
                        following = [sorted(o) for o in options].index(sorted(rest))
                        send_stage(p, stage + 1, following, rest, col)
                else:
                    @pl.when(d < nc)
                    def _(p=p):
                        encode(local_index((), col), p, z_send.at[p, d - 1], zs_send.at[p, d - 1])
                        for copy in far_copy(p, d):
                            copy.start()

    mine = local_index((), c)

    def gather_far(d, carry):
        for p in range(2):
            for copy in far_copy(p, d):
                copy.wait_recv()
            decode(mine, p, z_recv.at[p, d - 1], zs_recv.at[p, d - 1])
        return carry


    def turn_of(t, carry):
        @pl.when(t <= nc)
        def _():
            join(t)

        for stage in range(plan.stages):
            d = t - 1 - stage

            @pl.when((d >= 1) & (d <= nc))
            def _(stage=stage, d=d):
                take(stage, d)

        @pl.when((t > nc) & (t - nc < nc))
        def _():
            gather_far(column_of(t - nc), 0)

        return carry

    lax.fori_loop(1, nc + plan.stages + 1, turn_of, 0)

    def gather_rest(q, carry):
        return gather_far(column_of(q), carry)

    lax.fori_loop(min(plan.stages + 1, nc), nc, gather_rest, 0)

    offset = lax.rem(share * me, 8)
    low_end, high_end = share * me * LANES, share * (me + 1) * LANES
    for number, (shift_rows, shift_lanes, begin, end) in enumerate(SHIFTS):
        def turn(b, carry, number=number, shift_lanes=shift_lanes):
            at = pl.ds(pl.multiple_of(b * plan.block, plan.block), plan.block)
            rolled[number, at, :] = pltpu.roll(acc[mine, at, :], LANES - shift_lanes, 1)
            return carry

        @pl.when((low_end < end) & (high_end > begin))
        def _(turn=turn):
            lax.fori_loop(0, 2 * plan.blocks, turn, 0)

    def share_rows(start, length, chosen):
        lane = lax.broadcasted_iota(jnp.int32, (length, LANES), 1)
        out = jnp.zeros((length, LANES), jnp.float32)
        if len(chosen) > 1:
            line = lax.broadcasted_iota(jnp.int32, (length, LANES), 0)
            flat = (share * me + start + line) * LANES + lane
        for number in chosen:
            shift_rows, shift_lanes, begin, end = SHIFTS[number]
            here = rolled[number, pl.ds(offset + start + shift_rows, length), :]
            after = rolled[number, pl.ds(offset + start + shift_rows + 1, length), :]
            value = jnp.where(lane < LANES - shift_lanes, here, after)
            if len(chosen) > 1:
                value = jnp.where((flat >= begin) & (flat < end), value, out)
            out = value
        return out

    chunk = 32
    whole, tail = share // chunk, share % chunk
    stats[me, 8:16, :] = extra[...]

    def squares(chosen):
        def square(b, total):
            start = pl.multiple_of(b * chunk, chunk)
            value = share_rows(start, chunk, chosen)
            step[pl.ds(start, chunk), :] = value
            return total + jnp.sum((value * value).reshape(chunk // 8, 8, LANES), axis=0)

        total = lax.fori_loop(0, whole, square, jnp.zeros((8, LANES), jnp.float32))
        stats[me, 0:8, :] = total
        if tail:
            value = share_rows(whole * chunk, tail, chosen)
            step[whole * chunk : share, :] = value
            stats[me, 0:1, :] += jnp.sum(value * value, axis=0, keepdims=True)

    largest = max(range(len(SHIFTS)), key=lambda i: SHIFTS[i][3] - SHIFTS[i][2])
    alone = (low_end >= SHIFTS[largest][2]) & (high_end <= SHIFTS[largest][3])

    @pl.when(alone)
    def _():
        squares((largest,))

    @pl.when(jnp.logical_not(alone))
    def _():
        squares(tuple(range(len(SHIFTS))))

    def stat_copy(target, source):
        return remote(
            stats.at[me], stats.at[me], sem_ts.at[target], sem_tr.at[me], target // nc, target % nc
        )

    def stat_wait(source):
        return remote(
            stats.at[source], stats.at[source], sem_ts.at[source], sem_tr.at[source],
            source // nc, source % nc,
        )

    def send_stat(d, carry):
        stat_copy(lax.rem(me + d, n), me).start()
        return carry

    lax.fori_loop(1, n, send_stat, 0)

    def wait_stat(d, carry):
        stat_wait(lax.rem(me + d, n)).wait_recv()
        return carry

    lax.fori_loop(1, n, wait_stat, 0)

    def add_stat(k, total):
        return total + stats[k]

    sums = lax.fori_loop(0, n, add_stat, jnp.zeros((16, LANES), jnp.float32))
    norm = jnp.sqrt(jnp.sum(sums[0:8], keepdims=True))
    totals[0:1, :] = jnp.broadcast_to(jnp.sum(sums[8:9], keepdims=True), (1, LANES))
    totals[1:2, :] = jnp.broadcast_to(jnp.sum(sums[9:10], keepdims=True), (1, LANES))
    totals[2:8, :] = jnp.zeros((6, LANES), jnp.float32)
    totals[8:16, :] = jnp.broadcast_to(norm, (8, LANES))
    clip = jnp.minimum(1.0, clip_limit / norm)

    def update(start, length):
        clipped = step[pl.ds(start, length), :] * clip
        one = decay_first * m_first[pl.ds(start, length), :] + (1.0 - decay_first) * clipped
        two = decay_second * m_second[pl.ds(start, length), :] + (1.0 - decay_second) * clipped * clipped
        first[pl.ds(start, length), :] = one
        second[pl.ds(start, length), :] = two
        step[pl.ds(start, length), :] = (
            one / (1.0 - decay_first**STEP) / (jnp.sqrt(two / (1.0 - decay_second**STEP)) + epsilon)
        )

    def update_chunk(b, carry):
        update(pl.multiple_of(b * chunk, chunk), chunk)
        return carry

    lax.fori_loop(0, whole, update_chunk, 0)
    if tail:
        update(whole * chunk, tail)
    if plan.padded > share:
        step[share : plan.padded, :] = jnp.zeros((plan.padded - share, LANES), jnp.float32)

    def narrow(b, carry):
        at = pl.ds(pl.multiple_of(b * 16, 16), 16)
        low[at, :] = step[at, :].astype(jnp.bfloat16)
        return carry

    lax.fori_loop(0, plan.padded // 16, narrow, 0)

    own = pltpu.make_async_copy(low, full.at[me], sem_own)
    own.start()
    own.wait()

    back = [list(reversed(order)) for order in plan.orders]

    def piece(mask, col, p):
        begin, length = plan.cuts[p]
        return full.at[flipped(mask) * nc + col, pl.ds(begin, length)]

    def along(direction, col, p, receive):
        step_col = 1 if direction == 0 else -1
        target = c - step_col if receive else c + step_col
        ref = piece((), col, p)
        return remote(ref, ref, sem_gs.at[direction, col, p], sem_gr.at[direction, col, p], r, target)

    def gather_masks(p, stage):
        return bit_masks(back[p][:stage])

    def gather_base(stage):
        return sum(1 << s for s in range(stage)) * nc

    def across(p, stage, number, mask, col):
        at = gather_base(stage) + number * nc + col
        ref = piece(mask, col, p)
        return remote(ref, ref, sem_hs.at[p, at], sem_hr.at[p, at], flipped((back[p][stage],)), c)

    def across_recv(p, stage, number, mask, col):
        at = gather_base(stage) + number * nc + col
        ref = piece(mask + (back[p][stage],), col, p)
        return remote(ref, ref, sem_hs.at[p, at], sem_hr.at[p, at], flipped((back[p][stage],)), c)

    def inward(p, mask, col):
        number = masks.index(tuple(sorted(mask)))
        at = number * nc + col
        ref = piece(mask, col, p)
        return remote(ref, ref, sem_cs.at[p, at], sem_cr.at[p, at], flipped((0,)), c)

    def inward_recv(p, mask, col):
        number = masks.index(tuple(sorted(mask)))
        at = number * nc + col
        ref = piece(mask + (0,), col, p)
        return remote(ref, ref, sem_cs.at[p, at], sem_cr.at[p, at], flipped((0,)), c)

    def spread(p, mask, col, stage):
        for later in range(stage, plan.stages):
            options = [sorted(o) for o in gather_masks(p, later)]
            if sorted(mask) in options:
                across(p, later, options.index(sorted(mask)), mask, col).start()
        inward(p, mask, col).start()

    def near_cols(t):
        if t == 0:
            return [(0, c)]
        return [(0, c - t), (1, c + t)]

    def inside(col):
        return (col >= 0) & (col < nc)

    for time in range(nc + plan.stages):
        for stage in range(plan.stages + 1):
            t = time - stage
            if not 0 <= t < nc:
                continue
            if stage == 0:
                if t == 0:
                    for p in range(2):
                        @pl.when(c < nc - 1)
                        def _(p=p):
                            along(0, c, p, False).start()

                        @pl.when(c > 0)
                        def _(p=p):
                            along(1, c, p, False).start()

                        spread(p, (), c, 0)
                else:
                    for direction, col in near_cols(t):
                        @pl.when(inside(col))
                        def _(direction=direction, col=col):
                            for p in range(2):
                                along(direction, col, p, True).wait_recv()
                                if direction == 0:
                                    @pl.when(c < nc - 1)
                                    def _():
                                        along(0, col, p, False).start()
                                else:
                                    @pl.when(c > 0)
                                    def _():
                                        along(1, col, p, False).start()
                                spread(p, (), col, 0)
            else:
                for direction, col in near_cols(t):
                    @pl.when(inside(col))
                    def _(col=col, stage=stage):
                        for number in range(1 << (stage - 1)):
                            for p in range(2):
                                mask = gather_masks(p, stage - 1)[number]
                                across_recv(p, stage - 1, number, mask, col).wait_recv()
                                spread(p, mask + (back[p][stage - 1],), col, stage)

    for mask in masks:
        def finish(col, carry, mask=mask):
            for p in range(2):
                inward_recv(p, mask, col).wait_recv()
                inward(p, mask, col).wait_send()
            near_copy(mask, col).wait_send()
            return carry

        lax.fori_loop(0, nc, finish, 0)
    for p in range(2):
        for stage in range(plan.stages):
            for number, mask in enumerate(gather_masks(p, stage)):
                def sent(col, carry, p=p, stage=stage, number=number, mask=mask):
                    across(p, stage, number, mask, col).wait_send()
                    return carry

                lax.fori_loop(0, nc, sent, 0)
            for number in range(1 << (plan.stages - 1 - stage)):
                def left(col, carry, p=p, stage=stage, number=number):
                    for copy in hop(p, stage, number * nc + col):
                        copy.wait_send()
                    return carry

                lax.fori_loop(0, nc, left, 0)

        def gone(col, carry, p=p):
            @pl.when((col <= c) & (c < nc - 1))
            def _():
                along(0, col, p, False).wait_send()

            @pl.when((col >= c) & (c > 0))
            def _():
                along(1, col, p, False).wait_send()

            return carry

        lax.fori_loop(0, nc, gone, 0)

        def far_gone(d, carry, p=p):
            for copy in far_copy(p, d):
                copy.wait_send()
            return carry

        lax.fori_loop(1, nc, far_gone, 0)

    def stat_gone(d, carry):
        stat_copy(lax.rem(me + d, n), me).wait_send()
        return carry

    lax.fori_loop(1, n, stat_gone, 0)


def exchange(rows, cols, grad, m_first, m_second, extra):
    plan = Plan(rows, cols, m_first.size * rows * cols)
    n, nc, share = plan.count, plan.cols, plan.share
    hops = sum(1 << s for s in range(plan.stages)) * nc
    dma = pltpu.SemaphoreType.DMA
    far = max(nc - 1, 1)
    vmem = pl.BlockSpec(memory_space=pltpu.VMEM)
    hbm = pl.BlockSpec(memory_space=pl.ANY)
    return plan, pl.pallas_call(
        functools.partial(exchange_kernel, plan),
        out_shape=(
            jax.ShapeDtypeStruct((n, plan.padded, LANES), jnp.bfloat16),
            jax.ShapeDtypeStruct((share, LANES), jnp.float32),
            jax.ShapeDtypeStruct((share, LANES), jnp.float32),
            jax.ShapeDtypeStruct((16, LANES), jnp.float32),
        ),
        in_specs=[hbm, vmem, vmem, vmem],
        out_specs=(hbm, vmem, vmem, vmem),
        scratch_shapes=[
            pltpu.VMEM((plan.local, plan.window, LANES), jnp.float32),
            pltpu.VMEM((plan.local, plan.window, LANES), jnp.float32),
            pltpu.VMEM((2, hops, plan.part, LANES), jnp.int16),
            pltpu.VMEM((2, hops, plan.part, LANES), jnp.int16),
            pltpu.VMEM((2, hops, plan.scales, LANES), jnp.float32),
            pltpu.VMEM((2, hops, plan.scales, LANES), jnp.float32),
            pltpu.VMEM((2, far, plan.part, LANES), jnp.int16),
            pltpu.VMEM((2, far, plan.part, LANES), jnp.int16),
            pltpu.VMEM((2, far, plan.scales, LANES), jnp.float32),
            pltpu.VMEM((2, far, plan.scales, LANES), jnp.float32),
            pltpu.VMEM((len(SHIFTS), plan.window, LANES), jnp.float32),
            pltpu.VMEM((plan.padded, LANES), jnp.float32),
            pltpu.VMEM((plan.padded, LANES), jnp.bfloat16),
            pltpu.VMEM((n, 16, LANES), jnp.float32),
            dma((plan.local,)), dma((plan.local,)), dma((plan.local,)),
            dma((2, hops)), dma((2, hops)), dma((2, hops)), dma((2, hops)),
            dma((2, far)), dma((2, far)), dma((2, far)), dma((2, far)),
            dma((n,)), dma((n,)), dma,
            dma((2, nc, 2)), dma((2, nc, 2)),
            dma((2, hops)), dma((2, hops)),
            dma((2, plan.local)), dma((2, plan.local)),
        ],
        compiler_params=pltpu.CompilerParams(
            collective_id=0, has_side_effects=True, vmem_limit_bytes=56 << 20
        ),
    )(grad, m_first.reshape(share, LANES), m_second.reshape(share, LANES), extra)


WIDE = CH + LANES
KEPT = ((8, 1104), (6096, 6408), (51400, 51584))
PLACES = tuple(divmod(FLAT_AT[i], LANES) for i in (3, 4, 5, 1))

SLOTS = 6
HALF = WIDE // 2
PITCH = 33


def unpack_kernel(
    plan, gathered, old_up, old_down, narrow, wide, hidden_out, rows_out, up_out, down_out, small_a, small_b, small_c,
    held, flat, woven, hidden, by_row, rows_low, up, down, sems, sem_out,
):
    n, share = plan.count, plan.share
    step = CH // LANES

    def fetch(k, slot):
        return pltpu.make_async_copy(gathered.at[k], held.at[slot], sems.at[slot])

    for k in range(SLOTS - 1):
        fetch(k, k).start()

    def widen(k, carry):
        slot = lax.rem(k, SLOTS)

        @pl.when(k + SLOTS - 1 < n)
        def _():
            fetch(k + SLOTS - 1, lax.rem(k + SLOTS - 1, SLOTS)).start()

        fetch(k, slot).wait()

        def body(b, inner):
            at = pl.ds(pl.multiple_of(b * 16, 16), 16)
            flat[pl.ds(share * k + b * 16, 16), :] = held[slot, at, :].astype(jnp.float32)
            return inner

        lax.fori_loop(0, plan.padded // 16, body, 0, unroll=4)
        return carry

    lax.fori_loop(0, n, widen, 0)

    copies = [
        pltpu.make_async_copy(source, target, sem_out.at[i])
        for i, (source, target) in enumerate(
            (
                (hidden, hidden_out.at[:, pl.ds(0, HALF)]), (rows_low, rows_out), (up, up_out),
                (down, down_out), (hidden, hidden_out.at[:, pl.ds(HALF, HALF)]),
            )
        )
    ]
    row, lane = PLACES[0]

    def spread(a, carry):
        by_row[pl.ds(narrow[a] * PITCH, 32), :] = flat[pl.ds(row + a * step, 32), :]
        return carry

    lax.fori_loop(0, C1, spread, 0, unroll=4)

    def columns(half):
        def column(t, carry):
            for begin in range(0, C1, 160):
                at = begin * PITCH + half * (HALF // LANES) + t
                values = by_row[pl.ds(at, 160, stride=PITCH), :]
                at = pl.ds(pl.multiple_of(t * LANES, LANES), LANES)
                hidden[begin : begin + 160, at] = values.astype(jnp.bfloat16)
            return carry

        lax.fori_loop(0, HALF // LANES, column, 0)

    columns(0)
    copies[0].start()

    quarter = C1 // 4
    for number, (ref, old, (line, begin)) in enumerate(zip((up, down), (old_up, old_down), PLACES[2:])):
        for u in range(-(-C1 // LANES)):
            width = min(LANES, C1 - u * LANES)
            place = lax.broadcasted_iota(jnp.int32, (quarter, LANES), 1)
            for b in range(4):
                first, rest = divmod(C1 * b + begin, LANES)
                here = flat[pl.ds(line + first + u, quarter, stride=step), :]
                after = flat[pl.ds(line + first + u + 1, quarter, stride=step), :]
                value = pltpu.roll(jnp.where(place >= rest, here, after), LANES - rest, 1)
                woven[pl.ds(b, quarter, stride=4), :] = value
            at = slice(u * LANES, u * LANES + width)
            ref[:, at] = moved(old[:, at], woven[:, :width])
        copies[2 + number].start()

    for ref, (begin, end) in zip((small_a, small_b, small_c), KEPT):
        ref[...] = flat[begin:end, :]
    copies[0].wait()
    columns(1)
    copies[4].start()

    row, lane = PLACES[1]

    def align(part, carry):
        place = lax.broadcasted_iota(jnp.int32, (40, LANES), 1)
        for b in range(4):
            first, rest = divmod(C1 * b + lane, LANES)
            tiles = [
                flat[pl.ds(row + part * (40 * step) + first + u, 40, stride=step), :]
                for u in range(C1P // LANES + 1)
            ]
            values = [
                pltpu.roll(jnp.where(place >= rest, here, after), LANES - rest, 1)
                for here, after in zip(tiles, tiles[1:])
            ]
            for u, value in enumerate(values):
                flat[pl.ds(part * (40 * PITCH) + b * 8 + u, 40, stride=PITCH), :] = value
        return carry

    lax.fori_loop(0, C1 // 40, align, 0)

    def scatter(a, carry):
        for b in range(4):
            by_row[pl.ds(wide[a * 4 + b] * 9, 8), :] = flat[pl.ds(a * PITCH + b * 8, 8), :]
        return carry

    lax.fori_loop(0, CH // 4, scatter, 0, unroll=4)

    def by_lane(part, carry):
        for u in range(C1P // LANES):
            values = by_row[pl.ds(part * (160 * 9) + u, 160, stride=9), :]
            at = pl.ds(pl.multiple_of(part * 160, 160), 160)
            rows_low[at, u * LANES : (u + 1) * LANES] = values.astype(jnp.bfloat16)
        return carry

    lax.fori_loop(0, CH // 160, by_lane, 0)
    copies[1].start()
    for copy in copies[1:]:
        copy.wait()


def unpack(plan, gathered, old_up, old_down, narrow, wide):
    lines = PADDED // LANES
    vmem = pl.BlockSpec(memory_space=pltpu.VMEM)
    hbm = pl.BlockSpec(memory_space=pl.ANY)
    dma = pltpu.SemaphoreType.DMA
    f32, low = jnp.float32, jnp.bfloat16
    return pl.pallas_call(
        functools.partial(unpack_kernel, plan),
        out_shape=(
            jax.ShapeDtypeStruct((C1, WIDE), low),
            jax.ShapeDtypeStruct((CH, C1P), low),
            jax.ShapeDtypeStruct((C1, C1), f32),
            jax.ShapeDtypeStruct((C1, C1), f32),
        )
        + tuple(jax.ShapeDtypeStruct((end - begin, LANES), f32) for begin, end in KEPT),
        in_specs=[hbm, vmem, vmem] + [pl.BlockSpec(memory_space=pltpu.SMEM)] * 2,
        out_specs=(hbm, hbm, hbm, hbm, vmem, vmem, vmem),
        scratch_shapes=[
            pltpu.VMEM((SLOTS, plan.padded, LANES), low),
            pltpu.VMEM((-(-lines // 8) * 8 + 16, LANES), f32),
            pltpu.VMEM((C1, LANES), f32),
            pltpu.VMEM((C1, HALF), low),
            pltpu.VMEM((CH * 9, LANES), f32),
            pltpu.VMEM((CH, C1P), low),
            pltpu.VMEM((C1, C1), f32),
            pltpu.VMEM((C1, C1), f32),
            dma((SLOTS,)),
            dma((5,)),
        ],
        compiler_params=pltpu.CompilerParams(vmem_limit_bytes=63 << 20),
    )(gathered, old_up, old_down, narrow, wide)


def moved(old, direction):
    return old.astype(jnp.float32) * (1.0 - learn_rate * weight_decay) - learn_rate * direction


def one_hot(condition):
    return jnp.where(condition, 1.0, 0.0).astype(jnp.bfloat16)


def product(left, right):
    return jnp.dot(left, right, preferred_element_type=jnp.float32)


def product_t(left, right):
    return lax.dot_general(left, right, (((1,), (1,)), ((), ())), preferred_element_type=jnp.float32)


TILE = 512
STEPS = -(-CH // TILE)
LAST = CH - (STEPS - 1) * TILE


DEEP = 256


def by_width(body):
    final = pl.program_id(0) == STEPS - 1

    @pl.when(jnp.logical_not(final))
    def _():
        body(TILE)

    @pl.when(final)
    def _():
        body(LAST)


def hidden_kernel(lines, wide, old, new):
    depth = lines.shape[1]
    base = pl.program_id(0) * TILE

    def body(width):
        direction = None
        for begin in range(0, depth, DEEP):
            end = min(begin + DEEP, depth)
            place = wide[begin:end, :] - base
            lane = lax.broadcasted_iota(jnp.int32, (end - begin, LANES), 1)
            hot = jnp.concatenate([one_hot(lane + u == place) for u in range(0, width, LANES)], axis=1)
            term = product(lines[:, begin:end], hot)
            direction = term if direction is None else direction + term
        new[:, :width] = moved(old[:, :width], direction)

    by_width(body)


def rebuild_hidden(lines, wide, old):
    lane = PLACES[0][1]
    wide = jnp.full((WIDE,), -1, jnp.int32).at[lane : lane + CH].set(wide)
    return pl.pallas_call(
        hidden_kernel,
        out_shape=jax.ShapeDtypeStruct((C1, CH), jnp.float32),
        grid=(STEPS,),
        in_specs=[
            pl.BlockSpec((C1, WIDE), lambda i: (0, 0)),
            pl.BlockSpec((WIDE, LANES), lambda i: (0, 0)),
            pl.BlockSpec((C1, TILE), lambda i: (0, i)),
        ],
        out_specs=pl.BlockSpec((C1, TILE), lambda i: (0, i)),
        compiler_params=pltpu.CompilerParams(vmem_limit_bytes=48 << 20),
    )(lines, jnp.broadcast_to(wide[:, None], (WIDE, LANES)), old)


def out_kernel(rows, narrow, old, new, turn):
    @pl.when(pl.program_id(0) == 0)
    def _():
        turn[...] = one_hot(lax.broadcasted_iota(jnp.int32, (C1, C1), 0) == narrow[...])

    def body(width):
        new[:, :width] = moved(old[:, :width], product_t(turn[...], rows[:width, :C1]))

    by_width(body)


def rebuild_out(rows, narrow, old):
    return pl.pallas_call(
        out_kernel,
        out_shape=jax.ShapeDtypeStruct((C1, CH), jnp.float32),
        grid=(STEPS,),
        in_specs=[
            pl.BlockSpec((TILE, C1P), lambda i: (i, 0)),
            pl.BlockSpec((1, C1), lambda i: (0, 0)),
            pl.BlockSpec((C1, TILE), lambda i: (0, i)),
        ],
        out_specs=pl.BlockSpec((C1, TILE), lambda i: (0, i)),
        scratch_shapes=[pltpu.VMEM((C1, C1), jnp.bfloat16)],
        compiler_params=pltpu.CompilerParams(vmem_limit_bytes=48 << 20),
    )(rows, narrow[None, :], old.T).T


def weave(source, rows, put, width=C1):
    group = CH // width
    for t in range(CH // LANES):
        b, begin = divmod(t * LANES, width)
        u, rest = divmod(begin, LANES)
        place = lax.broadcasted_iota(jnp.int32, (rows, LANES), 1)
        value = source[u, pl.ds(b, rows, stride=group), :]
        if rest:
            if begin + LANES - rest < width:
                after = source[u + 1, pl.ds(b, rows, stride=group), :]
                value = jnp.where(place >= rest, value, after)
            value = pltpu.roll(value, LANES - rest, 1)
        left = width - begin
        if left < LANES:
            following = source[0, pl.ds(b + 1, rows, stride=group), :]
            value = jnp.where(place < left, value, pltpu.roll(following, left, 1))
        put(t, value)


def place_kernel(
    nr, nc, normed, branch, pre, act, narrow_row, narrow_col, wide, up, cells,
    grad, padded, hidden, out, loose, up_rows, norm_t, branch_r, halo_cells, held_pre, held_act,
    sem_out, sems, sem_halo_s, sem_halo_r, sem_in,
):
    step = pl.program_id(0)
    steps = STEPS
    ratio = CH // LANES

    def out_copy(n, width):
        begin = n * (TILE // 4 * ratio)
        rows = width // 4 * ratio
        return pltpu.make_async_copy(
            out.at[pl.ds(pl.multiple_of(begin, 8), rows)],
            grad.at[pl.ds(pl.multiple_of(ROW_AT[4] + begin, 8), rows)],
            sem_out.at[n],
        )

    copies = [
        pltpu.make_async_copy(ref, grad.at[pl.ds(row, ref.shape[0])], sems.at[i])
        for i, (ref, row) in enumerate(((up_rows, ROW_AT[5]), (hidden, ROW_AT[3])))
    ] + [pltpu.make_async_copy(halo_cells, padded, sems.at[2])]

    fetch_pre = pltpu.make_async_copy(pre, held_pre, sem_in.at[0])
    fetch_act = pltpu.make_async_copy(act, held_act, sem_in.at[1])

    @pl.when(step == 0)
    def _():
        fetch_pre.start()
        fetch_act.start()
        halo_start(nr, nc, 3, cells, halo_cells, sem_halo_s, sem_halo_r)
        line = lax.broadcasted_iota(jnp.int32, (C1, C1), 1)
        norm_t[...] = product_t(one_hot(line == narrow_col[:, 0:1]), normed[:, :C1]).astype(jnp.bfloat16)
        line = lax.broadcasted_iota(jnp.int32, (C1, C1P), 0)
        branch_r[...] = product(branch[:, :C1], one_hot(line == narrow_row[...])).astype(jnp.bfloat16)
        for u in range(-(-C1 // LANES)):
            width = min(LANES, C1 - u * LANES)
            loose[u, :, 0:width] = up[0:C1, u * LANES : u * LANES + width]

        def put(t, value):
            up_rows[pl.ds(t, C1 // 4, stride=ratio), :] = value

        weave(loose, C1 // 4, put)
        copies[0].start()
        fetch_pre.wait()
        fetch_act.wait()

    def body(width):
        turned_pre = turned_act = None
        for begin in range(0, CH, DEEP):
            end = min(begin + DEEP, CH)
            line = lax.broadcasted_iota(jnp.int32, (end - begin, width), 0) + begin
            hot = one_hot(line == wide[:, :width])
            one = product(held_pre[:, begin:end], hot)
            two = product(held_act[:, begin:end], hot)
            turned_pre = one if turned_pre is None else turned_pre + one
            turned_act = two if turned_act is None else turned_act + two
        part = product(norm_t[...], turned_pre.astype(jnp.bfloat16))
        for t in range(width // LANES):
            at = pl.ds(step * (TILE // LANES) + t, C1, stride=ratio)
            hidden[at, :] = part[:, t * LANES : (t + 1) * LANES]
        part = inner_rows(turned_act.astype(jnp.bfloat16), branch_r[...])
        for u in range(-(-C1 // LANES)):
            loose[u, 0:width, :] = part[:, u * LANES : (u + 1) * LANES]

        def put_out(t, value):
            out[pl.ds(step * (TILE // 4 * ratio) + t, width // 4, stride=ratio), :] = value

        weave(loose, width // 4, put_out)
        out_copy(step, width).start()

    by_width(body)

    @pl.when(step == steps - 1)
    def _():
        copies[1].start()
        halo_finish(nr, nc, 3, cells, halo_cells, sem_halo_s, sem_halo_r)
        copies[2].start()

        def finish(n, carry):
            out_copy(n, TILE).wait()
            return carry

        lax.fori_loop(0, steps - 1, finish, 0)
        out_copy(steps - 1, LAST).wait()
        for copy in copies:
            copy.wait()


def place_gradients(nr, nc, space, normed, branch, pre, act, narrow, wide, up, cells):
    def whole(array):
        return pl.BlockSpec(
            array.shape, lambda i: (0,) * len(array.shape), pipeline_mode=pl.Buffered(1)
        )

    hbm = pl.BlockSpec(memory_space=pl.ANY)
    rows = pre.shape[0]
    batch, height, breadth, chans = cells.shape
    narrow_row = jnp.pad(narrow, (0, C1P - C1), constant_values=-1)[None, :]
    narrow_col = jnp.broadcast_to(narrow[:, None], (C1, LANES))
    framed = jax.ShapeDtypeStruct((batch, height + 6, breadth + 2 * EDGE, chans), cells.dtype)
    dma = pltpu.SemaphoreType.DMA
    return pl.pallas_call(
        functools.partial(place_kernel, nr, nc),
        out_shape=(jax.ShapeDtypeStruct((space, LANES), jnp.float32), framed),
        grid=(STEPS,),
        in_specs=[
            whole(normed), whole(branch), hbm, hbm, whole(narrow_row), whole(narrow_col),
            pl.BlockSpec((1, TILE), lambda i: (0, i)),
            whole(up), whole(cells),
        ],
        out_specs=(hbm, hbm),
        scratch_shapes=[
            pltpu.VMEM((C1 * CH // LANES, LANES), jnp.float32),
            pltpu.VMEM((C1 * CH // LANES, LANES), jnp.float32),
            pltpu.VMEM((C1P // LANES, C1, LANES), jnp.float32),
            pltpu.VMEM((C1 * C1 // LANES, LANES), jnp.float32),
            pltpu.VMEM((C1, rows), jnp.bfloat16),
            pltpu.VMEM((rows, C1P), jnp.bfloat16),
            pltpu.VMEM(framed.shape, framed.dtype),
            pltpu.VMEM(pre.shape, pre.dtype),
            pltpu.VMEM(act.shape, act.dtype),
            dma((STEPS,)), dma((3,)), dma((8,)), dma((8,)), dma((2,)),
        ],
        compiler_params=pltpu.CompilerParams(
            collective_id=3, has_side_effects=True, vmem_limit_bytes=60 << 20
        ),
    )(normed, branch, pre, act, narrow_row, narrow_col, wide[None, :], up, cells)


C0P = 256
C1P = 896
CIP = 128
EDGE = 16
CURVE = 0.7978845608028654
CUBE = 0.044715


def inner_rows(left, right):
    return lax.dot_general(left, right, (((0,), (0,)), ((), ())), preferred_element_type=jnp.float32)


def column_sum(values):
    return jnp.sum(values.astype(jnp.float32), axis=0, keepdims=True)


def gelu_and_slope(t):
    square = t * t
    bend = jnp.tanh(CURVE * (t + CUBE * (square * t)))
    half = 0.5 * (1.0 + bend)
    return t * half, half + 0.5 * t * (1.0 - bend * bend) * (CURVE * (1.0 + 3.0 * CUBE * square))


WAYS = [(dr, dc) for dr in (-1, 0, 1) for dc in (-1, 0, 1) if (dr, dc) != (0, 0)]
ORDER = sorted(range(8), key=lambda i: (WAYS[i][1] != 0, WAYS[i][0] == 0))


def halo_place(nr, nc):
    r = lax.axis_index("rows")
    return r, lax.axis_index("cols"), lambda dr: (r + dr >= 0) & (r + dr < nr)


def halo_copy(nr, nc, width, cells, out, sem_s, sem_r, i, receive):
    r, c, there = halo_place(nr, nc)
    height, breadth = cells.shape[1], cells.shape[2]
    dr, dc = WAYS[i]
    rows_from = {-1: (0, width), 0: (0, height), 1: (height - width, width)}[dr]
    rows_to = {-1: height + width, 0: width, 1: 0}[dr]
    cols_from = {-1: (0, EDGE), 0: (0, breadth), 1: (breadth - EDGE, EDGE)}[dc]
    cols_to = {-1: EDGE + breadth, 0: EDGE, 1: 0}[dc]
    sign = -1 if receive else 1
    return pltpu.make_async_remote_copy(
        src_ref=cells.at[:, pl.ds(*rows_from), pl.ds(*cols_from)],
        dst_ref=out.at[:, pl.ds(rows_to, rows_from[1]), pl.ds(cols_to, cols_from[1])],
        send_sem=sem_s.at[i],
        recv_sem=sem_r.at[i],
        device_id=(r + sign * dr, lax.rem(c + sign * dc + nc, nc)),
        device_id_type=MESH,
    )


def halo_start(nr, nc, width, cells, out, sem_s, sem_r):
    r, c, there = halo_place(nr, nc)
    height, breadth = cells.shape[1], cells.shape[2]
    barrier = pltpu.get_barrier_semaphore()
    for dr, dc in WAYS:
        @pl.when(there(dr))
        def _(dr=dr, dc=dc):
            pl.semaphore_signal(
                barrier, inc=1, device_id=(r + dr, lax.rem(c + dc + nc, nc)), device_id_type=MESH
            )

    edge = (r == 0) | (r == nr - 1)

    @pl.when(edge)
    def _():
        pl.semaphore_wait(barrier, 5)

    @pl.when(jnp.logical_not(edge))
    def _():
        pl.semaphore_wait(barrier, 8)

    for i in ORDER:
        @pl.when(there(WAYS[i][0]))
        def _(i=i):
            halo_copy(nr, nc, width, cells, out, sem_s, sem_r, i, False).start()

    for m in range(cells.shape[0]):
        for row in range(height):
            out[m, width + row, EDGE : EDGE + breadth, :] = cells[m, row]

    @pl.when(r == 0)
    def _():
        out[:, 0:width] = jnp.zeros((out.shape[0], width) + out.shape[2:], out.dtype)

    @pl.when(r == nr - 1)
    def _():
        out[:, height + width :] = jnp.zeros((out.shape[0], width) + out.shape[2:], out.dtype)


def halo_finish(nr, nc, width, cells, out, sem_s, sem_r):
    r, c, there = halo_place(nr, nc)
    for i in ORDER:
        @pl.when(there(-WAYS[i][0]))
        def _(i=i):
            halo_copy(nr, nc, width, cells, out, sem_s, sem_r, i, True).wait_recv()

        @pl.when(there(WAYS[i][0]))
        def _(i=i):
            halo_copy(nr, nc, width, cells, out, sem_s, sem_r, i, False).wait_send()


def halo_kernel(nr, nc, width, cells, out, sem_s, sem_r):
    halo_start(nr, nc, width, cells, out, sem_s, sem_r)
    halo_finish(nr, nc, width, cells, out, sem_s, sem_r)


def halo(nr, nc, width, cells, identity):
    batch, height, breadth, chans = cells.shape
    vmem = pl.BlockSpec(memory_space=pltpu.VMEM)
    return pl.pallas_call(
        functools.partial(halo_kernel, nr, nc, width),
        out_shape=jax.ShapeDtypeStruct(
            (batch, height + 2 * width, breadth + 2 * EDGE, chans), cells.dtype
        ),
        in_specs=[vmem],
        out_specs=vmem,
        scratch_shapes=[pltpu.SemaphoreType.DMA((8,)), pltpu.SemaphoreType.DMA((8,))],
        compiler_params=pltpu.CompilerParams(
            collective_id=identity, has_side_effects=True, vmem_limit_bytes=24 << 20
        ),
    )(cells)


SIDE = 8
REACH = 3
FINE_REACH = 2 * REACH + 1


def input_kernel(
    nr, state, w_in, w_down, vector, taps_out, slope_zero_out, h_zero_out, coarse, padded, lines,
    wide, taps_all, coarse_all, taps, slope_zero, h_zero, sems,
):
    r = lax.axis_index("rows")
    copies = [
        pltpu.make_async_copy(source, target, sems.at[i])
        for i, (source, target) in enumerate(((taps, taps_out), (slope_zero, slope_zero_out), (h_zero, h_zero_out)))
    ]
    lines[...] = jnp.zeros_like(lines)
    start = 0
    for number, size in enumerate((C0, C1, C1, C1, C1, CH, C1, C0, CI)):
        lines[number : number + 1, 0:size] = vector[:, start : start + size]
        start = start + size
    batch, rows, breadth, _ = state.shape
    half_h, half_w = rows // 2 - FINE_REACH, breadth // 2 - EDGE
    all_h, all_w = half_h + 2 * REACH, half_w + 2 * SIDE
    for m in range(batch):
        for y in range(rows):
            wide[m, y, SIDE : SIDE + breadth, :] = state[m, y].astype(jnp.float32)
    for m in range(batch):
        for y in range(rows):
            for f in range(4):
                start = SIDE + EDGE - 2 * SIDE - 1 + f
                line = wide[m, y, pl.ds(start, all_w, stride=2), :]
                low = line.astype(jnp.bfloat16)
                inner = line[SIDE : SIDE + half_w].astype(jnp.bfloat16)
                for dy in range(3):
                    i, sy = divmod(y - dy, 2)
                    if not 0 <= i < all_h:
                        continue
                    for dx in range(3):
                        if not 0 <= f - dx < 2:
                            continue
                        s, tap = sy * 2 + f - dx, slice((dy * 3 + dx) * CIP, (dy * 3 + dx + 1) * CIP)
                        begin = (m * all_h + i) * all_w
                        taps_all[s, begin : begin + all_w, tap] = low
                        if REACH <= i < REACH + half_h:
                            begin = (m * half_h + i - REACH) * half_w
                            taps[s, begin : begin + half_w, tap] = inner
    copies[0].start()
    size = all_h * all_w
    for m in range(batch):
        block = slice(m * size, (m + 1) * size)
        total = jnp.broadcast_to(lines[1:2, :C1P], (size, C1P))
        for s in range(4):
            value = product(taps_all[s, block, :], w_in[...]) + lines[0:1, :C0P]
            curved, slope = gelu_and_slope(value)
            for i in range(half_h):
                begin = (i + REACH) * all_w + SIDE
                at = slice((m * half_h + i) * half_w, (m * half_h + i + 1) * half_w)
                slope_zero[s, at, :] = slope[begin : begin + half_w]
                h_zero[s, at, :] = curved[begin : begin + half_w]
            total = total + product(curved.astype(jnp.bfloat16), w_down[s])
        coarse_all[...] = total
        for i in range(half_h):
            begin = (i + REACH) * all_w + SIDE
            at = slice((m * half_h + i) * half_w, (m * half_h + i + 1) * half_w)
            coarse[at, :] = coarse_all[begin : begin + half_w, :]
        if m == batch - 1:
            copies[1].start()
            copies[2].start()
        padded[m] = coarse_all[...].astype(jnp.bfloat16).reshape(padded.shape[1:])

    @pl.when(r == 0)
    def _():
        padded[:, 0:REACH] = jnp.zeros((batch, REACH) + padded.shape[2:], padded.dtype)

    @pl.when(r == nr - 1)
    def _():
        padded[:, all_h - REACH :] = jnp.zeros((batch, REACH) + padded.shape[2:], padded.dtype)

    for copy in copies:
        copy.wait()


def input_part(nr, state, w_in, w_down, vector):
    batch, rows, breadth, _ = state.shape
    half_h, half_w = rows // 2 - FINE_REACH, breadth // 2 - EDGE
    all_h, all_w = half_h + 2 * REACH, half_w + 2 * SIDE
    cells = batch * half_h * half_w
    vmem = pl.BlockSpec(memory_space=pltpu.VMEM)
    hbm = pl.BlockSpec(memory_space=pl.ANY)
    large = (
        jax.ShapeDtypeStruct((4, cells, 9 * CIP), jnp.bfloat16),
        jax.ShapeDtypeStruct((4, cells, C0P), jnp.float32),
        jax.ShapeDtypeStruct((4, cells, C0P), jnp.float32),
    )
    return pl.pallas_call(
        functools.partial(input_kernel, nr),
        out_shape=large
        + (
            jax.ShapeDtypeStruct((cells, C1P), jnp.float32),
            jax.ShapeDtypeStruct((batch, all_h, all_w, C1P), jnp.bfloat16),
            jax.ShapeDtypeStruct((16, CH), jnp.float32),
        ),
        in_specs=[vmem] * 4,
        out_specs=(hbm, hbm, hbm, vmem, vmem, vmem),
        scratch_shapes=[
            pltpu.VMEM((batch, rows, breadth + 2 * SIDE, CIP), jnp.float32),
            pltpu.VMEM((4, batch * all_h * all_w, 9 * CIP), jnp.bfloat16),
            pltpu.VMEM((all_h * all_w, C1P), jnp.float32),
        ]
        + [pltpu.VMEM(shape.shape, shape.dtype) for shape in large]
        + [pltpu.SemaphoreType.DMA((3,))],
        compiler_params=pltpu.CompilerParams(vmem_limit_bytes=60 << 20),
    )(state, w_in, w_down, vector)


def spread_lanes(padded, held):
    for m in range(padded.shape[0]):
        def body(y, carry, m=m):
            for u in range(C1P // LANES):
                held[u, m, y, 0 : padded.shape[2], :] = padded[m, y, :, u * LANES : (u + 1) * LANES].astype(jnp.float32)
            return carry

        lax.fori_loop(0, padded.shape[1], body, 0)


def convolve(held, w_dw, half_w, edge, put, back):
    tiles, batch, rows = held.shape[:3]
    height = rows - 2 * REACH

    def body(number, carry):
        u, m = number // batch, number % batch
        sums = [jnp.zeros((half_w, LANES), jnp.float32) for _ in range(height)]
        for x in range(7):
            for y in range(rows):
                window = held[u, m, y, pl.ds(edge - REACH + x, half_w), :]
                for i in range(height):
                    if 0 <= y - i < 7:
                        tap = (6 - (y - i)) * 7 + 6 - x if back else (y - i) * 7 + x
                        sums[i] = sums[i] + window * w_dw[pl.ds(tap, 1), lanes_at(u)]
        for i in range(height):
            put(u, m, i, sums[i])
        return carry

    lax.fori_loop(0, tiles * batch, body, 0)


def rows_at(m, i, height, half_w):
    return pl.ds(pl.multiple_of((m * height + i) * half_w, half_w), half_w)


def lanes_at(u):
    return pl.ds(pl.multiple_of(u * LANES, LANES), LANES)


PART = 640


def middle_kernel(names, late, early, *refs):
    table = dict(zip(names, refs))
    ref = types.SimpleNamespace(**table)
    batch, rows, breadth, _ = ref.padded.shape
    cells = ref.coarse.shape[0]
    height, half_w = rows - 2 * REACH, breadth - 2 * SIDE
    held_in = {name: table["held_" + name] for name in late}
    held_out = {name: table["held_" + name] for name in early}
    fetch = {
        name: pltpu.make_async_copy(table[name], held_in[name], ref.sem_in.at[i])
        for i, name in enumerate(late)
    }
    stores = {
        name: pltpu.make_async_copy(held_out[name], table[name], ref.sem_out.at[i])
        for i, name in enumerate(early)
    }
    for copy in fetch.values():
        copy.start()
    conv = ref.conv

    def depthwise(held):
        spread_lanes(ref.padded, held)

        def put(u, m, i, value):
            conv[rows_at(m, i, height, half_w), lanes_at(u)] = value

        convolve(held, ref.w_dw, half_w, SIDE, put, False)

    pl.run_scoped(depthwise, pltpu.VMEM((C1P // LANES, batch, rows, breadth, LANES), jnp.float32))
    pl.run_scoped(
        functools.partial(
            pointwise_part, ref, *(types.SimpleNamespace(**t) for t in (fetch, stores, held_in, held_out))
        ),
        pltpu.VMEM((cells, CH), jnp.float32),
        pltpu.VMEM((cells, C1), jnp.bfloat16),
    )
    for copy in stores.values():
        copy.wait()


def pointwise_part(ref, fetch, store, held_in, held_out, slopes, spread_all):
    conv, total, sums, extra = ref.conv, ref.total, ref.sums, ref.extra
    gain, w_head = ref.lines.at[3:4, 0:C1P], ref.w_head
    normed, act = held_out.normed, held_out.act
    grad_mixed, grad_branch, grad_summed = (
        held_out.grad_mixed, held_out.grad_branch, held_out.grad_summed
    )
    w_hidden, w_out_t, w_up = held_in.w_hidden, held_in.w_out_t, held_in.w_up
    target, weight, h_zero = held_in.target, held_in.weight, held_in.h_zero
    batch, rows, breadth, _ = ref.padded.shape
    height, half_w = rows - 2 * REACH, breadth - 2 * SIDE

    inside = lax.broadcasted_iota(jnp.int32, (1, C1P), 1) < C1
    values = conv[...] + ref.lines[2:3, :C1P]
    mean = jnp.sum(values, axis=1, keepdims=True) * (1.0 / C1)
    centered = jnp.where(inside, values - mean, 0.0)
    scale = lax.rsqrt(jnp.sum(centered * centered, axis=1, keepdims=True) * (1.0 / C1) + 1e-06)
    conv[...] = centered * scale
    normed[...] = (conv[...] * gain[...] + ref.lines[4:5, :C1P]).astype(jnp.bfloat16)
    store.normed.start()

    fetch.coarse.wait()
    fetch.w_hidden.wait()
    fetch.w_out_t.wait()
    total[...] = held_in.coarse[...]
    for begin in range(0, CH, PART):
        span = slice(begin, min(begin + PART, CH))
        value = product(normed[:, :C1], w_hidden[:, span]) + ref.lines[5:6, span]
        curved, slope = gelu_and_slope(value)
        slopes[:, span] = slope
        act[:, span] = curved.astype(jnp.bfloat16)
        total[:, :C1] += product_t(act[:, span], w_out_t[:, span])
    store.act.start()
    mixed = (total[...] + ref.lines[6:7, :C1P]).astype(jnp.bfloat16)

    for copy in (fetch.h_zero, fetch.target, fetch.weight, fetch.w_up):
        copy.wait()
    grad_mixed[...] = jnp.zeros_like(grad_mixed)
    loss = jnp.zeros((1, CI), jnp.float32)
    head_sum = jnp.zeros((1, CI), jnp.float32)
    up_sum = jnp.zeros((1, C0), jnp.float32)
    for s in range(4):
        sub_y, sub_x = divmod(s, 2)
        for m in range(batch):
            for i in range(height):
                at = rows_at(m, i, height, half_w)
                line = pl.ds(sub_x, half_w, stride=2)
                ref.goal[at, :] = target[m, 2 * i + sub_y, line, :]
                ref.load[at, :] = weight[2 * i + sub_y, line, :]
        w_up_s = w_up[:, s * C0 : (s + 1) * C0]
        upper = product(mixed[:, :C1], w_up_s) + ref.lines[7:8, :C0]
        summed = (upper + h_zero[s, :, :C0]).astype(jnp.bfloat16)
        error = product(summed, w_head[...]) + ref.lines[8:9, :CI] - ref.goal[:, :CI]
        weighted = ref.load[:, :CI] * error
        loss = loss + column_sum(weighted * error)
        grad_out = (2.0 * weighted).astype(jnp.bfloat16)
        head_sum = head_sum + column_sum(grad_out)
        if s == 0:
            ref.d_head[...] = inner_rows(summed, grad_out)
        else:
            ref.d_head[...] += inner_rows(summed, grad_out)
        spread = product_t(grad_out, w_head[...])
        grad_summed[s] = spread
        grad_upper = spread.astype(jnp.bfloat16)
        up_sum = up_sum + column_sum(grad_upper)
        spread_all[:, s * C0 : (s + 1) * C0] = grad_upper
        grad_mixed[:, :C1] += product_t(grad_upper, w_up_s)
    store.grad_summed.start()
    store.grad_mixed.start()
    held_out.d_up[...] = inner_rows(mixed[:, :C1], spread_all[...])
    store.d_up.start()
    grad_branch[...] = grad_mixed[...].astype(jnp.bfloat16)
    store.grad_branch.start()
    sums[...] = jnp.zeros_like(sums)
    extra[...] = jnp.zeros_like(extra)
    extra[0:1, 0:CI] = loss
    extra[1:2, :] = column_sum(ref.weight_map[...])
    sums[1:2, 0:CI] = head_sum
    sums[2:3, 0:C0] = up_sum
    sums[3:4, 0:C1P] = column_sum(grad_branch[...])

    total[...] = jnp.zeros_like(total)
    for begin in range(0, CH, PART):
        span = slice(begin, min(begin + PART, CH))
        value = product(grad_branch[:, :C1], w_out_t[:, span]) * slopes[:, span]
        low = value.astype(jnp.bfloat16)
        ref.grad_pre[:, span] = low
        sums[4:5, span] = column_sum(low)
        total[:, :C1] += product_t(low, w_hidden[:, span])

    grad_normed = total[...]
    sums[5:6, 0:C1P] = column_sum(grad_normed * conv[...])
    sums[6:7, 0:C1P] = column_sum(grad_normed)
    inward = grad_normed * gain[...]
    first = jnp.sum(inward, axis=1, keepdims=True) * (1.0 / C1)
    second = jnp.sum(inward * conv[...], axis=1, keepdims=True) * (1.0 / C1)
    value = scale * jnp.where(inside, inward - first - conv[...] * second, 0.0)
    low = value.astype(jnp.bfloat16)
    sums[7:8, 0:C1P] = column_sum(low)
    ref.grad_conv[...] = low.reshape(ref.grad_conv.shape)


def middle_part(late, **given):
    cells = late["coarse"].shape[0]
    batch, rows, breadth, _ = given["padded"].shape
    half_h, half_w = rows - 2 * REACH, breadth - 2 * SIDE
    vmem = pl.BlockSpec(memory_space=pltpu.VMEM)
    hbm = pl.BlockSpec(memory_space=pl.ANY)
    f32, low = jnp.float32, jnp.bfloat16
    early = dict(
        normed=((cells, C1P), low),
        act=((cells, CH), low),
        grad_mixed=((cells, C1P), f32),
        grad_branch=((cells, C1P), low),
        grad_summed=((4, cells, C0), f32),
        d_up=((C1, C1), f32),
    )
    outs = dict(
        grad_pre=((cells, CH), low),
        grad_conv=((batch, half_h, half_w, C1P), low),
        d_head=((C0, CI), f32),
        sums=((8, CH), f32),
        extra=((8, LANES), f32),
    )
    scratch = dict(
        conv=pltpu.VMEM((cells, C1P), f32),
        total=pltpu.VMEM((cells, C1P), f32),
        goal=pltpu.VMEM((cells, LANES), f32),
        load=pltpu.VMEM((cells, LANES), f32),
        sem_in=pltpu.SemaphoreType.DMA((len(late),)),
        sem_out=pltpu.SemaphoreType.DMA((len(early),)),
    )
    for name, array in late.items():
        scratch["held_" + name] = pltpu.VMEM(array.shape, array.dtype)
    for name, out in early.items():
        scratch["held_" + name] = pltpu.VMEM(*out)
    names = tuple(late) + tuple(given) + tuple(early) + tuple(outs) + tuple(scratch)
    found = pl.pallas_call(
        functools.partial(middle_kernel, names, tuple(late), tuple(early)),
        out_shape=tuple(jax.ShapeDtypeStruct(*out) for out in (early | outs).values()),
        in_specs=[hbm] * len(late) + [vmem] * len(given),
        out_specs=(hbm,) * len(early) + (vmem,) * len(outs),
        scratch_shapes=list(scratch.values()),
        compiler_params=pltpu.CompilerParams(vmem_limit_bytes=62 << 20),
    )(*late.values(), *given.values())
    return types.SimpleNamespace(**dict(zip(early | outs, found)))


def place_rows(source, rows, start, target, width=C1):
    def put(t, value):
        target[pl.ds(start + t, rows, stride=CH // LANES), :] = value

    weave(source, rows, put, width)


def outer_kernel(names, late, *refs):
    table = dict(zip(names, refs))
    ref = types.SimpleNamespace(**table)
    fetch = [
        pltpu.make_async_copy(table[name], table["held_" + name], ref.sem_in.at[i])
        for i, name in enumerate(late)
    ]
    for copy in fetch:
        copy.start()
    stores = [
        pltpu.make_async_copy(
            source.at[pl.ds(0, count)], ref.grad.at[pl.ds(row, count)], ref.sem_out.at[i]
        )
        for i, (source, row, count) in enumerate(
            (
                (ref.piece_head, ROW_AT[6], ROW_AT[7] - ROW_AT[6]),
                (ref.dw_rows, ROW_AT[2], ROW_AT[3] - ROW_AT[2]),
                (ref.down_rows, ROW_AT[1], ROW_AT[2] - ROW_AT[1]),
                (ref.in_rows, 0, ROW_AT[1]),
                (ref.vector_rows, ROW_AT[7], ref.vector_rows.shape[0]),
            )
        )
    ]
    stores[0].start()
    grad_mixed, grad_summed, slope_zero, h_zero, taps, w_down = (table["held_" + name] for name in late)
    held, conv, sums, d_dw, d_in = ref.held, ref.conv, ref.sums, ref.d_dw, ref.d_in
    vector, loose = ref.vector, ref.loose
    grad_conv = ref.grad_conv
    batch, height, half_w, _ = grad_conv.shape
    spread_lanes(ref.padded, held)
    tiles = C1P // LANES
    d_dw[...] = jnp.zeros_like(d_dw)

    def taps_of(number, carry):
        u, m = number // batch, number % batch
        grads = [grad_conv[m, i, :, lanes_at(u)].astype(jnp.float32) for i in range(height)]
        for x in range(7):
            found = [jnp.zeros((8, LANES), jnp.float32) for _ in range(7)]
            for y in range(height + 6):
                window = held[u, m, y, pl.ds(SIDE - REACH + x, half_w), :]
                for i in range(height):
                    if 0 <= y - i < 7:
                        term = (window * grads[i]).reshape(half_w // 8, 8, LANES)
                        found[y - i] = found[y - i] + jnp.sum(term, axis=0)
            for dy in range(7):
                d_dw[u, pl.ds(dy * 7 + x, 1), :] += jnp.sum(found[dy], axis=0, keepdims=True)
        return carry

    lax.fori_loop(0, tiles * batch, taps_of, 0)
    place_rows(d_dw, 13, 0, ref.dw_rows)
    stores[1].start()
    spread_lanes(ref.grad_padded, held)

    def put(u, m, i, value):
        conv[rows_at(m, i, height, half_w), lanes_at(u)] = value

    convolve(held, ref.w_dw, half_w, EDGE, put, True)
    for copy in fetch:
        copy.wait()
    grad_coarse = (conv[...] + grad_mixed[...]).astype(jnp.bfloat16)
    vector[...] = jnp.zeros_like(vector)
    pieces = [(column_sum(grad_coarse), C1)] + [(sums[i : i + 1, :], C1) for i in (7, 5, 6)]
    pieces += [(sums[4:5, :], CH), (sums[3:4, :], C1), (sums[2:3, :], C0), (sums[1:2, :], CI)]
    start = C0
    for piece, size in pieces:
        vector[:, start : start + size] = piece[:, :size]
        start = start + size
    for s in range(4):
        part = inner_rows(h_zero[s].astype(jnp.bfloat16), grad_coarse)
        for u in range(tiles):
            loose[u, s * C0 : (s + 1) * C0, :] = part[:C0, u * LANES : (u + 1) * LANES]
    place_rows(loose, C1 // 4, 0, ref.down_rows)
    stores[2].start()
    in_sum = jnp.zeros((1, C0), jnp.float32)
    for s in range(4):
        grad_h = product_t(grad_coarse, w_down[s])[:, :C0] + grad_summed[s]
        grad_a = (slope_zero[s, :, :C0] * grad_h).astype(jnp.bfloat16)
        in_sum = in_sum + column_sum(grad_a)
        if s == 0:
            d_in[...] = inner_rows(taps[s], grad_a)
        else:
            d_in[...] += inner_rows(taps[s], grad_a)
    vector[:, 0:C0] = in_sum
    for row in range(ref.vector_rows.shape[0]):
        ref.vector_rows[row : row + 1, :] = vector[:, row * LANES : (row + 1) * LANES]
    stores[4].start()

    close = ref.close
    used = 9 * CI
    close[:, used:, :] = jnp.zeros((2, close.shape[1] - used, LANES), jnp.float32)
    for tap in range(9):
        at = slice(tap * CI, (tap + 1) * CI)
        close[0, at, :] = d_in[tap * CIP : tap * CIP + CI, 0:LANES]
        close[1, at, 0 : C0 - LANES] = d_in[tap * CIP : tap * CIP + CI, LANES:C0]
    ref.in_rows[0 : ROW_AT[0], :] = jnp.zeros((ROW_AT[0], LANES), jnp.float32)
    place_rows(close, close.shape[1] * C0 // CH, ROW_AT[0], ref.in_rows, C0)
    stores[3].start()
    for store in stores:
        store.wait()


def outer_part(grad, piece_head, late, **given):
    cells = late["grad_mixed"].shape[0]
    batch, rows, breadth, _ = given["grad_padded"].shape
    vmem = pl.BlockSpec(memory_space=pltpu.VMEM)
    hbm = pl.BlockSpec(memory_space=pl.ANY)
    f32 = jnp.float32
    groups = -(-9 * CI * C0 // CH)
    rest = grad.shape[0] - ROW_AT[7]
    scratch = dict(
        held=pltpu.VMEM((C1P // LANES, batch, rows, breadth, LANES), f32),
        conv=pltpu.VMEM((cells, C1P), f32),
        d_dw=pltpu.VMEM((C1P // LANES, 56, LANES), f32),
        d_in=pltpu.VMEM((9 * CIP, C0), f32),
        vector=pltpu.VMEM((1, rest * LANES), f32),
        vector_rows=pltpu.VMEM((rest, LANES), f32),
        loose=pltpu.VMEM((C1P // LANES, C1, LANES), f32),
        close=pltpu.VMEM((2, groups * CH // C0, LANES), f32),
        dw_rows=pltpu.VMEM((13 * CH // LANES + 3, LANES), f32),
        down_rows=pltpu.VMEM((ROW_AT[2] - ROW_AT[1], LANES), f32),
        in_rows=pltpu.VMEM((ROW_AT[0] + groups * CH // LANES + 4, LANES), f32),
        sem_in=pltpu.SemaphoreType.DMA((len(late),)),
        sem_out=pltpu.SemaphoreType.DMA((5,)),
    )
    for name, array in late.items():
        scratch["held_" + name] = pltpu.VMEM(array.shape, array.dtype)
    names = ("before", "piece_head") + tuple(late) + tuple(given) + ("grad",) + tuple(scratch)
    return pl.pallas_call(
        functools.partial(outer_kernel, names, tuple(late)),
        out_shape=jax.ShapeDtypeStruct(grad.shape, grad.dtype),
        in_specs=[hbm] * (2 + len(late)) + [vmem] * len(given),
        out_specs=hbm,
        input_output_aliases={0: 0},
        scratch_shapes=list(scratch.values()),
        compiler_params=pltpu.CompilerParams(vmem_limit_bytes=62 << 20),
    )(grad, piece_head, *late.values(), *given.values())


def as_rows(piece, rows):
    flat = piece.reshape(-1)
    return jnp.pad(flat, (0, rows * LANES - flat.shape[0])).reshape(rows, LANES)


def widened(array, *shape):
    return jnp.pad(array, [(0, full - now) for full, now in zip(shape, array.shape)])


def on_device(
    inputs,
    targets,
    land_mask,
    volume,
    date_index,
    perm_narrow,
    perm_wide,
    w_in,
    w_down,
    w_dw,
    w_hidden,
    w_out,
    w_up,
    w_head,
    biases_gains,
    moment_first,
    moment_second,
):
    rows, cols = lax.axis_size("rows"), lax.axis_size("cols")
    weight = land_mask.astype(jnp.float32) * volume
    height, breadth = weight.shape
    half_h, half_w = (height // 2, breadth // 2)
    cells = MB * half_h * half_w
    matrices = (w_in, w_down, w_dw, w_hidden, w_out, w_up, w_head)

    def dates(field):
        picked = jnp.concatenate(
            [lax.dynamic_slice_in_dim(field, date_index[m], 1, 0, allow_negative_indices=False) for m in range(MB)]
        )
        return widened(picked, MB, height, breadth, CIP)

    w_in_p = widened(w_in.reshape(9, CI, C0), 9, CIP, C0P).reshape(9 * CIP, C0P)
    w_down_p = widened(w_down.reshape(4, C0, C1), 4, C0P, C1P)
    w_dw_p = widened(w_dw.astype(jnp.float32), 56, C1P)
    weight_map = jnp.broadcast_to(weight[:, :, None], (height, breadth, LANES))

    state = halo(rows, cols, FINE_REACH, dates(inputs), 1)
    taps, slope_zero, h_zero, coarse, padded, lines = input_part(
        rows, state, w_in_p, w_down_p, biases_gains[None, :]
    )
    mid = middle_part(
        dict(
            coarse=coarse, h_zero=h_zero, target=dates(targets).astype(jnp.float32), weight=weight_map,
            w_hidden=w_hidden, w_out_t=w_out.T, w_up=w_up,
        ),
        padded=padded, weight_map=weight, w_dw=w_dw_p, w_head=w_head, lines=lines,
    )
    space = Plan(rows, cols, PADDED).space
    grad, grad_padded = place_gradients(
        rows, cols, space, mid.normed, mid.grad_branch, mid.grad_pre, mid.act,
        perm_narrow, perm_wide, mid.d_up, mid.grad_conv,
    )
    grad = outer_part(
        grad,
        as_rows(mid.d_head, ROW_AT[7] - ROW_AT[6]),
        dict(
            grad_mixed=mid.grad_mixed, grad_summed=mid.grad_summed, slope_zero=slope_zero,
            h_zero=h_zero, taps=taps, w_down=w_down_p,
        ),
        padded=padded, grad_padded=grad_padded, grad_conv=mid.grad_conv, w_dw=w_dw_p, sums=mid.sums,
    )
    plan, (gathered, first, second, totals) = exchange(
        rows, cols, grad, moment_first, moment_second, mid.extra
    )
    hidden_p, out_p, new_up, new_down, small_a, small_b, small_c = unpack(plan, gathered, w_up, w_down, perm_narrow, perm_wide)
    small = {0: (small_a, 0), 2: (small_b, 1), 6: (small_c, 2), 7: (small_c, 2)}
    whole = {
        1: new_down,
        3: rebuild_hidden(hidden_p, perm_wide, w_hidden),
        4: rebuild_out(out_p, perm_narrow, w_out),
        5: new_up,
    }
    olds = matrices + (biases_gains,)
    news = []
    for index, old in enumerate(olds):
        if index in whole:
            news.append(whole[index])
        else:
            source, which = small[index]
            start = FLAT_AT[index] - KEPT[which][0] * LANES
            piece = source.reshape(-1)[start : start + old.size].reshape(old.shape)
            news.append(moved(old, piece) if index < 7 else old - learn_rate * piece)
    return tuple(news) + (
        first.reshape(-1),
        second.reshape(-1),
        totals[0, 0],
        MB * CI * totals[1, 0],
        totals[8, 0],
    )


def solution(mesh):
    return jax.shard_map(
        on_device,
        mesh=mesh,
        in_specs=(
            P(None, "rows", "cols", None),
            P(None, "rows", "cols", None),
            P("rows", "cols"),
            P("rows", "cols"),
            P(),
            P(),
            P(),
            P(),
            P(),
            P(),
            P(),
            P(),
            P(),
            P(),
            P(),
            P(("rows", "cols")),
            P(("rows", "cols")),
        ),
        out_specs=(
            P(),
            P(),
            P(),
            P(),
            P(),
            P(),
            P(),
            P(),
            P(("rows", "cols")),
            P(("rows", "cols")),
            P(),
            P(),
            P(),
        ),
        check_vma=False,
    )
```

```python
import functools
import types

import jax
import jax.numpy as jnp
from jax import lax
from jax.experimental import pallas as pl
from jax.experimental.pallas import tpu as pltpu
from jax.sharding import PartitionSpec as P

CI = 77
C0 = 200
C1 = 800
CH = 3200
MB = 2
STEP = 5
LANES = 128
MESH = pl.DeviceIdType.MESH
ROUNDER = 12582912.0

decay_first = 0.9
decay_second = 0.99
epsilon = 1e-08
learn_rate = 0.02
weight_decay = 0.1
clip_limit = 1.0

VEC = 4 * C1 + CH + C1 + 2 * C0 + CI
SIZES = (9 * CI * C0, 4 * C0 * C1, 49 * C1, C1 * CH, CH * C1, C1 * 4 * C0, C0 * CI, VEC)
PADDED = 6602752
FLAT_AT = []
ROW_AT = []
for size in SIZES:
    flat_here = FLAT_AT[-1] + SIZES[len(FLAT_AT) - 1] if FLAT_AT else PADDED - sum(SIZES)
    row_here = ROW_AT[-1] + -(-SIZES[len(ROW_AT) - 1] // 1024) * 8 if ROW_AT else 0
    row_here = max(row_here, -(-flat_here // 1024) * 8)
    FLAT_AT.append(flat_here)
    ROW_AT.append(row_here)
SHIFTS = []
for flat_here, row_here, size in zip(FLAT_AT, ROW_AT, SIZES):
    moved = divmod(row_here * LANES - flat_here, LANES)
    if SHIFTS and SHIFTS[-1][:2] == moved:
        SHIFTS[-1] = moved + (SHIFTS[-1][2], flat_here + size)
    else:
        SHIFTS.append(moved + (flat_here, flat_here + size))
MAX_SHIFT = max(s[0] for s in SHIFTS) + 1


def bit_masks(bits):
    masks = [()]
    for bit in bits:
        masks = masks + [m + (bit,) for m in masks]
    return sorted(masks, key=lambda m: -len(m))


class Plan:
    def __init__(self, rows, cols, total):
        self.rows, self.cols, self.count = rows, cols, rows * cols
        self.share = total // LANES // self.count
        self.bits = rows.bit_length() - 1
        need = 7 + self.share + MAX_SHIFT + 1
        self.block = 64 if need > 1024 else 32
        self.window = -(-need // (2 * self.block)) * 2 * self.block
        self.part = self.window // 2
        self.blocks = self.part // self.block
        self.scales = self.blocks
        upper = list(range(1, self.bits))
        self.orders = [upper, upper[1:] + upper[:1]]
        self.stages = len(upper)
        self.space = (self.share * (self.count - 1)) // 8 * 8 + self.window
        self.padded = -(-self.share // 16) * 16
        cut = -(-self.padded // 32) * 16
        self.cuts = [(0, cut), (cut, self.padded - cut)]
        self.local = self.count // 2


def exchange_kernel(
    plan, grad, m_first, m_second, extra, full, first, second, totals,
    acc, near, q_send, q_recv, s_send, s_recv, z_send, z_recv, zs_send, zs_recv,
    rolled, step, low, stats,
    sem_load, sem_near_s, sem_near_r, sem_qs, sem_qr, sem_ss, sem_sr,
    sem_zs, sem_zr, sem_zss, sem_zsr, sem_ts, sem_tr, sem_own,
    sem_gs, sem_gr, sem_hs, sem_hr, sem_cs, sem_cr,
):
    nr, nc, n = plan.rows, plan.cols, plan.count
    r = lax.axis_index("rows")
    c = lax.axis_index("cols")
    me = r * nc + c
    part, window, share = plan.part, plan.window, plan.share

    def flipped(mask):
        out = r
        for bit in mask:
            here = (r // (1 << bit)) % 2
            out = out + (1 - 2 * here) * (1 << bit)
        return out

    def remote(src, dst, send, recv, row, col):
        return pltpu.make_async_remote_copy(
            src_ref=src, dst_ref=dst, send_sem=send, recv_sem=recv,
            device_id=(row, col), device_id_type=MESH,
        )

    barrier = pltpu.get_barrier_semaphore()

    def greet(d, carry):
        k = lax.rem(me + d, n)
        pl.semaphore_signal(barrier, inc=1, device_id=(k // nc, k % nc), device_id_type=MESH)
        return carry

    lax.fori_loop(1, n, greet, 0)
    pl.semaphore_wait(barrier, n - 1)

    upper = list(range(1, plan.bits))
    masks = bit_masks(upper)

    def local_index(mask, col):
        return (flipped(mask) // 2) * nc + col

    def window_start(row, col):
        return pl.multiple_of((share * (row * nc + col)) // 8 * 8, 8)

    def near_copy(mask, col):
        row = flipped(mask + (0,))
        return remote(
            grad.at[pl.ds(window_start(row, col), window)],
            near.at[local_index(mask, col)],
            sem_near_s.at[local_index(mask, col)], sem_near_r.at[local_index(mask, col)],
            flipped((0,)), c,
        )

    def load_copy(mask, col):
        index = local_index(mask, col)
        return pltpu.make_async_copy(
            grad.at[pl.ds(window_start(flipped(mask), col), window)], acc.at[index], sem_load.at[index]
        )

    half_way = nc // 2

    def column_of(t):
        return jnp.where(t == 1, half_way, jnp.where(t <= half_way, t - 1, t))

    def begin(t, carry):
        col = lax.rem(c + column_of(t), nc)
        for mask in masks:
            near_copy(mask, col).start()
            load_copy(mask, col).start()
        return carry

    lax.fori_loop(1, nc + 1, begin, 0)

    def encode(index, p, q_ref, s_ref):
        def body(b, carry):
            at = pl.ds(pl.multiple_of(b * plan.block, plan.block), plan.block)
            rows_at = pl.ds(pl.multiple_of(p * part + b * plan.block, 8), plan.block)
            values = acc[index, rows_at, :]
            top = jnp.maximum(jnp.max(jnp.abs(values), axis=0, keepdims=True), 1e-30)
            scaled = values * (32766.0 / top)
            scaled = (scaled + ROUNDER) - ROUNDER
            q_ref[at, :] = scaled.astype(jnp.int32).astype(jnp.int16)
            s_ref[pl.ds(b, 1), :] = top * (1.0 / 32766.0)
            return carry

        lax.fori_loop(0, plan.blocks, body, 0)

    def decode(index, p, q_ref, s_ref):
        def body(b, carry):
            at = pl.ds(pl.multiple_of(b * plan.block, plan.block), plan.block)
            rows_at = pl.ds(pl.multiple_of(p * part + b * plan.block, 8), plan.block)
            acc[index, rows_at, :] += q_ref[at, :].astype(jnp.float32) * s_ref[pl.ds(b, 1), :]
            return carry

        lax.fori_loop(0, plan.blocks, body, 0)

    def stage_base(stage):
        return sum((1 << (plan.stages - 1 - s)) for s in range(stage)) * nc

    def hop(p, stage, slot):
        row = flipped((plan.orders[p][stage],))
        at = stage_base(stage) + slot
        return (
            remote(q_send.at[p, at], q_recv.at[p, at], sem_qs.at[p, at], sem_qr.at[p, at], row, c),
            remote(s_send.at[p, at], s_recv.at[p, at], sem_ss.at[p, at], sem_sr.at[p, at], row, c),
        )

    def send_stage(p, stage, number, mask, col):
        bit = plan.orders[p][stage]
        index = local_index(mask + (bit,), col)
        slot = number * nc + col
        at = stage_base(stage) + slot
        encode(index, p, q_send.at[p, at], s_send.at[p, at])
        for copy in hop(p, stage, slot):
            copy.start()

    def take_stage(p, stage, number, mask, col):
        slot = number * nc + col
        for copy in hop(p, stage, slot):
            copy.wait_recv()
        at = stage_base(stage) + slot
        decode(local_index(mask, col), p, q_recv.at[p, at], s_recv.at[p, at])

    def free_masks(p, stage):
        rest = plan.orders[p][stage + 1 :]
        found = bit_masks(rest)
        if rest:
            found = [m for m in found if rest[0] in m] + [m for m in found if rest[0] not in m]
        return found

    def far_copy(p, d):
        col = lax.rem(c + d, nc)
        return (
            remote(z_send.at[p, d - 1], z_recv.at[p, d - 1], sem_zs.at[p, d - 1], sem_zr.at[p, d - 1], r, col),
            remote(zs_send.at[p, d - 1], zs_recv.at[p, d - 1], sem_zss.at[p, d - 1], sem_zsr.at[p, d - 1], r, col),
        )

    def join(t):
        d = column_of(t)
        col = lax.rem(c + d, nc)
        for mask in masks:
            index = local_index(mask, col)
            near_copy(mask, col).wait_recv()
            load_copy(mask, col).wait()

            def body(b, inner, index=index):
                at = pl.ds(pl.multiple_of(b * plan.block, plan.block), plan.block)
                acc[index, at, :] += near[index, at, :]
                return inner

            lax.fori_loop(0, 2 * plan.blocks, body, 0)
            for p in range(2):
                bit = plan.orders[p][0]
                if bit in mask:
                    rest = tuple(b for b in mask if b != bit)
                    options = free_masks(p, 0)
                    number = [sorted(o) for o in options].index(sorted(rest))
                    send_stage(p, 0, number, rest, col)

    def take(stage, t):
        d = column_of(t)
        col = lax.rem(c + d, nc)
        for number in range(1 << (plan.stages - 1 - stage)):
            for p in range(2):
                mask = free_masks(p, stage)[number]
                take_stage(p, stage, number, mask, col)
                if stage + 1 < plan.stages:
                    bit = plan.orders[p][stage + 1]
                    if bit in mask:
                        rest = tuple(b for b in mask if b != bit)
                        options = free_masks(p, stage + 1)
                        following = [sorted(o) for o in options].index(sorted(rest))
                        send_stage(p, stage + 1, following, rest, col)
                else:
                    @pl.when(d < nc)
                    def _(p=p):
                        encode(local_index((), col), p, z_send.at[p, d - 1], zs_send.at[p, d - 1])
                        for copy in far_copy(p, d):
                            copy.start()

    mine = local_index((), c)

    def gather_far(d, carry):
        for p in range(2):
            for copy in far_copy(p, d):
                copy.wait_recv()
            decode(mine, p, z_recv.at[p, d - 1], zs_recv.at[p, d - 1])
        return carry


    def turn_of(t, carry):
        @pl.when(t <= nc)
        def _():
            join(t)

        for stage in range(plan.stages):
            d = t - 1 - stage

            @pl.when((d >= 1) & (d <= nc))
            def _(stage=stage, d=d):
                take(stage, d)

        @pl.when((t > nc) & (t - nc < nc))
        def _():
            gather_far(column_of(t - nc), 0)

        return carry

    lax.fori_loop(1, nc + plan.stages + 1, turn_of, 0)

    def gather_rest(q, carry):
        return gather_far(column_of(q), carry)

    lax.fori_loop(min(plan.stages + 1, nc), nc, gather_rest, 0)

    offset = lax.rem(share * me, 8)
    low_end, high_end = share * me * LANES, share * (me + 1) * LANES
    for number, (shift_rows, shift_lanes, begin, end) in enumerate(SHIFTS):
        def turn(b, carry, number=number, shift_lanes=shift_lanes):
            at = pl.ds(pl.multiple_of(b * plan.block, plan.block), plan.block)
            rolled[number, at, :] = pltpu.roll(acc[mine, at, :], LANES - shift_lanes, 1)
            return carry

        @pl.when((low_end < end) & (high_end > begin))
        def _(turn=turn):
            lax.fori_loop(0, 2 * plan.blocks, turn, 0)

    def share_rows(start, length, chosen):
        lane = lax.broadcasted_iota(jnp.int32, (length, LANES), 1)
        out = jnp.zeros((length, LANES), jnp.float32)
        if len(chosen) > 1:
            line = lax.broadcasted_iota(jnp.int32, (length, LANES), 0)
            flat = (share * me + start + line) * LANES + lane
        for number in chosen:
            shift_rows, shift_lanes, begin, end = SHIFTS[number]
            here = rolled[number, pl.ds(offset + start + shift_rows, length), :]
            after = rolled[number, pl.ds(offset + start + shift_rows + 1, length), :]
            value = jnp.where(lane < LANES - shift_lanes, here, after)
            if len(chosen) > 1:
                value = jnp.where((flat >= begin) & (flat < end), value, out)
            out = value
        return out

    chunk = 32
    whole, tail = share // chunk, share % chunk
    stats[me, 8:16, :] = extra[...]

    def squares(chosen):
        def square(b, total):
            start = pl.multiple_of(b * chunk, chunk)
            value = share_rows(start, chunk, chosen)
            step[pl.ds(start, chunk), :] = value
            return total + jnp.sum((value * value).reshape(chunk // 8, 8, LANES), axis=0)

        total = lax.fori_loop(0, whole, square, jnp.zeros((8, LANES), jnp.float32))
        stats[me, 0:8, :] = total
        if tail:
            value = share_rows(whole * chunk, tail, chosen)
            step[whole * chunk : share, :] = value
            stats[me, 0:1, :] += jnp.sum(value * value, axis=0, keepdims=True)

    largest = max(range(len(SHIFTS)), key=lambda i: SHIFTS[i][3] - SHIFTS[i][2])
    alone = (low_end >= SHIFTS[largest][2]) & (high_end <= SHIFTS[largest][3])

    @pl.when(alone)
    def _():
        squares((largest,))

    @pl.when(jnp.logical_not(alone))
    def _():
        squares(tuple(range(len(SHIFTS))))

    def stat_copy(target, source):
        return remote(
            stats.at[me], stats.at[me], sem_ts.at[target], sem_tr.at[me], target // nc, target % nc
        )

    def stat_wait(source):
        return remote(
            stats.at[source], stats.at[source], sem_ts.at[source], sem_tr.at[source],
            source // nc, source % nc,
        )

    def send_stat(d, carry):
        stat_copy(lax.rem(me + d, n), me).start()
        return carry

    lax.fori_loop(1, n, send_stat, 0)

    def wait_stat(d, carry):
        stat_wait(lax.rem(me + d, n)).wait_recv()
        return carry

    lax.fori_loop(1, n, wait_stat, 0)

    def add_stat(k, total):
        return total + stats[k]

    sums = lax.fori_loop(0, n, add_stat, jnp.zeros((16, LANES), jnp.float32))
    norm = jnp.sqrt(jnp.sum(sums[0:8], keepdims=True))
    totals[0:1, :] = jnp.broadcast_to(jnp.sum(sums[8:9], keepdims=True), (1, LANES))
    totals[1:2, :] = jnp.broadcast_to(jnp.sum(sums[9:10], keepdims=True), (1, LANES))
    totals[2:8, :] = jnp.zeros((6, LANES), jnp.float32)
    totals[8:16, :] = jnp.broadcast_to(norm, (8, LANES))
    clip = jnp.minimum(1.0, clip_limit / norm)

    def update(start, length):
        clipped = step[pl.ds(start, length), :] * clip
        one = decay_first * m_first[pl.ds(start, length), :] + (1.0 - decay_first) * clipped
        two = decay_second * m_second[pl.ds(start, length), :] + (1.0 - decay_second) * clipped * clipped
        first[pl.ds(start, length), :] = one
        second[pl.ds(start, length), :] = two
        step[pl.ds(start, length), :] = (
            one / (1.0 - decay_first**STEP) / (jnp.sqrt(two / (1.0 - decay_second**STEP)) + epsilon)
        )

    def update_chunk(b, carry):
        update(pl.multiple_of(b * chunk, chunk), chunk)
        return carry

    lax.fori_loop(0, whole, update_chunk, 0)
    if tail:
        update(whole * chunk, tail)
    if plan.padded > share:
        step[share : plan.padded, :] = jnp.zeros((plan.padded - share, LANES), jnp.float32)

    def narrow(b, carry):
        at = pl.ds(pl.multiple_of(b * 16, 16), 16)
        low[at, :] = step[at, :].astype(jnp.bfloat16)
        return carry

    lax.fori_loop(0, plan.padded // 16, narrow, 0)

    own = pltpu.make_async_copy(low, full.at[me], sem_own)
    own.start()

    back = [list(reversed(order)) for order in plan.orders]

    def piece(mask, col, p):
        begin, length = plan.cuts[p]
        return full.at[flipped(mask) * nc + col, pl.ds(begin, length)]

    def mine_low(p):
        return low.at[pl.ds(*plan.cuts[p])]

    def along(direction, col, p, receive, first=False):
        step_col = 1 if direction == 0 else -1
        target = c - step_col if receive else c + step_col
        ref = piece((), col, p)
        return remote(mine_low(p) if first else ref, ref, sem_gs.at[direction, col, p], sem_gr.at[direction, col, p], r, target)

    def gather_masks(p, stage):
        return bit_masks(back[p][:stage])

    def gather_base(stage):
        return sum(1 << s for s in range(stage)) * nc

    def across(p, stage, number, mask, col, first=False):
        at = gather_base(stage) + number * nc + col
        ref = piece(mask, col, p)
        return remote(mine_low(p) if first else ref, ref, sem_hs.at[p, at], sem_hr.at[p, at], flipped((back[p][stage],)), c)

    def across_recv(p, stage, number, mask, col):
        at = gather_base(stage) + number * nc + col
        ref = piece(mask + (back[p][stage],), col, p)
        return remote(ref, ref, sem_hs.at[p, at], sem_hr.at[p, at], flipped((back[p][stage],)), c)

    def inward(p, mask, col, first=False):
        number = masks.index(tuple(sorted(mask)))
        at = number * nc + col
        ref = piece(mask, col, p)
        return remote(mine_low(p) if first else ref, ref, sem_cs.at[p, at], sem_cr.at[p, at], flipped((0,)), c)

    def inward_recv(p, mask, col):
        number = masks.index(tuple(sorted(mask)))
        at = number * nc + col
        ref = piece(mask + (0,), col, p)
        return remote(ref, ref, sem_cs.at[p, at], sem_cr.at[p, at], flipped((0,)), c)

    def spread(p, mask, col, stage, first=False):
        for later in range(stage, plan.stages):
            options = [sorted(o) for o in gather_masks(p, later)]
            if sorted(mask) in options:
                across(p, later, options.index(sorted(mask)), mask, col, first).start()
        inward(p, mask, col, first).start()

    def near_cols(t):
        if t == 0:
            return [(0, c)]
        return [(0, c - t), (1, c + t)]

    def inside(col):
        return (col >= 0) & (col < nc)

    for time in range(nc + plan.stages):
        for stage in range(plan.stages + 1):
            t = time - stage
            if not 0 <= t < nc:
                continue
            if stage == 0:
                if t == 0:
                    for p in range(2):
                        @pl.when(c < nc - 1)
                        def _(p=p):
                            along(0, c, p, False, True).start()

                        @pl.when(c > 0)
                        def _(p=p):
                            along(1, c, p, False, True).start()

                        spread(p, (), c, 0, True)
                else:
                    for direction, col in near_cols(t):
                        @pl.when(inside(col))
                        def _(direction=direction, col=col):
                            for p in range(2):
                                along(direction, col, p, True).wait_recv()
                                if direction == 0:
                                    @pl.when(c < nc - 1)
                                    def _():
                                        along(0, col, p, False).start()
                                else:
                                    @pl.when(c > 0)
                                    def _():
                                        along(1, col, p, False).start()
                                spread(p, (), col, 0)
            else:
                for direction, col in near_cols(t):
                    @pl.when(inside(col))
                    def _(col=col, stage=stage):
                        for number in range(1 << (stage - 1)):
                            for p in range(2):
                                mask = gather_masks(p, stage - 1)[number]
                                across_recv(p, stage - 1, number, mask, col).wait_recv()
                                spread(p, mask + (back[p][stage - 1],), col, stage)

    own.wait()
    for mask in masks:
        def finish(col, carry, mask=mask):
            for p in range(2):
                inward_recv(p, mask, col).wait_recv()
                inward(p, mask, col).wait_send()
            near_copy(mask, col).wait_send()
            return carry

        lax.fori_loop(0, nc, finish, 0)
    for p in range(2):
        for stage in range(plan.stages):
            for number, mask in enumerate(gather_masks(p, stage)):
                def sent(col, carry, p=p, stage=stage, number=number, mask=mask):
                    across(p, stage, number, mask, col).wait_send()
                    return carry

                lax.fori_loop(0, nc, sent, 0)
            for number in range(1 << (plan.stages - 1 - stage)):
                def left(col, carry, p=p, stage=stage, number=number):
                    for copy in hop(p, stage, number * nc + col):
                        copy.wait_send()
                    return carry

                lax.fori_loop(0, nc, left, 0)

        def gone(col, carry, p=p):
            @pl.when((col <= c) & (c < nc - 1))
            def _():
                along(0, col, p, False).wait_send()

            @pl.when((col >= c) & (c > 0))
            def _():
                along(1, col, p, False).wait_send()

            return carry

        lax.fori_loop(0, nc, gone, 0)

        def far_gone(d, carry, p=p):
            for copy in far_copy(p, d):
                copy.wait_send()
            return carry

        lax.fori_loop(1, nc, far_gone, 0)

    def stat_gone(d, carry):
        stat_copy(lax.rem(me + d, n), me).wait_send()
        return carry

    lax.fori_loop(1, n, stat_gone, 0)


def exchange(rows, cols, grad, m_first, m_second, extra):
    plan = Plan(rows, cols, m_first.size * rows * cols)
    n, nc, share = plan.count, plan.cols, plan.share
    hops = sum(1 << s for s in range(plan.stages)) * nc
    dma = pltpu.SemaphoreType.DMA
    far = max(nc - 1, 1)
    vmem = pl.BlockSpec(memory_space=pltpu.VMEM)
    hbm = pl.BlockSpec(memory_space=pl.ANY)
    return plan, pl.pallas_call(
        functools.partial(exchange_kernel, plan),
        out_shape=(
            jax.ShapeDtypeStruct((n, plan.padded, LANES), jnp.bfloat16),
            jax.ShapeDtypeStruct((share, LANES), jnp.float32),
            jax.ShapeDtypeStruct((share, LANES), jnp.float32),
            jax.ShapeDtypeStruct((16, LANES), jnp.float32),
        ),
        in_specs=[hbm, vmem, vmem, vmem],
        out_specs=(hbm, vmem, vmem, vmem),
        scratch_shapes=[
            pltpu.VMEM((plan.local, plan.window, LANES), jnp.float32),
            pltpu.VMEM((plan.local, plan.window, LANES), jnp.float32),
            pltpu.VMEM((2, hops, plan.part, LANES), jnp.int16),
            pltpu.VMEM((2, hops, plan.part, LANES), jnp.int16),
            pltpu.VMEM((2, hops, plan.scales, LANES), jnp.float32),
            pltpu.VMEM((2, hops, plan.scales, LANES), jnp.float32),
            pltpu.VMEM((2, far, plan.part, LANES), jnp.int16),
            pltpu.VMEM((2, far, plan.part, LANES), jnp.int16),
            pltpu.VMEM((2, far, plan.scales, LANES), jnp.float32),
            pltpu.VMEM((2, far, plan.scales, LANES), jnp.float32),
            pltpu.VMEM((len(SHIFTS), plan.window, LANES), jnp.float32),
            pltpu.VMEM((plan.padded, LANES), jnp.float32),
            pltpu.VMEM((plan.padded, LANES), jnp.bfloat16),
            pltpu.VMEM((n, 16, LANES), jnp.float32),
            dma((plan.local,)), dma((plan.local,)), dma((plan.local,)),
            dma((2, hops)), dma((2, hops)), dma((2, hops)), dma((2, hops)),
            dma((2, far)), dma((2, far)), dma((2, far)), dma((2, far)),
            dma((n,)), dma((n,)), dma,
            dma((2, nc, 2)), dma((2, nc, 2)),
            dma((2, hops)), dma((2, hops)),
            dma((2, plan.local)), dma((2, plan.local)),
        ],
        compiler_params=pltpu.CompilerParams(
            collective_id=0, has_side_effects=True, vmem_limit_bytes=56 << 20
        ),
    )(grad, m_first.reshape(share, LANES), m_second.reshape(share, LANES), extra)


WIDE = CH + LANES
KEPT = ((8, 1104), (6096, 6408), (51400, 51584))
PLACES = tuple(divmod(FLAT_AT[i], LANES) for i in (3, 4, 5, 1))

SLOTS = 6
HALF = WIDE // 2
PITCH = 33


def unpack_kernel(
    plan, gathered, old_up, old_down, narrow, wide, hidden_out, rows_out, up_out, down_out, small_a, small_b, small_c,
    held, flat, woven, hidden, by_row, rows_low, up, down, sems, sem_out,
):
    n, share = plan.count, plan.share
    step = CH // LANES

    def fetch(k, slot):
        return pltpu.make_async_copy(gathered.at[k], held.at[slot], sems.at[slot])

    for k in range(SLOTS - 1):
        fetch(k, k).start()

    def widen(k, carry):
        slot = lax.rem(k, SLOTS)

        @pl.when(k + SLOTS - 1 < n)
        def _():
            fetch(k + SLOTS - 1, lax.rem(k + SLOTS - 1, SLOTS)).start()

        fetch(k, slot).wait()

        def body(b, inner):
            at = pl.ds(pl.multiple_of(b * 16, 16), 16)
            flat[pl.ds(share * k + b * 16, 16), :] = held[slot, at, :].astype(jnp.float32)
            return inner

        lax.fori_loop(0, plan.padded // 16, body, 0, unroll=4)
        return carry

    lax.fori_loop(0, n, widen, 0)

    copies = [
        pltpu.make_async_copy(source, target, sem_out.at[i])
        for i, (source, target) in enumerate(
            (
                (hidden, hidden_out.at[:, pl.ds(0, HALF)]), (rows_low, rows_out), (up, up_out),
                (down, down_out), (hidden, hidden_out.at[:, pl.ds(HALF, HALF)]),
            )
        )
    ]
    row, lane = PLACES[0]

    def spread(a, carry):
        by_row[pl.ds(narrow[a] * PITCH, 32), :] = flat[pl.ds(row + a * step, 32), :]
        return carry

    lax.fori_loop(0, C1, spread, 0, unroll=4)

    def columns(half):
        def column(t, carry):
            for begin in range(0, C1, 160):
                at = begin * PITCH + half * (HALF // LANES) + t
                values = by_row[pl.ds(at, 160, stride=PITCH), :]
                at = pl.ds(pl.multiple_of(t * LANES, LANES), LANES)
                hidden[begin : begin + 160, at] = values.astype(jnp.bfloat16)
            return carry

        lax.fori_loop(0, HALF // LANES, column, 0)

    columns(0)
    copies[0].start()

    quarter = C1 // 4
    for number, (ref, old, (line, begin)) in enumerate(zip((up, down), (old_up, old_down), PLACES[2:])):
        for u in range(-(-C1 // LANES)):
            width = min(LANES, C1 - u * LANES)
            place = lax.broadcasted_iota(jnp.int32, (quarter, LANES), 1)
            for b in range(4):
                first, rest = divmod(C1 * b + begin, LANES)
                here = flat[pl.ds(line + first + u, quarter, stride=step), :]
                after = flat[pl.ds(line + first + u + 1, quarter, stride=step), :]
                value = pltpu.roll(jnp.where(place >= rest, here, after), LANES - rest, 1)
                woven[pl.ds(b, quarter, stride=4), :] = value
            at = slice(u * LANES, u * LANES + width)
            ref[:, at] = moved(old[:, at], woven[:, :width])
        copies[2 + number].start()

    for ref, (begin, end) in zip((small_a, small_b, small_c), KEPT):
        ref[...] = flat[begin:end, :]
    copies[0].wait()
    columns(1)
    copies[4].start()

    row, lane = PLACES[1]

    def align(part, carry):
        place = lax.broadcasted_iota(jnp.int32, (40, LANES), 1)
        for b in range(4):
            first, rest = divmod(C1 * b + lane, LANES)
            tiles = [
                flat[pl.ds(row + part * (40 * step) + first + u, 40, stride=step), :]
                for u in range(C1P // LANES + 1)
            ]
            values = [
                pltpu.roll(jnp.where(place >= rest, here, after), LANES - rest, 1)
                for here, after in zip(tiles, tiles[1:])
            ]
            for u, value in enumerate(values):
                flat[pl.ds(part * (40 * PITCH) + b * 8 + u, 40, stride=PITCH), :] = value
        return carry

    lax.fori_loop(0, C1 // 40, align, 0)

    def scatter(a, carry):
        for b in range(4):
            by_row[pl.ds(wide[a * 4 + b] * 9, 8), :] = flat[pl.ds(a * PITCH + b * 8, 8), :]
        return carry

    lax.fori_loop(0, CH // 4, scatter, 0, unroll=4)

    def by_lane(part, carry):
        for u in range(C1P // LANES):
            values = by_row[pl.ds(part * (160 * 9) + u, 160, stride=9), :]
            at = pl.ds(pl.multiple_of(part * 160, 160), 160)
            rows_low[at, u * LANES : (u + 1) * LANES] = values.astype(jnp.bfloat16)
        return carry

    lax.fori_loop(0, CH // 160, by_lane, 0)
    copies[1].start()
    for copy in copies[1:]:
        copy.wait()


def unpack(plan, gathered, old_up, old_down, narrow, wide):
    lines = PADDED // LANES
    vmem = pl.BlockSpec(memory_space=pltpu.VMEM)
    hbm = pl.BlockSpec(memory_space=pl.ANY)
    dma = pltpu.SemaphoreType.DMA
    f32, low = jnp.float32, jnp.bfloat16
    return pl.pallas_call(
        functools.partial(unpack_kernel, plan),
        out_shape=(
            jax.ShapeDtypeStruct((C1, WIDE), low),
            jax.ShapeDtypeStruct((CH, C1P), low),
            jax.ShapeDtypeStruct((C1, C1), f32),
            jax.ShapeDtypeStruct((C1, C1), f32),
        )
        + tuple(jax.ShapeDtypeStruct((end - begin, LANES), f32) for begin, end in KEPT),
        in_specs=[hbm, vmem, vmem] + [pl.BlockSpec(memory_space=pltpu.SMEM)] * 2,
        out_specs=(hbm, hbm, hbm, hbm, vmem, vmem, vmem),
        scratch_shapes=[
            pltpu.VMEM((SLOTS, plan.padded, LANES), low),
            pltpu.VMEM((-(-lines // 8) * 8 + 16, LANES), f32),
            pltpu.VMEM((C1, LANES), f32),
            pltpu.VMEM((C1, HALF), low),
            pltpu.VMEM((CH * 9, LANES), f32),
            pltpu.VMEM((CH, C1P), low),
            pltpu.VMEM((C1, C1), f32),
            pltpu.VMEM((C1, C1), f32),
            dma((SLOTS,)),
            dma((5,)),
        ],
        compiler_params=pltpu.CompilerParams(vmem_limit_bytes=63 << 20),
    )(gathered, old_up, old_down, narrow, wide)


def moved(old, direction):
    return old.astype(jnp.float32) * (1.0 - learn_rate * weight_decay) - learn_rate * direction


def one_hot(condition):
    return jnp.where(condition, 1.0, 0.0).astype(jnp.bfloat16)


def product(left, right):
    return jnp.dot(left, right, preferred_element_type=jnp.float32)


def product_t(left, right):
    return lax.dot_general(left, right, (((1,), (1,)), ((), ())), preferred_element_type=jnp.float32)


TILE = 512
STEPS = -(-CH // TILE)
LAST = CH - (STEPS - 1) * TILE


DEEP = 256


def by_width(body):
    final = pl.program_id(0) == STEPS - 1

    @pl.when(jnp.logical_not(final))
    def _():
        body(TILE)

    @pl.when(final)
    def _():
        body(LAST)


def hidden_kernel(lines, wide, old, new):
    depth = lines.shape[1]
    base = pl.program_id(0) * TILE

    def body(width):
        direction = None
        for begin in range(0, depth, DEEP):
            end = min(begin + DEEP, depth)
            place = wide[begin:end, :] - base
            lane = lax.broadcasted_iota(jnp.int32, (end - begin, LANES), 1)
            hot = jnp.concatenate([one_hot(lane + u == place) for u in range(0, width, LANES)], axis=1)
            term = product(lines[:, begin:end], hot)
            direction = term if direction is None else direction + term
        new[:, :width] = moved(old[:, :width], direction)

    by_width(body)


def rebuild_hidden(lines, wide, old):
    lane = PLACES[0][1]
    wide = jnp.full((WIDE,), -1, jnp.int32).at[lane : lane + CH].set(wide)
    return pl.pallas_call(
        hidden_kernel,
        out_shape=jax.ShapeDtypeStruct((C1, CH), jnp.float32),
        grid=(STEPS,),
        in_specs=[
            pl.BlockSpec((C1, WIDE), lambda i: (0, 0)),
            pl.BlockSpec((WIDE, LANES), lambda i: (0, 0)),
            pl.BlockSpec((C1, TILE), lambda i: (0, i)),
        ],
        out_specs=pl.BlockSpec((C1, TILE), lambda i: (0, i)),
        compiler_params=pltpu.CompilerParams(vmem_limit_bytes=48 << 20),
    )(lines, jnp.broadcast_to(wide[:, None], (WIDE, LANES)), old)


def out_kernel(rows, narrow, old, new, turn):
    @pl.when(pl.program_id(0) == 0)
    def _():
        turn[...] = one_hot(lax.broadcasted_iota(jnp.int32, (C1, C1), 0) == narrow[...])

    def body(width):
        new[:, :width] = moved(old[:, :width], product_t(turn[...], rows[:width, :C1]))

    by_width(body)


def rebuild_out(rows, narrow, old):
    return pl.pallas_call(
        out_kernel,
        out_shape=jax.ShapeDtypeStruct((C1, CH), jnp.float32),
        grid=(STEPS,),
        in_specs=[
            pl.BlockSpec((TILE, C1P), lambda i: (i, 0)),
            pl.BlockSpec((1, C1), lambda i: (0, 0)),
            pl.BlockSpec((C1, TILE), lambda i: (0, i)),
        ],
        out_specs=pl.BlockSpec((C1, TILE), lambda i: (0, i)),
        scratch_shapes=[pltpu.VMEM((C1, C1), jnp.bfloat16)],
        compiler_params=pltpu.CompilerParams(vmem_limit_bytes=48 << 20),
    )(rows, narrow[None, :], old.T).T


def weave(source, rows, put, width=C1):
    group = CH // width
    for t in range(CH // LANES):
        b, begin = divmod(t * LANES, width)
        u, rest = divmod(begin, LANES)
        place = lax.broadcasted_iota(jnp.int32, (rows, LANES), 1)
        value = source[u, pl.ds(b, rows, stride=group), :]
        if rest:
            if begin + LANES - rest < width:
                after = source[u + 1, pl.ds(b, rows, stride=group), :]
                value = jnp.where(place >= rest, value, after)
            value = pltpu.roll(value, LANES - rest, 1)
        left = width - begin
        if left < LANES:
            following = source[0, pl.ds(b + 1, rows, stride=group), :]
            value = jnp.where(place < left, value, pltpu.roll(following, left, 1))
        put(t, value)


def place_kernel(
    nr, nc, normed, branch, pre, act, narrow_row, narrow_col, wide, up, cells,
    grad, padded, hidden, out, loose, up_rows, norm_t, branch_r, halo_cells, held_pre, held_act,
    sem_out, sems, sem_halo_s, sem_halo_r, sem_in,
):
    step = pl.program_id(0)
    steps = STEPS
    ratio = CH // LANES

    def out_copy(n, width):
        begin = n * (TILE // 4 * ratio)
        rows = width // 4 * ratio
        return pltpu.make_async_copy(
            out.at[pl.ds(pl.multiple_of(begin, 8), rows)],
            grad.at[pl.ds(pl.multiple_of(ROW_AT[4] + begin, 8), rows)],
            sem_out.at[n],
        )

    copies = [
        pltpu.make_async_copy(ref, grad.at[pl.ds(row, ref.shape[0])], sems.at[i])
        for i, (ref, row) in enumerate(((up_rows, ROW_AT[5]), (hidden, ROW_AT[3])))
    ] + [pltpu.make_async_copy(halo_cells, padded, sems.at[2])]

    fetch_pre = pltpu.make_async_copy(pre, held_pre, sem_in.at[0])
    fetch_act = pltpu.make_async_copy(act, held_act, sem_in.at[1])

    @pl.when(step == 0)
    def _():
        fetch_pre.start()
        fetch_act.start()
        halo_start(nr, nc, 3, cells, halo_cells, sem_halo_s, sem_halo_r)
        line = lax.broadcasted_iota(jnp.int32, (C1, C1), 1)
        norm_t[...] = product_t(one_hot(line == narrow_col[:, 0:1]), normed[:, :C1]).astype(jnp.bfloat16)
        line = lax.broadcasted_iota(jnp.int32, (C1, C1P), 0)
        branch_r[...] = product(branch[:, :C1], one_hot(line == narrow_row[...])).astype(jnp.bfloat16)
        for u in range(-(-C1 // LANES)):
            width = min(LANES, C1 - u * LANES)
            loose[u, :, 0:width] = up[0:C1, u * LANES : u * LANES + width]

        def put(t, value):
            up_rows[pl.ds(t, C1 // 4, stride=ratio), :] = value

        weave(loose, C1 // 4, put)
        copies[0].start()
        fetch_pre.wait()
        fetch_act.wait()

    def body(width):
        turned_pre = turned_act = None
        for begin in range(0, CH, DEEP):
            end = min(begin + DEEP, CH)
            line = lax.broadcasted_iota(jnp.int32, (end - begin, width), 0) + begin
            hot = one_hot(line == wide[:, :width])
            one = product(held_pre[:, begin:end], hot)
            two = product(held_act[:, begin:end], hot)
            turned_pre = one if turned_pre is None else turned_pre + one
            turned_act = two if turned_act is None else turned_act + two
        part = product(norm_t[...], turned_pre.astype(jnp.bfloat16))
        for t in range(width // LANES):
            at = pl.ds(step * (TILE // LANES) + t, C1, stride=ratio)
            hidden[at, :] = part[:, t * LANES : (t + 1) * LANES]
        part = inner_rows(turned_act.astype(jnp.bfloat16), branch_r[...])
        for u in range(-(-C1 // LANES)):
            loose[u, 0:width, :] = part[:, u * LANES : (u + 1) * LANES]

        def put_out(t, value):
            out[pl.ds(step * (TILE // 4 * ratio) + t, width // 4, stride=ratio), :] = value

        weave(loose, width // 4, put_out)
        out_copy(step, width).start()

    by_width(body)

    @pl.when(step == steps - 1)
    def _():
        copies[1].start()
        halo_finish(nr, nc, 3, cells, halo_cells, sem_halo_s, sem_halo_r)
        copies[2].start()

        def finish(n, carry):
            out_copy(n, TILE).wait()
            return carry

        lax.fori_loop(0, steps - 1, finish, 0)
        out_copy(steps - 1, LAST).wait()
        for copy in copies:
            copy.wait()


def place_gradients(nr, nc, space, normed, branch, pre, act, narrow, wide, up, cells):
    def whole(array):
        return pl.BlockSpec(
            array.shape, lambda i: (0,) * len(array.shape), pipeline_mode=pl.Buffered(1)
        )

    hbm = pl.BlockSpec(memory_space=pl.ANY)
    rows = pre.shape[0]
    batch, height, breadth, chans = cells.shape
    narrow_row = jnp.pad(narrow, (0, C1P - C1), constant_values=-1)[None, :]
    narrow_col = jnp.broadcast_to(narrow[:, None], (C1, LANES))
    framed = jax.ShapeDtypeStruct((batch, height + 6, breadth + 2 * EDGE, chans), cells.dtype)
    dma = pltpu.SemaphoreType.DMA
    return pl.pallas_call(
        functools.partial(place_kernel, nr, nc),
        out_shape=(jax.ShapeDtypeStruct((space, LANES), jnp.float32), framed),
        grid=(STEPS,),
        in_specs=[
            whole(normed), whole(branch), hbm, hbm, whole(narrow_row), whole(narrow_col),
            pl.BlockSpec((1, TILE), lambda i: (0, i)),
            whole(up), whole(cells),
        ],
        out_specs=(hbm, hbm),
        scratch_shapes=[
            pltpu.VMEM((C1 * CH // LANES, LANES), jnp.float32),
            pltpu.VMEM((C1 * CH // LANES, LANES), jnp.float32),
            pltpu.VMEM((C1P // LANES, C1, LANES), jnp.float32),
            pltpu.VMEM((C1 * C1 // LANES, LANES), jnp.float32),
            pltpu.VMEM((C1, rows), jnp.bfloat16),
            pltpu.VMEM((rows, C1P), jnp.bfloat16),
            pltpu.VMEM(framed.shape, framed.dtype),
            pltpu.VMEM(pre.shape, pre.dtype),
            pltpu.VMEM(act.shape, act.dtype),
            dma((STEPS,)), dma((3,)), dma((8,)), dma((8,)), dma((2,)),
        ],
        compiler_params=pltpu.CompilerParams(
            collective_id=3, has_side_effects=True, vmem_limit_bytes=60 << 20
        ),
    )(normed, branch, pre, act, narrow_row, narrow_col, wide[None, :], up, cells)


C0P = 256
C1P = 896
CIP = 128
EDGE = 16
CURVE = 0.7978845608028654
CUBE = 0.044715


def inner_rows(left, right):
    return lax.dot_general(left, right, (((0,), (0,)), ((), ())), preferred_element_type=jnp.float32)


def column_sum(values):
    return jnp.sum(values.astype(jnp.float32), axis=0, keepdims=True)


def gelu_and_slope(t):
    square = t * t
    bend = jnp.tanh(CURVE * (t + CUBE * (square * t)))
    half = 0.5 * (1.0 + bend)
    return t * half, half + 0.5 * t * (1.0 - bend * bend) * (CURVE * (1.0 + 3.0 * CUBE * square))


WAYS = [(dr, dc) for dr in (-1, 0, 1) for dc in (-1, 0, 1) if (dr, dc) != (0, 0)]
ORDER = sorted(range(8), key=lambda i: (WAYS[i][1] != 0, WAYS[i][0] == 0))


def halo_place(nr, nc):
    r = lax.axis_index("rows")
    return r, lax.axis_index("cols"), lambda dr: (r + dr >= 0) & (r + dr < nr)


def halo_copy(nr, nc, width, cells, out, sem_s, sem_r, i, receive):
    r, c, there = halo_place(nr, nc)
    height, breadth = cells.shape[1], cells.shape[2]
    dr, dc = WAYS[i]
    rows_from = {-1: (0, width), 0: (0, height), 1: (height - width, width)}[dr]
    rows_to = {-1: height + width, 0: width, 1: 0}[dr]
    cols_from = {-1: (0, EDGE), 0: (0, breadth), 1: (breadth - EDGE, EDGE)}[dc]
    cols_to = {-1: EDGE + breadth, 0: EDGE, 1: 0}[dc]
    sign = -1 if receive else 1
    return pltpu.make_async_remote_copy(
        src_ref=cells.at[:, pl.ds(*rows_from), pl.ds(*cols_from)],
        dst_ref=out.at[:, pl.ds(rows_to, rows_from[1]), pl.ds(cols_to, cols_from[1])],
        send_sem=sem_s.at[i],
        recv_sem=sem_r.at[i],
        device_id=(r + sign * dr, lax.rem(c + sign * dc + nc, nc)),
        device_id_type=MESH,
    )


def halo_start(nr, nc, width, cells, out, sem_s, sem_r):
    r, c, there = halo_place(nr, nc)
    height, breadth = cells.shape[1], cells.shape[2]
    barrier = pltpu.get_barrier_semaphore()
    for dr, dc in WAYS:
        @pl.when(there(dr))
        def _(dr=dr, dc=dc):
            pl.semaphore_signal(
                barrier, inc=1, device_id=(r + dr, lax.rem(c + dc + nc, nc)), device_id_type=MESH
            )

    edge = (r == 0) | (r == nr - 1)

    @pl.when(edge)
    def _():
        pl.semaphore_wait(barrier, 5)

    @pl.when(jnp.logical_not(edge))
    def _():
        pl.semaphore_wait(barrier, 8)

    for i in ORDER:
        @pl.when(there(WAYS[i][0]))
        def _(i=i):
            halo_copy(nr, nc, width, cells, out, sem_s, sem_r, i, False).start()

    for m in range(cells.shape[0]):
        for row in range(height):
            out[m, width + row, EDGE : EDGE + breadth, :] = cells[m, row]

    @pl.when(r == 0)
    def _():
        out[:, 0:width] = jnp.zeros((out.shape[0], width) + out.shape[2:], out.dtype)

    @pl.when(r == nr - 1)
    def _():
        out[:, height + width :] = jnp.zeros((out.shape[0], width) + out.shape[2:], out.dtype)


def halo_finish(nr, nc, width, cells, out, sem_s, sem_r):
    r, c, there = halo_place(nr, nc)
    for i in ORDER:
        @pl.when(there(-WAYS[i][0]))
        def _(i=i):
            halo_copy(nr, nc, width, cells, out, sem_s, sem_r, i, True).wait_recv()

        @pl.when(there(WAYS[i][0]))
        def _(i=i):
            halo_copy(nr, nc, width, cells, out, sem_s, sem_r, i, False).wait_send()


def halo_kernel(nr, nc, width, cells, out, sem_s, sem_r):
    halo_start(nr, nc, width, cells, out, sem_s, sem_r)
    halo_finish(nr, nc, width, cells, out, sem_s, sem_r)


def halo(nr, nc, width, cells, identity):
    batch, height, breadth, chans = cells.shape
    vmem = pl.BlockSpec(memory_space=pltpu.VMEM)
    return pl.pallas_call(
        functools.partial(halo_kernel, nr, nc, width),
        out_shape=jax.ShapeDtypeStruct(
            (batch, height + 2 * width, breadth + 2 * EDGE, chans), cells.dtype
        ),
        in_specs=[vmem],
        out_specs=vmem,
        scratch_shapes=[pltpu.SemaphoreType.DMA((8,)), pltpu.SemaphoreType.DMA((8,))],
        compiler_params=pltpu.CompilerParams(
            collective_id=identity, has_side_effects=True, vmem_limit_bytes=24 << 20
        ),
    )(cells)


SIDE = 8
REACH = 3
FINE_REACH = 2 * REACH + 1


def input_kernel(
    nr, state, w_in, w_down, vector, taps_out, slope_zero_out, h_zero_out, coarse, padded, lines,
    wide, taps_all, coarse_all, taps, slope_zero, h_zero, sems,
):
    r = lax.axis_index("rows")
    copies = [
        pltpu.make_async_copy(source, target, sems.at[i])
        for i, (source, target) in enumerate(((taps, taps_out), (slope_zero, slope_zero_out), (h_zero, h_zero_out)))
    ]
    lines[...] = jnp.zeros_like(lines)
    start = 0
    for number, size in enumerate((C0, C1, C1, C1, C1, CH, C1, C0, CI)):
        lines[number : number + 1, 0:size] = vector[:, start : start + size]
        start = start + size
    batch, rows, breadth, _ = state.shape
    half_h, half_w = rows // 2 - FINE_REACH, breadth // 2 - EDGE
    all_h, all_w = half_h + 2 * REACH, half_w + 2 * SIDE
    for m in range(batch):
        for y in range(rows):
            wide[m, y, SIDE : SIDE + breadth, :] = state[m, y].astype(jnp.float32)
    for m in range(batch):
        for y in range(rows):
            for f in range(4):
                start = SIDE + EDGE - 2 * SIDE - 1 + f
                line = wide[m, y, pl.ds(start, all_w, stride=2), :]
                low = line.astype(jnp.bfloat16)
                inner = line[SIDE : SIDE + half_w].astype(jnp.bfloat16)
                for dy in range(3):
                    i, sy = divmod(y - dy, 2)
                    if not 0 <= i < all_h:
                        continue
                    for dx in range(3):
                        if not 0 <= f - dx < 2:
                            continue
                        s, tap = sy * 2 + f - dx, slice((dy * 3 + dx) * CIP, (dy * 3 + dx + 1) * CIP)
                        begin = (m * all_h + i) * all_w
                        taps_all[s, begin : begin + all_w, tap] = low
                        if REACH <= i < REACH + half_h:
                            begin = (m * half_h + i - REACH) * half_w
                            taps[s, begin : begin + half_w, tap] = inner
    copies[0].start()
    size = all_h * all_w
    for m in range(batch):
        block = slice(m * size, (m + 1) * size)
        total = jnp.broadcast_to(lines[1:2, :C1P], (size, C1P))
        for s in range(4):
            value = product(taps_all[s, block, :], w_in[...]) + lines[0:1, :C0P]
            curved, slope = gelu_and_slope(value)
            for i in range(half_h):
                begin = (i + REACH) * all_w + SIDE
                at = slice((m * half_h + i) * half_w, (m * half_h + i + 1) * half_w)
                slope_zero[s, at, :] = slope[begin : begin + half_w]
                h_zero[s, at, :] = curved[begin : begin + half_w]
            total = total + product(curved.astype(jnp.bfloat16), w_down[s])
        coarse_all[...] = total
        for i in range(half_h):
            begin = (i + REACH) * all_w + SIDE
            at = slice((m * half_h + i) * half_w, (m * half_h + i + 1) * half_w)
            coarse[at, :] = coarse_all[begin : begin + half_w, :]
        if m == batch - 1:
            copies[1].start()
            copies[2].start()
        padded[m] = coarse_all[...].astype(jnp.bfloat16).reshape(padded.shape[1:])

    @pl.when(r == 0)
    def _():
        padded[:, 0:REACH] = jnp.zeros((batch, REACH) + padded.shape[2:], padded.dtype)

    @pl.when(r == nr - 1)
    def _():
        padded[:, all_h - REACH :] = jnp.zeros((batch, REACH) + padded.shape[2:], padded.dtype)

    for copy in copies:
        copy.wait()


def input_part(nr, state, w_in, w_down, vector):
    batch, rows, breadth, _ = state.shape
    half_h, half_w = rows // 2 - FINE_REACH, breadth // 2 - EDGE
    all_h, all_w = half_h + 2 * REACH, half_w + 2 * SIDE
    cells = batch * half_h * half_w
    vmem = pl.BlockSpec(memory_space=pltpu.VMEM)
    hbm = pl.BlockSpec(memory_space=pl.ANY)
    large = (
        jax.ShapeDtypeStruct((4, cells, 9 * CIP), jnp.bfloat16),
        jax.ShapeDtypeStruct((4, cells, C0P), jnp.float32),
        jax.ShapeDtypeStruct((4, cells, C0P), jnp.float32),
    )
    return pl.pallas_call(
        functools.partial(input_kernel, nr),
        out_shape=large
        + (
            jax.ShapeDtypeStruct((cells, C1P), jnp.float32),
            jax.ShapeDtypeStruct((batch, all_h, all_w, C1P), jnp.bfloat16),
            jax.ShapeDtypeStruct((16, CH), jnp.float32),
        ),
        in_specs=[vmem] * 4,
        out_specs=(hbm, hbm, hbm, vmem, vmem, vmem),
        scratch_shapes=[
            pltpu.VMEM((batch, rows, breadth + 2 * SIDE, CIP), jnp.float32),
            pltpu.VMEM((4, batch * all_h * all_w, 9 * CIP), jnp.bfloat16),
            pltpu.VMEM((all_h * all_w, C1P), jnp.float32),
        ]
        + [pltpu.VMEM(shape.shape, shape.dtype) for shape in large]
        + [pltpu.SemaphoreType.DMA((3,))],
        compiler_params=pltpu.CompilerParams(vmem_limit_bytes=50 << 20),
    )(state, w_in, w_down, vector)


def spread_lanes(padded, held):
    for m in range(padded.shape[0]):
        def body(y, carry, m=m):
            for u in range(C1P // LANES):
                held[u, m, y, 0 : padded.shape[2], :] = padded[m, y, :, u * LANES : (u + 1) * LANES].astype(jnp.float32)
            return carry

        lax.fori_loop(0, padded.shape[1], body, 0)


def convolve(held, w_dw, half_w, edge, put, back):
    tiles, batch, rows = held.shape[:3]
    height = rows - 2 * REACH

    def body(number, carry):
        u, m = number // batch, number % batch
        sums = [jnp.zeros((half_w, LANES), jnp.float32) for _ in range(height)]
        for x in range(7):
            for y in range(rows):
                window = held[u, m, y, pl.ds(edge - REACH + x, half_w), :]
                for i in range(height):
                    if 0 <= y - i < 7:
                        tap = (6 - (y - i)) * 7 + 6 - x if back else (y - i) * 7 + x
                        sums[i] = sums[i] + window * w_dw[pl.ds(tap, 1), lanes_at(u)]
        for i in range(height):
            put(u, m, i, sums[i])
        return carry

    lax.fori_loop(0, tiles * batch, body, 0)


def rows_at(m, i, height, half_w):
    return pl.ds(pl.multiple_of((m * height + i) * half_w, half_w), half_w)


def lanes_at(u):
    return pl.ds(pl.multiple_of(u * LANES, LANES), LANES)


PART = 1280


def middle_kernel(names, late, early, *refs):
    table = dict(zip(names, refs))
    ref = types.SimpleNamespace(**table)
    batch, rows, breadth, _ = ref.padded.shape
    cells = ref.coarse.shape[0]
    height, half_w = rows - 2 * REACH, breadth - 2 * SIDE
    held_in = {name: table["held_" + name] for name in late}
    held_out = {name: table["held_" + name] for name in early}
    fetch = {
        name: pltpu.make_async_copy(table[name], held_in[name], ref.sem_in.at[i])
        for i, name in enumerate(late)
    }
    stores = {
        name: pltpu.make_async_copy(held_out[name], table[name], ref.sem_out.at[i])
        for i, name in enumerate(early)
    }
    for copy in fetch.values():
        copy.start()
    conv = ref.conv

    def depthwise(held):
        spread_lanes(ref.padded, held)

        def put(u, m, i, value):
            conv[rows_at(m, i, height, half_w), lanes_at(u)] = value

        convolve(held, ref.w_dw, half_w, SIDE, put, False)

    pl.run_scoped(depthwise, pltpu.VMEM((C1P // LANES, batch, rows, breadth, LANES), jnp.float32))
    pl.run_scoped(
        functools.partial(
            pointwise_part, ref, *(types.SimpleNamespace(**t) for t in (fetch, stores, held_in, held_out))
        ),
        pltpu.VMEM((cells, CH), jnp.float32),
        pltpu.VMEM((cells, C1), jnp.bfloat16),
    )
    for copy in stores.values():
        copy.wait()


def pointwise_part(ref, fetch, store, held_in, held_out, slopes, spread_all):
    conv, total, sums, extra = ref.conv, ref.total, ref.sums, ref.extra
    gain, w_head = ref.lines.at[3:4, 0:C1P], ref.w_head
    normed, act = held_out.normed, held_out.act
    grad_mixed, grad_branch, grad_summed = (
        held_out.grad_mixed, held_out.grad_branch, held_out.grad_summed
    )
    w_hidden, w_out_t, w_up = held_in.w_hidden, held_in.w_out_t, held_in.w_up
    target, weight, h_zero = held_in.target, held_in.weight, held_in.h_zero
    batch, rows, breadth, _ = ref.padded.shape
    height, half_w = rows - 2 * REACH, breadth - 2 * SIDE

    inside = lax.broadcasted_iota(jnp.int32, (1, C1P), 1) < C1
    values = conv[...] + ref.lines[2:3, :C1P]
    mean = jnp.sum(values, axis=1, keepdims=True) * (1.0 / C1)
    centered = jnp.where(inside, values - mean, 0.0)
    scale = lax.rsqrt(jnp.sum(centered * centered, axis=1, keepdims=True) * (1.0 / C1) + 1e-06)
    conv[...] = centered * scale
    normed[...] = (conv[...] * gain[...] + ref.lines[4:5, :C1P]).astype(jnp.bfloat16)
    store.normed.start()

    fetch.coarse.wait()
    fetch.w_hidden.wait()
    fetch.w_out_t.wait()
    total[...] = held_in.coarse[...]
    for begin in range(0, CH, PART):
        span = slice(begin, min(begin + PART, CH))
        value = product(normed[:, :C1], w_hidden[:, span]) + ref.lines[5:6, span]
        curved, slope = gelu_and_slope(value)
        slopes[:, span] = slope
        act[:, span] = curved.astype(jnp.bfloat16)
        total[:, :C1] += product_t(act[:, span], w_out_t[:, span])
    store.act.start()
    mixed = (total[...] + ref.lines[6:7, :C1P]).astype(jnp.bfloat16)

    for copy in (fetch.h_zero, fetch.target, fetch.weight, fetch.w_up):
        copy.wait()
    grad_mixed[...] = jnp.zeros_like(grad_mixed)
    loss = jnp.zeros((1, CI), jnp.float32)
    head_sum = jnp.zeros((1, CI), jnp.float32)
    up_sum = jnp.zeros((1, C0), jnp.float32)
    for s in range(4):
        sub_y, sub_x = divmod(s, 2)
        for m in range(batch):
            for i in range(height):
                at = rows_at(m, i, height, half_w)
                line = pl.ds(sub_x, half_w, stride=2)
                ref.goal[at, :] = target[m, 2 * i + sub_y, line, :]
                ref.load[at, :] = weight[2 * i + sub_y, line, :]
        w_up_s = w_up[:, s * C0 : (s + 1) * C0]
        upper = product(mixed[:, :C1], w_up_s) + ref.lines[7:8, :C0]
        summed = (upper + h_zero[s, :, :C0]).astype(jnp.bfloat16)
        error = product(summed, w_head[...]) + ref.lines[8:9, :CI] - ref.goal[:, :CI]
        weighted = ref.load[:, :CI] * error
        loss = loss + column_sum(weighted * error)
        grad_out = (2.0 * weighted).astype(jnp.bfloat16)
        head_sum = head_sum + column_sum(grad_out)
        if s == 0:
            ref.d_head[...] = inner_rows(summed, grad_out)
        else:
            ref.d_head[...] += inner_rows(summed, grad_out)
        spread = product_t(grad_out, w_head[...])
        grad_summed[s] = spread
        grad_upper = spread.astype(jnp.bfloat16)
        up_sum = up_sum + column_sum(grad_upper)
        spread_all[:, s * C0 : (s + 1) * C0] = grad_upper
        grad_mixed[:, :C1] += product_t(grad_upper, w_up_s)
    store.grad_summed.start()
    store.grad_mixed.start()
    held_out.d_up[...] = inner_rows(mixed[:, :C1], spread_all[...])
    store.d_up.start()
    grad_branch[...] = grad_mixed[...].astype(jnp.bfloat16)
    store.grad_branch.start()
    sums[...] = jnp.zeros_like(sums)
    extra[...] = jnp.zeros_like(extra)
    extra[0:1, 0:CI] = loss
    extra[1:2, :] = column_sum(ref.weight_map[...])
    sums[1:2, 0:CI] = head_sum
    sums[2:3, 0:C0] = up_sum
    sums[3:4, 0:C1P] = column_sum(grad_branch[...])

    total[...] = jnp.zeros_like(total)
    for begin in range(0, CH, PART):
        span = slice(begin, min(begin + PART, CH))
        value = product(grad_branch[:, :C1], w_out_t[:, span]) * slopes[:, span]
        low = value.astype(jnp.bfloat16)
        ref.grad_pre[:, span] = low
        sums[4:5, span] = column_sum(low)
        total[:, :C1] += product_t(low, w_hidden[:, span])

    grad_normed = total[...]
    sums[5:6, 0:C1P] = column_sum(grad_normed * conv[...])
    sums[6:7, 0:C1P] = column_sum(grad_normed)
    inward = grad_normed * gain[...]
    first = jnp.sum(inward, axis=1, keepdims=True) * (1.0 / C1)
    second = jnp.sum(inward * conv[...], axis=1, keepdims=True) * (1.0 / C1)
    value = scale * jnp.where(inside, inward - first - conv[...] * second, 0.0)
    low = value.astype(jnp.bfloat16)
    sums[7:8, 0:C1P] = column_sum(low)
    ref.grad_conv[...] = low.reshape(ref.grad_conv.shape)


def middle_part(late, **given):
    cells = late["coarse"].shape[0]
    batch, rows, breadth, _ = given["padded"].shape
    half_h, half_w = rows - 2 * REACH, breadth - 2 * SIDE
    vmem = pl.BlockSpec(memory_space=pltpu.VMEM)
    hbm = pl.BlockSpec(memory_space=pl.ANY)
    f32, low = jnp.float32, jnp.bfloat16
    early = dict(
        normed=((cells, C1P), low),
        act=((cells, CH), low),
        grad_mixed=((cells, C1P), f32),
        grad_branch=((cells, C1P), low),
        grad_summed=((4, cells, C0), f32),
        d_up=((C1, C1), f32),
    )
    outs = dict(
        grad_pre=((cells, CH), low),
        grad_conv=((batch, half_h, half_w, C1P), low),
        d_head=((C0, CI), f32),
        sums=((8, CH), f32),
        extra=((8, LANES), f32),
    )
    scratch = dict(
        conv=pltpu.VMEM((cells, C1P), f32),
        total=pltpu.VMEM((cells, C1P), f32),
        goal=pltpu.VMEM((cells, LANES), f32),
        load=pltpu.VMEM((cells, LANES), f32),
        sem_in=pltpu.SemaphoreType.DMA((len(late),)),
        sem_out=pltpu.SemaphoreType.DMA((len(early),)),
    )
    for name, array in late.items():
        scratch["held_" + name] = pltpu.VMEM(array.shape, array.dtype)
    for name, out in early.items():
        scratch["held_" + name] = pltpu.VMEM(*out)
    names = tuple(late) + tuple(given) + tuple(early) + tuple(outs) + tuple(scratch)
    found = pl.pallas_call(
        functools.partial(middle_kernel, names, tuple(late), tuple(early)),
        out_shape=tuple(jax.ShapeDtypeStruct(*out) for out in (early | outs).values()),
        in_specs=[hbm] * len(late) + [vmem] * len(given),
        out_specs=(hbm,) * len(early) + (vmem,) * len(outs),
        scratch_shapes=list(scratch.values()),
        compiler_params=pltpu.CompilerParams(vmem_limit_bytes=62 << 20),
    )(*late.values(), *given.values())
    return types.SimpleNamespace(**dict(zip(early | outs, found)))


def place_rows(source, rows, start, target, width=C1):
    def put(t, value):
        target[pl.ds(start + t, rows, stride=CH // LANES), :] = value

    weave(source, rows, put, width)


def outer_kernel(names, late, *refs):
    table = dict(zip(names, refs))
    ref = types.SimpleNamespace(**table)
    fetch = [
        pltpu.make_async_copy(table[name], table["held_" + name], ref.sem_in.at[i])
        for i, name in enumerate(late)
    ]
    for copy in fetch:
        copy.start()
    stores = [
        pltpu.make_async_copy(
            source.at[pl.ds(0, count)], ref.grad.at[pl.ds(row, count)], ref.sem_out.at[i]
        )
        for i, (source, row, count) in enumerate(
            (
                (ref.piece_head, ROW_AT[6], ROW_AT[7] - ROW_AT[6]),
                (ref.dw_rows, ROW_AT[2], ROW_AT[3] - ROW_AT[2]),
                (ref.down_rows, ROW_AT[1], ROW_AT[2] - ROW_AT[1]),
                (ref.in_rows, 0, ROW_AT[1]),
                (ref.vector_rows, ROW_AT[7], ref.vector_rows.shape[0]),
            )
        )
    ]
    stores[0].start()
    grad_mixed, grad_summed, slope_zero, h_zero, taps, w_down = (table["held_" + name] for name in late)
    held, conv, sums, d_dw, d_in = ref.held, ref.conv, ref.sums, ref.d_dw, ref.d_in
    vector, loose = ref.vector, ref.loose
    grad_conv = ref.grad_conv
    batch, height, half_w, _ = grad_conv.shape
    spread_lanes(ref.padded, held)
    tiles = C1P // LANES
    d_dw[...] = jnp.zeros_like(d_dw)

    def taps_of(number, carry):
        u, m = number // batch, number % batch
        grads = [grad_conv[m, i, :, lanes_at(u)].astype(jnp.float32) for i in range(height)]
        for x in range(7):
            found = [jnp.zeros((8, LANES), jnp.float32) for _ in range(7)]
            for y in range(height + 6):
                window = held[u, m, y, pl.ds(SIDE - REACH + x, half_w), :]
                for i in range(height):
                    if 0 <= y - i < 7:
                        term = (window * grads[i]).reshape(half_w // 8, 8, LANES)
                        found[y - i] = found[y - i] + jnp.sum(term, axis=0)
            for dy in range(7):
                d_dw[u, pl.ds(dy * 7 + x, 1), :] += jnp.sum(found[dy], axis=0, keepdims=True)
        return carry

    lax.fori_loop(0, tiles * batch, taps_of, 0)
    place_rows(d_dw, 13, 0, ref.dw_rows)
    stores[1].start()
    spread_lanes(ref.grad_padded, held)

    def put(u, m, i, value):
        conv[rows_at(m, i, height, half_w), lanes_at(u)] = value

    convolve(held, ref.w_dw, half_w, EDGE, put, True)
    for copy in fetch:
        copy.wait()
    grad_coarse = (conv[...] + grad_mixed[...]).astype(jnp.bfloat16)
    vector[...] = jnp.zeros_like(vector)
    pieces = [(column_sum(grad_coarse), C1)] + [(sums[i : i + 1, :], C1) for i in (7, 5, 6)]
    pieces += [(sums[4:5, :], CH), (sums[3:4, :], C1), (sums[2:3, :], C0), (sums[1:2, :], CI)]
    start = C0
    for piece, size in pieces:
        vector[:, start : start + size] = piece[:, :size]
        start = start + size
    for s in range(4):
        part = inner_rows(h_zero[s].astype(jnp.bfloat16), grad_coarse)
        for u in range(tiles):
            loose[u, s * C0 : (s + 1) * C0, :] = part[:C0, u * LANES : (u + 1) * LANES]
    place_rows(loose, C1 // 4, 0, ref.down_rows)
    stores[2].start()
    in_sum = jnp.zeros((1, C0), jnp.float32)
    for s in range(4):
        grad_h = product_t(grad_coarse, w_down[s])[:, :C0] + grad_summed[s]
        grad_a = (slope_zero[s, :, :C0] * grad_h).astype(jnp.bfloat16)
        in_sum = in_sum + column_sum(grad_a)
        if s == 0:
            d_in[...] = inner_rows(taps[s], grad_a)
        else:
            d_in[...] += inner_rows(taps[s], grad_a)
    vector[:, 0:C0] = in_sum
    for row in range(ref.vector_rows.shape[0]):
        ref.vector_rows[row : row + 1, :] = vector[:, row * LANES : (row + 1) * LANES]
    stores[4].start()

    close = ref.close
    used = 9 * CI
    close[:, used:, :] = jnp.zeros((2, close.shape[1] - used, LANES), jnp.float32)
    for tap in range(9):
        at = slice(tap * CI, (tap + 1) * CI)
        close[0, at, :] = d_in[tap * CIP : tap * CIP + CI, 0:LANES]
        close[1, at, 0 : C0 - LANES] = d_in[tap * CIP : tap * CIP + CI, LANES:C0]
    ref.in_rows[0 : ROW_AT[0], :] = jnp.zeros((ROW_AT[0], LANES), jnp.float32)
    place_rows(close, close.shape[1] * C0 // CH, ROW_AT[0], ref.in_rows, C0)
    stores[3].start()
    for store in stores:
        store.wait()


def outer_part(grad, piece_head, late, **given):
    cells = late["grad_mixed"].shape[0]
    batch, rows, breadth, _ = given["grad_padded"].shape
    vmem = pl.BlockSpec(memory_space=pltpu.VMEM)
    hbm = pl.BlockSpec(memory_space=pl.ANY)
    f32 = jnp.float32
    groups = -(-9 * CI * C0 // CH)
    rest = grad.shape[0] - ROW_AT[7]
    scratch = dict(
        held=pltpu.VMEM((C1P // LANES, batch, rows, breadth, LANES), f32),
        conv=pltpu.VMEM((cells, C1P), f32),
        d_dw=pltpu.VMEM((C1P // LANES, 56, LANES), f32),
        d_in=pltpu.VMEM((9 * CIP, C0), f32),
        vector=pltpu.VMEM((1, rest * LANES), f32),
        vector_rows=pltpu.VMEM((rest, LANES), f32),
        loose=pltpu.VMEM((C1P // LANES, C1, LANES), f32),
        close=pltpu.VMEM((2, groups * CH // C0, LANES), f32),
        dw_rows=pltpu.VMEM((13 * CH // LANES + 3, LANES), f32),
        down_rows=pltpu.VMEM((ROW_AT[2] - ROW_AT[1], LANES), f32),
        in_rows=pltpu.VMEM((ROW_AT[0] + groups * CH // LANES + 4, LANES), f32),
        sem_in=pltpu.SemaphoreType.DMA((len(late),)),
        sem_out=pltpu.SemaphoreType.DMA((5,)),
    )
    for name, array in late.items():
        scratch["held_" + name] = pltpu.VMEM(array.shape, array.dtype)
    names = ("before", "piece_head") + tuple(late) + tuple(given) + ("grad",) + tuple(scratch)
    return pl.pallas_call(
        functools.partial(outer_kernel, names, tuple(late)),
        out_shape=jax.ShapeDtypeStruct(grad.shape, grad.dtype),
        in_specs=[hbm] * (2 + len(late)) + [vmem] * len(given),
        out_specs=hbm,
        input_output_aliases={0: 0},
        scratch_shapes=list(scratch.values()),
        compiler_params=pltpu.CompilerParams(vmem_limit_bytes=62 << 20),
    )(grad, piece_head, *late.values(), *given.values())


def as_rows(piece, rows):
    flat = piece.reshape(-1)
    return jnp.pad(flat, (0, rows * LANES - flat.shape[0])).reshape(rows, LANES)


def widened(array, *shape):
    return jnp.pad(array, [(0, full - now) for full, now in zip(shape, array.shape)])


def on_device(
    inputs,
    targets,
    land_mask,
    volume,
    date_index,
    perm_narrow,
    perm_wide,
    w_in,
    w_down,
    w_dw,
    w_hidden,
    w_out,
    w_up,
    w_head,
    biases_gains,
    moment_first,
    moment_second,
):
    rows, cols = lax.axis_size("rows"), lax.axis_size("cols")
    weight = land_mask.astype(jnp.float32) * volume
    height, breadth = weight.shape
    half_h, half_w = (height // 2, breadth // 2)
    cells = MB * half_h * half_w
    matrices = (w_in, w_down, w_dw, w_hidden, w_out, w_up, w_head)

    def dates(field):
        picked = jnp.concatenate(
            [lax.dynamic_slice_in_dim(field, date_index[m], 1, 0, allow_negative_indices=False) for m in range(MB)]
        )
        return widened(picked, MB, height, breadth, CIP)

    w_in_p = widened(w_in.reshape(9, CI, C0), 9, CIP, C0P).reshape(9 * CIP, C0P)
    w_down_p = widened(w_down.reshape(4, C0, C1), 4, C0P, C1P)
    w_dw_p = widened(w_dw.astype(jnp.float32), 56, C1P)
    weight_map = jnp.broadcast_to(weight[:, :, None], (height, breadth, LANES))

    state = halo(rows, cols, FINE_REACH, dates(inputs), 1)
    taps, slope_zero, h_zero, coarse, padded, lines = input_part(
        rows, state, w_in_p, w_down_p, biases_gains[None, :]
    )
    mid = middle_part(
        dict(
            coarse=coarse, h_zero=h_zero, target=dates(targets).astype(jnp.float32), weight=weight_map,
            w_hidden=w_hidden, w_out_t=w_out.T, w_up=w_up,
        ),
        padded=padded, weight_map=weight, w_dw=w_dw_p, w_head=w_head, lines=lines,
    )
    space = Plan(rows, cols, PADDED).space
    grad, grad_padded = place_gradients(
        rows, cols, space, mid.normed, mid.grad_branch, mid.grad_pre, mid.act,
        perm_narrow, perm_wide, mid.d_up, mid.grad_conv,
    )
    grad = outer_part(
        grad,
        as_rows(mid.d_head, ROW_AT[7] - ROW_AT[6]),
        dict(
            grad_mixed=mid.grad_mixed, grad_summed=mid.grad_summed, slope_zero=slope_zero,
            h_zero=h_zero, taps=taps, w_down=w_down_p,
        ),
        padded=padded, grad_padded=grad_padded, grad_conv=mid.grad_conv, w_dw=w_dw_p, sums=mid.sums,
    )
    plan, (gathered, first, second, totals) = exchange(
        rows, cols, grad, moment_first, moment_second, mid.extra
    )
    hidden_p, out_p, new_up, new_down, small_a, small_b, small_c = unpack(plan, gathered, w_up, w_down, perm_narrow, perm_wide)
    small = {0: (small_a, 0), 2: (small_b, 1), 6: (small_c, 2), 7: (small_c, 2)}
    whole = {
        1: new_down,
        3: rebuild_hidden(hidden_p, perm_wide, w_hidden),
        4: rebuild_out(out_p, perm_narrow, w_out),
        5: new_up,
    }
    olds = matrices + (biases_gains,)
    news = []
    for index, old in enumerate(olds):
        if index in whole:
            news.append(whole[index])
        else:
            source, which = small[index]
            start = FLAT_AT[index] - KEPT[which][0] * LANES
            piece = source.reshape(-1)[start : start + old.size].reshape(old.shape)
            news.append(moved(old, piece) if index < 7 else old - learn_rate * piece)
    return tuple(news) + (
        first.reshape(-1),
        second.reshape(-1),
        totals[0, 0],
        MB * CI * totals[1, 0],
        totals[8, 0],
    )


def solution(mesh):
    return jax.shard_map(
        on_device,
        mesh=mesh,
        in_specs=(
            P(None, "rows", "cols", None),
            P(None, "rows", "cols", None),
            P("rows", "cols"),
            P("rows", "cols"),
            P(),
            P(),
            P(),
            P(),
            P(),
            P(),
            P(),
            P(),
            P(),
            P(),
            P(),
            P(("rows", "cols")),
            P(("rows", "cols")),
        ),
        out_specs=(
            P(),
            P(),
            P(),
            P(),
            P(),
            P(),
            P(),
            P(),
            P(("rows", "cols")),
            P(("rows", "cols")),
            P(),
            P(),
            P(),
        ),
        check_vma=False,
    )
```
